32 devices in a mesh: groups: 2 (over y), dp: 4 (over z), tensor: 4 (over x, core).
Axes of the slice: x: 2, y: 2, z: 4, core: 2. Of those that a mesh axis runs over, the one named last changes fastest.
Arguments:
- inputs: bfloat16 [2048, 11008], P(('groups', 'dp'), 'tensor'), parts along dimension 0, may hold values from -6 to 6
- out_grads: bfloat16 [2048, 4096], P(('groups', 'dp'), 'tensor'), parts along dimension 0
- in_proj: bfloat16 [11008, 64], P('tensor'), may hold values from -0.0546875 to 0.0546875
- out_proj: bfloat16 [4096, 64], P('tensor'), may hold values from -0.09375 to 0.09375
- seq_ids: int32 [2048], P(('groups', 'dp')), parts along dimension 0, may hold values from 0 to 63, as said below
- counts: int32 [128], P(('groups', 'dp')), parts along dimension 0, may hold values from 1 to 241, as said below
- queries: float32 [32, 4096], P(('groups', 'dp')), parts along dimension 0, may hold values from -128 to 128
Outputs:
- scores: float32 [32, 64], P('groups', 'dp'), parts along dimension 0
The draws below stay inside these ranges and needn't reach their ends.
There are 2 independent parts, one for each index of `groups`. The reference program is written for one: setup_inputs(seed, part) draws one part's arguments, and reference() takes and returns one part's arrays. A program takes and returns all parts, laid end to end along the dimension named above; an argument that names none is the same for every part. Nothing has to cross between parts.
Inputs may be any that keep to these rules, and one draw needn't show every extreme that they name: `seq_ids`: never falls along the tokens; tokens 256 * b to 256 * (b + 1) - 1 belong to sequences 16 * b to 16 * (b + 1) - 1, each of which has one token or more. counts[s] is at most the number of tokens of sequence s; some sequence's count equals its number of tokens.
All inputs are finite; a program needn't handle non-finite values.
Results may differ from the reference program's by a relative error of at most 0.0003.
Values sent between devices are 32-bit elements; how exact they have to be, the bound alone decides.
No kernel may reach another device: no remote copies, remote signals or barrier semaphores. Data moves between devices by JAX's collectives and lax.ppermute only.
A program may use at most 128 MiB of HBM per device.

```python
import jax
import jax.numpy as jnp
from jax import lax

D = 4096
FF = 11008
RANK = 64
TOK_DEV = 256
SEQ_DEV = 16
KK = 4096
TOKENS = 1024
SEQS = 64
NQ = 16


def sequence_layout(key):
    blocks = TOKENS // TOK_DEV
    cut_keys = jax.random.split(jax.random.fold_in(key, 71), blocks)

    def cuts_of(one_key):
        return jnp.sort(jax.random.permutation(one_key, TOK_DEV - 1)[:SEQ_DEV - 1] + 1).astype(jnp.int32)
    cuts = jax.vmap(cuts_of)(cut_keys)
    cuts = cuts.at[0].set(jnp.arange(1, SEQ_DEV, dtype=jnp.int32))
    places = jnp.arange(TOK_DEV, dtype=jnp.int32)
    local_ids = jnp.sum((cuts[:, None, :] <= places[None, :, None]).astype(jnp.int32), axis=2)
    base = (jnp.arange(blocks, dtype=jnp.int32) * SEQ_DEV)[:, None]
    seq_ids = (local_ids + base).reshape(TOKENS).astype(jnp.int32)
    edges = jnp.concatenate([jnp.zeros((blocks, 1), jnp.int32), cuts, jnp.full((blocks, 1), TOK_DEV, jnp.int32)], axis=1)
    lengths = edges[:, 1:] - edges[:, :-1]
    counts = jax.random.randint(jax.random.fold_in(key, 72), (blocks, SEQ_DEV), 1, lengths + 1)
    counts = counts.at[0, SEQ_DEV - 1].set(lengths[0, SEQ_DEV - 1])
    return (seq_ids, counts.reshape(SEQS).astype(jnp.int32))


def draw_seq_ids(key, part):
    return sequence_layout(key)[0]


def draw_counts(key, part):
    return sequence_layout(key)[1]


def draw_out_grads(key, part):
    key = jax.random.fold_in(key, 5)
    entry_key, rough_key = jax.random.split(key, 2)
    entries = jax.random.normal(entry_key, (TOKENS, D), jnp.float32)
    place = jnp.arange(TOKENS, dtype=jnp.float32) / TOKENS
    rough = jnp.exp(jax.random.uniform(rough_key, (TOKENS,), jnp.float32, -1.2, 1.2))
    base = entries
    rise = jnp.power(3.0, place)
    return (base * (rise * rough)[:, None]).astype(jnp.bfloat16)


def shard_levels(stream_key, extent, shards, low, top_value):
    factor_of = 1.0
    for axis_at, shards_of in shards:
        draws = jax.random.uniform(jax.random.fold_in(jax.random.fold_in(stream_key, 6), axis_at), (shards_of,), jnp.float32, low / len(shards), top_value / len(shards))
        factor_of = factor_of * jnp.repeat(jnp.exp(draws), extent[axis_at] // shards_of).reshape((-1,) + (1,) * (len(extent) - 1 - axis_at))
    return factor_of


def normal_values(own_key, shape, scale, limit, cuts=(), held_as=jnp.bfloat16):
    result = jax.random.normal(own_key, shape, jnp.float32) * scale
    if len(cuts) > 0:
        result = shard_levels(own_key, shape, cuts, -0.22, 0.18) * result
    return jnp.clip(result, min=-limit, max=limit).astype(held_as)


def setup_inputs(seed: int = 0, part: int = 0) -> dict:
    keys = jax.random.split(jax.random.key(seed), 8)
    part_keys = jax.random.split(jax.random.fold_in(keys[7], part), 8)
    inputs = normal_values(part_keys[0], (TOKENS, FF), 1.0, 6.0, ((0, 4), (1, 4)))
    out_grads = draw_out_grads(jax.random.fold_in(jax.random.fold_in(keys[7], part), 71), part)
    in_proj = normal_values(keys[2], (FF, RANK), FF ** -0.5, 0.0546875, ((0, 4),))
    out_proj = normal_values(keys[3], (D, RANK), D ** -0.5, 0.09375, ((0, 4),))
    seq_ids = draw_seq_ids(jax.random.fold_in(jax.random.fold_in(keys[7], part), 71), part)
    counts = draw_counts(jax.random.fold_in(jax.random.fold_in(keys[7], part), 71), part)
    queries = normal_values(part_keys[6], (NQ, KK), 20.0, 128.0, ((0, 4),), jnp.float32)
    return {"inputs": inputs, "out_grads": out_grads, "in_proj": in_proj, "out_proj": out_proj, "seq_ids": seq_ids, "counts": counts, "queries": queries}


damping = 0.5

def reference(inputs, out_grads, in_proj, out_proj, seq_ids, counts, queries):
    blocks = TOKENS // TOK_DEV
    positions = jnp.arange(TOKENS, dtype=jnp.int32)
    per_seq = jax.ops.segment_sum(jnp.ones((TOKENS,), jnp.int32), seq_ids, num_segments=SEQS)
    starts = (jnp.cumsum(per_seq) - per_seq).astype(jnp.int32)
    offset = positions - starts[seq_ids]
    tok_count = counts[seq_ids]
    weight = jnp.where(offset < tok_count, 1.0 / tok_count.astype(jnp.float32), 0.0).astype(jnp.float32)
    in_f = in_proj.astype(jnp.float32)
    out_f = out_proj.astype(jnp.float32)

    def add_block(total, block):
        x_blk, g_blk, w_blk, id_blk = block
        input_part = jnp.dot(x_blk.astype(jnp.float32), in_f.astype(jnp.float32), precision=lax.Precision.HIGHEST, preferred_element_type=jnp.float32)
        grad_part = jnp.dot(g_blk.astype(jnp.float32), out_f.astype(jnp.float32), precision=lax.Precision.HIGHEST, preferred_element_type=jnp.float32)
        outer = (w_blk[:, None, None] * grad_part[:, :, None] * input_part[:, None, :]).reshape(TOK_DEV, RANK * RANK)
        return (total + jax.ops.segment_sum(outer, id_blk, num_segments=SEQS), None)
    grads, _ = lax.scan(add_block, jnp.zeros((SEQS, RANK * RANK), jnp.float32), (inputs.reshape(blocks, TOK_DEV, FF), out_grads.reshape(blocks, TOK_DEV, D), weight.reshape(blocks, TOK_DEV), seq_ids.reshape(blocks, TOK_DEV)))
    total = jnp.sum(grads * grads)
    damp = damping * total / SEQS
    fisher = jnp.dot(grads.T.astype(jnp.float32), grads.astype(jnp.float32), precision=lax.Precision.HIGHEST, preferred_element_type=jnp.float32)
    fisher = fisher + damp * jnp.eye(RANK * RANK, dtype=jnp.float32)
    factor = jnp.linalg.cholesky(fisher)
    precond = jax.scipy.linalg.cho_solve((factor, True), grads.T)
    return jnp.dot(queries.astype(jnp.float32), precond.astype(jnp.float32), precision=lax.Precision.HIGHEST, preferred_element_type=jnp.float32)
```

```python
import functools

import jax
import jax.numpy as jnp
from jax import lax
from jax.experimental import pallas as pl
from jax.experimental.pallas import tpu as pltpu
from jax.sharding import PartitionSpec as P

damping = 0.5
VMEM_LIMIT = 32 * 1024 * 1024
SMALL = 4


def token_weights(seq_ids, counts, first):
    local_ids = seq_ids - first
    slots = jnp.arange(counts.shape[0], dtype=jnp.int32)
    member = local_ids[None, :] == slots[:, None]
    starts = jnp.sum((local_ids[None, :] < slots[:, None]).astype(jnp.int32), axis=1)
    offset = jnp.arange(seq_ids.shape[0], dtype=jnp.int32)[None, :] - starts[:, None]
    scale = 1.0 / counts.astype(jnp.float32)
    return jnp.where(member & (offset < counts[:, None]), scale[:, None], 0.0)


def cuts_of(extent, step):
    return [(at, min(step, extent - at)) for at in range(0, extent, step)]


def two_terms(value):
    high = value.astype(jnp.bfloat16)
    low = (value - high.astype(jnp.float32)).astype(jnp.bfloat16)
    return high, low


def dot_nt(left, right):
    dims = (((1,), (1,)), ((), ()))
    lh, ll = two_terms(left)
    rh, rl = two_terms(right)
    mul = functools.partial(
        lax.dot_general, dimension_numbers=dims, preferred_element_type=jnp.float32
    )
    return mul(lh, rh) + (mul(lh, rl) + mul(ll, rh))


def project_kernel(parts, own, rank_ref, x_hbm, g_hbm, wx_hbm, wg_hbm, *rest):
    outs = rest[:parts]
    x_ref, g_ref, wx_ref, wg_ref, grad_ref, sems = rest[parts:]
    copies = []

    def fetch(src, dst, index):
        copy = pltpu.make_async_copy(src, dst, sems.at[index])
        copy.start()
        return copy

    g_cuts = cuts_of(g_ref.shape[1], 512)
    x_cuts = cuts_of(x_ref.shape[0], 768)
    wg_copy = fetch(wg_hbm, wg_ref, 0)
    index = 2
    g_copies = []
    for at, size in g_cuts:
        columns = pl.ds(at, size)
        g_copies.append(fetch(g_hbm.at[:, columns], g_ref.at[:, columns], index))
        index += 1
    wx_copy = fetch(wx_hbm, wx_ref, 1)
    x_copies = []
    for at, size in x_cuts:
        rows = pl.ds(at, size)
        x_copies.append(fetch(x_hbm.at[rows, :], x_ref.at[rows, :], index))
        index += 1

    def project(w_copy, w_ref, cuts, copies, ref, along):
        order = 1 if along == 0 else -1
        total = None
        w_copy.wait()
        for (at, size), copy in zip(cuts, copies):
            copy.wait()
            term = lax.dot_general(
                w_ref[:, at : at + size],
                ref[(slice(at, at + size), slice(None))[::order]],
                (((1,), (along,)), ((), ())),
                preferred_element_type=jnp.float32,
            )
            total = term if total is None else total + term
        return total

    grad_ref[...] = project(wg_copy, wg_ref, g_cuts, g_copies, g_ref, 1)
    inputs_t = project(wx_copy, wx_ref, x_cuts, x_copies, x_ref, 0)
    me = rank_ref[0]
    for m in range(parts):
        start = pl.multiple_of((me ^ m) * own, own)
        outs[m][:own, :] = grad_ref[pl.ds(start, own), :]
        outs[m][own:, :] = inputs_t


def project(inputs, out_grads, in_proj, out_proj, me, parts):
    rank = in_proj.shape[1]
    own = rank // parts
    tokens, hidden = inputs.shape
    width = out_grads.shape[1]
    copies = 2 + len(cuts_of(width, 512)) + len(cuts_of(hidden, 768))
    anywhere = pl.BlockSpec(memory_space=pltpu.HBM)
    return pl.pallas_call(
        functools.partial(project_kernel, parts, own),
        out_shape=[jax.ShapeDtypeStruct((own + rank, tokens), jnp.float32)] * parts,
        in_specs=[pl.BlockSpec(memory_space=pltpu.SMEM)] + [anywhere] * 4,
        out_specs=[pl.BlockSpec(memory_space=pltpu.VMEM)] * parts,
        scratch_shapes=[
            pltpu.VMEM((hidden, tokens), jnp.bfloat16),
            pltpu.VMEM((tokens, width), jnp.bfloat16),
            pltpu.VMEM((rank, hidden), jnp.bfloat16),
            pltpu.VMEM((rank, width), jnp.bfloat16),
            pltpu.VMEM((rank, tokens), jnp.float32),
            pltpu.SemaphoreType.DMA((copies,)),
        ],
        compiler_params=pltpu.CompilerParams(vmem_limit_bytes=VMEM_LIMIT),
        name="project",
    )(me, inputs.T, out_grads, in_proj.T, out_proj.T)


def grads_kernel(own, pair, weights_ref, *refs):
    parts, out_ref = refs[:-1], refs[-1]
    while len(parts) > 1:
        parts = [
            (a[...] + b[...]) if b is not None else a[...]
            for a, b in zip(parts[::2], list(parts[1::2]) + [None])
        ]
    summed = parts[0][...]
    weights = weights_ref[...]
    seqs = weights.shape[0]
    inputs_t = summed[own:, :]
    zero = jnp.zeros_like(inputs_t)
    right = jnp.concatenate(
        [
            jnp.concatenate([inputs_t if j == k else zero for k in range(pair)], axis=1)
            for j in range(pair)
        ],
        axis=0,
    )
    rows = []
    for i in range(own // pair):
        rows.append(
            jnp.concatenate(
                [weights * summed[pair * i + j : pair * i + j + 1, :] for j in range(pair)],
                axis=1,
            )
        )
    left = jnp.concatenate(rows, axis=0)
    out_ref[...] = dot_nt(left, right).reshape(own // pair, seqs, right.shape[0])


def gradients(weights, pieces, rank):
    own = pieces[0].shape[0] - rank
    pair = 128 // rank
    return pl.pallas_call(
        functools.partial(grads_kernel, own, pair),
        out_shape=jax.ShapeDtypeStruct(
            (own // pair, weights.shape[0], pair * rank), jnp.float32
        ),
        compiler_params=pltpu.CompilerParams(vmem_limit_bytes=VMEM_LIMIT),
        name="gradients",
    )(weights, *pieces)


def grams_kernel(count, me_ref, *refs):
    grads, queries, out_ref = refs[:count], refs[count:-1], refs[-1]
    me = me_ref[0]
    lanes = [
        jnp.concatenate([block[i] for block in grads], axis=0)
        for i in range(grads[0].shape[0])
    ]
    every = jnp.concatenate(lanes, axis=1)
    given = [block[...] for block in queries]
    ordered = []
    for place in range(count):
        chosen = given[0]
        for m in range(1, count):
            chosen = jnp.where((me ^ place) == m, given[m], chosen)
        ordered.append(chosen)
    both = jnp.concatenate([every] + ordered, axis=0)
    result = dot_nt(both, every)
    half = result.shape[0] // 2
    out_ref[...] = jnp.concatenate([result[:half, :], result[half:, :]], axis=1)


def grams(me, grads, queries):
    seqs = len(grads) * grads[0].shape[1]
    asked = len(queries) * queries[0].shape[0]
    whole = pl.BlockSpec(memory_space=pltpu.VMEM)
    return pl.pallas_call(
        functools.partial(grams_kernel, len(grads)),
        out_shape=jax.ShapeDtypeStruct(((seqs + asked) // 2, 2 * seqs), jnp.float32),
        in_specs=[pl.BlockSpec(memory_space=pltpu.SMEM)] + [whole] * (2 * len(grads)),
        out_specs=whole,
        compiler_params=pltpu.CompilerParams(vmem_limit_bytes=VMEM_LIMIT),
        name="grams",
    )(me, *grads, *queries)


def scales(count):
    first = 2.0 / (1.0 + 1.0 / count)
    off = count / (count + 1.0)
    steps = []
    while off > 1e-7:
        steps.append(2.0 / (2.0 - off * off))
        off = off * off / (2.0 - off * off)
    return first, steps


def solve_kernel(seqs, *refs):
    parts, out_ref = refs[:-1], refs[-1]
    packed = (parts[0][...] + parts[1][...]) + (parts[2][...] + parts[3][...])
    half = packed.shape[0]
    lane = lax.broadcasted_iota(jnp.int32, packed.shape, 1)
    turned = pltpu.roll(packed, seqs, 1)
    both = jnp.concatenate(
        [jnp.where(lane < seqs, packed, turned), jnp.where(lane < seqs, turned, packed)], axis=0
    )
    lane = lax.broadcasted_iota(jnp.int32, both.shape, 1)
    row = lax.broadcasted_iota(jnp.int32, both.shape, 0)
    unit = jnp.where((lane & (seqs - 1)) == row, 1.0, 0.0)
    total = jnp.sum(jnp.where(lane == row, both, 0.0)[:seqs], axis=(0, 1), keepdims=True)
    first, steps = scales(seqs)
    state = first * (both / total + unit * (damping / seqs))
    left_lanes = lane < seqs
    for at, step in enumerate(steps):
        high = state.astype(jnp.bfloat16).astype(jnp.float32)
        low = state - high
        left = jnp.where(left_lanes, high, low).astype(jnp.bfloat16)
        high = high[:seqs].astype(jnp.bfloat16)
        low = low[:seqs].astype(jnp.bfloat16)
        right = jnp.concatenate([high, high, low, low], axis=0)
        if at + 1 == len(steps):
            left, state = left[seqs:], state[seqs:]
        product = jnp.dot(
            jnp.concatenate([left, left], axis=1), right, preferred_element_type=jnp.float32
        )
        state = step * (2.0 * state - product)
    out_ref[...] = state[:, : out_ref.shape[1]]


def solve(parts, seqs, asked, seq_dev):
    return pl.pallas_call(
        functools.partial(solve_kernel, seqs),
        out_shape=jax.ShapeDtypeStruct((asked, seq_dev), jnp.float32),
        compiler_params=pltpu.CompilerParams(vmem_limit_bytes=VMEM_LIMIT),
        name="solve",
    )(*parts)


def from_partners(values, axis, size):
    taken = [values[0]]
    for m in range(1, size):
        taken.append(lax.ppermute(values[m], axis, [(i, i ^ m) for i in range(size)]))
    return taken


def finish_long(grads, queries, first, seq_dev):
    every = lax.all_gather(grads, "dp", axis=0)
    steps, seqs, lanes = grads.shape
    every = every.transpose(0, 2, 1, 3).reshape(-1, steps * lanes)
    asked = lax.all_gather(queries, "dp", axis=0, tiled=True)
    both = jnp.einsum(
        "ik,jk->ij", jnp.concatenate([every, asked], axis=0), every,
        precision=lax.Precision.HIGHEST,
    )
    both = lax.psum(both, "tensor")
    count = every.shape[0]
    kernel, products = both[:count], both[count:]
    damp = damping * jnp.trace(kernel) / count
    unit = jnp.eye(count, dtype=jnp.float32)
    factor = jnp.linalg.cholesky(kernel + damp * unit)
    picks = lax.dynamic_slice_in_dim(unit, first, seq_dev, 1)
    solved = jax.scipy.linalg.cho_solve((factor, True), picks)
    return jnp.dot(products, solved, precision=lax.Precision.HIGHEST)


def per_device(sizes, inputs, out_grads, in_proj, out_proj, seq_ids, counts, queries):
    parts, blocks = sizes
    rank = in_proj.shape[1]
    seq_dev = counts.shape[0]
    me = lax.axis_index("tensor")
    place = lax.axis_index("dp")
    first = place * seq_dev
    own = rank // parts
    pieces = project(inputs, out_grads, in_proj, out_proj, me.reshape(1), parts)
    asked = lax.dynamic_slice_in_dim(queries, me * (own * rank), own * rank, 1)
    weights = token_weights(seq_ids, counts, first)
    pieces = from_partners(pieces, "tensor", parts)
    grads = gradients(weights, pieces, rank)
    if blocks > SMALL:
        return finish_long(grads, asked, first, seq_dev)
    asked = from_partners([asked] * blocks, "dp", blocks)
    grads = from_partners([grads] * blocks, "dp", blocks)
    partial = grams(place.reshape(1), grads, asked)
    partial = from_partners([partial] * parts, "tensor", parts)
    return solve(partial, blocks * seq_dev, blocks * queries.shape[0], seq_dev)


def solution(mesh):
    in_specs = (
        P(("groups", "dp"), "tensor"),
        P(("groups", "dp"), "tensor"),
        P("tensor", None),
        P("tensor", None),
        P(("groups", "dp")),
        P(("groups", "dp")),
        P(("groups", "dp"), None),
    )
    sizes = (mesh.shape["tensor"], mesh.shape["dp"])
    return jax.shard_map(
        functools.partial(per_device, sizes),
        mesh=mesh,
        in_specs=in_specs,
        out_specs=P("groups", "dp"),
        check_vma=False,
    )
```

```python
import functools

import jax
import jax.numpy as jnp
from jax import lax
from jax.experimental import pallas as pl
from jax.experimental.pallas import tpu as pltpu
from jax.sharding import PartitionSpec as P

damping = 0.5
VMEM_LIMIT = 32 * 1024 * 1024
SMALL = 4


def token_weights(seq_ids, counts, first):
    local_ids = seq_ids - first
    slots = jnp.arange(counts.shape[0], dtype=jnp.int32)
    member = local_ids[None, :] == slots[:, None]
    starts = jnp.sum((local_ids[None, :] < slots[:, None]).astype(jnp.int32), axis=1)
    offset = jnp.arange(seq_ids.shape[0], dtype=jnp.int32)[None, :] - starts[:, None]
    scale = 1.0 / counts.astype(jnp.float32)
    return jnp.where(member & (offset < counts[:, None]), scale[:, None], 0.0)


def cuts_of(extent, step):
    return [(at, min(step, extent - at)) for at in range(0, extent, step)]


def two_terms(value):
    high = value.astype(jnp.bfloat16)
    low = (value - high.astype(jnp.float32)).astype(jnp.bfloat16)
    return high, low


def dot_nt(left, right):
    dims = (((1,), (1,)), ((), ()))
    lh, ll = two_terms(left)
    rh, rl = two_terms(right)
    mul = functools.partial(
        lax.dot_general, dimension_numbers=dims, preferred_element_type=jnp.float32
    )
    return mul(lh, rh) + (mul(lh, rl) + mul(ll, rh))


def project_kernel(parts, own, rank_ref, x_hbm, g_hbm, wx_hbm, wg_hbm, *rest):
    outs = rest[:2]
    x_ref, g_ref, wx_ref, wg_ref, grad_ref, sems = rest[2:]
    copies = []

    def fetch(src, dst, index):
        copy = pltpu.make_async_copy(src, dst, sems.at[index])
        copy.start()
        return copy

    g_cuts = cuts_of(g_ref.shape[1], 512)
    x_cuts = cuts_of(x_ref.shape[0], 768)
    wg_copy = fetch(wg_hbm, wg_ref, 0)
    index = 2
    g_copies = []
    for at, size in g_cuts:
        columns = pl.ds(at, size)
        g_copies.append(fetch(g_hbm.at[:, columns], g_ref.at[:, columns], index))
        index += 1
    wx_copy = fetch(wx_hbm, wx_ref, 1)
    x_copies = []
    for at, size in x_cuts:
        rows = pl.ds(at, size)
        x_copies.append(fetch(x_hbm.at[rows, :], x_ref.at[rows, :], index))
        index += 1

    def project(w_copy, w_ref, cuts, copies, ref, along):
        order = 1 if along == 0 else -1
        total = None
        w_copy.wait()
        for (at, size), copy in zip(cuts, copies):
            copy.wait()
            term = lax.dot_general(
                w_ref[:, at : at + size],
                ref[(slice(at, at + size), slice(None))[::order]],
                (((1,), (along,)), ((), ())),
                preferred_element_type=jnp.float32,
            )
            total = term if total is None else total + term
        return total

    grad_ref[...] = project(wg_copy, wg_ref, g_cuts, g_copies, g_ref, 1)
    inputs_t = project(wx_copy, wx_ref, x_cuts, x_copies, x_ref, 0)
    me = rank_ref[0]
    for out, side in zip(outs, (me & 1, (me & 1) ^ 1)):
        for place in range(parts // 2):
            start = pl.multiple_of((2 * place + side) * own, own)
            out[place * own : (place + 1) * own, :] = grad_ref[pl.ds(start, own), :]
        out[parts // 2 * own :, :] = inputs_t


def project(inputs, out_grads, in_proj, out_proj, me, parts):
    rank = in_proj.shape[1]
    own = rank // parts
    tokens, hidden = inputs.shape
    width = out_grads.shape[1]
    copies = 2 + len(cuts_of(width, 512)) + len(cuts_of(hidden, 768))
    arrays = (inputs.T, out_grads, in_proj.T, out_proj.T)
    in_hbm = pl.BlockSpec(memory_space=pltpu.HBM)
    return pl.pallas_call(
        functools.partial(project_kernel, parts, own),
        out_shape=[jax.ShapeDtypeStruct((parts // 2 * own + rank, tokens), jnp.float32)] * 2,
        in_specs=[pl.BlockSpec(memory_space=pltpu.SMEM)] + [in_hbm] * len(arrays),
        out_specs=[pl.BlockSpec(memory_space=pltpu.VMEM)] * 2,
        scratch_shapes=[
            pltpu.VMEM((hidden, tokens), jnp.bfloat16),
            pltpu.VMEM((tokens, width), jnp.bfloat16),
            pltpu.VMEM((rank, hidden), jnp.bfloat16),
            pltpu.VMEM((rank, width), jnp.bfloat16),
            pltpu.VMEM((rank, tokens), jnp.float32),
            pltpu.SemaphoreType.DMA((copies,)),
        ],
        compiler_params=pltpu.CompilerParams(vmem_limit_bytes=VMEM_LIMIT),
        name="project",
    )(me, *(pltpu.with_memory_space_constraint(array, pltpu.HBM) for array in arrays))


def halve_kernel(parts, own, rank_ref, kept_ref, came_ref, keep_ref, send_ref, sum_ref):
    sum_ref[...] = kept_ref[...] + came_ref[...]
    me = rank_ref[0]
    for out, place in ((keep_ref, me // 2), (send_ref, me // 2 ^ 1)):
        start = pl.multiple_of(place * own, own)
        out[:own, :] = sum_ref[pl.ds(start, own), :]
        out[own:, :] = sum_ref[parts // 2 * own :, :]


def halve(kept, came, me, parts, own):
    rows, tokens = kept.shape
    left = rows - (parts // 2 - 1) * own
    whole = pl.BlockSpec(memory_space=pltpu.VMEM)
    return pl.pallas_call(
        functools.partial(halve_kernel, parts, own),
        out_shape=[jax.ShapeDtypeStruct((left, tokens), jnp.float32)] * 2,
        in_specs=[pl.BlockSpec(memory_space=pltpu.SMEM), whole, whole],
        out_specs=[whole] * 2,
        scratch_shapes=[pltpu.VMEM((rows, tokens), jnp.float32)],
        compiler_params=pltpu.CompilerParams(vmem_limit_bytes=VMEM_LIMIT),
        name="halve",
    )(me, kept, came)


def grads_kernel(own, pair, weights_ref, *refs):
    kept_ref, came_ref, out_ref = refs
    summed = kept_ref[...] + came_ref[...]
    weights = weights_ref[...]
    seqs = weights.shape[0]
    inputs_t = summed[own:, :]
    zero = jnp.zeros_like(inputs_t)
    right = jnp.concatenate(
        [
            jnp.concatenate([inputs_t if j == k else zero for k in range(pair)], axis=1)
            for j in range(pair)
        ],
        axis=0,
    )
    rows = []
    for i in range(own // pair):
        rows.append(
            jnp.concatenate(
                [weights * summed[pair * i + j : pair * i + j + 1, :] for j in range(pair)],
                axis=1,
            )
        )
    left = jnp.concatenate(rows, axis=0)
    out_ref[...] = dot_nt(left, right).reshape(own // pair, seqs, right.shape[0])


def gradients(weights, pieces, rank):
    own = pieces[0].shape[0] - rank
    pair = 128 // rank
    return pl.pallas_call(
        functools.partial(grads_kernel, own, pair),
        out_shape=jax.ShapeDtypeStruct(
            (own // pair, weights.shape[0], pair * rank), jnp.float32
        ),
        compiler_params=pltpu.CompilerParams(vmem_limit_bytes=VMEM_LIMIT),
        name="gradients",
    )(weights, *pieces)


def grams_kernel(count, me_ref, *refs):
    grads, queries, out_ref = refs[:count], refs[count:-1], refs[-1]
    me = me_ref[0]
    lanes = [
        jnp.concatenate([block[i] for block in grads], axis=0)
        for i in range(grads[0].shape[0])
    ]
    every = jnp.concatenate(lanes, axis=1)
    given = [block[...] for block in queries]
    ordered = []
    for place in range(count):
        chosen = given[0]
        for m in range(1, count):
            chosen = jnp.where((me ^ place) == m, given[m], chosen)
        ordered.append(chosen)
    both = jnp.concatenate([every] + ordered, axis=0)
    result = dot_nt(both, every)
    half = result.shape[0] // 2
    out_ref[...] = jnp.concatenate([result[:half, :], result[half:, :]], axis=1)


def grams(me, grads, queries):
    seqs = len(grads) * grads[0].shape[1]
    asked = len(queries) * queries[0].shape[0]
    whole = pl.BlockSpec(memory_space=pltpu.VMEM)
    return pl.pallas_call(
        functools.partial(grams_kernel, len(grads)),
        out_shape=jax.ShapeDtypeStruct(((seqs + asked) // 2, 2 * seqs), jnp.float32),
        in_specs=[pl.BlockSpec(memory_space=pltpu.SMEM)] + [whole] * (2 * len(grads)),
        out_specs=whole,
        compiler_params=pltpu.CompilerParams(vmem_limit_bytes=VMEM_LIMIT),
        name="grams",
    )(me, *grads, *queries)


def scales(count):
    first = 2.0 / (1.0 + 1.0 / count)
    off = count / (count + 1.0)
    steps = []
    while off > 1e-7:
        steps.append(2.0 / (2.0 - off * off))
        off = off * off / (2.0 - off * off)
    return first, steps


def solve_kernel(seqs, *refs):
    parts, out_ref = refs[:-1], refs[-1]
    packed = (parts[0][...] + parts[1][...]) + (parts[2][...] + parts[3][...])
    half = packed.shape[0]
    lane = lax.broadcasted_iota(jnp.int32, packed.shape, 1)
    turned = pltpu.roll(packed, seqs, 1)
    both = jnp.concatenate(
        [jnp.where(lane < seqs, packed, turned), jnp.where(lane < seqs, turned, packed)], axis=0
    )
    lane = lax.broadcasted_iota(jnp.int32, both.shape, 1)
    row = lax.broadcasted_iota(jnp.int32, both.shape, 0)
    unit = jnp.where((lane & (seqs - 1)) == row, 1.0, 0.0)
    total = jnp.sum(jnp.where(lane == row, both, 0.0)[:seqs], axis=(0, 1), keepdims=True)
    first, steps = scales(seqs)
    state = first * (both / total + unit * (damping / seqs))
    left_lanes = lane < seqs
    for at, step in enumerate(steps):
        high = state.astype(jnp.bfloat16).astype(jnp.float32)
        low = state - high
        left = jnp.where(left_lanes, high, low).astype(jnp.bfloat16)
        high = high[:seqs].astype(jnp.bfloat16)
        low = low[:seqs].astype(jnp.bfloat16)
        right = jnp.concatenate([high, high, low, low], axis=0)
        if at + 1 == len(steps):
            left, state = left[seqs:], state[seqs:]
        product = jnp.dot(
            jnp.concatenate([left, left], axis=1), right, preferred_element_type=jnp.float32
        )
        state = step * (2.0 * state - product)
    out_ref[...] = state[:, : out_ref.shape[1]]


def solve(parts, seqs, asked, seq_dev):
    return pl.pallas_call(
        functools.partial(solve_kernel, seqs),
        out_shape=jax.ShapeDtypeStruct((asked, seq_dev), jnp.float32),
        compiler_params=pltpu.CompilerParams(vmem_limit_bytes=VMEM_LIMIT),
        name="solve",
    )(*parts)


def from_partner(value, axis, size, m):
    return lax.ppermute(value, axis, [(i, i ^ m) for i in range(size)])


def from_partners(values, axis, size):
    taken = [values[0]]
    for m in range(1, size):
        taken.append(from_partner(values[m], axis, size, m))
    return taken


def finish_long(grads, queries, first, seq_dev):
    every = lax.all_gather(grads, "dp", axis=0)
    steps, seqs, lanes = grads.shape
    every = every.transpose(0, 2, 1, 3).reshape(-1, steps * lanes)
    asked = lax.all_gather(queries, "dp", axis=0, tiled=True)
    both = jnp.einsum(
        "ik,jk->ij", jnp.concatenate([every, asked], axis=0), every,
        precision=lax.Precision.HIGHEST,
    )
    both = lax.psum(both, "tensor")
    count = every.shape[0]
    kernel, products = both[:count], both[count:]
    damp = damping * jnp.trace(kernel) / count
    unit = jnp.eye(count, dtype=jnp.float32)
    factor = jnp.linalg.cholesky(kernel + damp * unit)
    picks = lax.dynamic_slice_in_dim(unit, first, seq_dev, 1)
    solved = jax.scipy.linalg.cho_solve((factor, True), picks)
    return jnp.dot(products, solved, precision=lax.Precision.HIGHEST)


def per_device(sizes, inputs, out_grads, in_proj, out_proj, seq_ids, counts, queries):
    parts, blocks = sizes
    rank = in_proj.shape[1]
    seq_dev = counts.shape[0]
    me = lax.axis_index("tensor")
    place = lax.axis_index("dp")
    first = place * seq_dev
    own = rank // parts
    rank_of = me.reshape(1)
    kept, sent = project(inputs, out_grads, in_proj, out_proj, rank_of, parts)
    asked = lax.dynamic_slice_in_dim(queries, me * (own * rank), own * rank, 1)
    weights = token_weights(seq_ids, counts, first)
    came = from_partner(sent, "tensor", parts, 1)
    kept, sent = halve(kept, came, rank_of, parts, own)
    came = from_partner(sent, "tensor", parts, 2)
    grads = gradients(weights, [kept, came], rank)
    if blocks > SMALL:
        return finish_long(grads, asked, first, seq_dev)
    asked = from_partners([asked] * blocks, "dp", blocks)
    grads, *asked = lax.optimization_barrier((grads, *asked))
    grads = from_partners([grads] * blocks, "dp", blocks)
    partial = grams(place.reshape(1), grads, asked)
    partial = from_partners([partial] * parts, "tensor", parts)
    return solve(partial, blocks * seq_dev, blocks * queries.shape[0], seq_dev)


def solution(mesh):
    in_specs = (
        P(("groups", "dp"), "tensor"),
        P(("groups", "dp"), "tensor"),
        P("tensor", None),
        P("tensor", None),
        P(("groups", "dp")),
        P(("groups", "dp")),
        P(("groups", "dp"), None),
    )
    sizes = (mesh.shape["tensor"], mesh.shape["dp"])
    return jax.shard_map(
        functools.partial(per_device, sizes),
        mesh=mesh,
        in_specs=in_specs,
        out_specs=P("groups", "dp"),
        check_vma=False,
    )
```

```python
import functools

import jax
import jax.numpy as jnp
from jax import lax
from jax.experimental import pallas as pl
from jax.experimental.pallas import tpu as pltpu
from jax.sharding import PartitionSpec as P

damping = 0.5
VMEM_LIMIT = 32 * 1024 * 1024
SMALL = 4


def token_weights(seq_ids, counts, first):
    local_ids = seq_ids - first
    slots = jnp.arange(counts.shape[0], dtype=jnp.int32)
    member = local_ids[None, :] == slots[:, None]
    starts = jnp.sum((local_ids[None, :] < slots[:, None]).astype(jnp.int32), axis=1)
    offset = jnp.arange(seq_ids.shape[0], dtype=jnp.int32)[None, :] - starts[:, None]
    scale = 1.0 / counts.astype(jnp.float32)
    return jnp.where(member & (offset < counts[:, None]), scale[:, None], 0.0)


def cuts_of(extent, step):
    return [(at, min(step, extent - at)) for at in range(0, extent, step)]


def two_terms(value):
    high = value.astype(jnp.bfloat16)
    low = (value - high.astype(jnp.float32)).astype(jnp.bfloat16)
    return high, low


def dot_nt(left, right):
    dims = (((1,), (1,)), ((), ()))
    lh, ll = two_terms(left)
    rh, rl = two_terms(right)
    mul = functools.partial(
        lax.dot_general, dimension_numbers=dims, preferred_element_type=jnp.float32
    )
    return mul(lh, rh) + (mul(lh, rl) + mul(ll, rh))


def project_kernel(parts, own, rank_ref, x_hbm, g_hbm, wx_hbm, wg_hbm, *rest):
    outs = rest[:2]
    x_ref, g_ref, wx_ref, wg_ref, grad_ref, sems = rest[2:]
    copies = []

    def fetch(src, dst, index):
        copy = pltpu.make_async_copy(src, dst, sems.at[index])
        copy.start()
        return copy

    g_cuts = cuts_of(g_ref.shape[1], 512)
    x_cuts = cuts_of(x_ref.shape[0], 768)
    wg_copy = fetch(wg_hbm, wg_ref, 0)
    index = 2
    g_copies = []
    for at, size in g_cuts:
        columns = pl.ds(at, size)
        g_copies.append(fetch(g_hbm.at[:, columns], g_ref.at[:, columns], index))
        index += 1
    wx_copy = fetch(wx_hbm, wx_ref, 1)
    x_copies = []
    for at, size in x_cuts:
        rows = pl.ds(at, size)
        x_copies.append(fetch(x_hbm.at[rows, :], x_ref.at[rows, :], index))
        index += 1

    def project(w_copy, w_ref, cuts, copies, ref, along):
        order = 1 if along == 0 else -1
        total = None
        w_copy.wait()
        for (at, size), copy in zip(cuts, copies):
            copy.wait()
            term = lax.dot_general(
                w_ref[:, at : at + size],
                ref[(slice(at, at + size), slice(None))[::order]],
                (((1,), (along,)), ((), ())),
                preferred_element_type=jnp.float32,
            )
            total = term if total is None else total + term
        return total

    grad_ref[...] = project(wg_copy, wg_ref, g_cuts, g_copies, g_ref, 1)
    inputs_t = project(wx_copy, wx_ref, x_cuts, x_copies, x_ref, 0)
    me = rank_ref[0]
    for out, side in zip(outs, (me & 1, (me & 1) ^ 1)):
        for place in range(parts // 2):
            start = pl.multiple_of((2 * place + side) * own, own)
            out[place * own : (place + 1) * own, :] = grad_ref[pl.ds(start, own), :]
        out[parts // 2 * own :, :] = inputs_t


def project(inputs, out_grads, in_proj, out_proj, me, parts):
    rank = in_proj.shape[1]
    own = rank // parts
    tokens, hidden = inputs.shape
    width = out_grads.shape[1]
    copies = 2 + len(cuts_of(width, 512)) + len(cuts_of(hidden, 768))
    arrays = (inputs.T, out_grads, in_proj.T, out_proj.T)
    in_hbm = pl.BlockSpec(memory_space=pltpu.HBM)
    return pl.pallas_call(
        functools.partial(project_kernel, parts, own),
        out_shape=[jax.ShapeDtypeStruct((parts // 2 * own + rank, tokens), jnp.float32)] * 2,
        in_specs=[pl.BlockSpec(memory_space=pltpu.SMEM)] + [in_hbm] * len(arrays),
        out_specs=[pl.BlockSpec(memory_space=pltpu.VMEM)] * 2,
        scratch_shapes=[
            pltpu.VMEM((hidden, tokens), jnp.bfloat16),
            pltpu.VMEM((tokens, width), jnp.bfloat16),
            pltpu.VMEM((rank, hidden), jnp.bfloat16),
            pltpu.VMEM((rank, width), jnp.bfloat16),
            pltpu.VMEM((rank, tokens), jnp.float32),
            pltpu.SemaphoreType.DMA((copies,)),
        ],
        compiler_params=pltpu.CompilerParams(vmem_limit_bytes=VMEM_LIMIT),
        name="project",
    )(me, *(pltpu.with_memory_space_constraint(array, pltpu.HBM) for array in arrays))


def halve_kernel(parts, own, rank_ref, kept_ref, came_ref, keep_ref, send_ref, sum_ref):
    sum_ref[...] = kept_ref[...] + came_ref[...]
    me = rank_ref[0]
    for out, place in ((keep_ref, me // 2), (send_ref, me // 2 ^ 1)):
        start = pl.multiple_of(place * own, own)
        out[:own, :] = sum_ref[pl.ds(start, own), :]
        out[own:, :] = sum_ref[parts // 2 * own :, :]


def halve(kept, came, me, parts, own):
    rows, tokens = kept.shape
    left = rows - (parts // 2 - 1) * own
    whole = pl.BlockSpec(memory_space=pltpu.VMEM)
    return pl.pallas_call(
        functools.partial(halve_kernel, parts, own),
        out_shape=[jax.ShapeDtypeStruct((left, tokens), jnp.float32)] * 2,
        in_specs=[pl.BlockSpec(memory_space=pltpu.SMEM), whole, whole],
        out_specs=[whole] * 2,
        scratch_shapes=[pltpu.VMEM((rows, tokens), jnp.float32)],
        compiler_params=pltpu.CompilerParams(vmem_limit_bytes=VMEM_LIMIT),
        name="halve",
    )(me, kept, came)


def grads_kernel(own, pair, weights_ref, *refs):
    kept_ref, came_ref, out_ref = refs
    summed = kept_ref[...] + came_ref[...]
    weights = weights_ref[...]
    seqs = weights.shape[0]
    inputs_t = summed[own:, :]
    zero = jnp.zeros_like(inputs_t)
    right = jnp.concatenate(
        [
            jnp.concatenate([inputs_t if j == k else zero for k in range(pair)], axis=1)
            for j in range(pair)
        ],
        axis=0,
    )
    rows = []
    for i in range(own // pair):
        rows.append(
            jnp.concatenate(
                [weights * summed[pair * i + j : pair * i + j + 1, :] for j in range(pair)],
                axis=1,
            )
        )
    left = jnp.concatenate(rows, axis=0)
    made = dot_nt(left, right).reshape(out_ref.shape[1:])
    for place in range(out_ref.shape[0]):
        out_ref[place] = made


def gradients(weights, pieces, rank, copies):
    own = pieces[0].shape[0] - rank
    pair = 128 // rank
    return pl.pallas_call(
        functools.partial(grads_kernel, own, pair),
        out_shape=jax.ShapeDtypeStruct(
            (copies, own // pair, weights.shape[0], pair * rank), jnp.float32
        ),
        compiler_params=pltpu.CompilerParams(vmem_limit_bytes=VMEM_LIMIT),
        name="gradients",
    )(weights, *pieces)


def grams_kernel(grads_ref, queries_ref, out_ref):
    count, steps = grads_ref.shape[:2]
    lanes = [
        jnp.concatenate([grads_ref[place, i] for place in range(count)], axis=0)
        for i in range(steps)
    ]
    every = jnp.concatenate(lanes, axis=1)
    both = jnp.concatenate([every] + [queries_ref[place] for place in range(count)], axis=0)
    result = dot_nt(both, every)
    half = result.shape[0] // 2
    packed = jnp.concatenate([result[:half, :], result[half:, :]], axis=1)
    for place in range(out_ref.shape[0]):
        out_ref[place] = packed


def grams(grads, queries, copies):
    seqs = grads.shape[0] * grads.shape[2]
    asked = queries.shape[0] * queries.shape[1]
    return pl.pallas_call(
        grams_kernel,
        out_shape=jax.ShapeDtypeStruct((copies, (seqs + asked) // 2, 2 * seqs), jnp.float32),
        compiler_params=pltpu.CompilerParams(vmem_limit_bytes=VMEM_LIMIT),
        name="grams",
    )(grads, queries)


def scales(count):
    first = 2.0 / (1.0 + 1.0 / count)
    off = count / (count + 1.0)
    steps = []
    while off > 1e-7:
        steps.append(2.0 / (2.0 - off * off))
        off = off * off / (2.0 - off * off)
    return first, steps


def solve_kernel(seqs, place_ref, parts_ref, out_ref):
    packed = parts_ref[0]
    for part in range(1, parts_ref.shape[0]):
        packed = packed + parts_ref[part]
    lane = lax.broadcasted_iota(jnp.int32, packed.shape, 1)
    turned = pltpu.roll(packed, seqs, 1)
    both = jnp.concatenate(
        [jnp.where(lane < seqs, packed, turned), jnp.where(lane < seqs, turned, packed)], axis=0
    )
    lane = lax.broadcasted_iota(jnp.int32, both.shape, 1)
    row = lax.broadcasted_iota(jnp.int32, both.shape, 0)
    unit = jnp.where((lane & (seqs - 1)) == row, 1.0, 0.0)
    total = jnp.sum(jnp.where(lane == row, both, 0.0)[:seqs], axis=(0, 1), keepdims=True)
    first, steps = scales(seqs)
    state = first * (both / total + unit * (damping / seqs))
    left_lanes = lane < seqs
    for at, step in enumerate(steps):
        high = state.astype(jnp.bfloat16).astype(jnp.float32)
        low = state - high
        left = jnp.where(left_lanes, high, low).astype(jnp.bfloat16)
        high = high[:seqs].astype(jnp.bfloat16)
        low = low[:seqs].astype(jnp.bfloat16)
        right = jnp.concatenate([high, high, low, low], axis=0)
        if at + 1 == len(steps):
            left, state = left[seqs:], state[seqs:]
        product = jnp.dot(
            jnp.concatenate([left, left], axis=1), right, preferred_element_type=jnp.float32
        )
        state = step * (2.0 * state - product)
    turn = 2 * seqs - place_ref[0] * out_ref.shape[1]
    out_ref[...] = pltpu.roll(state, turn, 1)[:, : out_ref.shape[1]]


def solve(place, parts, seqs, asked, seq_dev):
    return pl.pallas_call(
        functools.partial(solve_kernel, seqs),
        out_shape=jax.ShapeDtypeStruct((asked, seq_dev), jnp.float32),
        in_specs=[
            pl.BlockSpec(memory_space=pltpu.SMEM),
            pl.BlockSpec(memory_space=pltpu.VMEM),
        ],
        compiler_params=pltpu.CompilerParams(vmem_limit_bytes=VMEM_LIMIT),
        name="solve",
    )(place, parts)


def from_partner(value, axis, size, m):
    return lax.ppermute(value, axis, [(i, i ^ m) for i in range(size)])


def swap(copies, axis):
    return lax.all_to_all(copies, axis, 0, 0, tiled=True)


def finish_long(grads, queries, first, seq_dev):
    every = lax.all_gather(grads, "dp", axis=0)
    steps, seqs, lanes = grads.shape
    every = every.transpose(0, 2, 1, 3).reshape(-1, steps * lanes)
    asked = lax.all_gather(queries, "dp", axis=0, tiled=True)
    both = jnp.einsum(
        "ik,jk->ij", jnp.concatenate([every, asked], axis=0), every,
        precision=lax.Precision.HIGHEST,
    )
    both = lax.psum(both, "tensor")
    count = every.shape[0]
    kernel, products = both[:count], both[count:]
    damp = damping * jnp.trace(kernel) / count
    unit = jnp.eye(count, dtype=jnp.float32)
    factor = jnp.linalg.cholesky(kernel + damp * unit)
    picks = lax.dynamic_slice_in_dim(unit, first, seq_dev, 1)
    solved = jax.scipy.linalg.cho_solve((factor, True), picks)
    return jnp.dot(products, solved, precision=lax.Precision.HIGHEST)


def per_device(sizes, inputs, out_grads, in_proj, out_proj, seq_ids, counts, queries):
    parts, blocks = sizes
    rank = in_proj.shape[1]
    seq_dev = counts.shape[0]
    me = lax.axis_index("tensor")
    place = lax.axis_index("dp")
    first = place * seq_dev
    own = rank // parts
    rank_of = me.reshape(1)
    kept, sent = project(inputs, out_grads, in_proj, out_proj, rank_of, parts)
    asked = lax.dynamic_slice_in_dim(queries, me * (own * rank), own * rank, 1)
    weights = token_weights(seq_ids, counts, first)
    came = from_partner(sent, "tensor", parts, 1)
    kept, sent = halve(kept, came, rank_of, parts, own)
    came = from_partner(sent, "tensor", parts, 2)
    grads = gradients(weights, [kept, came], rank, blocks if blocks <= SMALL else 1)
    if blocks > SMALL:
        return finish_long(grads[0], asked, first, seq_dev)
    asked = swap(jnp.broadcast_to(asked, (blocks, *asked.shape)), "dp")
    grads, asked = lax.optimization_barrier((grads, asked))
    partial = grams(swap(grads, "dp"), asked, parts)
    summed = swap(partial, "tensor")
    return solve(place.reshape(1), summed, blocks * seq_dev, blocks * queries.shape[0], seq_dev)


def solution(mesh):
    in_specs = (
        P(("groups", "dp"), "tensor"),
        P(("groups", "dp"), "tensor"),
        P("tensor", None),
        P("tensor", None),
        P(("groups", "dp")),
        P(("groups", "dp")),
        P(("groups", "dp"), None),
    )
    sizes = (mesh.shape["tensor"], mesh.shape["dp"])
    return jax.shard_map(
        functools.partial(per_device, sizes),
        mesh=mesh,
        in_specs=in_specs,
        out_specs=P("groups", "dp"),
        check_vma=False,
    )
```

```python
import functools

import jax
import jax.numpy as jnp
from jax import lax
from jax.experimental import pallas as pl
from jax.experimental.pallas import tpu as pltpu
from jax.sharding import PartitionSpec as P

damping = 0.5
VMEM_LIMIT = 32 * 1024 * 1024
SMALL = 4


def token_weights(seq_ids, counts, first):
    local_ids = seq_ids - first
    slots = jnp.arange(counts.shape[0], dtype=jnp.int32)
    member = local_ids[None, :] == slots[:, None]
    starts = jnp.sum((local_ids[None, :] < slots[:, None]).astype(jnp.int32), axis=1)
    offset = jnp.arange(seq_ids.shape[0], dtype=jnp.int32)[None, :] - starts[:, None]
    scale = 1.0 / counts.astype(jnp.float32)
    return jnp.where(member & (offset < counts[:, None]), scale[:, None], 0.0)


def cuts_of(extent, step):
    return [(at, min(step, extent - at)) for at in range(0, extent, step)]


def two_terms(value):
    high = value.astype(jnp.bfloat16)
    low = (value - high.astype(jnp.float32)).astype(jnp.bfloat16)
    return high, low


def dot_nt(left, right):
    dims = (((1,), (1,)), ((), ()))
    lh, ll = two_terms(left)
    rh, rl = two_terms(right)
    mul = functools.partial(
        lax.dot_general, dimension_numbers=dims, preferred_element_type=jnp.float32
    )
    return mul(lh, rh) + (mul(lh, rl) + mul(ll, rh))


def project_kernel(parts, own, rank_ref, x_hbm, g_hbm, wx_hbm, wg_hbm, *rest):
    outs = rest[:2]
    x_ref, g_ref, wx_ref, wg_ref, grad_ref, sems = rest[2:]
    copies = []

    def fetch(src, dst, index):
        copy = pltpu.make_async_copy(src, dst, sems.at[index])
        copy.start()
        return copy

    g_cuts = cuts_of(g_ref.shape[1], 512)
    x_cuts = cuts_of(x_ref.shape[0], 768)
    wg_copy = fetch(wg_hbm, wg_ref, 0)
    index = 2
    g_copies = []
    for at, size in g_cuts:
        columns = pl.ds(at, size)
        g_copies.append(fetch(g_hbm.at[:, columns], g_ref.at[:, columns], index))
        index += 1
    wx_copy = fetch(wx_hbm, wx_ref, 1)
    x_copies = []
    for at, size in x_cuts:
        rows = pl.ds(at, size)
        x_copies.append(fetch(x_hbm.at[rows, :], x_ref.at[rows, :], index))
        index += 1

    def project(w_copy, w_ref, cuts, copies, ref, along):
        order = 1 if along == 0 else -1
        total = None
        w_copy.wait()
        for (at, size), copy in zip(cuts, copies):
            copy.wait()
            term = lax.dot_general(
                w_ref[:, at : at + size],
                ref[(slice(at, at + size), slice(None))[::order]],
                (((1,), (along,)), ((), ())),
                preferred_element_type=jnp.float32,
            )
            total = term if total is None else total + term
        return total

    grad_ref[...] = project(wg_copy, wg_ref, g_cuts, g_copies, g_ref, 1)
    inputs_t = project(wx_copy, wx_ref, x_cuts, x_copies, x_ref, 0)
    me = rank_ref[0]
    for out, side in zip(outs, (me & 1, (me & 1) ^ 1)):
        for place in range(parts // 2):
            start = pl.multiple_of((2 * place + side) * own, own)
            out[place * own : (place + 1) * own, :] = grad_ref[pl.ds(start, own), :]
        out[parts // 2 * own :, :] = inputs_t


def project(inputs, out_grads, in_proj, out_proj, me, parts):
    rank = in_proj.shape[1]
    own = rank // parts
    tokens, hidden = inputs.shape
    width = out_grads.shape[1]
    copies = 2 + len(cuts_of(width, 512)) + len(cuts_of(hidden, 768))
    arrays = (inputs.T, out_grads, in_proj.T, out_proj.T)
    in_hbm = pl.BlockSpec(memory_space=pltpu.HBM)
    return pl.pallas_call(
        functools.partial(project_kernel, parts, own),
        out_shape=[jax.ShapeDtypeStruct((parts // 2 * own + rank, tokens), jnp.float32)] * 2,
        in_specs=[pl.BlockSpec(memory_space=pltpu.SMEM)] + [in_hbm] * len(arrays),
        out_specs=[pl.BlockSpec(memory_space=pltpu.VMEM)] * 2,
        scratch_shapes=[
            pltpu.VMEM((hidden, tokens), jnp.bfloat16),
            pltpu.VMEM((tokens, width), jnp.bfloat16),
            pltpu.VMEM((rank, hidden), jnp.bfloat16),
            pltpu.VMEM((rank, width), jnp.bfloat16),
            pltpu.VMEM((rank, tokens), jnp.float32),
            pltpu.SemaphoreType.DMA((copies,)),
        ],
        compiler_params=pltpu.CompilerParams(vmem_limit_bytes=VMEM_LIMIT),
        name="project",
    )(me, *(pltpu.with_memory_space_constraint(array, pltpu.HBM) for array in arrays))


def halve_kernel(parts, own, rank_ref, kept_ref, came_ref, keep_ref, send_ref, sum_ref):
    sum_ref[...] = kept_ref[...] + came_ref[...]
    me = rank_ref[0]
    for out, place in ((keep_ref, me // 2), (send_ref, me // 2 ^ 1)):
        start = pl.multiple_of(place * own, own)
        out[:own, :] = sum_ref[pl.ds(start, own), :]
        out[own:, :] = sum_ref[parts // 2 * own :, :]


def halve(kept, came, me, parts, own):
    rows, tokens = kept.shape
    left = rows - (parts // 2 - 1) * own
    whole = pl.BlockSpec(memory_space=pltpu.VMEM)
    return pl.pallas_call(
        functools.partial(halve_kernel, parts, own),
        out_shape=[jax.ShapeDtypeStruct((left, tokens), jnp.float32)] * 2,
        in_specs=[pl.BlockSpec(memory_space=pltpu.SMEM), whole, whole],
        out_specs=[whole] * 2,
        scratch_shapes=[pltpu.VMEM((rows, tokens), jnp.float32)],
        compiler_params=pltpu.CompilerParams(vmem_limit_bytes=VMEM_LIMIT),
        name="halve",
    )(me, kept, came)


def grads_kernel(own, pair, weights_ref, *refs):
    kept_ref, came_ref, out_ref = refs
    summed = kept_ref[...] + came_ref[...]
    weights = weights_ref[...]
    seqs = weights.shape[0]
    inputs_t = summed[own:, :]
    zero = jnp.zeros_like(inputs_t)
    right = jnp.concatenate(
        [
            jnp.concatenate([inputs_t if j == k else zero for k in range(pair)], axis=1)
            for j in range(pair)
        ],
        axis=0,
    )
    rows = []
    for i in range(own // pair):
        rows.append(
            jnp.concatenate(
                [weights * summed[pair * i + j : pair * i + j + 1, :] for j in range(pair)],
                axis=1,
            )
        )
    left = jnp.concatenate(rows, axis=0)
    out_ref[...] = dot_nt(left, right).reshape(own // pair, seqs, right.shape[0])


def gradients(weights, pieces, rank):
    own = pieces[0].shape[0] - rank
    pair = 128 // rank
    return pl.pallas_call(
        functools.partial(grads_kernel, own, pair),
        out_shape=jax.ShapeDtypeStruct(
            (own // pair, weights.shape[0], pair * rank), jnp.float32
        ),
        compiler_params=pltpu.CompilerParams(vmem_limit_bytes=VMEM_LIMIT),
        name="gradients",
    )(weights, *pieces)


def grams_kernel(count, me_ref, *refs):
    grads, queries, out_ref = refs[:count], refs[count:-1], refs[-1]
    me = me_ref[0]
    grads, queries = grads[::-1], queries[::-1]
    lanes = [
        jnp.concatenate([block[i] for block in grads], axis=0)
        for i in range(grads[0].shape[0])
    ]
    every = jnp.concatenate(lanes, axis=1)
    given = [block[...] for block in queries]
    ordered = []
    for place in range(count):
        chosen = given[0]
        for m in range(1, count):
            chosen = jnp.where((me ^ place) == m, given[m], chosen)
        ordered.append(chosen)
    both = jnp.concatenate([every] + ordered, axis=0)
    result = dot_nt(both, every)
    half = result.shape[0] // 2
    out_ref[...] = jnp.concatenate([result[:half, :], result[half:, :]], axis=1)


def grams(me, grads, queries):
    seqs = len(grads) * grads[0].shape[1]
    asked = len(queries) * queries[0].shape[0]
    whole = pl.BlockSpec(memory_space=pltpu.VMEM)
    return pl.pallas_call(
        functools.partial(grams_kernel, len(grads)),
        out_shape=jax.ShapeDtypeStruct(((seqs + asked) // 2, 2 * seqs), jnp.float32),
        in_specs=[pl.BlockSpec(memory_space=pltpu.SMEM)] + [whole] * (2 * len(grads)),
        out_specs=whole,
        compiler_params=pltpu.CompilerParams(vmem_limit_bytes=VMEM_LIMIT),
        name="grams",
    )(me, *grads, *queries)


def scales(count):
    first = 2.0 / (1.0 + 1.0 / count)
    off = count / (count + 1.0)
    steps = []
    while off > 1e-7:
        steps.append(2.0 / (2.0 - off * off))
        off = off * off / (2.0 - off * off)
    return first, steps


def solve_kernel(seqs, *refs):
    parts, out_ref = refs[:-1], refs[-1]
    packed = parts[0][...] + parts[1][...]
    lane = lax.broadcasted_iota(jnp.int32, packed.shape, 1)
    turned = pltpu.roll(packed, seqs, 1)
    both = jnp.concatenate(
        [jnp.where(lane < seqs, packed, turned), jnp.where(lane < seqs, turned, packed)], axis=0
    )
    lane = lax.broadcasted_iota(jnp.int32, both.shape, 1)
    row = lax.broadcasted_iota(jnp.int32, both.shape, 0)
    unit = jnp.where((lane & (seqs - 1)) == row, 1.0, 0.0)
    total = jnp.sum(jnp.where(lane == row, both, 0.0)[:seqs], axis=(0, 1), keepdims=True)
    first, steps = scales(seqs)
    state = first * (both / total + unit * (damping / seqs))
    left_lanes = lane < seqs
    for at, step in enumerate(steps):
        high = state.astype(jnp.bfloat16).astype(jnp.float32)
        low = state - high
        left = jnp.where(left_lanes, high, low).astype(jnp.bfloat16)
        high = high[:seqs].astype(jnp.bfloat16)
        low = low[:seqs].astype(jnp.bfloat16)
        right = jnp.concatenate([high, high, low, low], axis=0)
        if at + 1 == len(steps):
            left, state = left[seqs:], state[seqs:]
        product = jnp.dot(
            jnp.concatenate([left, left], axis=1), right, preferred_element_type=jnp.float32
        )
        state = step * (2.0 * state - product)
    out_ref[...] = state[:, : out_ref.shape[1]]


def solve(parts, seqs, asked, seq_dev):
    return pl.pallas_call(
        functools.partial(solve_kernel, seqs),
        out_shape=jax.ShapeDtypeStruct((asked, seq_dev), jnp.float32),
        compiler_params=pltpu.CompilerParams(vmem_limit_bytes=VMEM_LIMIT),
        name="solve",
    )(*parts)


def add_kernel(left_ref, right_ref, out_ref):
    out_ref[...] = left_ref[...] + right_ref[...]


def add(left, right):
    return pl.pallas_call(
        add_kernel,
        out_shape=jax.ShapeDtypeStruct(left.shape, left.dtype),
        compiler_params=pltpu.CompilerParams(vmem_limit_bytes=VMEM_LIMIT),
        name="add",
    )(left, right)


def from_partner(value, axis, size, m):
    return lax.ppermute(value, axis, [(i, i ^ m) for i in range(size)])


def from_partners(value, axis, size):
    return [from_partner(value, axis, size, m) for m in reversed(range(1, size))] + [value]


def finish_long(grads, queries, first, seq_dev):
    every = lax.all_gather(grads, "dp", axis=0)
    steps, seqs, lanes = grads.shape
    every = every.transpose(0, 2, 1, 3).reshape(-1, steps * lanes)
    asked = lax.all_gather(queries, "dp", axis=0, tiled=True)
    both = jnp.einsum(
        "ik,jk->ij", jnp.concatenate([every, asked], axis=0), every,
        precision=lax.Precision.HIGHEST,
    )
    both = lax.psum(both, "tensor")
    count = every.shape[0]
    kernel, products = both[:count], both[count:]
    damp = damping * jnp.trace(kernel) / count
    unit = jnp.eye(count, dtype=jnp.float32)
    factor = jnp.linalg.cholesky(kernel + damp * unit)
    picks = lax.dynamic_slice_in_dim(unit, first, seq_dev, 1)
    solved = jax.scipy.linalg.cho_solve((factor, True), picks)
    return jnp.dot(products, solved, precision=lax.Precision.HIGHEST)


def per_device(sizes, inputs, out_grads, in_proj, out_proj, seq_ids, counts, queries):
    parts, blocks = sizes
    rank = in_proj.shape[1]
    seq_dev = counts.shape[0]
    me = lax.axis_index("tensor")
    place = lax.axis_index("dp")
    first = place * seq_dev
    own = rank // parts
    rank_of = me.reshape(1)
    kept, sent = project(inputs, out_grads, in_proj, out_proj, rank_of, parts)
    asked = lax.dynamic_slice_in_dim(queries, me * (own * rank), own * rank, 1)
    came = from_partner(sent, "tensor", parts, 1)
    kept, sent = halve(kept, came, rank_of, parts, own)
    came = from_partner(sent, "tensor", parts, 2)
    kept, counts = lax.optimization_barrier((kept, counts))
    weights = token_weights(seq_ids, counts, first)
    if blocks <= SMALL:
        weights, asked = lax.optimization_barrier((weights, asked))
        asked = from_partners(asked, "dp", blocks)
    grads = gradients(weights, [kept, came], rank)
    if blocks > SMALL:
        return finish_long(grads, asked, first, seq_dev)
    grads, *asked = lax.optimization_barrier((grads, *asked))
    partial = grams(place.reshape(1), from_partners(grads, "dp", blocks), asked)
    partial = add(partial, from_partner(partial, "tensor", parts, 1))
    partial = [partial, from_partner(partial, "tensor", parts, 2)]
    return solve(partial, blocks * seq_dev, blocks * queries.shape[0], seq_dev)


def solution(mesh):
    in_specs = (
        P(("groups", "dp"), "tensor"),
        P(("groups", "dp"), "tensor"),
        P("tensor", None),
        P("tensor", None),
        P(("groups", "dp")),
        P(("groups", "dp")),
        P(("groups", "dp"), None),
    )
    sizes = (mesh.shape["tensor"], mesh.shape["dp"])
    return jax.shard_map(
        functools.partial(per_device, sizes),
        mesh=mesh,
        in_specs=in_specs,
        out_specs=P("groups", "dp"),
        check_vma=False,
    )
```

```python
import functools

import jax
import jax.numpy as jnp
from jax import lax
from jax.experimental import pallas as pl
from jax.experimental.pallas import tpu as pltpu
from jax.sharding import PartitionSpec as P

damping = 0.5
VMEM_LIMIT = 32 * 1024 * 1024
SMALL = 4


def token_weights(seq_ids, counts, first, works):
    local_ids = seq_ids - first
    slots = jnp.arange(counts.shape[0], dtype=jnp.int32)
    member = local_ids[None, :] == slots[:, None]
    starts = jnp.sum((local_ids[None, :] < slots[:, None]).astype(jnp.int32), axis=1)
    offset = jnp.arange(seq_ids.shape[0], dtype=jnp.int32)[None, :] - starts[:, None]
    scale = works.astype(jnp.float32) / counts.astype(jnp.float32)
    return jnp.where(member & (offset < counts[:, None]), scale[:, None], 0.0)


def cuts_of(extent, step):
    return [(at, min(step, extent - at)) for at in range(0, extent, step)]


def two_terms(value):
    high = value.astype(jnp.bfloat16)
    low = (value - high.astype(jnp.float32)).astype(jnp.bfloat16)
    return high, low


def dot_nt(left, right):
    dims = (((1,), (1,)), ((), ()))
    lh, ll = two_terms(left)
    rh, rl = two_terms(right)
    mul = functools.partial(
        lax.dot_general, dimension_numbers=dims, preferred_element_type=jnp.float32
    )
    return mul(lh, rh) + (mul(lh, rl) + mul(ll, rh))


def project_kernel(x_hbm, g_hbm, wx_hbm, wg_hbm, out_ref, x_ref, g_ref, wx_ref, wg_ref, sems):
    copies = []

    def fetch(src, dst, index):
        copy = pltpu.make_async_copy(src, dst, sems.at[index])
        copy.start()
        return copy

    g_cuts = cuts_of(g_ref.shape[1], 512)
    x_cuts = cuts_of(x_ref.shape[0], 768)
    wg_copy = fetch(wg_hbm, wg_ref, 0)
    index = 2
    g_copies = []
    for at, size in g_cuts:
        columns = pl.ds(at, size)
        g_copies.append(fetch(g_hbm.at[:, columns], g_ref.at[:, columns], index))
        index += 1
    wx_copy = fetch(wx_hbm, wx_ref, 1)
    x_copies = []
    for at, size in x_cuts:
        rows = pl.ds(at, size)
        x_copies.append(fetch(x_hbm.at[rows, :], x_ref.at[rows, :], index))
        index += 1

    def project(w_copy, w_ref, cuts, copies, ref, along):
        order = 1 if along == 0 else -1
        total = None
        w_copy.wait()
        for (at, size), copy in zip(cuts, copies):
            copy.wait()
            term = lax.dot_general(
                w_ref[:, at : at + size],
                ref[(slice(at, at + size), slice(None))[::order]],
                (((1,), (along,)), ((), ())),
                preferred_element_type=jnp.float32,
            )
            total = term if total is None else total + term
        return total

    rank = wg_ref.shape[0]
    out_ref[:rank, :] = project(wg_copy, wg_ref, g_cuts, g_copies, g_ref, 1)
    out_ref[rank:, :] = project(wx_copy, wx_ref, x_cuts, x_copies, x_ref, 0)


def project(inputs, out_grads, in_proj, out_proj):
    rank = in_proj.shape[1]
    tokens, hidden = inputs.shape
    width = out_grads.shape[1]
    copies = 2 + len(cuts_of(width, 512)) + len(cuts_of(hidden, 768))
    arrays = (inputs.T, out_grads, in_proj.T, out_proj.T)
    return pl.pallas_call(
        project_kernel,
        out_shape=jax.ShapeDtypeStruct((2 * rank, tokens), jnp.float32),
        in_specs=[pl.BlockSpec(memory_space=pltpu.HBM)] * len(arrays),
        out_specs=pl.BlockSpec(memory_space=pltpu.VMEM),
        scratch_shapes=[
            pltpu.VMEM((hidden, tokens), jnp.bfloat16),
            pltpu.VMEM((tokens, width), jnp.bfloat16),
            pltpu.VMEM((rank, hidden), jnp.bfloat16),
            pltpu.VMEM((rank, width), jnp.bfloat16),
            pltpu.SemaphoreType.DMA((copies,)),
        ],
        compiler_params=pltpu.CompilerParams(vmem_limit_bytes=VMEM_LIMIT),
        name="project",
    )(*(pltpu.with_memory_space_constraint(array, pltpu.HBM) for array in arrays))


def halve_kernel(own, rank_ref, kept_ref, came_ref, keep_ref, send_ref, sum_ref):
    sum_ref[...] = kept_ref[...] + came_ref[...]
    rank = sum_ref.shape[0] // 2
    place = rank_ref[0] // 2
    for out, taken in ((keep_ref, place), (send_ref, place ^ 1)):
        out[:own, :] = sum_ref[pl.ds(pl.multiple_of(taken * own, own), own), :]
        out[own:, :] = sum_ref[rank:, :]


def halve(kept, came, me, own):
    rows, tokens = kept.shape
    whole = pl.BlockSpec(memory_space=pltpu.VMEM)
    return pl.pallas_call(
        functools.partial(halve_kernel, own),
        out_shape=[jax.ShapeDtypeStruct((own + rows // 2, tokens), jnp.float32)] * 2,
        in_specs=[pl.BlockSpec(memory_space=pltpu.SMEM), whole, whole],
        out_specs=[whole] * 2,
        scratch_shapes=[pltpu.VMEM((rows, tokens), jnp.float32)],
        compiler_params=pltpu.CompilerParams(vmem_limit_bytes=VMEM_LIMIT),
        name="halve",
    )(me, kept, came)


def grads_kernel(own, pair, weights_ref, *refs):
    kept_ref, came_ref, out_ref = refs
    summed = kept_ref[...] + came_ref[...]
    weights = weights_ref[...]
    seqs = weights.shape[0]
    inputs_t = summed[own:, :]
    zero = jnp.zeros_like(inputs_t)
    right = jnp.concatenate(
        [
            jnp.concatenate([inputs_t if j == k else zero for k in range(pair)], axis=1)
            for j in range(pair)
        ],
        axis=0,
    )
    rows = []
    for i in range(own // pair):
        rows.append(
            jnp.concatenate(
                [weights * summed[pair * i + j : pair * i + j + 1, :] for j in range(pair)],
                axis=1,
            )
        )
    left = jnp.concatenate(rows, axis=0)
    out_ref[...] = dot_nt(left, right).reshape(own // pair, seqs, right.shape[0])


def gradients(weights, pieces, rank):
    own = pieces[0].shape[0] - rank
    pair = 128 // rank
    return pl.pallas_call(
        functools.partial(grads_kernel, own, pair),
        out_shape=jax.ShapeDtypeStruct(
            (own // pair, weights.shape[0], pair * rank), jnp.float32
        ),
        compiler_params=pltpu.CompilerParams(vmem_limit_bytes=VMEM_LIMIT),
        name="gradients",
    )(weights, *pieces)


def collect_kernel(place_ref, *refs):
    given, out_ref = [ref[...] for ref in refs[:-1]], refs[-1]
    count = len(given)
    rows = given[0].shape[0]
    ordered = []
    for place in range(count):
        chosen = given[0]
        for m in range(1, count):
            chosen = jnp.where((place_ref[0] ^ place) == m, given[m], chosen)
        ordered.append(chosen)
    out_ref[...] = jnp.concatenate(ordered, axis=0)


def collect(place, blocks):
    rows, columns = blocks[0].shape
    whole = pl.BlockSpec(memory_space=pltpu.VMEM)
    return pl.pallas_call(
        collect_kernel,
        out_shape=jax.ShapeDtypeStruct((len(blocks) * rows, columns), jnp.float32),
        in_specs=[pl.BlockSpec(memory_space=pltpu.SMEM)] + [whole] * len(blocks),
        out_specs=whole,
        compiler_params=pltpu.CompilerParams(vmem_limit_bytes=VMEM_LIMIT),
        name="collect",
    )(place, *blocks)


def grams_kernel(*refs):
    grads, queries_ref, out_ref = refs[-3::-1], refs[-2], refs[-1]
    lanes = [
        jnp.concatenate([block[i] for block in grads], axis=0)
        for i in range(grads[0].shape[0])
    ]
    every = jnp.concatenate(lanes, axis=1)
    both = jnp.concatenate([every, queries_ref[...]], axis=0)
    result = dot_nt(both, every)
    half = result.shape[0] // 2
    out_ref[...] = jnp.concatenate([result[:half, :], result[half:, :]], axis=1)


def grams(grads, queries):
    seqs = len(grads) * grads[0].shape[1]
    return pl.pallas_call(
        grams_kernel,
        out_shape=jax.ShapeDtypeStruct(((seqs + queries.shape[0]) // 2, 2 * seqs), jnp.float32),
        compiler_params=pltpu.CompilerParams(vmem_limit_bytes=VMEM_LIMIT),
        name="grams",
    )(*grads, queries)


def scales(count):
    first = 2.0 / (1.0 + 1.0 / count)
    off = count / (count + 1.0)
    steps = []
    while off > 1e-7:
        steps.append(2.0 / (2.0 - off * off))
        off = off * off / (2.0 - off * off)
    return first, steps


def solve_kernel(seqs, *refs):
    parts, out_ref = refs[:-1], refs[-1]
    packed = (parts[0][...] + parts[1][...]) + (parts[2][...] + parts[3][...])
    lane = lax.broadcasted_iota(jnp.int32, packed.shape, 1)
    turned = pltpu.roll(packed, seqs, 1)
    both = jnp.concatenate(
        [jnp.where(lane < seqs, packed, turned), jnp.where(lane < seqs, turned, packed)], axis=0
    )
    lane = lax.broadcasted_iota(jnp.int32, both.shape, 1)
    row = lax.broadcasted_iota(jnp.int32, both.shape, 0)
    unit = jnp.where((lane & (seqs - 1)) == row, 1.0, 0.0)
    total = jnp.sum(jnp.where(lane == row, both, 0.0)[:seqs], axis=(0, 1), keepdims=True)
    first, steps = scales(seqs)
    state = first * (both / total + unit * (damping / seqs))
    left_lanes = lane < seqs
    for at, step in enumerate(steps):
        high = state.astype(jnp.bfloat16).astype(jnp.float32)
        low = state - high
        left = jnp.where(left_lanes, high, low).astype(jnp.bfloat16)
        high = high[:seqs].astype(jnp.bfloat16)
        low = low[:seqs].astype(jnp.bfloat16)
        right = jnp.concatenate([high, high, low, low], axis=0)
        if at + 1 == len(steps):
            left, state = left[seqs:], state[seqs:]
        product = jnp.dot(
            jnp.concatenate([left, left], axis=1), right, preferred_element_type=jnp.float32
        )
        state = step * (2.0 * state - product)
    out_ref[...] = state[:, : out_ref.shape[1]]


def solve(parts, seqs, asked, seq_dev):
    return pl.pallas_call(
        functools.partial(solve_kernel, seqs),
        out_shape=jax.ShapeDtypeStruct((asked, seq_dev), jnp.float32),
        compiler_params=pltpu.CompilerParams(vmem_limit_bytes=VMEM_LIMIT),
        name="solve",
    )(*parts)


def move(value, sizes, target):
    parts, blocks = sizes
    pairs = []
    for d in range(blocks):
        for r in range(parts):
            to = target(d, r)
            if to is not None:
                pairs.append((d * parts + r, to[0] * parts + to[1]))
    return lax.ppermute(value, ("dp", "tensor"), pairs)


def over_blocks(value, sizes, side):
    came = [
        move(value, sizes, lambda d, r: (d ^ m, r) if r % 2 == side else None)
        for m in reversed(range(1, sizes[1]))
    ]
    return came + [value]


def finish_long(grads, queries, first, seq_dev):
    every = lax.all_gather(grads, "dp", axis=0)
    steps, seqs, lanes = grads.shape
    every = every.transpose(0, 2, 1, 3).reshape(-1, steps * lanes)
    asked = lax.all_gather(queries, "dp", axis=0, tiled=True)
    both = jnp.einsum(
        "ik,jk->ij", jnp.concatenate([every, asked], axis=0), every,
        precision=lax.Precision.HIGHEST,
    )
    both = lax.psum(both, "tensor")
    count = every.shape[0]
    kernel, products = both[:count], both[count:]
    damp = damping * jnp.trace(kernel) / count
    unit = jnp.eye(count, dtype=jnp.float32)
    factor = jnp.linalg.cholesky(kernel + damp * unit)
    picks = lax.dynamic_slice_in_dim(unit, first, seq_dev, 1)
    solved = jax.scipy.linalg.cho_solve((factor, True), picks)
    return jnp.dot(products, solved, precision=lax.Precision.HIGHEST)


def per_device(sizes, inputs, out_grads, in_proj, out_proj, seq_ids, counts, queries):
    parts, blocks = sizes
    rank = in_proj.shape[1]
    seq_dev = counts.shape[0]
    me = lax.axis_index("tensor")
    place = lax.axis_index("dp")
    first = place * seq_dev
    own = rank // (parts // 2)
    rank_of = me.reshape(1)
    weights = token_weights(seq_ids, counts, first, me % 2)
    asked = lax.dynamic_slice_in_dim(queries, (me // 2) * (own * rank), own * rank, 1)
    kept = project(inputs, out_grads, in_proj, out_proj)
    came = move(kept, sizes, lambda d, r: (d, r + 1) if r % 2 == 0 else None)
    kept, sent = halve(kept, came, rank_of, own)
    came = move(sent, sizes, lambda d, r: (d, r ^ 2) if r % 2 == 1 else None)
    grads = gradients(weights, [kept, came], rank)
    if blocks > SMALL:
        return finish_long(grads, asked, first, seq_dev)
    sent, asked = lax.optimization_barrier((sent, asked))
    asked = collect(place.reshape(1), over_blocks(asked, sizes, 0)[::-1])
    asked = move(asked, sizes, lambda d, r: (d, r + 1) if r % 2 == 0 else None)
    partial = grams(over_blocks(grads, sizes, 1), asked)
    partial = [partial] + [
        move(partial, sizes, lambda d, r: (d, r ^ m) if r % 2 == 1 else None) for m in (2, 3, 1)
    ]
    return solve(partial, blocks * seq_dev, asked.shape[0], seq_dev)


def solution(mesh):
    in_specs = (
        P(("groups", "dp"), "tensor"),
        P(("groups", "dp"), "tensor"),
        P("tensor", None),
        P("tensor", None),
        P(("groups", "dp")),
        P(("groups", "dp")),
        P(("groups", "dp"), None),
    )
    sizes = (mesh.shape["tensor"], mesh.shape["dp"])
    return jax.shard_map(
        functools.partial(per_device, sizes),
        mesh=mesh,
        in_specs=in_specs,
        out_specs=P("groups", "dp"),
        check_vma=False,
    )
```

```python
import functools

import jax
import jax.numpy as jnp
from jax import lax
from jax.experimental import pallas as pl
from jax.experimental.pallas import tpu as pltpu
from jax.sharding import PartitionSpec as P

damping = 0.5
VMEM_LIMIT = 32 * 1024 * 1024
SMALL = 4


def token_weights(seq_ids, counts, first):
    local_ids = seq_ids - first
    slots = jnp.arange(counts.shape[0], dtype=jnp.int32)
    member = local_ids[None, :] == slots[:, None]
    starts = jnp.sum((local_ids[None, :] < slots[:, None]).astype(jnp.int32), axis=1)
    offset = jnp.arange(seq_ids.shape[0], dtype=jnp.int32)[None, :] - starts[:, None]
    scale = 1.0 / counts.astype(jnp.float32)
    return jnp.where(member & (offset < counts[:, None]), scale[:, None], 0.0)


def cuts_of(extent, step):
    return [(at, min(step, extent - at)) for at in range(0, extent, step)]


def two_terms(value):
    high = value.astype(jnp.bfloat16)
    low = (value - high.astype(jnp.float32)).astype(jnp.bfloat16)
    return high, low


def dot_nt(left, right):
    dims = (((1,), (1,)), ((), ()))
    lh, ll = two_terms(left)
    rh, rl = two_terms(right)
    mul = functools.partial(
        lax.dot_general, dimension_numbers=dims, preferred_element_type=jnp.float32
    )
    return mul(lh, rh) + (mul(lh, rl) + mul(ll, rh))


def project_kernel(parts, own, rank_ref, x_hbm, g_hbm, wx_hbm, wg_hbm, *rest):
    outs = rest[:2]
    x_ref, g_ref, wx_ref, wg_ref, grad_ref, sems = rest[2:]
    copies = []

    def fetch(src, dst, index):
        copy = pltpu.make_async_copy(src, dst, sems.at[index])
        copy.start()
        return copy

    g_cuts = cuts_of(g_ref.shape[1], 512)
    x_cuts = cuts_of(x_ref.shape[0], 768)
    wg_copy = fetch(wg_hbm, wg_ref, 0)
    index = 2
    g_copies = []
    for at, size in g_cuts:
        columns = pl.ds(at, size)
        g_copies.append(fetch(g_hbm.at[:, columns], g_ref.at[:, columns], index))
        index += 1
    wx_copy = fetch(wx_hbm, wx_ref, 1)
    x_copies = []
    for at, size in x_cuts:
        rows = pl.ds(at, size)
        x_copies.append(fetch(x_hbm.at[rows, :], x_ref.at[rows, :], index))
        index += 1

    def project(w_copy, w_ref, cuts, copies, ref, along):
        order = 1 if along == 0 else -1
        total = None
        w_copy.wait()
        for (at, size), copy in zip(cuts, copies):
            copy.wait()
            term = lax.dot_general(
                w_ref[:, at : at + size],
                ref[(slice(at, at + size), slice(None))[::order]],
                (((1,), (along,)), ((), ())),
                preferred_element_type=jnp.float32,
            )
            total = term if total is None else total + term
        return total

    grad_ref[...] = project(wg_copy, wg_ref, g_cuts, g_copies, g_ref, 1)
    inputs_t = project(wx_copy, wx_ref, x_cuts, x_copies, x_ref, 0)
    me = rank_ref[0]
    for out, side in zip(outs, (me & 1, (me & 1) ^ 1)):
        for place in range(parts // 2):
            start = pl.multiple_of((2 * place + side) * own, own)
            out[place * own : (place + 1) * own, :] = grad_ref[pl.ds(start, own), :]
        out[parts // 2 * own :, :] = inputs_t


def project(inputs, out_grads, in_proj, out_proj, me, parts):
    rank = in_proj.shape[1]
    own = rank // parts
    tokens, hidden = inputs.shape
    width = out_grads.shape[1]
    copies = 2 + len(cuts_of(width, 512)) + len(cuts_of(hidden, 768))
    arrays = (inputs.T, out_grads, in_proj.T, out_proj.T)
    in_hbm = pl.BlockSpec(memory_space=pltpu.HBM)
    return pl.pallas_call(
        functools.partial(project_kernel, parts, own),
        out_shape=[jax.ShapeDtypeStruct((parts // 2 * own + rank, tokens), jnp.float32)] * 2,
        in_specs=[pl.BlockSpec(memory_space=pltpu.SMEM)] + [in_hbm] * len(arrays),
        out_specs=[pl.BlockSpec(memory_space=pltpu.VMEM)] * 2,
        scratch_shapes=[
            pltpu.VMEM((hidden, tokens), jnp.bfloat16),
            pltpu.VMEM((tokens, width), jnp.bfloat16),
            pltpu.VMEM((rank, hidden), jnp.bfloat16),
            pltpu.VMEM((rank, width), jnp.bfloat16),
            pltpu.VMEM((rank, tokens), jnp.float32),
            pltpu.SemaphoreType.DMA((copies,)),
        ],
        compiler_params=pltpu.CompilerParams(vmem_limit_bytes=VMEM_LIMIT),
        name="project",
    )(me, *(pltpu.with_memory_space_constraint(array, pltpu.HBM) for array in arrays))


def halve_kernel(parts, own, rank_ref, kept_ref, came_ref, keep_ref, send_ref, sum_ref):
    sum_ref[...] = kept_ref[...] + came_ref[...]
    me = rank_ref[0]
    for out, place in ((keep_ref, me // 2), (send_ref, me // 2 ^ 1)):
        start = pl.multiple_of(place * own, own)
        out[:own, :] = sum_ref[pl.ds(start, own), :]
        out[own:, :] = sum_ref[parts // 2 * own :, :]


def halve(kept, came, me, parts, own):
    rows, tokens = kept.shape
    left = rows - (parts // 2 - 1) * own
    whole = pl.BlockSpec(memory_space=pltpu.VMEM)
    return pl.pallas_call(
        functools.partial(halve_kernel, parts, own),
        out_shape=[jax.ShapeDtypeStruct((left, tokens), jnp.float32)] * 2,
        in_specs=[pl.BlockSpec(memory_space=pltpu.SMEM), whole, whole],
        out_specs=[whole] * 2,
        scratch_shapes=[pltpu.VMEM((rows, tokens), jnp.float32)],
        compiler_params=pltpu.CompilerParams(vmem_limit_bytes=VMEM_LIMIT),
        name="halve",
    )(me, kept, came)


def grads_kernel(own, pair, weights_ref, kept_ref, came_ref, asked_ref, out_ref):
    summed = kept_ref[...] + came_ref[...]
    weights = weights_ref[...]
    seqs = weights.shape[0]
    inputs_t = summed[own:, :]
    zero = jnp.zeros_like(inputs_t)
    right = jnp.concatenate(
        [
            jnp.concatenate([inputs_t if j == k else zero for k in range(pair)], axis=1)
            for j in range(pair)
        ],
        axis=0,
    )
    rows = []
    for i in range(own // pair):
        rows.append(
            jnp.concatenate(
                [weights * summed[pair * i + j : pair * i + j + 1, :] for j in range(pair)],
                axis=1,
            )
        )
    left = jnp.concatenate(rows, axis=0)
    count, lanes = left.shape[0], right.shape[0]
    out_ref[:count, :] = dot_nt(left, right)
    asked = asked_ref.shape[0]
    for i in range(own // pair):
        start = count + i * asked
        out_ref[start : start + asked, :] = asked_ref[:, i * lanes : (i + 1) * lanes]


def gradients(weights, kept, came, asked, rank):
    own = kept.shape[0] - rank
    pair = 128 // rank
    steps = own // pair
    rows = steps * (weights.shape[0] + asked.shape[0])
    return pl.pallas_call(
        functools.partial(grads_kernel, own, pair),
        out_shape=jax.ShapeDtypeStruct((rows, pair * rank), jnp.float32),
        compiler_params=pltpu.CompilerParams(vmem_limit_bytes=VMEM_LIMIT),
        name="gradients",
    )(weights, kept, came, asked)


def grams_kernel(steps, seqs, me_ref, *refs):
    blocks, out_ref = refs[-2::-1], refs[-1]
    count = steps * seqs
    asked = (blocks[0].shape[0] - count) // steps
    given = [block[count:, :] for block in blocks]
    ordered = []
    for place in range(len(blocks)):
        chosen = given[0]
        for m in range(1, len(blocks)):
            chosen = jnp.where((me_ref[0] ^ place) == m, given[m], chosen)
        ordered.append(chosen)
    lanes = []
    for i in range(steps):
        rows = [block[i * seqs : (i + 1) * seqs, :] for block in blocks]
        rows += [chosen[i * asked : (i + 1) * asked, :] for chosen in ordered]
        lanes.append(jnp.concatenate(rows, axis=0))
    both = jnp.concatenate(lanes, axis=1)
    result = dot_nt(both, both[: len(blocks) * seqs])
    half = result.shape[0] // 2
    out_ref[...] = jnp.concatenate([result[:half, :], result[half:, :]], axis=1)


def grams(me, blocks, steps, seqs):
    asked = blocks[0].shape[0] // steps - seqs
    total = len(blocks) * seqs
    whole = pl.BlockSpec(memory_space=pltpu.VMEM)
    return pl.pallas_call(
        functools.partial(grams_kernel, steps, seqs),
        out_shape=jax.ShapeDtypeStruct(((total + len(blocks) * asked) // 2, 2 * total), jnp.float32),
        in_specs=[pl.BlockSpec(memory_space=pltpu.SMEM)] + [whole] * len(blocks),
        out_specs=whole,
        compiler_params=pltpu.CompilerParams(vmem_limit_bytes=VMEM_LIMIT),
        name="grams",
    )(me, *blocks)


def scales(count):
    first = 2.0 / (1.0 + 1.0 / count)
    off = count / (count + 1.0)
    steps = []
    while off > 1e-7:
        steps.append(2.0 / (2.0 - off * off))
        off = off * off / (2.0 - off * off)
    return first, steps


def solve_kernel(seqs, *refs):
    parts, out_ref = refs[:-1], refs[-1]
    packed = (parts[0][...] + parts[1][...]) + (parts[2][...] + parts[3][...])
    lane = lax.broadcasted_iota(jnp.int32, packed.shape, 1)
    turned = pltpu.roll(packed, seqs, 1)
    both = jnp.concatenate(
        [jnp.where(lane < seqs, packed, turned), jnp.where(lane < seqs, turned, packed)], axis=0
    )
    lane = lax.broadcasted_iota(jnp.int32, both.shape, 1)
    row = lax.broadcasted_iota(jnp.int32, both.shape, 0)
    unit = jnp.where((lane & (seqs - 1)) == row, 1.0, 0.0)
    total = jnp.sum(jnp.where(lane == row, both, 0.0)[:seqs], axis=(0, 1), keepdims=True)
    first, steps = scales(seqs)
    state = first * (both / total + unit * (damping / seqs))
    left_lanes = lane < seqs
    for at, step in enumerate(steps):
        high = state.astype(jnp.bfloat16).astype(jnp.float32)
        low = state - high
        left = jnp.where(left_lanes, high, low).astype(jnp.bfloat16)
        high = high[:seqs].astype(jnp.bfloat16)
        low = low[:seqs].astype(jnp.bfloat16)
        right = jnp.concatenate([high, high, low, low], axis=0)
        if at + 1 == len(steps):
            left, state = left[seqs:], state[seqs:]
        product = jnp.dot(
            jnp.concatenate([left, left], axis=1), right, preferred_element_type=jnp.float32
        )
        state = step * (2.0 * state - product)
    out_ref[...] = state[:, : out_ref.shape[1]]


def solve(parts, seqs, asked, seq_dev):
    return pl.pallas_call(
        functools.partial(solve_kernel, seqs),
        out_shape=jax.ShapeDtypeStruct((asked, seq_dev), jnp.float32),
        compiler_params=pltpu.CompilerParams(vmem_limit_bytes=VMEM_LIMIT),
        name="solve",
    )(*parts)


def from_partner(value, axis, size, m):
    return lax.ppermute(value, axis, [(i, i ^ m) for i in range(size)])


def from_partners(value, axis, size):
    return [from_partner(value, axis, size, m) for m in reversed(range(1, size))] + [value]


def finish_long(message, steps, first, seq_dev):
    every = lax.all_gather(message, "dp", axis=0)
    lanes = message.shape[1]

    def rows_of(block):
        block = block.reshape(block.shape[0], steps, -1, lanes).transpose(0, 2, 1, 3)
        return block.reshape(-1, steps * lanes)

    count = steps * seq_dev
    grads, asked = rows_of(every[:, :count]), rows_of(every[:, count:])
    both = jnp.einsum(
        "ik,jk->ij", jnp.concatenate([grads, asked], axis=0), grads,
        precision=lax.Precision.HIGHEST,
    )
    both = lax.psum(both, "tensor")
    count = grads.shape[0]
    kernel, products = both[:count], both[count:]
    damp = damping * jnp.trace(kernel) / count
    unit = jnp.eye(count, dtype=jnp.float32)
    factor = jnp.linalg.cholesky(kernel + damp * unit)
    picks = lax.dynamic_slice_in_dim(unit, first, seq_dev, 1)
    solved = jax.scipy.linalg.cho_solve((factor, True), picks)
    return jnp.dot(products, solved, precision=lax.Precision.HIGHEST)


def per_device(sizes, inputs, out_grads, in_proj, out_proj, seq_ids, counts, queries):
    parts, blocks = sizes
    rank = in_proj.shape[1]
    seq_dev = counts.shape[0]
    me = lax.axis_index("tensor")
    place = lax.axis_index("dp")
    first = place * seq_dev
    own = rank // parts
    rank_of = me.reshape(1)
    kept, sent = project(inputs, out_grads, in_proj, out_proj, rank_of, parts)
    asked = lax.dynamic_slice_in_dim(queries, me * (own * rank), own * rank, 1)
    weights = token_weights(seq_ids, counts, first)
    came = from_partner(sent, "tensor", parts, 1)
    kept, sent = halve(kept, came, rank_of, parts, own)
    came = from_partner(sent, "tensor", parts, 2)
    message = gradients(weights, kept, came, asked, rank)
    steps = own * rank // message.shape[1]
    if blocks > SMALL:
        return finish_long(message, steps, first, seq_dev)
    partial = grams(place.reshape(1), from_partners(message, "dp", blocks), steps, seq_dev)
    partial = from_partners(partial, "tensor", parts)
    return solve(partial, blocks * seq_dev, blocks * queries.shape[0], seq_dev)


def solution(mesh):
    in_specs = (
        P(("groups", "dp"), "tensor"),
        P(("groups", "dp"), "tensor"),
        P("tensor", None),
        P("tensor", None),
        P(("groups", "dp")),
        P(("groups", "dp")),
        P(("groups", "dp"), None),
    )
    sizes = (mesh.shape["tensor"], mesh.shape["dp"])
    return jax.shard_map(
        functools.partial(per_device, sizes),
        mesh=mesh,
        in_specs=in_specs,
        out_specs=P("groups", "dp"),
        check_vma=False,
    )
```

```python
import functools

import jax
import jax.numpy as jnp
from jax import lax
from jax.experimental import pallas as pl
from jax.experimental.pallas import tpu as pltpu
from jax.sharding import PartitionSpec as P

damping = 0.5
VMEM_LIMIT = 32 * 1024 * 1024
SMALL = 4


def token_weights(seq_ids, counts, first):
    local_ids = seq_ids - first
    slots = jnp.arange(counts.shape[0], dtype=jnp.int32)
    member = local_ids[None, :] == slots[:, None]
    starts = jnp.sum((local_ids[None, :] < slots[:, None]).astype(jnp.int32), axis=1)
    offset = jnp.arange(seq_ids.shape[0], dtype=jnp.int32)[None, :] - starts[:, None]
    scale = 1.0 / counts.astype(jnp.float32)
    return jnp.where(member & (offset < counts[:, None]), scale[:, None], 0.0)


def cuts_of(extent, step):
    return [(at, min(step, extent - at)) for at in range(0, extent, step)]


def two_terms(value):
    high = value.astype(jnp.bfloat16)
    low = (value - high.astype(jnp.float32)).astype(jnp.bfloat16)
    return high, low


def dot_nt(left, right):
    dims = (((1,), (1,)), ((), ()))
    lh, ll = two_terms(left)
    rh, rl = two_terms(right)
    mul = functools.partial(
        lax.dot_general, dimension_numbers=dims, preferred_element_type=jnp.float32
    )
    return mul(lh, rh) + (mul(lh, rl) + mul(ll, rh))


def project_kernel(parts, own, rank_ref, x_hbm, g_hbm, wx_hbm, wg_hbm, *rest):
    outs = rest[:2]
    x_ref, g_ref, wx_ref, wg_ref, grad_ref, sems = rest[2:]
    copies = []

    def fetch(src, dst, index):
        copy = pltpu.make_async_copy(src, dst, sems.at[index])
        copy.start()
        return copy

    g_cuts = cuts_of(g_ref.shape[1], 512)
    x_cuts = cuts_of(x_ref.shape[0], 768)
    wg_copy = fetch(wg_hbm, wg_ref, 0)
    index = 2
    g_copies = []
    for at, size in g_cuts:
        columns = pl.ds(at, size)
        g_copies.append(fetch(g_hbm.at[:, columns], g_ref.at[:, columns], index))
        index += 1
    wx_copy = fetch(wx_hbm, wx_ref, 1)
    x_copies = []
    for at, size in x_cuts:
        rows = pl.ds(at, size)
        x_copies.append(fetch(x_hbm.at[rows, :], x_ref.at[rows, :], index))
        index += 1

    def project(w_copy, w_ref, cuts, copies, ref, along):
        order = 1 if along == 0 else -1
        total = None
        w_copy.wait()
        for (at, size), copy in zip(cuts, copies):
            copy.wait()
            term = lax.dot_general(
                w_ref[:, at : at + size],
                ref[(slice(at, at + size), slice(None))[::order]],
                (((1,), (along,)), ((), ())),
                preferred_element_type=jnp.float32,
            )
            total = term if total is None else total + term
        return total

    grad_ref[...] = project(wg_copy, wg_ref, g_cuts, g_copies, g_ref, 1)
    inputs_t = project(wx_copy, wx_ref, x_cuts, x_copies, x_ref, 0)
    me = rank_ref[0]
    for out, side in zip(outs, (me & 1, (me & 1) ^ 1)):
        for place in range(parts // 2):
            start = pl.multiple_of((2 * place + side) * own, own)
            out[place * own : (place + 1) * own, :] = grad_ref[pl.ds(start, own), :]
        out[parts // 2 * own :, :] = inputs_t


def project(inputs, out_grads, in_proj, out_proj, me, parts):
    rank = in_proj.shape[1]
    own = rank // parts
    tokens, hidden = inputs.shape
    width = out_grads.shape[1]
    copies = 2 + len(cuts_of(width, 512)) + len(cuts_of(hidden, 768))
    arrays = (inputs.T, out_grads, in_proj.T, out_proj.T)
    in_hbm = pl.BlockSpec(memory_space=pltpu.HBM)
    return pl.pallas_call(
        functools.partial(project_kernel, parts, own),
        out_shape=[jax.ShapeDtypeStruct((parts // 2 * own + rank, tokens), jnp.float32)] * 2,
        in_specs=[pl.BlockSpec(memory_space=pltpu.SMEM)] + [in_hbm] * len(arrays),
        out_specs=[pl.BlockSpec(memory_space=pltpu.VMEM)] * 2,
        scratch_shapes=[
            pltpu.VMEM((hidden, tokens), jnp.bfloat16),
            pltpu.VMEM((tokens, width), jnp.bfloat16),
            pltpu.VMEM((rank, hidden), jnp.bfloat16),
            pltpu.VMEM((rank, width), jnp.bfloat16),
            pltpu.VMEM((rank, tokens), jnp.float32),
            pltpu.SemaphoreType.DMA((copies,)),
        ],
        compiler_params=pltpu.CompilerParams(vmem_limit_bytes=VMEM_LIMIT),
        name="project",
    )(me, *(pltpu.with_memory_space_constraint(array, pltpu.HBM) for array in arrays))


def halve_kernel(parts, own, rank_ref, kept_ref, came_ref, keep_ref, send_ref, sum_ref):
    sum_ref[...] = kept_ref[...] + came_ref[...]
    me = rank_ref[0]
    for out, place in ((keep_ref, me // 2), (send_ref, me // 2 ^ 1)):
        start = pl.multiple_of(place * own, own)
        out[:own, :] = sum_ref[pl.ds(start, own), :]
        out[own:, :] = sum_ref[parts // 2 * own :, :]


def halve(kept, came, me, parts, own):
    rows, tokens = kept.shape
    left = rows - (parts // 2 - 1) * own
    whole = pl.BlockSpec(memory_space=pltpu.VMEM)
    return pl.pallas_call(
        functools.partial(halve_kernel, parts, own),
        out_shape=[jax.ShapeDtypeStruct((left, tokens), jnp.float32)] * 2,
        in_specs=[pl.BlockSpec(memory_space=pltpu.SMEM), whole, whole],
        out_specs=[whole] * 2,
        scratch_shapes=[pltpu.VMEM((rows, tokens), jnp.float32)],
        compiler_params=pltpu.CompilerParams(vmem_limit_bytes=VMEM_LIMIT),
        name="halve",
    )(me, kept, came)


def grads_kernel(own, pair, weights_ref, kept_ref, came_ref, out_ref):
    summed = kept_ref[...] + came_ref[...]
    weights = weights_ref[...]
    seqs = weights.shape[0]
    inputs_t = summed[own:, :]
    zero = jnp.zeros_like(inputs_t)
    right = jnp.concatenate(
        [
            jnp.concatenate([inputs_t if j == k else zero for k in range(pair)], axis=1)
            for j in range(pair)
        ],
        axis=0,
    )
    rows = []
    for i in range(own // pair):
        rows.append(
            jnp.concatenate(
                [weights * summed[pair * i + j : pair * i + j + 1, :] for j in range(pair)],
                axis=1,
            )
        )
    left = jnp.concatenate(rows, axis=0)
    out_ref[...] = dot_nt(left, right)


def gradients(weights, kept, came, rank):
    own = kept.shape[0] - rank
    pair = 128 // rank
    return pl.pallas_call(
        functools.partial(grads_kernel, own, pair),
        out_shape=jax.ShapeDtypeStruct((own // pair * weights.shape[0], pair * rank), jnp.float32),
        compiler_params=pltpu.CompilerParams(vmem_limit_bytes=VMEM_LIMIT),
        name="gradients",
    )(weights, kept, came)


def join_kernel(upper_ref, lower_ref, out_ref):
    out_ref[...] = jnp.concatenate([upper_ref[...], lower_ref[...]], axis=0)


def join(upper, lower):
    return pl.pallas_call(
        join_kernel,
        out_shape=jax.ShapeDtypeStruct((2 * upper.shape[0], upper.shape[1]), upper.dtype),
        compiler_params=pltpu.CompilerParams(vmem_limit_bytes=VMEM_LIMIT),
        name="join",
    )(upper, lower)


def grams_kernel(seqs, me_ref, *refs):
    blocks, pairs, out_ref = refs[-4::-1], refs[-3:-1], refs[-1]
    steps = blocks[0].shape[0] // seqs
    asked = pairs[0].shape[0] // 2
    lanes = [
        jnp.concatenate([block[i * seqs : (i + 1) * seqs, :] for block in blocks], axis=0)
        for i in range(steps)
    ]
    every = jnp.concatenate(lanes, axis=1)
    given = [pair[at * asked : (at + 1) * asked, :] for at in (0, 1) for pair in pairs]
    ordered = []
    for place in range(len(blocks)):
        chosen = given[0]
        for m in range(1, len(blocks)):
            chosen = jnp.where((me_ref[0] ^ place) == m, given[m], chosen)
        ordered.append(chosen)
    result = dot_nt(jnp.concatenate([every] + ordered, axis=0), every)
    half = result.shape[0] // 2
    out_ref[...] = jnp.concatenate([result[:half, :], result[half:, :]], axis=1)


def grams(me, blocks, seqs, pairs):
    total = len(blocks) * seqs
    rows = total + 2 * pairs[0].shape[0]
    whole = pl.BlockSpec(memory_space=pltpu.VMEM)
    return pl.pallas_call(
        functools.partial(grams_kernel, seqs),
        out_shape=jax.ShapeDtypeStruct((rows // 2, 2 * total), jnp.float32),
        in_specs=[pl.BlockSpec(memory_space=pltpu.SMEM)] + [whole] * (len(blocks) + 2),
        out_specs=whole,
        compiler_params=pltpu.CompilerParams(vmem_limit_bytes=VMEM_LIMIT),
        name="grams",
    )(me, *blocks, *pairs)


def scales(count):
    first = 2.0 / (1.0 + 1.0 / count)
    off = count / (count + 1.0)
    steps = []
    while off > 1e-7:
        steps.append(2.0 / (2.0 - off * off))
        off = off * off / (2.0 - off * off)
    return first, steps


def solve_kernel(seqs, *refs):
    parts, out_ref = refs[:-1], refs[-1]
    packed = (parts[0][...] + parts[1][...]) + (parts[2][...] + parts[3][...])
    lane = lax.broadcasted_iota(jnp.int32, packed.shape, 1)
    turned = pltpu.roll(packed, seqs, 1)
    both = jnp.concatenate(
        [jnp.where(lane < seqs, packed, turned), jnp.where(lane < seqs, turned, packed)], axis=0
    )
    lane = lax.broadcasted_iota(jnp.int32, both.shape, 1)
    row = lax.broadcasted_iota(jnp.int32, both.shape, 0)
    unit = jnp.where((lane & (seqs - 1)) == row, 1.0, 0.0)
    total = jnp.sum(jnp.where(lane == row, both, 0.0)[:seqs], axis=(0, 1), keepdims=True)
    first, steps = scales(seqs)
    state = first * (both / total + unit * (damping / seqs))
    left_lanes = lane < seqs
    for at, step in enumerate(steps):
        high = state.astype(jnp.bfloat16).astype(jnp.float32)
        low = state - high
        left = jnp.where(left_lanes, high, low).astype(jnp.bfloat16)
        high = high[:seqs].astype(jnp.bfloat16)
        low = low[:seqs].astype(jnp.bfloat16)
        right = jnp.concatenate([high, high, low, low], axis=0)
        if at + 1 == len(steps):
            left, state = left[seqs:], state[seqs:]
        product = jnp.dot(
            jnp.concatenate([left, left], axis=1), right, preferred_element_type=jnp.float32
        )
        state = step * (2.0 * state - product)
    out_ref[...] = state[:, : out_ref.shape[1]]


def solve(parts, seqs, asked, seq_dev):
    return pl.pallas_call(
        functools.partial(solve_kernel, seqs),
        out_shape=jax.ShapeDtypeStruct((asked, seq_dev), jnp.float32),
        compiler_params=pltpu.CompilerParams(vmem_limit_bytes=VMEM_LIMIT),
        name="solve",
    )(*parts)


def from_partner(value, axis, size, m):
    return lax.ppermute(value, axis, [(i, i ^ m) for i in range(size)])


def from_partners(value, axis, size):
    return [from_partner(value, axis, size, m) for m in reversed(range(1, size))] + [value]


def finish_long(grads, asked, first, seq_dev):
    lanes = grads.shape[1]
    every = lax.all_gather(grads, "dp", axis=0)
    every = every.reshape(every.shape[0], -1, seq_dev, lanes).transpose(0, 2, 1, 3)
    every = every.reshape(-1, asked.shape[1])
    asked = lax.all_gather(asked, "dp", axis=0, tiled=True)
    both = jnp.einsum(
        "ik,jk->ij", jnp.concatenate([every, asked], axis=0), every,
        precision=lax.Precision.HIGHEST,
    )
    both = lax.psum(both, "tensor")
    count = every.shape[0]
    kernel, products = both[:count], both[count:]
    damp = damping * jnp.trace(kernel) / count
    unit = jnp.eye(count, dtype=jnp.float32)
    factor = jnp.linalg.cholesky(kernel + damp * unit)
    picks = lax.dynamic_slice_in_dim(unit, first, seq_dev, 1)
    solved = jax.scipy.linalg.cho_solve((factor, True), picks)
    return jnp.dot(products, solved, precision=lax.Precision.HIGHEST)


def per_device(sizes, inputs, out_grads, in_proj, out_proj, seq_ids, counts, queries):
    parts, blocks = sizes
    rank = in_proj.shape[1]
    seq_dev = counts.shape[0]
    me = lax.axis_index("tensor")
    place = lax.axis_index("dp")
    first = place * seq_dev
    own = rank // parts
    rank_of = me.reshape(1)
    kept, sent = project(inputs, out_grads, in_proj, out_proj, rank_of, parts)
    asked = lax.dynamic_slice_in_dim(queries, me * (own * rank), own * rank, 1)
    came = from_partner(sent, "tensor", parts, 1)
    kept, sent = halve(kept, came, rank_of, parts, own)
    came = from_partner(sent, "tensor", parts, 2)
    kept, counts = lax.optimization_barrier((kept, counts))
    weights = token_weights(seq_ids, counts, first)
    weights, asked = lax.optimization_barrier((weights, asked))
    if blocks <= SMALL:
        asked = join(asked, from_partner(asked, "dp", blocks, 2))
    grads = gradients(weights, kept, came, rank)
    if blocks > SMALL:
        return finish_long(grads, asked, first, seq_dev)
    grads, asked = lax.optimization_barrier((grads, asked))
    pairs = [asked, from_partner(asked, "dp", blocks, 1)]
    partial = grams(place.reshape(1), from_partners(grads, "dp", blocks), seq_dev, pairs)
    partial = from_partners(partial, "tensor", parts)
    return solve(partial, blocks * seq_dev, blocks * queries.shape[0], seq_dev)


def solution(mesh):
    in_specs = (
        P(("groups", "dp"), "tensor"),
        P(("groups", "dp"), "tensor"),
        P("tensor", None),
        P("tensor", None),
        P(("groups", "dp")),
        P(("groups", "dp")),
        P(("groups", "dp"), None),
    )
    sizes = (mesh.shape["tensor"], mesh.shape["dp"])
    return jax.shard_map(
        functools.partial(per_device, sizes),
        mesh=mesh,
        in_specs=in_specs,
        out_specs=P("groups", "dp"),
        check_vma=False,
    )
```

```python
import functools

import jax
import jax.numpy as jnp
from jax import lax
from jax.experimental import pallas as pl
from jax.experimental.pallas import tpu as pltpu
from jax.sharding import PartitionSpec as P

damping = 0.5
VMEM_LIMIT = 32 * 1024 * 1024
SMALL = 4


def token_weights(seq_ids, counts, first, works):
    local_ids = seq_ids - first
    slots = jnp.arange(counts.shape[0], dtype=jnp.int32)
    member = local_ids[None, :] == slots[:, None]
    starts = jnp.sum((local_ids[None, :] < slots[:, None]).astype(jnp.int32), axis=1)
    offset = jnp.arange(seq_ids.shape[0], dtype=jnp.int32)[None, :] - starts[:, None]
    scale = works.astype(jnp.float32) / counts.astype(jnp.float32)
    return jnp.where(member & (offset < counts[:, None]), scale[:, None], 0.0)


def cuts_of(extent, step):
    return [(at, min(step, extent - at)) for at in range(0, extent, step)]


def two_terms(value):
    high = value.astype(jnp.bfloat16)
    low = (value - high.astype(jnp.float32)).astype(jnp.bfloat16)
    return high, low


def dot_nt(left, right):
    dims = (((1,), (1,)), ((), ()))
    lh, ll = two_terms(left)
    rh, rl = two_terms(right)
    mul = functools.partial(
        lax.dot_general, dimension_numbers=dims, preferred_element_type=jnp.float32
    )
    return mul(lh, rh) + (mul(lh, rl) + mul(ll, rh))


def project_kernel(x_hbm, g_hbm, wx_hbm, wg_hbm, out_ref, x_ref, g_ref, wx_ref, wg_ref, sems):
    copies = []

    def fetch(src, dst, index):
        copy = pltpu.make_async_copy(src, dst, sems.at[index])
        copy.start()
        return copy

    g_cuts = cuts_of(g_ref.shape[1], 512)
    x_cuts = cuts_of(x_ref.shape[0], 768)
    wg_copy = fetch(wg_hbm, wg_ref, 0)
    index = 2
    g_copies = []
    for at, size in g_cuts:
        columns = pl.ds(at, size)
        g_copies.append(fetch(g_hbm.at[:, columns], g_ref.at[:, columns], index))
        index += 1
    wx_copy = fetch(wx_hbm, wx_ref, 1)
    x_copies = []
    for at, size in x_cuts:
        rows = pl.ds(at, size)
        x_copies.append(fetch(x_hbm.at[rows, :], x_ref.at[rows, :], index))
        index += 1

    def project(w_copy, w_ref, cuts, copies, ref, along):
        order = 1 if along == 0 else -1
        total = None
        w_copy.wait()
        for (at, size), copy in zip(cuts, copies):
            copy.wait()
            term = lax.dot_general(
                w_ref[:, at : at + size],
                ref[(slice(at, at + size), slice(None))[::order]],
                (((1,), (along,)), ((), ())),
                preferred_element_type=jnp.float32,
            )
            total = term if total is None else total + term
        return total

    rank = wg_ref.shape[0]
    out_ref[:rank, :] = project(wg_copy, wg_ref, g_cuts, g_copies, g_ref, 1)
    out_ref[rank:, :] = project(wx_copy, wx_ref, x_cuts, x_copies, x_ref, 0)


def project(inputs, out_grads, in_proj, out_proj):
    rank = in_proj.shape[1]
    tokens, hidden = inputs.shape
    width = out_grads.shape[1]
    copies = 2 + len(cuts_of(width, 512)) + len(cuts_of(hidden, 768))
    arrays = (inputs.T, out_grads, in_proj.T, out_proj.T)
    return pl.pallas_call(
        project_kernel,
        out_shape=jax.ShapeDtypeStruct((2 * rank, tokens), jnp.float32),
        in_specs=[pl.BlockSpec(memory_space=pltpu.HBM)] * len(arrays),
        out_specs=pl.BlockSpec(memory_space=pltpu.VMEM),
        scratch_shapes=[
            pltpu.VMEM((hidden, tokens), jnp.bfloat16),
            pltpu.VMEM((tokens, width), jnp.bfloat16),
            pltpu.VMEM((rank, hidden), jnp.bfloat16),
            pltpu.VMEM((rank, width), jnp.bfloat16),
            pltpu.SemaphoreType.DMA((copies,)),
        ],
        compiler_params=pltpu.CompilerParams(vmem_limit_bytes=VMEM_LIMIT),
        name="project",
    )(*(pltpu.with_memory_space_constraint(array, pltpu.HBM) for array in arrays))


def halve_kernel(own, rank_ref, kept_ref, came_ref, keep_ref, send_ref, sum_ref):
    sum_ref[...] = kept_ref[...] + came_ref[...]
    rank = sum_ref.shape[0] // 2
    place = rank_ref[0] // 2
    for out, taken in ((keep_ref, place), (send_ref, place ^ 1)):
        out[:own, :] = sum_ref[pl.ds(pl.multiple_of(taken * own, own), own), :]
        out[own:, :] = sum_ref[rank:, :]


def halve(kept, came, me, own):
    rows, tokens = kept.shape
    whole = pl.BlockSpec(memory_space=pltpu.VMEM)
    return pl.pallas_call(
        functools.partial(halve_kernel, own),
        out_shape=[jax.ShapeDtypeStruct((own + rows // 2, tokens), jnp.float32)] * 2,
        in_specs=[pl.BlockSpec(memory_space=pltpu.SMEM), whole, whole],
        out_specs=[whole] * 2,
        scratch_shapes=[pltpu.VMEM((rows, tokens), jnp.float32)],
        compiler_params=pltpu.CompilerParams(vmem_limit_bytes=VMEM_LIMIT),
        name="halve",
    )(me, kept, came)


def grads_kernel(own, pair, weights_ref, *refs):
    kept_ref, came_ref, out_ref = refs
    summed = kept_ref[...] + came_ref[...]
    weights = weights_ref[...]
    seqs = weights.shape[0]
    inputs_t = summed[own:, :]
    zero = jnp.zeros_like(inputs_t)
    right = jnp.concatenate(
        [
            jnp.concatenate([inputs_t if j == k else zero for k in range(pair)], axis=1)
            for j in range(pair)
        ],
        axis=0,
    )
    rows = []
    for i in range(own // pair):
        rows.append(
            jnp.concatenate(
                [weights * summed[pair * i + j : pair * i + j + 1, :] for j in range(pair)],
                axis=1,
            )
        )
    left = jnp.concatenate(rows, axis=0)
    out_ref[...] = dot_nt(left, right).reshape(own // pair, seqs, right.shape[0])


def gradients(weights, pieces, rank):
    own = pieces[0].shape[0] - rank
    pair = 128 // rank
    return pl.pallas_call(
        functools.partial(grads_kernel, own, pair),
        out_shape=jax.ShapeDtypeStruct(
            (own // pair, weights.shape[0], pair * rank), jnp.float32
        ),
        compiler_params=pltpu.CompilerParams(vmem_limit_bytes=VMEM_LIMIT),
        name="gradients",
    )(weights, *pieces)


def collect_kernel(place_ref, *refs):
    given, out_ref = [ref[...] for ref in refs[:-1]], refs[-1]
    count = len(given)
    rows = given[0].shape[0]
    ordered = []
    for place in range(count):
        chosen = given[0]
        for m in range(1, count):
            chosen = jnp.where((place_ref[0] ^ place) == m, given[m], chosen)
        ordered.append(chosen)
    out_ref[...] = jnp.concatenate(ordered, axis=0)


def collect(place, blocks):
    rows, columns = blocks[0].shape
    whole = pl.BlockSpec(memory_space=pltpu.VMEM)
    return pl.pallas_call(
        collect_kernel,
        out_shape=jax.ShapeDtypeStruct((len(blocks) * rows, columns), jnp.float32),
        in_specs=[pl.BlockSpec(memory_space=pltpu.SMEM)] + [whole] * len(blocks),
        out_specs=whole,
        compiler_params=pltpu.CompilerParams(vmem_limit_bytes=VMEM_LIMIT),
        name="collect",
    )(place, *blocks)


def grams_kernel(*refs):
    queries_ref, grads, out_ref = refs[0], refs[1:-1], refs[-1]
    lanes = [
        jnp.concatenate([block[i] for block in grads], axis=0)
        for i in range(grads[0].shape[0])
    ]
    every = jnp.concatenate(lanes, axis=1)
    both = jnp.concatenate([every, queries_ref[...]], axis=0)
    result = dot_nt(both, every)
    half = result.shape[0] // 2
    out_ref[...] = jnp.concatenate([result[:half, :], result[half:, :]], axis=1)


def grams(grads, queries):
    seqs = len(grads) * grads[0].shape[1]
    return pl.pallas_call(
        grams_kernel,
        out_shape=jax.ShapeDtypeStruct(((seqs + queries.shape[0]) // 2, 2 * seqs), jnp.float32),
        compiler_params=pltpu.CompilerParams(vmem_limit_bytes=VMEM_LIMIT),
        name="grams",
    )(queries, *grads)


def scales(count):
    first = 2.0 / (1.0 + 1.0 / count)
    off = count / (count + 1.0)
    steps = []
    while off > 1e-7:
        steps.append(2.0 / (2.0 - off * off))
        off = off * off / (2.0 - off * off)
    return first, steps


def solve_kernel(seqs, *refs):
    parts, out_ref = refs[:-1], refs[-1]
    packed = parts[0][...] + parts[1][...]
    lane = lax.broadcasted_iota(jnp.int32, packed.shape, 1)
    turned = pltpu.roll(packed, seqs, 1)
    both = jnp.concatenate(
        [jnp.where(lane < seqs, packed, turned), jnp.where(lane < seqs, turned, packed)], axis=0
    )
    lane = lax.broadcasted_iota(jnp.int32, both.shape, 1)
    row = lax.broadcasted_iota(jnp.int32, both.shape, 0)
    unit = jnp.where((lane & (seqs - 1)) == row, 1.0, 0.0)
    total = jnp.sum(jnp.where(lane == row, both, 0.0)[:seqs], axis=(0, 1), keepdims=True)
    first, steps = scales(seqs)
    state = first * (both / total + unit * (damping / seqs))
    left_lanes = lane < seqs
    for at, step in enumerate(steps):
        high = state.astype(jnp.bfloat16).astype(jnp.float32)
        low = state - high
        left = jnp.where(left_lanes, high, low).astype(jnp.bfloat16)
        high = high[:seqs].astype(jnp.bfloat16)
        low = low[:seqs].astype(jnp.bfloat16)
        right = jnp.concatenate([high, high, low, low], axis=0)
        if at + 1 == len(steps):
            left, state = left[seqs:], state[seqs:]
        product = jnp.dot(
            jnp.concatenate([left, left], axis=1), right, preferred_element_type=jnp.float32
        )
        state = step * (2.0 * state - product)
    out_ref[...] = state[:, : out_ref.shape[1]]


def solve(parts, seqs, asked, seq_dev):
    return pl.pallas_call(
        functools.partial(solve_kernel, seqs),
        out_shape=jax.ShapeDtypeStruct((asked, seq_dev), jnp.float32),
        compiler_params=pltpu.CompilerParams(vmem_limit_bytes=VMEM_LIMIT),
        name="solve",
    )(*parts)


def move(value, sizes, target):
    parts, blocks = sizes
    pairs = []
    for d in range(blocks):
        for r in range(parts):
            block, rank = target(d, r)
            pairs.append((d * parts + r, block * parts + rank))
    return lax.ppermute(value, ("dp", "tensor"), pairs)


def add_kernel(left_ref, right_ref, out_ref):
    out_ref[...] = left_ref[...] + right_ref[...]


def add(left, right):
    return pl.pallas_call(
        add_kernel,
        out_shape=jax.ShapeDtypeStruct(left.shape, left.dtype),
        compiler_params=pltpu.CompilerParams(vmem_limit_bytes=VMEM_LIMIT),
        name="add",
    )(left, right)


def over_blocks(value, sizes, side):
    came = [
        move(value, sizes, lambda d, r: (d ^ m, r) if r % 2 == side else (d, r))
        for m in reversed(range(1, sizes[1]))
    ]
    return came + [value]


def finish_long(grads, queries, first, seq_dev):
    every = lax.all_gather(grads, "dp", axis=0)
    steps, seqs, lanes = grads.shape
    every = every.transpose(0, 2, 1, 3).reshape(-1, steps * lanes)
    asked = lax.all_gather(queries, "dp", axis=0, tiled=True)
    both = jnp.einsum(
        "ik,jk->ij", jnp.concatenate([every, asked], axis=0), every,
        precision=lax.Precision.HIGHEST,
    )
    both = lax.psum(both, "tensor")
    count = every.shape[0]
    kernel, products = both[:count], both[count:]
    damp = damping * jnp.trace(kernel) / count
    unit = jnp.eye(count, dtype=jnp.float32)
    factor = jnp.linalg.cholesky(kernel + damp * unit)
    picks = lax.dynamic_slice_in_dim(unit, first, seq_dev, 1)
    solved = jax.scipy.linalg.cho_solve((factor, True), picks)
    return jnp.dot(products, solved, precision=lax.Precision.HIGHEST)


def per_device(sizes, inputs, out_grads, in_proj, out_proj, seq_ids, counts, queries):
    parts, blocks = sizes
    rank = in_proj.shape[1]
    seq_dev = counts.shape[0]
    me = lax.axis_index("tensor")
    place = lax.axis_index("dp")
    first = place * seq_dev
    own = rank // (parts // 2)
    rank_of = me.reshape(1)
    weights = token_weights(seq_ids, counts, first, me % 2)
    asked = lax.dynamic_slice_in_dim(queries, (me // 2) * (own * rank), own * rank, 1)
    kept = project(inputs, out_grads, in_proj, out_proj)
    came = move(kept, sizes, lambda d, r: (d, r ^ 1))
    kept, sent = halve(kept, came, rank_of, own)
    came = move(sent, sizes, lambda d, r: (d, r ^ 2) if r % 2 == 1 else (d, r))
    if blocks > SMALL:
        return finish_long(gradients(weights, [kept, came], rank), asked, first, seq_dev)
    sent, asked = lax.optimization_barrier((sent, asked))
    asked = over_blocks(asked, sizes, 0)
    grads = gradients(weights, [kept, came], rank)
    grads, *asked = lax.optimization_barrier((grads, *asked))
    grads = over_blocks(grads, sizes, 1)
    grads[0], *asked = lax.optimization_barrier((grads[0], *asked))
    asked = collect(place.reshape(1), asked[::-1])
    asked = move(asked, sizes, lambda d, r: (d, r ^ 1))
    partial = grams(grads[::-1], asked)
    partial = add(partial, move(partial, sizes, lambda d, r: (d, r ^ 2) if r % 2 == 1 else (d, r)))
    partial = [partial, move(partial, sizes, lambda d, r: (d, r ^ 1))]
    return solve(partial, blocks * seq_dev, asked.shape[0], seq_dev)


def solution(mesh):
    in_specs = (
        P(("groups", "dp"), "tensor"),
        P(("groups", "dp"), "tensor"),
        P("tensor", None),
        P("tensor", None),
        P(("groups", "dp")),
        P(("groups", "dp")),
        P(("groups", "dp"), None),
    )
    sizes = (mesh.shape["tensor"], mesh.shape["dp"])
    return jax.shard_map(
        functools.partial(per_device, sizes),
        mesh=mesh,
        in_specs=in_specs,
        out_specs=P("groups", "dp"),
        check_vma=False,
    )
```

```python
import functools

import jax
import jax.numpy as jnp
from jax import lax
from jax.experimental import pallas as pl
from jax.experimental.pallas import tpu as pltpu
from jax.sharding import PartitionSpec as P

damping = 0.5
VMEM_LIMIT = 32 * 1024 * 1024
SMALL = 4


def token_weights(seq_ids, counts, first):
    local_ids = seq_ids - first
    slots = jnp.arange(counts.shape[0], dtype=jnp.int32)
    member = local_ids[None, :] == slots[:, None]
    starts = jnp.sum((local_ids[None, :] < slots[:, None]).astype(jnp.int32), axis=1)
    offset = jnp.arange(seq_ids.shape[0], dtype=jnp.int32)[None, :] - starts[:, None]
    scale = 1.0 / counts.astype(jnp.float32)
    return jnp.where(member & (offset < counts[:, None]), scale[:, None], 0.0)


def cuts_of(extent, step):
    return [(at, min(step, extent - at)) for at in range(0, extent, step)]


def two_terms(value):
    high = value.astype(jnp.bfloat16)
    low = (value - high.astype(jnp.float32)).astype(jnp.bfloat16)
    return high, low


def dot_nt(left, right):
    dims = (((1,), (1,)), ((), ()))
    lh, ll = two_terms(left)
    rh, rl = two_terms(right)
    mul = functools.partial(
        lax.dot_general, dimension_numbers=dims, preferred_element_type=jnp.float32
    )
    return mul(lh, rh) + (mul(lh, rl) + mul(ll, rh))


def project_kernel(parts, own, rank_ref, x_hbm, g_hbm, wx_hbm, wg_hbm, *rest):
    outs = rest[:2]
    x_ref, g_ref, wx_ref, wg_ref, grad_ref, sems = rest[2:]
    copies = []

    def fetch(src, dst, index):
        copy = pltpu.make_async_copy(src, dst, sems.at[index])
        copy.start()
        return copy

    g_cuts = cuts_of(g_ref.shape[1], 512)
    x_cuts = cuts_of(x_ref.shape[0], 768)
    wg_copy = fetch(wg_hbm, wg_ref, 0)
    index = 2
    g_copies = []
    for at, size in g_cuts:
        columns = pl.ds(at, size)
        g_copies.append(fetch(g_hbm.at[:, columns], g_ref.at[:, columns], index))
        index += 1
    wx_copy = fetch(wx_hbm, wx_ref, 1)
    x_copies = []
    for at, size in x_cuts:
        rows = pl.ds(at, size)
        x_copies.append(fetch(x_hbm.at[rows, :], x_ref.at[rows, :], index))
        index += 1

    def project(w_copy, w_ref, cuts, copies, ref, along):
        order = 1 if along == 0 else -1
        total = None
        w_copy.wait()
        for (at, size), copy in zip(cuts, copies):
            copy.wait()
            term = lax.dot_general(
                w_ref[:, at : at + size],
                ref[(slice(at, at + size), slice(None))[::order]],
                (((1,), (along,)), ((), ())),
                preferred_element_type=jnp.float32,
            )
            total = term if total is None else total + term
        return total

    grad_ref[...] = project(wg_copy, wg_ref, g_cuts, g_copies, g_ref, 1)
    inputs_t = project(wx_copy, wx_ref, x_cuts, x_copies, x_ref, 0)
    me = rank_ref[0]
    for out, side in zip(outs, (me & 1, (me & 1) ^ 1)):
        for place in range(parts // 2):
            start = pl.multiple_of((2 * place + side) * own, own)
            out[place * own : (place + 1) * own, :] = grad_ref[pl.ds(start, own), :]
        out[parts // 2 * own :, :] = inputs_t


def project(inputs, out_grads, in_proj, out_proj, me, parts):
    rank = in_proj.shape[1]
    own = rank // parts
    tokens, hidden = inputs.shape
    width = out_grads.shape[1]
    copies = 2 + len(cuts_of(width, 512)) + len(cuts_of(hidden, 768))
    arrays = (inputs.T, out_grads, in_proj.T, out_proj.T)
    in_hbm = pl.BlockSpec(memory_space=pltpu.HBM)
    return pl.pallas_call(
        functools.partial(project_kernel, parts, own),
        out_shape=[jax.ShapeDtypeStruct((parts // 2 * own + rank, tokens), jnp.float32)] * 2,
        in_specs=[pl.BlockSpec(memory_space=pltpu.SMEM)] + [in_hbm] * len(arrays),
        out_specs=[pl.BlockSpec(memory_space=pltpu.VMEM)] * 2,
        scratch_shapes=[
            pltpu.VMEM((hidden, tokens), jnp.bfloat16),
            pltpu.VMEM((tokens, width), jnp.bfloat16),
            pltpu.VMEM((rank, hidden), jnp.bfloat16),
            pltpu.VMEM((rank, width), jnp.bfloat16),
            pltpu.VMEM((rank, tokens), jnp.float32),
            pltpu.SemaphoreType.DMA((copies,)),
        ],
        compiler_params=pltpu.CompilerParams(vmem_limit_bytes=VMEM_LIMIT),
        name="project",
    )(me, *(pltpu.with_memory_space_constraint(array, pltpu.HBM) for array in arrays))


def halve_kernel(parts, own, rank_ref, kept_ref, came_ref, keep_ref, send_ref, sum_ref):
    sum_ref[...] = kept_ref[...] + came_ref[...]
    me = rank_ref[0]
    for out, place in ((keep_ref, me // 2), (send_ref, me // 2 ^ 1)):
        start = pl.multiple_of(place * own, own)
        out[:own, :] = sum_ref[pl.ds(start, own), :]
        out[own:, :] = sum_ref[parts // 2 * own :, :]


def halve(kept, came, me, parts, own):
    rows, tokens = kept.shape
    left = rows - (parts // 2 - 1) * own
    whole = pl.BlockSpec(memory_space=pltpu.VMEM)
    return pl.pallas_call(
        functools.partial(halve_kernel, parts, own),
        out_shape=[jax.ShapeDtypeStruct((left, tokens), jnp.float32)] * 2,
        in_specs=[pl.BlockSpec(memory_space=pltpu.SMEM), whole, whole],
        out_specs=[whole] * 2,
        scratch_shapes=[pltpu.VMEM((rows, tokens), jnp.float32)],
        compiler_params=pltpu.CompilerParams(vmem_limit_bytes=VMEM_LIMIT),
        name="halve",
    )(me, kept, came)


def grads_kernel(own, pair, weights_ref, kept_ref, came_ref, out_ref):
    summed = kept_ref[...] + came_ref[...]
    weights = weights_ref[...]
    seqs = weights.shape[0]
    inputs_t = summed[own:, :]
    zero = jnp.zeros_like(inputs_t)
    right = jnp.concatenate(
        [
            jnp.concatenate([inputs_t if j == k else zero for k in range(pair)], axis=1)
            for j in range(pair)
        ],
        axis=0,
    )
    rows = []
    for i in range(own // pair):
        rows.append(
            jnp.concatenate(
                [weights * summed[pair * i + j : pair * i + j + 1, :] for j in range(pair)],
                axis=1,
            )
        )
    left = jnp.concatenate(rows, axis=0)
    out_ref[...] = dot_nt(left, right)


def gradients(weights, kept, came, rank):
    own = kept.shape[0] - rank
    pair = 128 // rank
    return pl.pallas_call(
        functools.partial(grads_kernel, own, pair),
        out_shape=jax.ShapeDtypeStruct((own // pair * weights.shape[0], pair * rank), jnp.float32),
        compiler_params=pltpu.CompilerParams(vmem_limit_bytes=VMEM_LIMIT),
        name="gradients",
    )(weights, kept, came)


def append_kernel(grads_ref, asked_ref, far_ref, out_ref):
    count, lanes = grads_ref.shape
    out_ref[:count, :] = grads_ref[...]
    for queries_ref in (asked_ref, far_ref):
        rows, columns = queries_ref.shape
        for at in range(0, columns, lanes):
            out_ref[count : count + rows, :] = queries_ref[:, at : at + lanes]
            count += rows


def append(grads, asked, far):
    count, lanes = grads.shape
    rows = count + 2 * asked.shape[0] * asked.shape[1] // lanes
    return pl.pallas_call(
        append_kernel,
        out_shape=jax.ShapeDtypeStruct((rows, lanes), jnp.float32),
        compiler_params=pltpu.CompilerParams(vmem_limit_bytes=VMEM_LIMIT),
        name="append",
    )(grads, asked, far)


def grams_kernel(seqs, me_ref, third_ref, second_ref, first_ref, own_ref, out_ref):
    blocks = (own_ref, first_ref, second_ref, third_ref)
    count = second_ref.shape[0]
    steps = count // seqs
    size = (own_ref.shape[0] - count) // 2
    asked = size // steps
    given = [ref[count + at * size : count + (at + 1) * size, :] for at in (0, 1) for ref in blocks[:2]]
    ordered = []
    for place in range(len(blocks)):
        chosen = given[0]
        for m in range(1, len(blocks)):
            chosen = jnp.where((me_ref[0] ^ place) == m, given[m], chosen)
        ordered.append(chosen)
    lanes = []
    for i in range(steps):
        rows = [block[i * seqs : (i + 1) * seqs, :] for block in blocks]
        rows += [chosen[i * asked : (i + 1) * asked, :] for chosen in ordered]
        lanes.append(jnp.concatenate(rows, axis=0))
    both = jnp.concatenate(lanes, axis=1)
    result = dot_nt(both, both[: len(blocks) * seqs])
    half = result.shape[0] // 2
    out_ref[...] = jnp.concatenate([result[:half, :], result[half:, :]], axis=1)


def grams(me, blocks, seqs):
    count = blocks[0].shape[0]
    total = len(blocks) * seqs
    rows = total + 2 * (blocks[-1].shape[0] - count) // (count // seqs)
    whole = pl.BlockSpec(memory_space=pltpu.VMEM)
    return pl.pallas_call(
        functools.partial(grams_kernel, seqs),
        out_shape=jax.ShapeDtypeStruct((rows // 2, 2 * total), jnp.float32),
        in_specs=[pl.BlockSpec(memory_space=pltpu.SMEM)] + [whole] * len(blocks),
        out_specs=whole,
        compiler_params=pltpu.CompilerParams(vmem_limit_bytes=VMEM_LIMIT),
        name="grams",
    )(me, *blocks)


def scales(count):
    first = 2.0 / (1.0 + 1.0 / count)
    off = count / (count + 1.0)
    steps = []
    while off > 1e-7:
        steps.append(2.0 / (2.0 - off * off))
        off = off * off / (2.0 - off * off)
    return first, steps


def solve_kernel(seqs, *refs):
    parts, out_ref = refs[:-1], refs[-1]
    packed = (parts[0][...] + parts[1][...]) + (parts[2][...] + parts[3][...])
    lane = lax.broadcasted_iota(jnp.int32, packed.shape, 1)
    turned = pltpu.roll(packed, seqs, 1)
    both = jnp.concatenate(
        [jnp.where(lane < seqs, packed, turned), jnp.where(lane < seqs, turned, packed)], axis=0
    )
    lane = lax.broadcasted_iota(jnp.int32, both.shape, 1)
    row = lax.broadcasted_iota(jnp.int32, both.shape, 0)
    unit = jnp.where((lane & (seqs - 1)) == row, 1.0, 0.0)
    total = jnp.sum(jnp.where(lane == row, both, 0.0)[:seqs], axis=(0, 1), keepdims=True)
    first, steps = scales(seqs)
    state = first * (both / total + unit * (damping / seqs))
    left_lanes = lane < seqs
    for at, step in enumerate(steps):
        high = state.astype(jnp.bfloat16).astype(jnp.float32)
        low = state - high
        left = jnp.where(left_lanes, high, low).astype(jnp.bfloat16)
        high = high[:seqs].astype(jnp.bfloat16)
        low = low[:seqs].astype(jnp.bfloat16)
        right = jnp.concatenate([high, high, low, low], axis=0)
        if at + 1 == len(steps):
            left, state = left[seqs:], state[seqs:]
        product = jnp.dot(
            jnp.concatenate([left, left], axis=1), right, preferred_element_type=jnp.float32
        )
        state = step * (2.0 * state - product)
    out_ref[...] = state[:, : out_ref.shape[1]]


def solve(parts, seqs, asked, seq_dev):
    return pl.pallas_call(
        functools.partial(solve_kernel, seqs),
        out_shape=jax.ShapeDtypeStruct((asked, seq_dev), jnp.float32),
        compiler_params=pltpu.CompilerParams(vmem_limit_bytes=VMEM_LIMIT),
        name="solve",
    )(*parts)


def from_partner(value, axis, size, m):
    return lax.ppermute(value, axis, [(i, i ^ m) for i in range(size)])


def from_partners(value, axis, size):
    return [from_partner(value, axis, size, m) for m in reversed(range(1, size))] + [value]


def finish_long(grads, asked, first, seq_dev):
    lanes = grads.shape[1]
    every = lax.all_gather(grads, "dp", axis=0)
    every = every.reshape(every.shape[0], -1, seq_dev, lanes).transpose(0, 2, 1, 3)
    every = every.reshape(-1, asked.shape[1])
    asked = lax.all_gather(asked, "dp", axis=0, tiled=True)
    both = jnp.einsum(
        "ik,jk->ij", jnp.concatenate([every, asked], axis=0), every,
        precision=lax.Precision.HIGHEST,
    )
    both = lax.psum(both, "tensor")
    count = every.shape[0]
    kernel, products = both[:count], both[count:]
    damp = damping * jnp.trace(kernel) / count
    unit = jnp.eye(count, dtype=jnp.float32)
    factor = jnp.linalg.cholesky(kernel + damp * unit)
    picks = lax.dynamic_slice_in_dim(unit, first, seq_dev, 1)
    solved = jax.scipy.linalg.cho_solve((factor, True), picks)
    return jnp.dot(products, solved, precision=lax.Precision.HIGHEST)


def per_device(sizes, inputs, out_grads, in_proj, out_proj, seq_ids, counts, queries):
    parts, blocks = sizes
    rank = in_proj.shape[1]
    seq_dev = counts.shape[0]
    me = lax.axis_index("tensor")
    place = lax.axis_index("dp")
    first = place * seq_dev
    own = rank // parts
    rank_of = me.reshape(1)
    kept, sent = project(inputs, out_grads, in_proj, out_proj, rank_of, parts)
    asked = lax.dynamic_slice_in_dim(queries, me * (own * rank), own * rank, 1)
    came = from_partner(sent, "tensor", parts, 1)
    kept, sent = halve(kept, came, rank_of, parts, own)
    came = from_partner(sent, "tensor", parts, 2)
    kept, counts = lax.optimization_barrier((kept, counts))
    weights = token_weights(seq_ids, counts, first)
    weights, asked = lax.optimization_barrier((weights, asked))
    far = from_partner(asked, "dp", blocks, 2)
    grads = gradients(weights, kept, came, rank)
    if blocks > SMALL:
        return finish_long(grads, asked, first, seq_dev)
    distant = [from_partner(grads, "dp", blocks, m) for m in (3, 2)]
    near = append(grads, asked, far)
    grads = distant + [from_partner(near, "dp", blocks, 1), near]
    partial = grams(place.reshape(1), grads, seq_dev)
    partial = from_partners(partial, "tensor", parts)
    return solve(partial, blocks * seq_dev, blocks * queries.shape[0], seq_dev)


def solution(mesh):
    in_specs = (
        P(("groups", "dp"), "tensor"),
        P(("groups", "dp"), "tensor"),
        P("tensor", None),
        P("tensor", None),
        P(("groups", "dp")),
        P(("groups", "dp")),
        P(("groups", "dp"), None),
    )
    sizes = (mesh.shape["tensor"], mesh.shape["dp"])
    return jax.shard_map(
        functools.partial(per_device, sizes),
        mesh=mesh,
        in_specs=in_specs,
        out_specs=P("groups", "dp"),
        check_vma=False,
    )
```

```python
import functools

import jax
import jax.numpy as jnp
from jax import lax
from jax.experimental import pallas as pl
from jax.experimental.pallas import tpu as pltpu
from jax.sharding import PartitionSpec as P

damping = 0.5
VMEM_LIMIT = 32 * 1024 * 1024
SMALL = 4


def token_weights(seq_ids, counts, first):
    local_ids = seq_ids - first
    slots = jnp.arange(counts.shape[0], dtype=jnp.int32)
    member = local_ids[None, :] == slots[:, None]
    starts = jnp.sum((local_ids[None, :] < slots[:, None]).astype(jnp.int32), axis=1)
    offset = jnp.arange(seq_ids.shape[0], dtype=jnp.int32)[None, :] - starts[:, None]
    scale = 1.0 / counts.astype(jnp.float32)
    return jnp.where(member & (offset < counts[:, None]), scale[:, None], 0.0)


def cuts_of(extent, step):
    return [(at, min(step, extent - at)) for at in range(0, extent, step)]


def two_terms(value):
    high = value.astype(jnp.bfloat16)
    low = (value - high.astype(jnp.float32)).astype(jnp.bfloat16)
    return high, low


def dot_nt(left, right):
    dims = (((1,), (1,)), ((), ()))
    lh, ll = two_terms(left)
    rh, rl = two_terms(right)
    mul = functools.partial(
        lax.dot_general, dimension_numbers=dims, preferred_element_type=jnp.float32
    )
    return mul(lh, rh) + (mul(lh, rl) + mul(ll, rh))


def project_kernel(own, rank_ref, x_hbm, g_hbm, wx_hbm, wg_hbm, keep_ref, send_ref, *scratch):
    x_ref, g_ref, wx_ref, wg_ref, wide_ref, sems = scratch
    copies = []

    def fetch(src, dst, index):
        copy = pltpu.make_async_copy(src, dst, sems.at[index])
        copy.start()
        return copy

    g_cuts = cuts_of(g_ref.shape[1], 512)
    x_cuts = cuts_of(x_ref.shape[0], 768)
    wg_copy = fetch(wg_hbm, wg_ref, 0)
    index = 2
    g_copies = []
    for at, size in g_cuts:
        columns = pl.ds(at, size)
        g_copies.append(fetch(g_hbm.at[:, columns], g_ref.at[:, columns], index))
        index += 1
    wx_copy = fetch(wx_hbm, wx_ref, 1)
    x_copies = []
    for at, size in x_cuts:
        rows = pl.ds(at, size)
        x_copies.append(fetch(x_hbm.at[rows, :], x_ref.at[rows, :], index))
        index += 1

    half = x_ref.shape[1] // 2

    def project(w_copy, w_ref, cuts, copies, cut, along):
        totals = [None, None]
        w_copy.wait()
        for (at, size), copy in zip(cuts, copies):
            copy.wait()
            for side in (0, 1):
                term = lax.dot_general(
                    w_ref[:, at : at + size],
                    cut(slice(at, at + size), slice(side * half, (side + 1) * half)),
                    (((1,), (along,)), ((), ())),
                    preferred_element_type=jnp.float32,
                )
                totals[side] = term if totals[side] is None else totals[side] + term
        return jnp.concatenate(totals, axis=1)

    grads_t = project(wg_copy, wg_ref, g_cuts, g_copies, lambda k, t: g_ref[t, k], 1)
    wide_ref[...] = project(wx_copy, wx_ref, x_cuts, x_copies, lambda k, t: x_ref[k, t], 0)
    rank = grads_t.shape[0]
    side = rank_ref[0] & 1
    for out, taken in ((keep_ref, side), (send_ref, side ^ 1)):
        out[:rank, :] = grads_t
        out[rank:, :] = wide_ref[pl.ds(pl.multiple_of(taken * own, own), own), :]


def project(inputs, out_grads, in_proj, out_proj, me, own):
    rank = in_proj.shape[1]
    tokens, hidden = inputs.shape
    width = out_grads.shape[1]
    copies = 2 + len(cuts_of(width, 512)) + len(cuts_of(hidden, 768))
    arrays = (inputs.T, out_grads, in_proj.T, out_proj.T)
    in_hbm = pl.BlockSpec(memory_space=pltpu.HBM)
    return pl.pallas_call(
        functools.partial(project_kernel, own),
        out_shape=[jax.ShapeDtypeStruct((rank + own, tokens), jnp.float32)] * 2,
        in_specs=[pl.BlockSpec(memory_space=pltpu.SMEM)] + [in_hbm] * len(arrays),
        out_specs=[pl.BlockSpec(memory_space=pltpu.VMEM)] * 2,
        scratch_shapes=[
            pltpu.VMEM((hidden, tokens), jnp.bfloat16),
            pltpu.VMEM((tokens, width), jnp.bfloat16),
            pltpu.VMEM((rank, hidden), jnp.bfloat16),
            pltpu.VMEM((rank, width), jnp.bfloat16),
            pltpu.VMEM((rank, tokens), jnp.float32),
            pltpu.SemaphoreType.DMA((copies,)),
        ],
        compiler_params=pltpu.CompilerParams(vmem_limit_bytes=VMEM_LIMIT),
        name="project",
    )(me, *(pltpu.with_memory_space_constraint(array, pltpu.HBM) for array in arrays))


def halve_kernel(own, rank_ref, kept_ref, came_ref, keep_ref, send_ref, sum_ref):
    sum_ref[...] = kept_ref[...] + came_ref[...]
    place = rank_ref[0] // 2
    for out, taken in ((keep_ref, place), (send_ref, place ^ 1)):
        out[:own, :] = sum_ref[pl.ds(pl.multiple_of(taken * own, own), own), :]
        out[own:, :] = sum_ref[-own:, :]


def halve(kept, came, me, own):
    rows, tokens = kept.shape
    whole = pl.BlockSpec(memory_space=pltpu.VMEM)
    return pl.pallas_call(
        functools.partial(halve_kernel, own),
        out_shape=[jax.ShapeDtypeStruct((2 * own, tokens), jnp.float32)] * 2,
        in_specs=[pl.BlockSpec(memory_space=pltpu.SMEM), whole, whole],
        out_specs=[whole] * 2,
        scratch_shapes=[pltpu.VMEM((rows, tokens), jnp.float32)],
        compiler_params=pltpu.CompilerParams(vmem_limit_bytes=VMEM_LIMIT),
        name="halve",
    )(me, kept, came)


def pick_kernel(rank, own, rank_ref, queries_ref, out_ref):
    lanes = out_ref.shape[1]
    wide = lanes * rank // own
    steps = own * own // lanes
    asked = queries_ref.shape[0]
    me = rank_ref[0]
    start = (me // 2) * (own * rank)
    rows = jnp.concatenate(
        [
            queries_ref[:, pl.ds(pl.multiple_of(start + i * wide, lanes), wide)]
            for i in range(steps)
        ],
        axis=0,
    )
    source = lax.broadcasted_iota(jnp.int32, (wide, lanes), 0)
    place = lax.broadcasted_iota(jnp.int32, (wide, lanes), 1)
    wanted = (place // own) * rank + place % own + (me & 1) * own
    chosen = jnp.where(source == wanted, 1.0, 0.0).astype(jnp.bfloat16)
    high = rows.astype(jnp.bfloat16)
    rest = rows - high.astype(jnp.float32)
    middle = rest.astype(jnp.bfloat16)
    low = (rest - middle.astype(jnp.float32)).astype(jnp.bfloat16)
    terms = [
        jnp.dot(term, chosen, preferred_element_type=jnp.float32) for term in (high, middle, low)
    ]
    out_ref[...] = terms[0] + (terms[1] + terms[2])


def pick(queries, me, rank, own):
    lanes = 128
    rows = queries.shape[0] * own * own // lanes
    whole = pl.BlockSpec(memory_space=pltpu.VMEM)
    return pl.pallas_call(
        functools.partial(pick_kernel, rank, own),
        out_shape=jax.ShapeDtypeStruct((rows, lanes), jnp.float32),
        in_specs=[pl.BlockSpec(memory_space=pltpu.SMEM), whole],
        out_specs=whole,
        compiler_params=pltpu.CompilerParams(vmem_limit_bytes=VMEM_LIMIT),
        name="pick",
    )(me, queries)


def grads_kernel(weights_ref, kept_ref, came_ref, asked_ref, out_ref):
    summed = kept_ref[...] + came_ref[...]
    weights = weights_ref[...]
    own = summed.shape[0] // 2
    group = out_ref.shape[1] // own
    inputs_t = summed[own:, :]
    zero = jnp.zeros_like(inputs_t)
    right = jnp.concatenate(
        [
            jnp.concatenate([inputs_t if j == k else zero for k in range(group)], axis=1)
            for j in range(group)
        ],
        axis=0,
    )
    rows = []
    for i in range(own // group):
        rows.append(
            jnp.concatenate(
                [weights * summed[group * i + j : group * i + j + 1, :] for j in range(group)],
                axis=1,
            )
        )
    left = jnp.concatenate(rows, axis=0)
    count = left.shape[0]
    out_ref[:count, :] = dot_nt(left, right)
    out_ref[count:, :] = asked_ref[...]


def gradients(weights, kept, came, asked):
    lanes = asked.shape[1]
    own = kept.shape[0] // 2
    rows = own * own // lanes * weights.shape[0] + asked.shape[0]
    return pl.pallas_call(
        grads_kernel,
        out_shape=jax.ShapeDtypeStruct((rows, lanes), jnp.float32),
        compiler_params=pltpu.CompilerParams(vmem_limit_bytes=VMEM_LIMIT),
        name="gradients",
    )(weights, kept, came, asked)


def grams_kernel(steps, seqs, me_ref, *refs):
    blocks, out_ref = refs[-2::-1], refs[-1]
    count = steps * seqs
    asked = (blocks[0].shape[0] - count) // steps
    given = [block[count:, :] for block in blocks]
    ordered = []
    for place in range(len(blocks)):
        chosen = given[0]
        for m in range(1, len(blocks)):
            chosen = jnp.where((me_ref[0] ^ place) == m, given[m], chosen)
        ordered.append(chosen)
    lanes = []
    for i in range(steps):
        rows = [block[i * seqs : (i + 1) * seqs, :] for block in blocks]
        rows += [chosen[i * asked : (i + 1) * asked, :] for chosen in ordered]
        lanes.append(jnp.concatenate(rows, axis=0))
    both = jnp.concatenate(lanes, axis=1)
    result = dot_nt(both, both[: len(blocks) * seqs])
    half = result.shape[0] // 2
    out_ref[...] = jnp.concatenate([result[:half, :], result[half:, :]], axis=1)


def grams(me, blocks, steps, seqs):
    asked = blocks[0].shape[0] // steps - seqs
    total = len(blocks) * seqs
    whole = pl.BlockSpec(memory_space=pltpu.VMEM)
    return pl.pallas_call(
        functools.partial(grams_kernel, steps, seqs),
        out_shape=jax.ShapeDtypeStruct(((total + len(blocks) * asked) // 2, 2 * total), jnp.float32),
        in_specs=[pl.BlockSpec(memory_space=pltpu.SMEM)] + [whole] * len(blocks),
        out_specs=whole,
        compiler_params=pltpu.CompilerParams(vmem_limit_bytes=VMEM_LIMIT),
        name="grams",
    )(me, *blocks)


def scales(count):
    first = 2.0 / (1.0 + 1.0 / count)
    off = count / (count + 1.0)
    steps = []
    while off > 1e-7:
        steps.append(2.0 / (2.0 - off * off))
        off = off * off / (2.0 - off * off)
    return first, steps


def solve_kernel(seqs, *refs):
    parts, out_ref = refs[:-1], refs[-1]
    packed = (parts[0][...] + parts[1][...]) + (parts[2][...] + parts[3][...])
    lane = lax.broadcasted_iota(jnp.int32, packed.shape, 1)
    turned = pltpu.roll(packed, seqs, 1)
    both = jnp.concatenate(
        [jnp.where(lane < seqs, packed, turned), jnp.where(lane < seqs, turned, packed)], axis=0
    )
    lane = lax.broadcasted_iota(jnp.int32, both.shape, 1)
    row = lax.broadcasted_iota(jnp.int32, both.shape, 0)
    unit = jnp.where((lane & (seqs - 1)) == row, 1.0, 0.0)
    total = jnp.sum(jnp.where(lane == row, both, 0.0)[:seqs], axis=(0, 1), keepdims=True)
    first, steps = scales(seqs)
    state = first * (both / total + unit * (damping / seqs))
    left_lanes = lane < seqs
    for at, step in enumerate(steps):
        high = state.astype(jnp.bfloat16).astype(jnp.float32)
        low = state - high
        left = jnp.where(left_lanes, high, low).astype(jnp.bfloat16)
        high = high[:seqs].astype(jnp.bfloat16)
        low = low[:seqs].astype(jnp.bfloat16)
        if at + 1 == len(steps):
            left, state = left[seqs:], state[seqs:]
        product = jnp.dot(
            left, jnp.concatenate([high, high], axis=0), preferred_element_type=jnp.float32
        ) + jnp.dot(left, jnp.concatenate([low, low], axis=0), preferred_element_type=jnp.float32)
        state = step * (2.0 * state - product)
    out_ref[...] = state[:, : out_ref.shape[1]]


def solve(parts, seqs, asked, seq_dev):
    return pl.pallas_call(
        functools.partial(solve_kernel, seqs),
        out_shape=jax.ShapeDtypeStruct((asked, seq_dev), jnp.float32),
        compiler_params=pltpu.CompilerParams(vmem_limit_bytes=VMEM_LIMIT),
        name="solve",
    )(*parts)


def from_partner(value, axis, size, m):
    return lax.ppermute(value, axis, [(i, i ^ m) for i in range(size)])


def from_partners(value, axis, size):
    return [from_partner(value, axis, size, m) for m in reversed(range(1, size))] + [value]


def finish_long(message, steps, first, seq_dev):
    every = lax.all_gather(message, "dp", axis=0)
    lanes = message.shape[1]

    def rows_of(block):
        block = block.reshape(block.shape[0], steps, -1, lanes).transpose(0, 2, 1, 3)
        return block.reshape(-1, steps * lanes)

    count = steps * seq_dev
    grads, asked = rows_of(every[:, :count]), rows_of(every[:, count:])
    both = jnp.einsum(
        "ik,jk->ij", jnp.concatenate([grads, asked], axis=0), grads,
        precision=lax.Precision.HIGHEST,
    )
    both = lax.psum(both, "tensor")
    count = grads.shape[0]
    kernel, products = both[:count], both[count:]
    damp = damping * jnp.trace(kernel) / count
    unit = jnp.eye(count, dtype=jnp.float32)
    factor = jnp.linalg.cholesky(kernel + damp * unit)
    picks = lax.dynamic_slice_in_dim(unit, first, seq_dev, 1)
    solved = jax.scipy.linalg.cho_solve((factor, True), picks)
    return jnp.dot(products, solved, precision=lax.Precision.HIGHEST)


def per_device(sizes, inputs, out_grads, in_proj, out_proj, seq_ids, counts, queries):
    parts, blocks = sizes
    rank = in_proj.shape[1]
    seq_dev = counts.shape[0]
    me = lax.axis_index("tensor")
    place = lax.axis_index("dp")
    first = place * seq_dev
    own = 2 * rank // parts
    rank_of = me.reshape(1)
    kept, sent = project(inputs, out_grads, in_proj, out_proj, rank_of, own)
    asked = pick(queries, rank_of, rank, own)
    weights = token_weights(seq_ids, counts, first)
    came = from_partner(sent, "tensor", parts, 1)
    kept, sent = halve(kept, came, rank_of, own)
    came = from_partner(sent, "tensor", parts, 2)
    message = gradients(weights, kept, came, asked)
    steps = own * own // message.shape[1]
    if blocks > SMALL:
        return finish_long(message, steps, first, seq_dev)
    partial = grams(place.reshape(1), from_partners(message, "dp", blocks), steps, seq_dev)
    partial = from_partners(partial, "tensor", parts)
    return solve(partial, blocks * seq_dev, blocks * queries.shape[0], seq_dev)


def solution(mesh):
    in_specs = (
        P(("groups", "dp"), "tensor"),
        P(("groups", "dp"), "tensor"),
        P("tensor", None),
        P("tensor", None),
        P(("groups", "dp")),
        P(("groups", "dp")),
        P(("groups", "dp"), None),
    )
    sizes = (mesh.shape["tensor"], mesh.shape["dp"])
    return jax.shard_map(
        functools.partial(per_device, sizes),
        mesh=mesh,
        in_specs=in_specs,
        out_specs=P("groups", "dp"),
        check_vma=False,
    )
```

```python
import functools

import jax
import jax.numpy as jnp
from jax import lax
from jax.experimental import pallas as pl
from jax.experimental.pallas import tpu as pltpu
from jax.sharding import PartitionSpec as P

damping = 0.5
VMEM_LIMIT = 32 * 1024 * 1024
SMALL = 4


def token_weights(seq_ids, counts, first):
    local_ids = seq_ids - first
    slots = jnp.arange(counts.shape[0], dtype=jnp.int32)
    member = local_ids[None, :] == slots[:, None]
    starts = jnp.sum((local_ids[None, :] < slots[:, None]).astype(jnp.int32), axis=1)
    offset = jnp.arange(seq_ids.shape[0], dtype=jnp.int32)[None, :] - starts[:, None]
    scale = 1.0 / counts.astype(jnp.float32)
    return jnp.where(member & (offset < counts[:, None]), scale[:, None], 0.0)


def cuts_of(extent, step):
    return [(at, min(step, extent - at)) for at in range(0, extent, step)]


def two_terms(value):
    high = value.astype(jnp.bfloat16)
    low = (value - high.astype(jnp.float32)).astype(jnp.bfloat16)
    return high, low


def dot_nt(left, right):
    dims = (((1,), (1,)), ((), ()))
    lh, ll = two_terms(left)
    rh, rl = two_terms(right)
    mul = functools.partial(
        lax.dot_general, dimension_numbers=dims, preferred_element_type=jnp.float32
    )
    return mul(lh, rh) + (mul(lh, rl) + mul(ll, rh))


def project_kernel(own, rank_ref, x_hbm, g_hbm, wx_hbm, wg_hbm, keep_ref, send_ref, *scratch):
    x_ref, g_ref, wx_ref, wg_ref, wide_ref, sems = scratch
    copies = []

    def fetch(src, dst, index):
        copy = pltpu.make_async_copy(src, dst, sems.at[index])
        copy.start()
        return copy

    g_cuts = cuts_of(g_ref.shape[1], 512)
    x_cuts = cuts_of(x_ref.shape[0], 768)
    wg_copy = fetch(wg_hbm, wg_ref, 0)
    index = 2
    g_copies = []
    for at, size in g_cuts:
        columns = pl.ds(at, size)
        g_copies.append(fetch(g_hbm.at[:, columns], g_ref.at[:, columns], index))
        index += 1
    wx_copy = fetch(wx_hbm, wx_ref, 1)
    x_copies = []
    for at, size in x_cuts:
        rows = pl.ds(at, size)
        x_copies.append(fetch(x_hbm.at[rows, :], x_ref.at[rows, :], index))
        index += 1

    def project(w_copy, w_ref, cuts, copies, ref, along):
        order = 1 if along == 0 else -1
        total = None
        w_copy.wait()
        for (at, size), copy in zip(cuts, copies):
            copy.wait()
            term = lax.dot_general(
                w_ref[:, at : at + size],
                ref[(slice(at, at + size), slice(None))[::order]],
                (((1,), (along,)), ((), ())),
                preferred_element_type=jnp.float32,
            )
            total = term if total is None else total + term
        return total

    grads_t = project(wg_copy, wg_ref, g_cuts, g_copies, g_ref, 1)
    wide_ref[...] = project(wx_copy, wx_ref, x_cuts, x_copies, x_ref, 0)
    rank = grads_t.shape[0]
    side = rank_ref[0] & 1
    for out, taken in ((keep_ref, side), (send_ref, side ^ 1)):
        out[:rank, :] = grads_t
        out[rank:, :] = wide_ref[pl.ds(pl.multiple_of(taken * own, own), own), :]


def project(inputs, out_grads, in_proj, out_proj, me, own):
    rank = in_proj.shape[1]
    tokens, hidden = inputs.shape
    width = out_grads.shape[1]
    copies = 2 + len(cuts_of(width, 512)) + len(cuts_of(hidden, 768))
    arrays = (inputs.T, out_grads, in_proj.T, out_proj.T)
    in_hbm = pl.BlockSpec(memory_space=pltpu.HBM)
    return pl.pallas_call(
        functools.partial(project_kernel, own),
        out_shape=[jax.ShapeDtypeStruct((rank + own, tokens), jnp.float32)] * 2,
        in_specs=[pl.BlockSpec(memory_space=pltpu.SMEM)] + [in_hbm] * len(arrays),
        out_specs=[pl.BlockSpec(memory_space=pltpu.VMEM)] * 2,
        scratch_shapes=[
            pltpu.VMEM((hidden, tokens), jnp.bfloat16),
            pltpu.VMEM((tokens, width), jnp.bfloat16),
            pltpu.VMEM((rank, hidden), jnp.bfloat16),
            pltpu.VMEM((rank, width), jnp.bfloat16),
            pltpu.VMEM((rank, tokens), jnp.float32),
            pltpu.SemaphoreType.DMA((copies,)),
        ],
        compiler_params=pltpu.CompilerParams(vmem_limit_bytes=VMEM_LIMIT),
        name="project",
    )(me, *(pltpu.with_memory_space_constraint(array, pltpu.HBM) for array in arrays))


def halve_kernel(own, rank_ref, kept_ref, came_ref, keep_ref, send_ref, same_ref, sum_ref):
    sum_ref[...] = kept_ref[...] + came_ref[...]
    place = rank_ref[0] // 2
    keep_ref[:own, :] = sum_ref[pl.ds(pl.multiple_of(place * own, own), own), :]
    keep_ref[own:, :] = sum_ref[-own:, :]
    send_ref[...] = sum_ref[pl.ds(pl.multiple_of((place ^ 1) * own, own), own), :]
    same_ref[...] = sum_ref[-own:, :]


def halve(kept, came, me, own):
    rows, tokens = kept.shape
    whole = pl.BlockSpec(memory_space=pltpu.VMEM)
    return pl.pallas_call(
        functools.partial(halve_kernel, own),
        out_shape=[
            jax.ShapeDtypeStruct((count * own, tokens), jnp.float32) for count in (2, 1, 1)
        ],
        in_specs=[pl.BlockSpec(memory_space=pltpu.SMEM), whole, whole],
        out_specs=[whole] * 3,
        scratch_shapes=[pltpu.VMEM((rows, tokens), jnp.float32)],
        compiler_params=pltpu.CompilerParams(vmem_limit_bytes=VMEM_LIMIT),
        name="halve",
    )(me, kept, came)


def pick_kernel(rank, own, rank_ref, queries_ref, out_ref):
    lanes = out_ref.shape[1]
    wide = lanes * rank // own
    steps = own * own // lanes
    asked = queries_ref.shape[0]
    me = rank_ref[0]
    start = (me // 2) * (own * rank)
    rows = jnp.concatenate(
        [
            queries_ref[:, pl.ds(pl.multiple_of(start + i * wide, lanes), wide)]
            for i in range(steps)
        ],
        axis=0,
    )
    source = lax.broadcasted_iota(jnp.int32, (wide, lanes), 0)
    place = lax.broadcasted_iota(jnp.int32, (wide, lanes), 1)
    wanted = (place // own) * rank + place % own + (me & 1) * own
    chosen = jnp.where(source == wanted, 1.0, 0.0).astype(jnp.bfloat16)
    high = rows.astype(jnp.bfloat16)
    rest = rows - high.astype(jnp.float32)
    middle = rest.astype(jnp.bfloat16)
    low = (rest - middle.astype(jnp.float32)).astype(jnp.bfloat16)
    terms = [
        jnp.dot(term, chosen, preferred_element_type=jnp.float32) for term in (high, middle, low)
    ]
    out_ref[...] = terms[0] + (terms[1] + terms[2])


def pick(queries, me, rank, own):
    lanes = 128
    rows = queries.shape[0] * own * own // lanes
    whole = pl.BlockSpec(memory_space=pltpu.VMEM)
    return pl.pallas_call(
        functools.partial(pick_kernel, rank, own),
        out_shape=jax.ShapeDtypeStruct((rows, lanes), jnp.float32),
        in_specs=[pl.BlockSpec(memory_space=pltpu.SMEM), whole],
        out_specs=whole,
        compiler_params=pltpu.CompilerParams(vmem_limit_bytes=VMEM_LIMIT),
        name="pick",
    )(me, queries)


def grads_kernel(weights_ref, kept_ref, grads_ref, inputs_ref, asked_ref, out_ref):
    own = kept_ref.shape[0] // 2
    summed = kept_ref[:own, :] + grads_ref[...]
    inputs_t = kept_ref[own:, :] + inputs_ref[...]
    weights = weights_ref[...]
    group = out_ref.shape[1] // own
    zero = jnp.zeros_like(inputs_t)
    right = jnp.concatenate(
        [
            jnp.concatenate([inputs_t if j == k else zero for k in range(group)], axis=1)
            for j in range(group)
        ],
        axis=0,
    )
    rows = []
    for i in range(own // group):
        rows.append(
            jnp.concatenate(
                [weights * summed[group * i + j : group * i + j + 1, :] for j in range(group)],
                axis=1,
            )
        )
    left = jnp.concatenate(rows, axis=0)
    count = left.shape[0]
    out_ref[:count, :] = dot_nt(left, right)
    out_ref[count:, :] = asked_ref[...]


def gradients(weights, kept, grads, inputs, asked):
    lanes = asked.shape[1]
    own = kept.shape[0] // 2
    rows = own * own // lanes * weights.shape[0] + asked.shape[0]
    return pl.pallas_call(
        grads_kernel,
        out_shape=jax.ShapeDtypeStruct((rows, lanes), jnp.float32),
        compiler_params=pltpu.CompilerParams(vmem_limit_bytes=VMEM_LIMIT),
        name="gradients",
    )(weights, kept, grads, inputs, asked)


def grams_kernel(steps, seqs, me_ref, *refs):
    blocks, out_ref = refs[-2::-1], refs[-1]
    count = steps * seqs
    asked = (blocks[0].shape[0] - count) // steps
    given = [block[count:, :] for block in blocks]
    ordered = []
    for place in range(len(blocks)):
        chosen = given[0]
        for m in range(1, len(blocks)):
            chosen = jnp.where((me_ref[0] ^ place) == m, given[m], chosen)
        ordered.append(chosen)
    lanes = []
    for i in range(steps):
        rows = [block[i * seqs : (i + 1) * seqs, :] for block in blocks]
        rows += [chosen[i * asked : (i + 1) * asked, :] for chosen in ordered]
        lanes.append(jnp.concatenate(rows, axis=0))
    both = jnp.concatenate(lanes, axis=1)
    result = dot_nt(both, both[: len(blocks) * seqs])
    half = result.shape[0] // 2
    out_ref[...] = jnp.concatenate([result[:half, :], result[half:, :]], axis=1)


def grams(me, blocks, steps, seqs):
    asked = blocks[0].shape[0] // steps - seqs
    total = len(blocks) * seqs
    whole = pl.BlockSpec(memory_space=pltpu.VMEM)
    return pl.pallas_call(
        functools.partial(grams_kernel, steps, seqs),
        out_shape=jax.ShapeDtypeStruct(((total + len(blocks) * asked) // 2, 2 * total), jnp.float32),
        in_specs=[pl.BlockSpec(memory_space=pltpu.SMEM)] + [whole] * len(blocks),
        out_specs=whole,
        compiler_params=pltpu.CompilerParams(vmem_limit_bytes=VMEM_LIMIT),
        name="grams",
    )(me, *blocks)


def scales(count):
    first = 2.0 / (1.0 + 1.0 / count)
    off = count / (count + 1.0)
    steps = []
    while off > 1e-7:
        steps.append(2.0 / (2.0 - off * off))
        off = off * off / (2.0 - off * off)
    return first, steps


def solve_kernel(seqs, *refs):
    parts, out_ref = refs[:-1], refs[-1]
    packed = (parts[0][...] + parts[1][...]) + (parts[2][...] + parts[3][...])
    lane = lax.broadcasted_iota(jnp.int32, packed.shape, 1)
    turned = pltpu.roll(packed, seqs, 1)
    both = jnp.concatenate(
        [jnp.where(lane < seqs, packed, turned), jnp.where(lane < seqs, turned, packed)], axis=0
    )
    lane = lax.broadcasted_iota(jnp.int32, both.shape, 1)
    row = lax.broadcasted_iota(jnp.int32, both.shape, 0)
    unit = jnp.where((lane & (seqs - 1)) == row, 1.0, 0.0)
    total = jnp.sum(jnp.where(lane == row, both, 0.0)[:seqs], axis=(0, 1), keepdims=True)
    first, steps = scales(seqs)
    state = first * (both / total + unit * (damping / seqs))
    left_lanes = lane < seqs
    for at, step in enumerate(steps):
        high = state.astype(jnp.bfloat16).astype(jnp.float32)
        low = state - high
        left = jnp.where(left_lanes, high, low).astype(jnp.bfloat16)
        high = high[:seqs].astype(jnp.bfloat16)
        low = low[:seqs].astype(jnp.bfloat16)
        right = jnp.concatenate([high, high, low, low], axis=0)
        if at + 1 == len(steps):
            left, state = left[seqs:], state[seqs:]
        product = jnp.dot(
            jnp.concatenate([left, left], axis=1), right, preferred_element_type=jnp.float32
        )
        state = step * (2.0 * state - product)
    out_ref[...] = state[:, : out_ref.shape[1]]


def solve(parts, seqs, asked, seq_dev):
    return pl.pallas_call(
        functools.partial(solve_kernel, seqs),
        out_shape=jax.ShapeDtypeStruct((asked, seq_dev), jnp.float32),
        compiler_params=pltpu.CompilerParams(vmem_limit_bytes=VMEM_LIMIT),
        name="solve",
    )(*parts)


def from_partner(value, axis, size, m):
    return lax.ppermute(value, axis, [(i, i ^ m) for i in range(size)])


def from_partners(value, axis, size):
    return [from_partner(value, axis, size, m) for m in reversed(range(1, size))] + [value]


def finish_long(message, steps, first, seq_dev):
    every = lax.all_gather(message, "dp", axis=0)
    lanes = message.shape[1]

    def rows_of(block):
        block = block.reshape(block.shape[0], steps, -1, lanes).transpose(0, 2, 1, 3)
        return block.reshape(-1, steps * lanes)

    count = steps * seq_dev
    grads, asked = rows_of(every[:, :count]), rows_of(every[:, count:])
    both = jnp.einsum(
        "ik,jk->ij", jnp.concatenate([grads, asked], axis=0), grads,
        precision=lax.Precision.HIGHEST,
    )
    both = lax.psum(both, "tensor")
    count = grads.shape[0]
    kernel, products = both[:count], both[count:]
    damp = damping * jnp.trace(kernel) / count
    unit = jnp.eye(count, dtype=jnp.float32)
    factor = jnp.linalg.cholesky(kernel + damp * unit)
    picks = lax.dynamic_slice_in_dim(unit, first, seq_dev, 1)
    solved = jax.scipy.linalg.cho_solve((factor, True), picks)
    return jnp.dot(products, solved, precision=lax.Precision.HIGHEST)


def per_device(sizes, inputs, out_grads, in_proj, out_proj, seq_ids, counts, queries):
    parts, blocks = sizes
    rank = in_proj.shape[1]
    seq_dev = counts.shape[0]
    me = lax.axis_index("tensor")
    place = lax.axis_index("dp")
    first = place * seq_dev
    own = 2 * rank // parts
    rank_of = me.reshape(1)
    kept, sent = project(inputs, out_grads, in_proj, out_proj, rank_of, own)
    asked = pick(queries, rank_of, rank, own)
    weights = token_weights(seq_ids, counts, first)
    came = from_partner(sent, "tensor", parts, 1)
    kept, *sent = halve(kept, came, rank_of, own)
    came = [from_partner(rows, "tensor", parts, 2) for rows in sent]
    message = gradients(weights, kept, *came, asked)
    steps = own * own // message.shape[1]
    if blocks > SMALL:
        return finish_long(message, steps, first, seq_dev)
    partial = grams(place.reshape(1), from_partners(message, "dp", blocks), steps, seq_dev)
    partial = from_partners(partial, "tensor", parts)
    return solve(partial, blocks * seq_dev, blocks * queries.shape[0], seq_dev)


def solution(mesh):
    in_specs = (
        P(("groups", "dp"), "tensor"),
        P(("groups", "dp"), "tensor"),
        P("tensor", None),
        P("tensor", None),
        P(("groups", "dp")),
        P(("groups", "dp")),
        P(("groups", "dp"), None),
    )
    sizes = (mesh.shape["tensor"], mesh.shape["dp"])
    return jax.shard_map(
        functools.partial(per_device, sizes),
        mesh=mesh,
        in_specs=in_specs,
        out_specs=P("groups", "dp"),
        check_vma=False,
    )
```

```python
import functools

import jax
import jax.numpy as jnp
from jax import lax
from jax.experimental import pallas as pl
from jax.experimental.pallas import tpu as pltpu
from jax.sharding import PartitionSpec as P

damping = 0.5
VMEM_LIMIT = 32 * 1024 * 1024
SMALL = 4


def token_weights(seq_ids, counts, first):
    local_ids = seq_ids - first
    slots = jnp.arange(counts.shape[0], dtype=jnp.int32)
    member = local_ids[None, :] == slots[:, None]
    starts = jnp.sum((local_ids[None, :] < slots[:, None]).astype(jnp.int32), axis=1)
    offset = jnp.arange(seq_ids.shape[0], dtype=jnp.int32)[None, :] - starts[:, None]
    scale = 1.0 / counts.astype(jnp.float32)
    return jnp.where(member & (offset < counts[:, None]), scale[:, None], 0.0)


def cuts_of(extent, step):
    return [(at, min(step, extent - at)) for at in range(0, extent, step)]


def two_terms(value):
    high = value.astype(jnp.bfloat16)
    low = (value - high.astype(jnp.float32)).astype(jnp.bfloat16)
    return high, low


def dot_nt(left, right):
    rows = left.shape[0]
    lh, ll = two_terms(left)
    rh, rl = two_terms(right)
    mul = functools.partial(
        lax.dot_general,
        dimension_numbers=(((1,), (1,)), ((), ())),
        preferred_element_type=jnp.float32,
    )
    both = mul(jnp.concatenate([lh, ll], axis=0), rh)
    return both[:rows] + (mul(lh, rl) + both[rows:])


def project_kernel(own, rank_ref, x_hbm, g_hbm, wx_hbm, wg_hbm, keep_ref, send_ref, *scratch):
    x_ref, g_ref, wx_ref, wg_ref, wide_ref, sems = scratch
    copies = []

    def fetch(src, dst, index):
        copy = pltpu.make_async_copy(src, dst, sems.at[index])
        copy.start()
        return copy

    g_cuts = cuts_of(g_ref.shape[1], 1024)
    x_cuts = cuts_of(x_ref.shape[0], 1024)
    wg_copy = fetch(wg_hbm, wg_ref, 0)
    index = 2
    g_copies = []
    for at, size in g_cuts:
        columns = pl.ds(at, size)
        g_copies.append(fetch(g_hbm.at[:, columns], g_ref.at[:, columns], index))
        index += 1
    wx_copy = fetch(wx_hbm, wx_ref, 1)
    x_copies = []
    for at, size in x_cuts:
        rows = pl.ds(at, size)
        x_copies.append(fetch(x_hbm.at[rows, :], x_ref.at[rows, :], index))
        index += 1

    def project(w_copy, w_ref, cuts, copies, ref, along):
        order = 1 if along == 0 else -1
        total = None
        w_copy.wait()
        for (at, size), copy in zip(cuts, copies):
            copy.wait()
            term = lax.dot_general(
                w_ref[:, at : at + size],
                ref[(slice(at, at + size), slice(None))[::order]],
                (((1,), (along,)), ((), ())),
                preferred_element_type=jnp.float32,
            )
            total = term if total is None else total + term
        return total

    grads_t = project(wg_copy, wg_ref, g_cuts, g_copies, g_ref, 1)
    wide_ref[...] = project(wx_copy, wx_ref, x_cuts, x_copies, x_ref, 0)
    rank = grads_t.shape[0]
    side = rank_ref[0] & 1
    for out, taken in ((keep_ref, side), (send_ref, side ^ 1)):
        out[:rank, :] = grads_t
        out[rank:, :] = wide_ref[pl.ds(pl.multiple_of(taken * own, own), own), :]


def project(inputs, out_grads, in_proj, out_proj, me, own):
    rank = in_proj.shape[1]
    tokens, hidden = inputs.shape
    width = out_grads.shape[1]
    copies = 2 + len(cuts_of(width, 1024)) + len(cuts_of(hidden, 1024))
    arrays = (inputs.T, out_grads, in_proj.T, out_proj.T)
    in_hbm = pl.BlockSpec(memory_space=pltpu.HBM)
    return pl.pallas_call(
        functools.partial(project_kernel, own),
        out_shape=[jax.ShapeDtypeStruct((rank + own, tokens), jnp.float32)] * 2,
        in_specs=[pl.BlockSpec(memory_space=pltpu.SMEM)] + [in_hbm] * len(arrays),
        out_specs=[pl.BlockSpec(memory_space=pltpu.VMEM)] * 2,
        scratch_shapes=[
            pltpu.VMEM((hidden, tokens), jnp.bfloat16),
            pltpu.VMEM((tokens, width), jnp.bfloat16),
            pltpu.VMEM((rank, hidden), jnp.bfloat16),
            pltpu.VMEM((rank, width), jnp.bfloat16),
            pltpu.VMEM((rank, tokens), jnp.float32),
            pltpu.SemaphoreType.DMA((copies,)),
        ],
        compiler_params=pltpu.CompilerParams(vmem_limit_bytes=VMEM_LIMIT),
        name="project",
    )(me, *(pltpu.with_memory_space_constraint(array, pltpu.HBM) for array in arrays))


def halve_kernel(own, rank_ref, kept_ref, came_ref, keep_ref, send_ref, sum_ref):
    sum_ref[...] = kept_ref[...] + came_ref[...]
    place = rank_ref[0] // 2
    for out, taken in ((keep_ref, place), (send_ref, place ^ 1)):
        out[:own, :] = sum_ref[pl.ds(pl.multiple_of(taken * own, own), own), :]
        out[own:, :] = sum_ref[-own:, :]


def halve(kept, came, me, own):
    rows, tokens = kept.shape
    whole = pl.BlockSpec(memory_space=pltpu.VMEM)
    return pl.pallas_call(
        functools.partial(halve_kernel, own),
        out_shape=[jax.ShapeDtypeStruct((2 * own, tokens), jnp.float32)] * 2,
        in_specs=[pl.BlockSpec(memory_space=pltpu.SMEM), whole, whole],
        out_specs=[whole] * 2,
        scratch_shapes=[pltpu.VMEM((rows, tokens), jnp.float32)],
        compiler_params=pltpu.CompilerParams(vmem_limit_bytes=VMEM_LIMIT),
        name="halve",
    )(me, kept, came)


def pick_kernel(rank, own, rank_ref, queries_ref, out_ref):
    lanes = out_ref.shape[1]
    wide = lanes * rank // own
    steps = own * own // lanes
    asked = queries_ref.shape[0]
    me = rank_ref[0]
    start = (me // 2) * (own * rank)
    rows = jnp.concatenate(
        [
            queries_ref[:, pl.ds(pl.multiple_of(start + i * wide, lanes), wide)]
            for i in range(steps)
        ],
        axis=0,
    )
    source = lax.broadcasted_iota(jnp.int32, (wide, lanes), 0)
    place = lax.broadcasted_iota(jnp.int32, (wide, lanes), 1)
    wanted = (place // own) * rank + place % own + (me & 1) * own
    chosen = jnp.where(source == wanted, 1.0, 0.0).astype(jnp.bfloat16)
    high = rows.astype(jnp.bfloat16)
    rest = rows - high.astype(jnp.float32)
    middle = rest.astype(jnp.bfloat16)
    low = (rest - middle.astype(jnp.float32)).astype(jnp.bfloat16)
    terms = [
        jnp.dot(term, chosen, preferred_element_type=jnp.float32) for term in (high, middle, low)
    ]
    out_ref[...] = terms[0] + (terms[1] + terms[2])


def pick(queries, me, rank, own):
    lanes = 128
    rows = queries.shape[0] * own * own // lanes
    whole = pl.BlockSpec(memory_space=pltpu.VMEM)
    return pl.pallas_call(
        functools.partial(pick_kernel, rank, own),
        out_shape=jax.ShapeDtypeStruct((rows, lanes), jnp.float32),
        in_specs=[pl.BlockSpec(memory_space=pltpu.SMEM), whole],
        out_specs=whole,
        compiler_params=pltpu.CompilerParams(vmem_limit_bytes=VMEM_LIMIT),
        name="pick",
    )(me, queries)


def grads_kernel(weights_ref, kept_ref, came_ref, asked_ref, out_ref):
    summed = kept_ref[...] + came_ref[...]
    weights = weights_ref[...]
    own = summed.shape[0] // 2
    group = out_ref.shape[1] // own
    inputs_t = summed[own:, :]
    made = []
    for j in range(group):
        left = [weights * summed[i + j : i + j + 1, :] for i in range(0, own, group)]
        made.append(dot_nt(jnp.concatenate(left, axis=0), inputs_t))
    count = made[0].shape[0]
    out_ref[:count, :] = jnp.concatenate(made, axis=1)
    out_ref[count:, :] = asked_ref[...]


def gradients(weights, kept, came, asked):
    lanes = asked.shape[1]
    own = kept.shape[0] // 2
    rows = own * own // lanes * weights.shape[0] + asked.shape[0]
    return pl.pallas_call(
        grads_kernel,
        out_shape=jax.ShapeDtypeStruct((rows, lanes), jnp.float32),
        compiler_params=pltpu.CompilerParams(vmem_limit_bytes=VMEM_LIMIT),
        name="gradients",
    )(weights, kept, came, asked)


def grams_kernel(steps, seqs, me_ref, *refs):
    blocks, out_ref = refs[-2::-1], refs[-1]
    count = steps * seqs
    asked = (blocks[0].shape[0] - count) // steps
    given = [block[count:, :] for block in blocks]
    ordered = []
    for place in range(len(blocks)):
        chosen = given[0]
        for m in range(1, len(blocks)):
            chosen = jnp.where((me_ref[0] ^ place) == m, given[m], chosen)
        ordered.append(chosen)
    lanes = []
    for i in range(steps):
        rows = [block[i * seqs : (i + 1) * seqs, :] for block in blocks]
        rows += [chosen[i * asked : (i + 1) * asked, :] for chosen in ordered]
        lanes.append(jnp.concatenate(rows, axis=0))
    both = jnp.concatenate(lanes, axis=1)
    result = dot_nt(both, both[: len(blocks) * seqs])
    half = result.shape[0] // 2
    out_ref[...] = jnp.concatenate([result[:half, :], result[half:, :]], axis=1)


def grams(me, blocks, steps, seqs):
    asked = blocks[0].shape[0] // steps - seqs
    total = len(blocks) * seqs
    whole = pl.BlockSpec(memory_space=pltpu.VMEM)
    return pl.pallas_call(
        functools.partial(grams_kernel, steps, seqs),
        out_shape=jax.ShapeDtypeStruct(((total + len(blocks) * asked) // 2, 2 * total), jnp.float32),
        in_specs=[pl.BlockSpec(memory_space=pltpu.SMEM)] + [whole] * len(blocks),
        out_specs=whole,
        compiler_params=pltpu.CompilerParams(vmem_limit_bytes=VMEM_LIMIT),
        name="grams",
    )(me, *blocks)


def scales(count):
    first = 2.0 / (1.0 + 1.0 / count)
    off = count / (count + 1.0)
    steps = []
    while off > 1e-7:
        steps.append(2.0 / (2.0 - off * off))
        off = off * off / (2.0 - off * off)
    return first, steps


def solve_kernel(seqs, *refs):
    parts, out_ref = refs[:-1], refs[-1]
    packed = (parts[0][...] + parts[1][...]) + (parts[2][...] + parts[3][...])
    lane = lax.broadcasted_iota(jnp.int32, packed.shape, 1)
    turned = pltpu.roll(packed, seqs, 1)
    both = jnp.concatenate(
        [jnp.where(lane < seqs, packed, turned), jnp.where(lane < seqs, turned, packed)], axis=0
    )
    lane = lax.broadcasted_iota(jnp.int32, both.shape, 1)
    row = lax.broadcasted_iota(jnp.int32, both.shape, 0)
    unit = jnp.where((lane & (seqs - 1)) == row, 1.0, 0.0)
    total = jnp.sum(jnp.where(lane == row, both, 0.0)[:seqs], axis=(0, 1), keepdims=True)
    first, steps = scales(seqs)
    state = first * (both / total + unit * (damping / seqs))
    left_lanes = lane < seqs
    for at, step in enumerate(steps):
        high = state.astype(jnp.bfloat16).astype(jnp.float32)
        low = state - high
        left = jnp.where(left_lanes, high, low).astype(jnp.bfloat16)
        high = high[:seqs].astype(jnp.bfloat16)
        low = low[:seqs].astype(jnp.bfloat16)
        right = jnp.concatenate([high, high, low, low], axis=0)
        if at + 1 == len(steps):
            left, state = left[seqs:], state[seqs:]
        product = jnp.dot(
            jnp.concatenate([left, left], axis=1), right, preferred_element_type=jnp.float32
        )
        state = step * (2.0 * state - product)
    out_ref[...] = state[:, : out_ref.shape[1]]


def solve(parts, seqs, asked, seq_dev):
    return pl.pallas_call(
        functools.partial(solve_kernel, seqs),
        out_shape=jax.ShapeDtypeStruct((asked, seq_dev), jnp.float32),
        compiler_params=pltpu.CompilerParams(vmem_limit_bytes=VMEM_LIMIT),
        name="solve",
    )(*parts)


def from_partner(value, axis, size, m):
    return lax.ppermute(value, axis, [(i, i ^ m) for i in range(size)])


def from_partners(value, axis, size):
    return [from_partner(value, axis, size, m) for m in reversed(range(1, size))] + [value]


def finish_long(message, steps, first, seq_dev):
    every = lax.all_gather(message, "dp", axis=0)
    lanes = message.shape[1]

    def rows_of(block):
        block = block.reshape(block.shape[0], steps, -1, lanes).transpose(0, 2, 1, 3)
        return block.reshape(-1, steps * lanes)

    count = steps * seq_dev
    grads, asked = rows_of(every[:, :count]), rows_of(every[:, count:])
    both = jnp.einsum(
        "ik,jk->ij", jnp.concatenate([grads, asked], axis=0), grads,
        precision=lax.Precision.HIGHEST,
    )
    both = lax.psum(both, "tensor")
    count = grads.shape[0]
    kernel, products = both[:count], both[count:]
    damp = damping * jnp.trace(kernel) / count
    unit = jnp.eye(count, dtype=jnp.float32)
    factor = jnp.linalg.cholesky(kernel + damp * unit)
    picks = lax.dynamic_slice_in_dim(unit, first, seq_dev, 1)
    solved = jax.scipy.linalg.cho_solve((factor, True), picks)
    return jnp.dot(products, solved, precision=lax.Precision.HIGHEST)


def per_device(sizes, inputs, out_grads, in_proj, out_proj, seq_ids, counts, queries):
    parts, blocks = sizes
    rank = in_proj.shape[1]
    seq_dev = counts.shape[0]
    me = lax.axis_index("tensor")
    place = lax.axis_index("dp")
    first = place * seq_dev
    own = 2 * rank // parts
    rank_of = me.reshape(1)
    kept, sent = project(inputs, out_grads, in_proj, out_proj, rank_of, own)
    asked = pick(queries, rank_of, rank, own)
    weights = token_weights(seq_ids, counts, first)
    came = from_partner(sent, "tensor", parts, 1)
    kept, sent = halve(kept, came, rank_of, own)
    came = from_partner(sent, "tensor", parts, 2)
    message = gradients(weights, kept, came, asked)
    steps = own * own // message.shape[1]
    if blocks > SMALL:
        return finish_long(message, steps, first, seq_dev)
    partial = grams(place.reshape(1), from_partners(message, "dp", blocks), steps, seq_dev)
    partial = from_partners(partial, "tensor", parts)
    return solve(partial, blocks * seq_dev, blocks * queries.shape[0], seq_dev)


def solution(mesh):
    in_specs = (
        P(("groups", "dp"), "tensor"),
        P(("groups", "dp"), "tensor"),
        P("tensor", None),
        P("tensor", None),
        P(("groups", "dp")),
        P(("groups", "dp")),
        P(("groups", "dp"), None),
    )
    sizes = (mesh.shape["tensor"], mesh.shape["dp"])
    return jax.shard_map(
        functools.partial(per_device, sizes),
        mesh=mesh,
        in_specs=in_specs,
        out_specs=P("groups", "dp"),
        check_vma=False,
    )
```

```python
import functools

import jax
import jax.numpy as jnp
from jax import lax
from jax.experimental import pallas as pl
from jax.experimental.pallas import tpu as pltpu
from jax.sharding import PartitionSpec as P

damping = 0.5
VMEM_LIMIT = 32 * 1024 * 1024
SMALL = 4


def token_weights(seq_ids, counts, first):
    local_ids = seq_ids - first
    slots = jnp.arange(counts.shape[0], dtype=jnp.int32)
    member = local_ids[None, :] == slots[:, None]
    starts = jnp.sum((local_ids[None, :] < slots[:, None]).astype(jnp.int32), axis=1)
    offset = jnp.arange(seq_ids.shape[0], dtype=jnp.int32)[None, :] - starts[:, None]
    scale = 1.0 / counts.astype(jnp.float32)
    return jnp.where(member & (offset < counts[:, None]), scale[:, None], 0.0)


def cuts_of(extent, step):
    return [(at, min(step, extent - at)) for at in range(0, extent, step)]


def two_terms(value):
    high = value.astype(jnp.bfloat16)
    low = (value - high.astype(jnp.float32)).astype(jnp.bfloat16)
    return high, low


def dot_nt(left, right):
    rows = left.shape[0]
    lh, ll = two_terms(left)
    rh, rl = two_terms(right)
    mul = functools.partial(
        lax.dot_general,
        dimension_numbers=(((1,), (1,)), ((), ())),
        preferred_element_type=jnp.float32,
    )
    both = mul(jnp.concatenate([lh, ll], axis=0), rh)
    return both[:rows] + (mul(lh, rl) + both[rows:])


def project_kernel(own, rank_ref, x_hbm, g_hbm, wx_hbm, wg_hbm, keep_ref, send_ref, *scratch):
    x_ref, g_ref, wx_ref, wg_ref, wide_ref, sems = scratch
    copies = []

    def fetch(src, dst, index):
        copy = pltpu.make_async_copy(src, dst, sems.at[index])
        copy.start()
        return copy

    g_cuts = cuts_of(g_ref.shape[1], 1024)
    x_cuts = cuts_of(x_ref.shape[0], 1024)
    wg_copy = fetch(wg_hbm, wg_ref, 0)
    index = 2
    g_copies = []
    for at, size in g_cuts:
        columns = pl.ds(at, size)
        g_copies.append(fetch(g_hbm.at[:, columns], g_ref.at[:, columns], index))
        index += 1
    wx_copy = fetch(wx_hbm, wx_ref, 1)
    x_copies = []
    for at, size in x_cuts:
        rows = pl.ds(at, size)
        x_copies.append(fetch(x_hbm.at[rows, :], x_ref.at[rows, :], index))
        index += 1

    def product(copies, terms):
        total = None
        for copy, (left, right, along) in zip(copies, terms):
            copy.wait()
            term = lax.dot_general(
                left(), right(), (((1,), (along,)), ((), ())), preferred_element_type=jnp.float32
            )
            total = term if total is None else total + term
        return total

    def cut(ref, at, size, along):
        return lambda: ref[at : at + size, :] if along == 0 else ref[:, at : at + size]

    wg_copy.wait()
    grads_t = product(
        g_copies, [(cut(g_ref, at, size, 1), cut(wg_ref, at, size, 1), 1) for at, size in g_cuts]
    ).T
    wx_copy.wait()
    wide_ref[...] = product(
        x_copies, [(cut(wx_ref, at, size, 1), cut(x_ref, at, size, 0), 0) for at, size in x_cuts]
    )
    rank = grads_t.shape[0]
    side = rank_ref[0] & 1
    for out, taken in ((keep_ref, side), (send_ref, side ^ 1)):
        out[:rank, :] = grads_t
        out[rank:, :] = wide_ref[pl.ds(pl.multiple_of(taken * own, own), own), :]


def project(inputs, out_grads, in_proj, out_proj, me, own):
    rank = in_proj.shape[1]
    tokens, hidden = inputs.shape
    width = out_grads.shape[1]
    copies = 2 + len(cuts_of(width, 1024)) + len(cuts_of(hidden, 1024))
    arrays = (inputs.T, out_grads, in_proj.T, out_proj.T)
    in_hbm = pl.BlockSpec(memory_space=pltpu.HBM)
    return pl.pallas_call(
        functools.partial(project_kernel, own),
        out_shape=[jax.ShapeDtypeStruct((rank + own, tokens), jnp.float32)] * 2,
        in_specs=[pl.BlockSpec(memory_space=pltpu.SMEM)] + [in_hbm] * len(arrays),
        out_specs=[pl.BlockSpec(memory_space=pltpu.VMEM)] * 2,
        scratch_shapes=[
            pltpu.VMEM((hidden, tokens), jnp.bfloat16),
            pltpu.VMEM((tokens, width), jnp.bfloat16),
            pltpu.VMEM((rank, hidden), jnp.bfloat16),
            pltpu.VMEM((rank, width), jnp.bfloat16),
            pltpu.VMEM((rank, tokens), jnp.float32),
            pltpu.SemaphoreType.DMA((copies,)),
        ],
        compiler_params=pltpu.CompilerParams(vmem_limit_bytes=VMEM_LIMIT),
        name="project",
    )(me, *(pltpu.with_memory_space_constraint(array, pltpu.HBM) for array in arrays))


def halve_kernel(own, rank_ref, kept_ref, came_ref, keep_ref, send_ref, sum_ref):
    sum_ref[...] = kept_ref[...] + came_ref[...]
    place = rank_ref[0] // 2
    for out, taken in ((keep_ref, place), (send_ref, place ^ 1)):
        out[:own, :] = sum_ref[pl.ds(pl.multiple_of(taken * own, own), own), :]
        out[own:, :] = sum_ref[-own:, :]


def halve(kept, came, me, own):
    rows, tokens = kept.shape
    whole = pl.BlockSpec(memory_space=pltpu.VMEM)
    return pl.pallas_call(
        functools.partial(halve_kernel, own),
        out_shape=[jax.ShapeDtypeStruct((2 * own, tokens), jnp.float32)] * 2,
        in_specs=[pl.BlockSpec(memory_space=pltpu.SMEM), whole, whole],
        out_specs=[whole] * 2,
        scratch_shapes=[pltpu.VMEM((rows, tokens), jnp.float32)],
        compiler_params=pltpu.CompilerParams(vmem_limit_bytes=VMEM_LIMIT),
        name="halve",
    )(me, kept, came)


def pick_kernel(rank, own, rank_ref, queries_ref, out_ref):
    lanes = out_ref.shape[1]
    wide = lanes * rank // own
    steps = own * own // lanes
    asked = queries_ref.shape[0]
    me = rank_ref[0]
    start = (me // 2) * (own * rank)
    rows = jnp.concatenate(
        [
            queries_ref[:, pl.ds(pl.multiple_of(start + i * wide, lanes), wide)]
            for i in range(steps)
        ],
        axis=0,
    )
    source = lax.broadcasted_iota(jnp.int32, (wide, lanes), 0)
    place = lax.broadcasted_iota(jnp.int32, (wide, lanes), 1)
    wanted = (place // own) * rank + place % own + (me & 1) * own
    chosen = jnp.where(source == wanted, 1.0, 0.0).astype(jnp.bfloat16)
    high = rows.astype(jnp.bfloat16)
    rest = rows - high.astype(jnp.float32)
    middle = rest.astype(jnp.bfloat16)
    low = (rest - middle.astype(jnp.float32)).astype(jnp.bfloat16)
    terms = [
        jnp.dot(term, chosen, preferred_element_type=jnp.float32) for term in (high, middle, low)
    ]
    out_ref[...] = terms[0] + (terms[1] + terms[2])


def pick(queries, me, rank, own):
    lanes = 128
    rows = queries.shape[0] * own * own // lanes
    whole = pl.BlockSpec(memory_space=pltpu.VMEM)
    return pl.pallas_call(
        functools.partial(pick_kernel, rank, own),
        out_shape=jax.ShapeDtypeStruct((rows, lanes), jnp.float32),
        in_specs=[pl.BlockSpec(memory_space=pltpu.SMEM), whole],
        out_specs=whole,
        compiler_params=pltpu.CompilerParams(vmem_limit_bytes=VMEM_LIMIT),
        name="pick",
    )(me, queries)


def grads_kernel(weights_ref, kept_ref, came_ref, asked_ref, out_ref):
    summed = kept_ref[...] + came_ref[...]
    weights = weights_ref[...]
    own = summed.shape[0] // 2
    group = out_ref.shape[1] // own
    inputs_t = summed[own:, :]
    zero = jnp.zeros_like(inputs_t)
    right = jnp.concatenate(
        [
            jnp.concatenate([inputs_t if j == k else zero for k in range(group)], axis=1)
            for j in range(group)
        ],
        axis=0,
    )
    rows = []
    for i in range(own // group):
        rows.append(
            jnp.concatenate(
                [weights * summed[group * i + j : group * i + j + 1, :] for j in range(group)],
                axis=1,
            )
        )
    left = jnp.concatenate(rows, axis=0)
    count = left.shape[0]
    out_ref[:count, :] = dot_nt(left, right)
    out_ref[count:, :] = asked_ref[...]


def gradients(weights, kept, came, asked):
    lanes = asked.shape[1]
    own = kept.shape[0] // 2
    rows = own * own // lanes * weights.shape[0] + asked.shape[0]
    return pl.pallas_call(
        grads_kernel,
        out_shape=jax.ShapeDtypeStruct((rows, lanes), jnp.float32),
        compiler_params=pltpu.CompilerParams(vmem_limit_bytes=VMEM_LIMIT),
        name="gradients",
    )(weights, kept, came, asked)


def grams_kernel(steps, seqs, me_ref, *refs):
    blocks, out_ref = refs[-2::-1], refs[-1]
    count = steps * seqs
    asked = (blocks[0].shape[0] - count) // steps
    given = [block[count:, :] for block in blocks]
    ordered = []
    for place in range(len(blocks)):
        chosen = given[0]
        for m in range(1, len(blocks)):
            chosen = jnp.where((me_ref[0] ^ place) == m, given[m], chosen)
        ordered.append(chosen)
    lanes = []
    for i in range(steps):
        rows = [block[i * seqs : (i + 1) * seqs, :] for block in blocks]
        rows += [chosen[i * asked : (i + 1) * asked, :] for chosen in ordered]
        lanes.append(jnp.concatenate(rows, axis=0))
    both = jnp.concatenate(lanes, axis=1)
    result = dot_nt(both, both[: len(blocks) * seqs])
    half = result.shape[0] // 2
    out_ref[...] = jnp.concatenate([result[:half, :], result[half:, :]], axis=1)


def grams(me, blocks, steps, seqs):
    asked = blocks[0].shape[0] // steps - seqs
    total = len(blocks) * seqs
    whole = pl.BlockSpec(memory_space=pltpu.VMEM)
    return pl.pallas_call(
        functools.partial(grams_kernel, steps, seqs),
        out_shape=jax.ShapeDtypeStruct(((total + len(blocks) * asked) // 2, 2 * total), jnp.float32),
        in_specs=[pl.BlockSpec(memory_space=pltpu.SMEM)] + [whole] * len(blocks),
        out_specs=whole,
        compiler_params=pltpu.CompilerParams(vmem_limit_bytes=VMEM_LIMIT),
        name="grams",
    )(me, *blocks)


def scales(count):
    first = 2.0 / (1.0 + 1.0 / count)
    off = count / (count + 1.0)
    steps = []
    while off > 1e-7:
        steps.append(2.0 / (2.0 - off * off))
        off = off * off / (2.0 - off * off)
    return first, steps


def solve_kernel(seqs, *refs):
    parts, out_ref = refs[:-1], refs[-1]
    packed = (parts[0][...] + parts[1][...]) + (parts[2][...] + parts[3][...])
    lane = lax.broadcasted_iota(jnp.int32, packed.shape, 1)
    turned = pltpu.roll(packed, seqs, 1)
    both = jnp.concatenate(
        [jnp.where(lane < seqs, packed, turned), jnp.where(lane < seqs, turned, packed)], axis=0
    )
    lane = lax.broadcasted_iota(jnp.int32, both.shape, 1)
    row = lax.broadcasted_iota(jnp.int32, both.shape, 0)
    unit = jnp.where((lane & (seqs - 1)) == row, 1.0, 0.0)
    total = jnp.sum(jnp.where(lane == row, both, 0.0)[:seqs], axis=(0, 1), keepdims=True)
    first, steps = scales(seqs)
    state = first * (both / total + unit * (damping / seqs))
    left_lanes = lane < seqs
    for at, step in enumerate(steps):
        high = state.astype(jnp.bfloat16).astype(jnp.float32)
        low = state - high
        left = jnp.where(left_lanes, high, low).astype(jnp.bfloat16)
        high = high[:seqs].astype(jnp.bfloat16)
        low = low[:seqs].astype(jnp.bfloat16)
        right = jnp.concatenate([high, high, low, low], axis=0)
        if at + 1 == len(steps):
            left, state = left[seqs:], state[seqs:]
        product = jnp.dot(
            jnp.concatenate([left, left], axis=1), right, preferred_element_type=jnp.float32
        )
        state = step * (2.0 * state - product)
    out_ref[...] = state[:, : out_ref.shape[1]]


def solve(parts, seqs, asked, seq_dev):
    return pl.pallas_call(
        functools.partial(solve_kernel, seqs),
        out_shape=jax.ShapeDtypeStruct((asked, seq_dev), jnp.float32),
        compiler_params=pltpu.CompilerParams(vmem_limit_bytes=VMEM_LIMIT),
        name="solve",
    )(*parts)


def from_partner(value, axis, size, m):
    return lax.ppermute(value, axis, [(i, i ^ m) for i in range(size)])


def from_partners(value, axis, size):
    return [from_partner(value, axis, size, m) for m in reversed(range(1, size))] + [value]


def finish_long(message, steps, first, seq_dev):
    every = lax.all_gather(message, "dp", axis=0)
    lanes = message.shape[1]

    def rows_of(block):
        block = block.reshape(block.shape[0], steps, -1, lanes).transpose(0, 2, 1, 3)
        return block.reshape(-1, steps * lanes)

    count = steps * seq_dev
    grads, asked = rows_of(every[:, :count]), rows_of(every[:, count:])
    both = jnp.einsum(
        "ik,jk->ij", jnp.concatenate([grads, asked], axis=0), grads,
        precision=lax.Precision.HIGHEST,
    )
    both = lax.psum(both, "tensor")
    count = grads.shape[0]
    kernel, products = both[:count], both[count:]
    damp = damping * jnp.trace(kernel) / count
    unit = jnp.eye(count, dtype=jnp.float32)
    factor = jnp.linalg.cholesky(kernel + damp * unit)
    picks = lax.dynamic_slice_in_dim(unit, first, seq_dev, 1)
    solved = jax.scipy.linalg.cho_solve((factor, True), picks)
    return jnp.dot(products, solved, precision=lax.Precision.HIGHEST)


def per_device(sizes, inputs, out_grads, in_proj, out_proj, seq_ids, counts, queries):
    parts, blocks = sizes
    rank = in_proj.shape[1]
    seq_dev = counts.shape[0]
    me = lax.axis_index("tensor")
    place = lax.axis_index("dp")
    first = place * seq_dev
    own = 2 * rank // parts
    rank_of = me.reshape(1)
    kept, sent = project(inputs, out_grads, in_proj, out_proj, rank_of, own)
    asked = pick(queries, rank_of, rank, own)
    weights = token_weights(seq_ids, counts, first)
    came = from_partner(sent, "tensor", parts, 1)
    kept, sent = halve(kept, came, rank_of, own)
    came = from_partner(sent, "tensor", parts, 2)
    message = gradients(weights, kept, came, asked)
    steps = own * own // message.shape[1]
    if blocks > SMALL:
        return finish_long(message, steps, first, seq_dev)
    partial = grams(place.reshape(1), from_partners(message, "dp", blocks), steps, seq_dev)
    partial = from_partners(partial, "tensor", parts)
    return solve(partial, blocks * seq_dev, blocks * queries.shape[0], seq_dev)


def solution(mesh):
    in_specs = (
        P(("groups", "dp"), "tensor"),
        P(("groups", "dp"), "tensor"),
        P("tensor", None),
        P("tensor", None),
        P(("groups", "dp")),
        P(("groups", "dp")),
        P(("groups", "dp"), None),
    )
    sizes = (mesh.shape["tensor"], mesh.shape["dp"])
    return jax.shard_map(
        functools.partial(per_device, sizes),
        mesh=mesh,
        in_specs=in_specs,
        out_specs=P("groups", "dp"),
        check_vma=False,
    )
```

```python
import functools

import jax
import jax.numpy as jnp
from jax import lax
from jax.experimental import pallas as pl
from jax.experimental.pallas import tpu as pltpu
from jax.sharding import PartitionSpec as P

damping = 0.5
VMEM_LIMIT = 32 * 1024 * 1024
SMALL = 4


def token_weights(seq_ids, counts, first):
    local_ids = seq_ids - first
    slots = jnp.arange(counts.shape[0], dtype=jnp.int32)
    member = local_ids[None, :] == slots[:, None]
    starts = jnp.sum((local_ids[None, :] < slots[:, None]).astype(jnp.int32), axis=1)
    offset = jnp.arange(seq_ids.shape[0], dtype=jnp.int32)[None, :] - starts[:, None]
    scale = 1.0 / counts.astype(jnp.float32)
    return jnp.where(member & (offset < counts[:, None]), scale[:, None], 0.0)


def cuts_of(extent, step):
    return [(at, min(step, extent - at)) for at in range(0, extent, step)]


def two_terms(value):
    high = value.astype(jnp.bfloat16)
    low = (value - high.astype(jnp.float32)).astype(jnp.bfloat16)
    return high, low


def dot_nt(left, right):
    rows = left.shape[0]
    lh, ll = two_terms(left)
    rh, rl = two_terms(right)
    mul = functools.partial(
        lax.dot_general,
        dimension_numbers=(((1,), (1,)), ((), ())),
        preferred_element_type=jnp.float32,
    )
    both = mul(jnp.concatenate([lh, ll], axis=0), rh)
    return both[:rows] + (mul(lh, rl) + both[rows:])


def project_kernel(own, rank_ref, x_hbm, g_hbm, wx_hbm, wg_hbm, keep_ref, send_ref, *scratch):
    x_ref, g_ref, wx_ref, wg_ref, wide_ref, sems = scratch
    copies = []

    def fetch(src, dst, index):
        copy = pltpu.make_async_copy(src, dst, sems.at[index])
        copy.start()
        return copy

    g_cuts = cuts_of(g_ref.shape[1], 1024)
    x_cuts = cuts_of(x_ref.shape[0], 1024)
    wg_copy = fetch(wg_hbm, wg_ref, 0)
    index = 2
    g_copies = []
    for at, size in g_cuts:
        columns = pl.ds(at, size)
        g_copies.append(fetch(g_hbm.at[:, columns], g_ref.at[:, columns], index))
        index += 1
    wx_copy = fetch(wx_hbm, wx_ref, 1)
    x_copies = []
    for at, size in x_cuts:
        rows = pl.ds(at, size)
        x_copies.append(fetch(x_hbm.at[rows, :], x_ref.at[rows, :], index))
        index += 1

    def product(copies, terms):
        total = None
        for copy, (left, right, along) in zip(copies, terms):
            copy.wait()
            term = lax.dot_general(
                left(), right(), (((1,), (along,)), ((), ())), preferred_element_type=jnp.float32
            )
            total = term if total is None else total + term
        return total

    def cut(ref, at, size, along):
        return lambda: ref[at : at + size, :] if along == 0 else ref[:, at : at + size]

    wg_copy.wait()
    grads_t = product(
        g_copies, [(cut(g_ref, at, size, 1), cut(wg_ref, at, size, 1), 1) for at, size in g_cuts]
    ).T
    wx_copy.wait()
    wide_ref[...] = product(
        x_copies, [(cut(wx_ref, at, size, 1), cut(x_ref, at, size, 0), 0) for at, size in x_cuts]
    )
    rank = grads_t.shape[0]
    side = rank_ref[0] & 1
    for out, taken in ((keep_ref, side), (send_ref, side ^ 1)):
        out[:rank, :] = grads_t
        out[rank:, :] = wide_ref[pl.ds(pl.multiple_of(taken * own, own), own), :]


def project(inputs, out_grads, in_proj, out_proj, me, own):
    rank = in_proj.shape[1]
    tokens, hidden = inputs.shape
    width = out_grads.shape[1]
    copies = 2 + len(cuts_of(width, 1024)) + len(cuts_of(hidden, 1024))
    arrays = (inputs.T, out_grads, in_proj.T, out_proj.T)
    in_hbm = pl.BlockSpec(memory_space=pltpu.HBM)
    return pl.pallas_call(
        functools.partial(project_kernel, own),
        out_shape=[jax.ShapeDtypeStruct((rank + own, tokens), jnp.float32)] * 2,
        in_specs=[pl.BlockSpec(memory_space=pltpu.SMEM)] + [in_hbm] * len(arrays),
        out_specs=[pl.BlockSpec(memory_space=pltpu.VMEM)] * 2,
        scratch_shapes=[
            pltpu.VMEM((hidden, tokens), jnp.bfloat16),
            pltpu.VMEM((tokens, width), jnp.bfloat16),
            pltpu.VMEM((rank, hidden), jnp.bfloat16),
            pltpu.VMEM((rank, width), jnp.bfloat16),
            pltpu.VMEM((rank, tokens), jnp.float32),
            pltpu.SemaphoreType.DMA((copies,)),
        ],
        compiler_params=pltpu.CompilerParams(vmem_limit_bytes=VMEM_LIMIT),
        name="project",
    )(me, *(pltpu.with_memory_space_constraint(array, pltpu.HBM) for array in arrays))


def halve_kernel(own, rank_ref, kept_ref, came_ref, keep_ref, send_ref, sum_ref):
    sum_ref[...] = kept_ref[...] + came_ref[...]
    place = rank_ref[0] // 2
    for out, taken in ((keep_ref, place), (send_ref, place ^ 1)):
        out[:own, :] = sum_ref[pl.ds(pl.multiple_of(taken * own, own), own), :]
        out[own:, :] = sum_ref[-own:, :]


def halve(kept, came, me, own):
    rows, tokens = kept.shape
    whole = pl.BlockSpec(memory_space=pltpu.VMEM)
    return pl.pallas_call(
        functools.partial(halve_kernel, own),
        out_shape=[jax.ShapeDtypeStruct((2 * own, tokens), jnp.float32)] * 2,
        in_specs=[pl.BlockSpec(memory_space=pltpu.SMEM), whole, whole],
        out_specs=[whole] * 2,
        scratch_shapes=[pltpu.VMEM((rows, tokens), jnp.float32)],
        compiler_params=pltpu.CompilerParams(vmem_limit_bytes=VMEM_LIMIT),
        name="halve",
    )(me, kept, came)


def pick_kernel(rank, own, rank_ref, queries_ref, out_ref):
    lanes = out_ref.shape[1]
    wide = lanes * rank // own
    steps = own * own // lanes
    asked = queries_ref.shape[0]
    me = rank_ref[0]
    start = (me // 2) * (own * rank)
    rows = jnp.concatenate(
        [
            queries_ref[:, pl.ds(pl.multiple_of(start + i * wide, lanes), wide)]
            for i in range(steps)
        ],
        axis=0,
    )
    source = lax.broadcasted_iota(jnp.int32, (wide, lanes), 0)
    place = lax.broadcasted_iota(jnp.int32, (wide, lanes), 1)
    wanted = (place // own) * rank + place % own + (me & 1) * own
    chosen = jnp.where(source == wanted, 1.0, 0.0).astype(jnp.bfloat16)
    high = rows.astype(jnp.bfloat16)
    rest = rows - high.astype(jnp.float32)
    middle = rest.astype(jnp.bfloat16)
    low = (rest - middle.astype(jnp.float32)).astype(jnp.bfloat16)
    terms = [
        jnp.dot(term, chosen, preferred_element_type=jnp.float32) for term in (high, middle, low)
    ]
    out_ref[...] = terms[0] + (terms[1] + terms[2])


def pick(queries, me, rank, own):
    lanes = 128
    rows = queries.shape[0] * own * own // lanes
    whole = pl.BlockSpec(memory_space=pltpu.VMEM)
    return pl.pallas_call(
        functools.partial(pick_kernel, rank, own),
        out_shape=jax.ShapeDtypeStruct((rows, lanes), jnp.float32),
        in_specs=[pl.BlockSpec(memory_space=pltpu.SMEM), whole],
        out_specs=whole,
        compiler_params=pltpu.CompilerParams(vmem_limit_bytes=VMEM_LIMIT),
        name="pick",
    )(me, queries)


def grads_kernel(weights_ref, kept_ref, came_ref, asked_ref, out_ref):
    summed = kept_ref[...] + came_ref[...]
    weights = weights_ref[...]
    own = summed.shape[0] // 2
    group = out_ref.shape[1] // own
    inputs_t = summed[own:, :]
    zero = jnp.zeros_like(inputs_t)
    right = jnp.concatenate(
        [
            jnp.concatenate([inputs_t if j == k else zero for k in range(group)], axis=1)
            for j in range(group)
        ],
        axis=0,
    )
    rows = []
    for i in range(own // group):
        rows.append(
            jnp.concatenate(
                [weights * summed[group * i + j : group * i + j + 1, :] for j in range(group)],
                axis=1,
            )
        )
    left = jnp.concatenate(rows, axis=0)
    count = left.shape[0]
    out_ref[:count, :] = dot_nt(left, right)
    out_ref[count:, :] = asked_ref[...]


def gradients(weights, kept, came, asked):
    lanes = asked.shape[1]
    own = kept.shape[0] // 2
    rows = own * own // lanes * weights.shape[0] + asked.shape[0]
    return pl.pallas_call(
        grads_kernel,
        out_shape=jax.ShapeDtypeStruct((rows, lanes), jnp.float32),
        compiler_params=pltpu.CompilerParams(vmem_limit_bytes=VMEM_LIMIT),
        name="gradients",
    )(weights, kept, came, asked)


def grams_kernel(steps, seqs, me_ref, *refs):
    blocks, out_ref = refs[-2::-1], refs[-1]
    count = steps * seqs
    asked = (blocks[0].shape[0] - count) // steps
    given = [block[count:, :] for block in blocks]
    ordered = []
    for place in range(len(blocks)):
        chosen = given[0]
        for m in range(1, len(blocks)):
            ahead = lax.rem(place - me_ref[0] + len(blocks), len(blocks))
            chosen = jnp.where(ahead == m, given[m], chosen)
        ordered.append(chosen)
    lanes = []
    for i in range(steps):
        rows = [block[i * seqs : (i + 1) * seqs, :] for block in blocks]
        rows += [chosen[i * asked : (i + 1) * asked, :] for chosen in ordered]
        lanes.append(jnp.concatenate(rows, axis=0))
    both = jnp.concatenate(lanes, axis=1)
    result = dot_nt(both, both[: len(blocks) * seqs])
    half = result.shape[0] // 2
    out_ref[...] = jnp.concatenate([result[:half, :], result[half:, :]], axis=1)


def grams(me, blocks, steps, seqs):
    asked = blocks[0].shape[0] // steps - seqs
    total = len(blocks) * seqs
    whole = pl.BlockSpec(memory_space=pltpu.VMEM)
    return pl.pallas_call(
        functools.partial(grams_kernel, steps, seqs),
        out_shape=jax.ShapeDtypeStruct(((total + len(blocks) * asked) // 2, 2 * total), jnp.float32),
        in_specs=[pl.BlockSpec(memory_space=pltpu.SMEM)] + [whole] * len(blocks),
        out_specs=whole,
        compiler_params=pltpu.CompilerParams(vmem_limit_bytes=VMEM_LIMIT),
        name="grams",
    )(me, *blocks)


def scales(count):
    first = 2.0 / (1.0 + 1.0 / count)
    off = count / (count + 1.0)
    steps = []
    while off > 1e-7:
        steps.append(2.0 / (2.0 - off * off))
        off = off * off / (2.0 - off * off)
    return first, steps


def solve_kernel(seqs, *refs):
    parts, out_ref = refs[:-1], refs[-1]
    packed = (parts[0][...] + parts[1][...]) + (parts[2][...] + parts[3][...])
    lane = lax.broadcasted_iota(jnp.int32, packed.shape, 1)
    turned = pltpu.roll(packed, seqs, 1)
    both = jnp.concatenate(
        [jnp.where(lane < seqs, packed, turned), jnp.where(lane < seqs, turned, packed)], axis=0
    )
    lane = lax.broadcasted_iota(jnp.int32, both.shape, 1)
    row = lax.broadcasted_iota(jnp.int32, both.shape, 0)
    unit = jnp.where((lane & (seqs - 1)) == row, 1.0, 0.0)
    total = jnp.sum(jnp.where(lane == row, both, 0.0)[:seqs], axis=(0, 1), keepdims=True)
    first, steps = scales(seqs)
    state = first * (both / total + unit * (damping / seqs))
    left_lanes = lane < seqs
    for at, step in enumerate(steps):
        high = state.astype(jnp.bfloat16).astype(jnp.float32)
        low = state - high
        left = jnp.where(left_lanes, high, low).astype(jnp.bfloat16)
        high = high[:seqs].astype(jnp.bfloat16)
        low = low[:seqs].astype(jnp.bfloat16)
        right = jnp.concatenate([high, high, low, low], axis=0)
        if at + 1 == len(steps):
            left, state = left[seqs:], state[seqs:]
        product = jnp.dot(
            jnp.concatenate([left, left], axis=1), right, preferred_element_type=jnp.float32
        )
        state = step * (2.0 * state - product)
    out_ref[...] = state[:, : out_ref.shape[1]]


def solve(parts, seqs, asked, seq_dev):
    return pl.pallas_call(
        functools.partial(solve_kernel, seqs),
        out_shape=jax.ShapeDtypeStruct((asked, seq_dev), jnp.float32),
        compiler_params=pltpu.CompilerParams(vmem_limit_bytes=VMEM_LIMIT),
        name="solve",
    )(*parts)


def from_partner(value, axis, size, m):
    return lax.ppermute(value, axis, [(i, i ^ m) for i in range(size)])


def from_partners(value, axis, size):
    return [from_partner(value, axis, size, m) for m in reversed(range(1, size))] + [value]


def from_all(value, axis, size):
    shifts = [[(i, (i + s) % size) for i in range(size)] for s in range(1, size)]
    return [lax.ppermute(value, axis, shift) for shift in shifts] + [value]


def finish_long(message, steps, first, seq_dev):
    every = lax.all_gather(message, "dp", axis=0)
    lanes = message.shape[1]

    def rows_of(block):
        block = block.reshape(block.shape[0], steps, -1, lanes).transpose(0, 2, 1, 3)
        return block.reshape(-1, steps * lanes)

    count = steps * seq_dev
    grads, asked = rows_of(every[:, :count]), rows_of(every[:, count:])
    both = jnp.einsum(
        "ik,jk->ij", jnp.concatenate([grads, asked], axis=0), grads,
        precision=lax.Precision.HIGHEST,
    )
    both = lax.psum(both, "tensor")
    count = grads.shape[0]
    kernel, products = both[:count], both[count:]
    damp = damping * jnp.trace(kernel) / count
    unit = jnp.eye(count, dtype=jnp.float32)
    factor = jnp.linalg.cholesky(kernel + damp * unit)
    picks = lax.dynamic_slice_in_dim(unit, first, seq_dev, 1)
    solved = jax.scipy.linalg.cho_solve((factor, True), picks)
    return jnp.dot(products, solved, precision=lax.Precision.HIGHEST)


def per_device(sizes, inputs, out_grads, in_proj, out_proj, seq_ids, counts, queries):
    parts, blocks = sizes
    rank = in_proj.shape[1]
    seq_dev = counts.shape[0]
    me = lax.axis_index("tensor")
    place = lax.axis_index("dp")
    first = place * seq_dev
    own = 2 * rank // parts
    rank_of = me.reshape(1)
    kept, sent = project(inputs, out_grads, in_proj, out_proj, rank_of, own)
    asked = pick(queries, rank_of, rank, own)
    weights = token_weights(seq_ids, counts, first)
    came = from_partner(sent, "tensor", parts, 1)
    kept, sent = halve(kept, came, rank_of, own)
    came = from_partner(sent, "tensor", parts, 2)
    message = gradients(weights, kept, came, asked)
    steps = own * own // message.shape[1]
    if blocks > SMALL:
        return finish_long(message, steps, first, seq_dev)
    partial = grams(place.reshape(1), from_all(message, "dp", blocks), steps, seq_dev)
    partial = from_partners(partial, "tensor", parts)
    return solve(partial, blocks * seq_dev, blocks * queries.shape[0], seq_dev)


def solution(mesh):
    in_specs = (
        P(("groups", "dp"), "tensor"),
        P(("groups", "dp"), "tensor"),
        P("tensor", None),
        P("tensor", None),
        P(("groups", "dp")),
        P(("groups", "dp")),
        P(("groups", "dp"), None),
    )
    sizes = (mesh.shape["tensor"], mesh.shape["dp"])
    return jax.shard_map(
        functools.partial(per_device, sizes),
        mesh=mesh,
        in_specs=in_specs,
        out_specs=P("groups", "dp"),
        check_vma=False,
    )
```

```python
import functools

import jax
import jax.numpy as jnp
from jax import lax
from jax.experimental import pallas as pl
from jax.experimental.pallas import tpu as pltpu
from jax.sharding import PartitionSpec as P

damping = 0.5
VMEM_LIMIT = 32 * 1024 * 1024
SMALL = 4
SHIFTS = {1: (), 2: (1,), 4: (2, 1, 3)}


def token_weights(seq_ids, counts, first):
    local_ids = seq_ids - first
    slots = jnp.arange(counts.shape[0], dtype=jnp.int32)
    member = local_ids[None, :] == slots[:, None]
    starts = jnp.sum((local_ids[None, :] < slots[:, None]).astype(jnp.int32), axis=1)
    offset = jnp.arange(seq_ids.shape[0], dtype=jnp.int32)[None, :] - starts[:, None]
    scale = 1.0 / counts.astype(jnp.float32)
    return jnp.where(member & (offset < counts[:, None]), scale[:, None], 0.0)


def cuts_of(extent, step):
    return [(at, min(step, extent - at)) for at in range(0, extent, step)]


def two_terms(value):
    high = value.astype(jnp.bfloat16)
    low = (value - high.astype(jnp.float32)).astype(jnp.bfloat16)
    return high, low


def dot_nt(left, right):
    rows = left.shape[0]
    lh, ll = two_terms(left)
    rh, rl = two_terms(right)
    mul = functools.partial(
        lax.dot_general,
        dimension_numbers=(((1,), (1,)), ((), ())),
        preferred_element_type=jnp.float32,
    )
    both = mul(jnp.concatenate([lh, ll], axis=0), rh)
    return both[:rows] + (mul(lh, rl) + both[rows:])


def project_kernel(own, rank_ref, x_hbm, g_hbm, wx_hbm, wg_hbm, keep_ref, send_ref, *scratch):
    x_ref, g_ref, wx_ref, wg_ref, wide_ref, sems = scratch
    copies = []

    def fetch(src, dst, index):
        copy = pltpu.make_async_copy(src, dst, sems.at[index])
        copy.start()
        return copy

    g_cuts = cuts_of(g_ref.shape[1], 1024)
    x_cuts = cuts_of(x_ref.shape[0], 1024)
    wg_copy = fetch(wg_hbm, wg_ref, 0)
    index = 2
    g_copies = []
    for at, size in g_cuts:
        columns = pl.ds(at, size)
        g_copies.append(fetch(g_hbm.at[:, columns], g_ref.at[:, columns], index))
        index += 1
    wx_copy = fetch(wx_hbm, wx_ref, 1)
    x_copies = []
    for at, size in x_cuts:
        rows = pl.ds(at, size)
        x_copies.append(fetch(x_hbm.at[rows, :], x_ref.at[rows, :], index))
        index += 1

    def product(copies, terms):
        total = None
        for copy, (left, right, along) in zip(copies, terms):
            copy.wait()
            term = lax.dot_general(
                left(), right(), (((1,), (along,)), ((), ())), preferred_element_type=jnp.float32
            )
            total = term if total is None else total + term
        return total

    def cut(ref, at, size, along):
        return lambda: ref[at : at + size, :] if along == 0 else ref[:, at : at + size]

    wg_copy.wait()
    grads_t = product(
        g_copies, [(cut(g_ref, at, size, 1), cut(wg_ref, at, size, 1), 1) for at, size in g_cuts]
    ).T
    wx_copy.wait()
    wide_ref[...] = product(
        x_copies, [(cut(wx_ref, at, size, 1), cut(x_ref, at, size, 0), 0) for at, size in x_cuts]
    )
    rank = grads_t.shape[0]
    side = rank_ref[0] & 1
    for out, taken in ((keep_ref, side), (send_ref, side ^ 1)):
        out[:rank, :] = grads_t
        out[rank:, :] = wide_ref[pl.ds(pl.multiple_of(taken * own, own), own), :]


def project(inputs, out_grads, in_proj, out_proj, me, own):
    rank = in_proj.shape[1]
    tokens, hidden = inputs.shape
    width = out_grads.shape[1]
    copies = 2 + len(cuts_of(width, 1024)) + len(cuts_of(hidden, 1024))
    arrays = (inputs.T, out_grads, in_proj.T, out_proj.T)
    in_hbm = pl.BlockSpec(memory_space=pltpu.HBM)
    return pl.pallas_call(
        functools.partial(project_kernel, own),
        out_shape=[jax.ShapeDtypeStruct((rank + own, tokens), jnp.float32)] * 2,
        in_specs=[pl.BlockSpec(memory_space=pltpu.SMEM)] + [in_hbm] * len(arrays),
        out_specs=[pl.BlockSpec(memory_space=pltpu.VMEM)] * 2,
        scratch_shapes=[
            pltpu.VMEM((hidden, tokens), jnp.bfloat16),
            pltpu.VMEM((tokens, width), jnp.bfloat16),
            pltpu.VMEM((rank, hidden), jnp.bfloat16),
            pltpu.VMEM((rank, width), jnp.bfloat16),
            pltpu.VMEM((rank, tokens), jnp.float32),
            pltpu.SemaphoreType.DMA((copies,)),
        ],
        compiler_params=pltpu.CompilerParams(vmem_limit_bytes=VMEM_LIMIT),
        name="project",
    )(me, *(pltpu.with_memory_space_constraint(array, pltpu.HBM) for array in arrays))


def halve_kernel(own, rank_ref, kept_ref, came_ref, keep_ref, send_ref, sum_ref):
    sum_ref[...] = kept_ref[...] + came_ref[...]
    place = rank_ref[0] // 2
    for out, taken in ((keep_ref, place), (send_ref, place ^ 1)):
        out[:own, :] = sum_ref[pl.ds(pl.multiple_of(taken * own, own), own), :]
        out[own:, :] = sum_ref[-own:, :]


def halve(kept, came, me, own):
    rows, tokens = kept.shape
    whole = pl.BlockSpec(memory_space=pltpu.VMEM)
    return pl.pallas_call(
        functools.partial(halve_kernel, own),
        out_shape=[jax.ShapeDtypeStruct((2 * own, tokens), jnp.float32)] * 2,
        in_specs=[pl.BlockSpec(memory_space=pltpu.SMEM), whole, whole],
        out_specs=[whole] * 2,
        scratch_shapes=[pltpu.VMEM((rows, tokens), jnp.float32)],
        compiler_params=pltpu.CompilerParams(vmem_limit_bytes=VMEM_LIMIT),
        name="halve",
    )(me, kept, came)


def pick_kernel(rank, own, rank_ref, queries_ref, out_ref):
    lanes = out_ref.shape[1]
    wide = lanes * rank // own
    steps = own * own // lanes
    asked = queries_ref.shape[0]
    me = rank_ref[0]
    start = (me // 2) * (own * rank)
    rows = jnp.concatenate(
        [
            queries_ref[:, pl.ds(pl.multiple_of(start + i * wide, lanes), wide)]
            for i in range(steps)
        ],
        axis=0,
    )
    source = lax.broadcasted_iota(jnp.int32, (wide, lanes), 0)
    place = lax.broadcasted_iota(jnp.int32, (wide, lanes), 1)
    wanted = (place // own) * rank + place % own + (me & 1) * own
    chosen = jnp.where(source == wanted, 1.0, 0.0).astype(jnp.bfloat16)
    high = rows.astype(jnp.bfloat16)
    rest = rows - high.astype(jnp.float32)
    middle = rest.astype(jnp.bfloat16)
    low = (rest - middle.astype(jnp.float32)).astype(jnp.bfloat16)
    terms = [
        jnp.dot(term, chosen, preferred_element_type=jnp.float32) for term in (high, middle, low)
    ]
    out_ref[...] = terms[0] + (terms[1] + terms[2])


def pick(queries, me, rank, own):
    lanes = 128
    rows = queries.shape[0] * own * own // lanes
    whole = pl.BlockSpec(memory_space=pltpu.VMEM)
    return pl.pallas_call(
        functools.partial(pick_kernel, rank, own),
        out_shape=jax.ShapeDtypeStruct((rows, lanes), jnp.float32),
        in_specs=[pl.BlockSpec(memory_space=pltpu.SMEM), whole],
        out_specs=whole,
        compiler_params=pltpu.CompilerParams(vmem_limit_bytes=VMEM_LIMIT),
        name="pick",
    )(me, queries)


def grads_kernel(weights_ref, kept_ref, came_ref, asked_ref, out_ref):
    summed = kept_ref[...] + came_ref[...]
    weights = weights_ref[...]
    own = summed.shape[0] // 2
    group = out_ref.shape[1] // own
    inputs_t = summed[own:, :]
    zero = jnp.zeros_like(inputs_t)
    right = jnp.concatenate(
        [
            jnp.concatenate([inputs_t if j == k else zero for k in range(group)], axis=1)
            for j in range(group)
        ],
        axis=0,
    )
    rows = []
    for i in range(own // group):
        rows.append(
            jnp.concatenate(
                [weights * summed[group * i + j : group * i + j + 1, :] for j in range(group)],
                axis=1,
            )
        )
    left = jnp.concatenate(rows, axis=0)
    count = left.shape[0]
    out_ref[:count, :] = dot_nt(left, right)
    out_ref[count:, :] = asked_ref[...]


def gradients(weights, kept, came, asked):
    lanes = asked.shape[1]
    own = kept.shape[0] // 2
    rows = own * own // lanes * weights.shape[0] + asked.shape[0]
    return pl.pallas_call(
        grads_kernel,
        out_shape=jax.ShapeDtypeStruct((rows, lanes), jnp.float32),
        compiler_params=pltpu.CompilerParams(vmem_limit_bytes=VMEM_LIMIT),
        name="gradients",
    )(weights, kept, came, asked)


def grams_kernel(steps, seqs, me_ref, *refs):
    blocks, out_ref = refs[:-1], refs[-1]
    shifts = (*SHIFTS[len(blocks)], 0)
    blocks = [blocks[shifts.index(-m % len(blocks))] for m in range(len(blocks))]
    count = steps * seqs
    asked = (blocks[0].shape[0] - count) // steps
    given = [block[count:, :] for block in blocks]
    ordered = []
    for place in range(len(blocks)):
        chosen = given[0]
        for m in range(1, len(blocks)):
            ahead = lax.rem(place - me_ref[0] + len(blocks), len(blocks))
            chosen = jnp.where(ahead == m, given[m], chosen)
        ordered.append(chosen)
    lanes = []
    for i in range(steps):
        rows = [block[i * seqs : (i + 1) * seqs, :] for block in blocks]
        rows += [chosen[i * asked : (i + 1) * asked, :] for chosen in ordered]
        lanes.append(jnp.concatenate(rows, axis=0))
    both = jnp.concatenate(lanes, axis=1)
    result = dot_nt(both, both[: len(blocks) * seqs])
    half = result.shape[0] // 2
    out_ref[...] = jnp.concatenate([result[:half, :], result[half:, :]], axis=1)


def grams(me, blocks, steps, seqs):
    asked = blocks[0].shape[0] // steps - seqs
    total = len(blocks) * seqs
    whole = pl.BlockSpec(memory_space=pltpu.VMEM)
    return pl.pallas_call(
        functools.partial(grams_kernel, steps, seqs),
        out_shape=jax.ShapeDtypeStruct(((total + len(blocks) * asked) // 2, 2 * total), jnp.float32),
        in_specs=[pl.BlockSpec(memory_space=pltpu.SMEM)] + [whole] * len(blocks),
        out_specs=whole,
        compiler_params=pltpu.CompilerParams(vmem_limit_bytes=VMEM_LIMIT),
        name="grams",
    )(me, *blocks)


def scales(count):
    first = 2.0 / (1.0 + 1.0 / count)
    off = count / (count + 1.0)
    steps = []
    while off > 1e-7:
        steps.append(2.0 / (2.0 - off * off))
        off = off * off / (2.0 - off * off)
    return first, steps


def solve_kernel(seqs, *refs):
    parts, out_ref = refs[:-1], refs[-1]
    packed = (parts[0][...] + parts[1][...]) + (parts[2][...] + parts[3][...])
    lane = lax.broadcasted_iota(jnp.int32, packed.shape, 1)
    turned = pltpu.roll(packed, seqs, 1)
    both = jnp.concatenate(
        [jnp.where(lane < seqs, packed, turned), jnp.where(lane < seqs, turned, packed)], axis=0
    )
    lane = lax.broadcasted_iota(jnp.int32, both.shape, 1)
    row = lax.broadcasted_iota(jnp.int32, both.shape, 0)
    unit = jnp.where((lane & (seqs - 1)) == row, 1.0, 0.0)
    total = jnp.sum(jnp.where(lane == row, both, 0.0)[:seqs], axis=(0, 1), keepdims=True)
    first, steps = scales(seqs)
    state = first * (both / total + unit * (damping / seqs))
    left_lanes = lane < seqs
    for at, step in enumerate(steps):
        high = state.astype(jnp.bfloat16).astype(jnp.float32)
        low = state - high
        left = jnp.where(left_lanes, high, low).astype(jnp.bfloat16)
        high = high[:seqs].astype(jnp.bfloat16)
        low = low[:seqs].astype(jnp.bfloat16)
        right = jnp.concatenate([high, high, low, low], axis=0)
        if at + 1 == len(steps):
            left, state = left[seqs:], state[seqs:]
        product = jnp.dot(
            jnp.concatenate([left, left], axis=1), right, preferred_element_type=jnp.float32
        )
        state = step * (2.0 * state - product)
    out_ref[...] = state[:, : out_ref.shape[1]]


def solve(parts, seqs, asked, seq_dev):
    return pl.pallas_call(
        functools.partial(solve_kernel, seqs),
        out_shape=jax.ShapeDtypeStruct((asked, seq_dev), jnp.float32),
        compiler_params=pltpu.CompilerParams(vmem_limit_bytes=VMEM_LIMIT),
        name="solve",
    )(*parts)


def from_partner(value, axis, size, m):
    return lax.ppermute(value, axis, [(i, i ^ m) for i in range(size)])


def from_partners(value, axis, size):
    return [from_partner(value, axis, size, m) for m in reversed(range(1, size))] + [value]


def from_all(value, axis, size):
    shifts = [[(i, (i + s) % size) for i in range(size)] for s in SHIFTS[size]]
    return [lax.ppermute(value, axis, shift) for shift in shifts] + [value]


def finish_long(message, steps, first, seq_dev):
    every = lax.all_gather(message, "dp", axis=0)
    lanes = message.shape[1]

    def rows_of(block):
        block = block.reshape(block.shape[0], steps, -1, lanes).transpose(0, 2, 1, 3)
        return block.reshape(-1, steps * lanes)

    count = steps * seq_dev
    grads, asked = rows_of(every[:, :count]), rows_of(every[:, count:])
    both = jnp.einsum(
        "ik,jk->ij", jnp.concatenate([grads, asked], axis=0), grads,
        precision=lax.Precision.HIGHEST,
    )
    both = lax.psum(both, "tensor")
    count = grads.shape[0]
    kernel, products = both[:count], both[count:]
    damp = damping * jnp.trace(kernel) / count
    unit = jnp.eye(count, dtype=jnp.float32)
    factor = jnp.linalg.cholesky(kernel + damp * unit)
    picks = lax.dynamic_slice_in_dim(unit, first, seq_dev, 1)
    solved = jax.scipy.linalg.cho_solve((factor, True), picks)
    return jnp.dot(products, solved, precision=lax.Precision.HIGHEST)


def per_device(sizes, inputs, out_grads, in_proj, out_proj, seq_ids, counts, queries):
    parts, blocks = sizes
    rank = in_proj.shape[1]
    seq_dev = counts.shape[0]
    me = lax.axis_index("tensor")
    place = lax.axis_index("dp")
    first = place * seq_dev
    own = 2 * rank // parts
    rank_of = me.reshape(1)
    kept, sent = project(inputs, out_grads, in_proj, out_proj, rank_of, own)
    asked = pick(queries, rank_of, rank, own)
    weights = token_weights(seq_ids, counts, first)
    came = from_partner(sent, "tensor", parts, 1)
    kept, sent = halve(kept, came, rank_of, own)
    came = from_partner(sent, "tensor", parts, 2)
    message = gradients(weights, kept, came, asked)
    steps = own * own // message.shape[1]
    if blocks > SMALL:
        return finish_long(message, steps, first, seq_dev)
    partial = grams(place.reshape(1), from_all(message, "dp", blocks), steps, seq_dev)
    partial = from_partners(partial, "tensor", parts)
    return solve(partial, blocks * seq_dev, blocks * queries.shape[0], seq_dev)


def solution(mesh):
    in_specs = (
        P(("groups", "dp"), "tensor"),
        P(("groups", "dp"), "tensor"),
        P("tensor", None),
        P("tensor", None),
        P(("groups", "dp")),
        P(("groups", "dp")),
        P(("groups", "dp"), None),
    )
    sizes = (mesh.shape["tensor"], mesh.shape["dp"])
    return jax.shard_map(
        functools.partial(per_device, sizes),
        mesh=mesh,
        in_specs=in_specs,
        out_specs=P("groups", "dp"),
        check_vma=False,
    )
```

```python
import functools

import jax
import jax.numpy as jnp
from jax import lax
from jax.experimental import pallas as pl
from jax.experimental.pallas import tpu as pltpu
from jax.sharding import PartitionSpec as P

damping = 0.5
VMEM_LIMIT = 32 * 1024 * 1024
SMALL = 4


def token_weights(seq_ids, counts, first):
    local_ids = seq_ids - first
    slots = jnp.arange(counts.shape[0], dtype=jnp.int32)
    member = local_ids[None, :] == slots[:, None]
    starts = jnp.sum((local_ids[None, :] < slots[:, None]).astype(jnp.int32), axis=1)
    offset = jnp.arange(seq_ids.shape[0], dtype=jnp.int32)[None, :] - starts[:, None]
    scale = 1.0 / counts.astype(jnp.float32)
    return jnp.where(member & (offset < counts[:, None]), scale[:, None], 0.0)


def cuts_of(extent, step):
    return [(at, min(step, extent - at)) for at in range(0, extent, step)]


def two_terms(value):
    high = value.astype(jnp.bfloat16)
    low = (value - high.astype(jnp.float32)).astype(jnp.bfloat16)
    return high, low


def dot_nt(left, right):
    rows = left.shape[0]
    lh, ll = two_terms(left)
    rh, rl = two_terms(right)
    mul = functools.partial(
        lax.dot_general,
        dimension_numbers=(((1,), (1,)), ((), ())),
        preferred_element_type=jnp.float32,
    )
    both = mul(jnp.concatenate([lh, ll], axis=0), rh)
    return both[:rows] + (mul(lh, rl) + both[rows:])


def project_kernel(own, rank_ref, x_hbm, g_hbm, wx_hbm, wg_hbm, keep_ref, send_ref, *scratch):
    x_ref, g_ref, wx_ref, wg_ref, wide_ref, sems = scratch
    copies = []

    def fetch(src, dst, index, priority=1):
        copy = pltpu.make_async_copy(src, dst, sems.at[index])
        copy.start(priority=priority)
        return copy

    g_cuts = cuts_of(g_ref.shape[1], 512)
    x_cuts = cuts_of(x_ref.shape[0], 512)
    wg_copy = fetch(wg_hbm, wg_ref, 0)
    index = 2
    g_copies = []
    for at, size in g_cuts:
        columns = pl.ds(at, size)
        g_copies.append(fetch(g_hbm.at[:, columns], g_ref.at[:, columns], index))
        index += 1
    wx_copy = fetch(wx_hbm, wx_ref, 1)
    x_copies = []
    for at, size in x_cuts:
        rows = pl.ds(at, size)
        x_copies.append(fetch(x_hbm.at[rows, :], x_ref.at[rows, :], index, int(at < 1024)))
        index += 1

    def product(copies, terms):
        total = None
        for copy, (left, right, along) in zip(copies, terms):
            copy.wait()
            term = lax.dot_general(
                left(), right(), (((1,), (along,)), ((), ())), preferred_element_type=jnp.float32
            )
            total = term if total is None else total + term
        return total

    def cut(ref, at, size, along):
        return lambda: ref[at : at + size, :] if along == 0 else ref[:, at : at + size]

    wg_copy.wait()
    grads_t = product(
        g_copies, [(cut(g_ref, at, size, 1), cut(wg_ref, at, size, 1), 1) for at, size in g_cuts]
    ).T
    wx_copy.wait()
    wide_ref[...] = product(
        x_copies, [(cut(wx_ref, at, size, 1), cut(x_ref, at, size, 0), 0) for at, size in x_cuts]
    )
    rank = grads_t.shape[0]
    side = rank_ref[0] & 1
    for out, taken in ((keep_ref, side), (send_ref, side ^ 1)):
        out[:rank, :] = grads_t
        out[rank:, :] = wide_ref[pl.ds(pl.multiple_of(taken * own, own), own), :]


def project(inputs, out_grads, in_proj, out_proj, me, own):
    rank = in_proj.shape[1]
    tokens, hidden = inputs.shape
    width = out_grads.shape[1]
    copies = 2 + len(cuts_of(width, 512)) + len(cuts_of(hidden, 512))
    arrays = (inputs.T, out_grads, in_proj.T, out_proj.T)
    in_hbm = pl.BlockSpec(memory_space=pltpu.HBM)
    return pl.pallas_call(
        functools.partial(project_kernel, own),
        out_shape=[jax.ShapeDtypeStruct((rank + own, tokens), jnp.float32)] * 2,
        in_specs=[pl.BlockSpec(memory_space=pltpu.SMEM)] + [in_hbm] * len(arrays),
        out_specs=[pl.BlockSpec(memory_space=pltpu.VMEM)] * 2,
        scratch_shapes=[
            pltpu.VMEM((hidden, tokens), jnp.bfloat16),
            pltpu.VMEM((tokens, width), jnp.bfloat16),
            pltpu.VMEM((rank, hidden), jnp.bfloat16),
            pltpu.VMEM((rank, width), jnp.bfloat16),
            pltpu.VMEM((rank, tokens), jnp.float32),
            pltpu.SemaphoreType.DMA((copies,)),
        ],
        compiler_params=pltpu.CompilerParams(vmem_limit_bytes=VMEM_LIMIT),
        name="project",
    )(me, *(pltpu.with_memory_space_constraint(array, pltpu.HBM) for array in arrays))


def halve_kernel(own, rank_ref, kept_ref, came_ref, keep_ref, send_ref, sum_ref):
    sum_ref[...] = kept_ref[...] + came_ref[...]
    place = rank_ref[0] // 2
    for out, taken in ((keep_ref, place), (send_ref, place ^ 1)):
        out[:own, :] = sum_ref[pl.ds(pl.multiple_of(taken * own, own), own), :]
        out[own:, :] = sum_ref[-own:, :]


def halve(kept, came, me, own):
    rows, tokens = kept.shape
    whole = pl.BlockSpec(memory_space=pltpu.VMEM)
    return pl.pallas_call(
        functools.partial(halve_kernel, own),
        out_shape=[jax.ShapeDtypeStruct((2 * own, tokens), jnp.float32)] * 2,
        in_specs=[pl.BlockSpec(memory_space=pltpu.SMEM), whole, whole],
        out_specs=[whole] * 2,
        scratch_shapes=[pltpu.VMEM((rows, tokens), jnp.float32)],
        compiler_params=pltpu.CompilerParams(vmem_limit_bytes=VMEM_LIMIT),
        name="halve",
    )(me, kept, came)


def pick_kernel(rank, own, rank_ref, queries_ref, out_ref):
    lanes = out_ref.shape[1]
    wide = lanes * rank // own
    steps = own * own // lanes
    asked = queries_ref.shape[0]
    me = rank_ref[0]
    start = (me // 2) * (own * rank)
    rows = jnp.concatenate(
        [
            queries_ref[:, pl.ds(pl.multiple_of(start + i * wide, lanes), wide)]
            for i in range(steps)
        ],
        axis=0,
    )
    source = lax.broadcasted_iota(jnp.int32, (wide, lanes), 0)
    place = lax.broadcasted_iota(jnp.int32, (wide, lanes), 1)
    wanted = (place // own) * rank + place % own + (me & 1) * own
    chosen = jnp.where(source == wanted, 1.0, 0.0).astype(jnp.bfloat16)
    high = rows.astype(jnp.bfloat16)
    rest = rows - high.astype(jnp.float32)
    middle = rest.astype(jnp.bfloat16)
    low = (rest - middle.astype(jnp.float32)).astype(jnp.bfloat16)
    terms = [
        jnp.dot(term, chosen, preferred_element_type=jnp.float32) for term in (high, middle, low)
    ]
    out_ref[...] = terms[0] + (terms[1] + terms[2])


def pick(queries, me, rank, own):
    lanes = 128
    rows = queries.shape[0] * own * own // lanes
    whole = pl.BlockSpec(memory_space=pltpu.VMEM)
    return pl.pallas_call(
        functools.partial(pick_kernel, rank, own),
        out_shape=jax.ShapeDtypeStruct((rows, lanes), jnp.float32),
        in_specs=[pl.BlockSpec(memory_space=pltpu.SMEM), whole],
        out_specs=whole,
        compiler_params=pltpu.CompilerParams(vmem_limit_bytes=VMEM_LIMIT),
        name="pick",
    )(me, queries)


def grads_kernel(weights_ref, kept_ref, came_ref, asked_ref, out_ref):
    summed = kept_ref[...] + came_ref[...]
    weights = weights_ref[...]
    own = summed.shape[0] // 2
    group = out_ref.shape[1] // own
    inputs_t = summed[own:, :]
    zero = jnp.zeros_like(inputs_t)
    right = jnp.concatenate(
        [
            jnp.concatenate([inputs_t if j == k else zero for k in range(group)], axis=1)
            for j in range(group)
        ],
        axis=0,
    )
    rows = []
    for i in range(own // group):
        rows.append(
            jnp.concatenate(
                [weights * summed[group * i + j : group * i + j + 1, :] for j in range(group)],
                axis=1,
            )
        )
    left = jnp.concatenate(rows, axis=0)
    count = left.shape[0]
    out_ref[:count, :] = dot_nt(left, right)
    out_ref[count:, :] = asked_ref[...]


def gradients(weights, kept, came, asked):
    lanes = asked.shape[1]
    own = kept.shape[0] // 2
    rows = own * own // lanes * weights.shape[0] + asked.shape[0]
    return pl.pallas_call(
        grads_kernel,
        out_shape=jax.ShapeDtypeStruct((rows, lanes), jnp.float32),
        compiler_params=pltpu.CompilerParams(vmem_limit_bytes=VMEM_LIMIT),
        name="gradients",
    )(weights, kept, came, asked)


def grams_kernel(steps, seqs, me_ref, *refs):
    blocks, out_ref = refs[-2::-1], refs[-1]
    count = steps * seqs
    asked = (blocks[0].shape[0] - count) // steps
    given = [block[count:, :] for block in blocks]
    ordered = []
    for place in range(len(blocks)):
        chosen = given[0]
        for m in range(1, len(blocks)):
            ahead = lax.rem(place - me_ref[0] + len(blocks), len(blocks))
            chosen = jnp.where(ahead == m, given[m], chosen)
        ordered.append(chosen)
    lanes = []
    for i in range(steps):
        rows = [block[i * seqs : (i + 1) * seqs, :] for block in blocks]
        rows += [chosen[i * asked : (i + 1) * asked, :] for chosen in ordered]
        lanes.append(jnp.concatenate(rows, axis=0))
    both = jnp.concatenate(lanes, axis=1)
    result = dot_nt(both, both[: len(blocks) * seqs])
    half = result.shape[0] // 2
    out_ref[...] = jnp.concatenate([result[:half, :], result[half:, :]], axis=1)


def grams(me, blocks, steps, seqs):
    asked = blocks[0].shape[0] // steps - seqs
    total = len(blocks) * seqs
    whole = pl.BlockSpec(memory_space=pltpu.VMEM)
    return pl.pallas_call(
        functools.partial(grams_kernel, steps, seqs),
        out_shape=jax.ShapeDtypeStruct(((total + len(blocks) * asked) // 2, 2 * total), jnp.float32),
        in_specs=[pl.BlockSpec(memory_space=pltpu.SMEM)] + [whole] * len(blocks),
        out_specs=whole,
        compiler_params=pltpu.CompilerParams(vmem_limit_bytes=VMEM_LIMIT),
        name="grams",
    )(me, *blocks)


def scales(count):
    first = 2.0 / (1.0 + 1.0 / count)
    off = count / (count + 1.0)
    steps = []
    while off > 1e-7:
        steps.append(2.0 / (2.0 - off * off))
        off = off * off / (2.0 - off * off)
    return first, steps


def solve_kernel(seqs, *refs):
    parts, out_ref = refs[:-1], refs[-1]
    packed = (parts[0][...] + parts[1][...]) + (parts[2][...] + parts[3][...])
    lane = lax.broadcasted_iota(jnp.int32, packed.shape, 1)
    turned = pltpu.roll(packed, seqs, 1)
    both = jnp.concatenate(
        [jnp.where(lane < seqs, packed, turned), jnp.where(lane < seqs, turned, packed)], axis=0
    )
    lane = lax.broadcasted_iota(jnp.int32, both.shape, 1)
    row = lax.broadcasted_iota(jnp.int32, both.shape, 0)
    unit = jnp.where((lane & (seqs - 1)) == row, 1.0, 0.0)
    total = jnp.sum(jnp.where(lane == row, both, 0.0)[:seqs], axis=(0, 1), keepdims=True)
    first, steps = scales(seqs)
    state = first * (both / total + unit * (damping / seqs))
    left_lanes = lane < seqs
    for at, step in enumerate(steps):
        high = state.astype(jnp.bfloat16).astype(jnp.float32)
        low = state - high
        left = jnp.where(left_lanes, high, low).astype(jnp.bfloat16)
        lead = high[:, :seqs].astype(jnp.bfloat16)
        high = high[:seqs].astype(jnp.bfloat16)
        low = low[:seqs].astype(jnp.bfloat16)
        if at + 1 == len(steps):
            left, lead, state = left[seqs:], lead[seqs:], state[seqs:]
        product = jnp.dot(
            left, jnp.concatenate([high, high], axis=0), preferred_element_type=jnp.float32
        ) + jnp.dot(lead, low, preferred_element_type=jnp.float32)
        state = step * (2.0 * state - product)
    out_ref[...] = state[:, : out_ref.shape[1]]


def solve(parts, seqs, asked, seq_dev):
    return pl.pallas_call(
        functools.partial(solve_kernel, seqs),
        out_shape=jax.ShapeDtypeStruct((asked, seq_dev), jnp.float32),
        compiler_params=pltpu.CompilerParams(vmem_limit_bytes=VMEM_LIMIT),
        name="solve",
    )(*parts)


def from_partner(value, axis, size, m):
    return lax.ppermute(value, axis, [(i, i ^ m) for i in range(size)])


def from_partners(value, axis, size):
    return [from_partner(value, axis, size, m) for m in reversed(range(1, size))] + [value]


def from_all(value, axis, size):
    shifts = [[(i, (i + s) % size) for i in range(size)] for s in range(1, size)]
    return [lax.ppermute(value, axis, shift) for shift in shifts] + [value]


def finish_long(message, steps, first, seq_dev):
    every = lax.all_gather(message, "dp", axis=0)
    lanes = message.shape[1]

    def rows_of(block):
        block = block.reshape(block.shape[0], steps, -1, lanes).transpose(0, 2, 1, 3)
        return block.reshape(-1, steps * lanes)

    count = steps * seq_dev
    grads, asked = rows_of(every[:, :count]), rows_of(every[:, count:])
    both = jnp.einsum(
        "ik,jk->ij", jnp.concatenate([grads, asked], axis=0), grads,
        precision=lax.Precision.HIGHEST,
    )
    both = lax.psum(both, "tensor")
    count = grads.shape[0]
    kernel, products = both[:count], both[count:]
    damp = damping * jnp.trace(kernel) / count
    unit = jnp.eye(count, dtype=jnp.float32)
    factor = jnp.linalg.cholesky(kernel + damp * unit)
    picks = lax.dynamic_slice_in_dim(unit, first, seq_dev, 1)
    solved = jax.scipy.linalg.cho_solve((factor, True), picks)
    return jnp.dot(products, solved, precision=lax.Precision.HIGHEST)


def per_device(sizes, inputs, out_grads, in_proj, out_proj, seq_ids, counts, queries):
    parts, blocks = sizes
    rank = in_proj.shape[1]
    seq_dev = counts.shape[0]
    me = lax.axis_index("tensor")
    place = lax.axis_index("dp")
    first = place * seq_dev
    own = 2 * rank // parts
    rank_of = me.reshape(1)
    kept, sent = project(inputs, out_grads, in_proj, out_proj, rank_of, own)
    asked = pick(queries, rank_of, rank, own)
    weights = token_weights(seq_ids, counts, first)
    came = from_partner(sent, "tensor", parts, 1)
    kept, sent = halve(kept, came, rank_of, own)
    came = from_partner(sent, "tensor", parts, 2)
    message = gradients(weights, kept, came, asked)
    steps = own * own // message.shape[1]
    if blocks > SMALL:
        return finish_long(message, steps, first, seq_dev)
    partial = grams(place.reshape(1), from_all(message, "dp", blocks), steps, seq_dev)
    partial = from_partners(partial, "tensor", parts)
    return solve(partial, blocks * seq_dev, blocks * queries.shape[0], seq_dev)


def solution(mesh):
    in_specs = (
        P(("groups", "dp"), "tensor"),
        P(("groups", "dp"), "tensor"),
        P("tensor", None),
        P("tensor", None),
        P(("groups", "dp")),
        P(("groups", "dp")),
        P(("groups", "dp"), None),
    )
    sizes = (mesh.shape["tensor"], mesh.shape["dp"])
    return jax.shard_map(
        functools.partial(per_device, sizes),
        mesh=mesh,
        in_specs=in_specs,
        out_specs=P("groups", "dp"),
        check_vma=False,
    )
```

```python
import functools

import jax
import jax.numpy as jnp
from jax import lax
from jax.experimental import pallas as pl
from jax.experimental.pallas import tpu as pltpu
from jax.sharding import PartitionSpec as P

damping = 0.5
VMEM_LIMIT = 32 * 1024 * 1024
SMALL = 4
SHIFTS = {1: (), 2: (1,), 4: (3, 2, 1)}


def token_weights(seq_ids, counts, first):
    local_ids = seq_ids - first
    slots = jnp.arange(counts.shape[0], dtype=jnp.int32)
    member = local_ids[None, :] == slots[:, None]
    starts = jnp.sum((local_ids[None, :] < slots[:, None]).astype(jnp.int32), axis=1)
    offset = jnp.arange(seq_ids.shape[0], dtype=jnp.int32)[None, :] - starts[:, None]
    scale = 1.0 / counts.astype(jnp.float32)
    return jnp.where(member & (offset < counts[:, None]), scale[:, None], 0.0)


def cuts_of(extent, step):
    return [(at, min(step, extent - at)) for at in range(0, extent, step)]


def two_terms(value):
    high = value.astype(jnp.bfloat16)
    low = (value - high.astype(jnp.float32)).astype(jnp.bfloat16)
    return high, low


def dot_nt(left, right):
    rows = left.shape[0]
    lh, ll = two_terms(left)
    rh, rl = two_terms(right)
    mul = functools.partial(
        lax.dot_general,
        dimension_numbers=(((1,), (1,)), ((), ())),
        preferred_element_type=jnp.float32,
    )
    both = mul(jnp.concatenate([lh, ll], axis=0), rh)
    return both[:rows] + (mul(lh, rl) + both[rows:])


def project_kernel(own, rank_ref, x_hbm, g_hbm, wx_hbm, wg_hbm, keep_ref, send_ref, *scratch):
    x_ref, g_ref, wx_ref, wg_ref, wide_ref, sems = scratch
    copies = []

    def fetch(src, dst, index):
        copy = pltpu.make_async_copy(src, dst, sems.at[index])
        copy.start()
        return copy

    g_cuts = cuts_of(g_ref.shape[1], 512)
    x_cuts = cuts_of(x_ref.shape[0], 768)
    wg_copy = fetch(wg_hbm, wg_ref, 0)
    index = 2
    g_copies = []
    for at, size in g_cuts:
        columns = pl.ds(at, size)
        g_copies.append(fetch(g_hbm.at[:, columns], g_ref.at[:, columns], index))
        index += 1
    wx_copy = fetch(wx_hbm, wx_ref, 1)
    x_copies = []
    for at, size in x_cuts:
        rows = pl.ds(at, size)
        x_copies.append(fetch(x_hbm.at[rows, :], x_ref.at[rows, :], index))
        index += 1

    def product(copies, terms):
        total = None
        for copy, (left, right, along) in zip(copies, terms):
            copy.wait()
            term = lax.dot_general(
                left(), right(), (((1,), (along,)), ((), ())), preferred_element_type=jnp.float32
            )
            total = term if total is None else total + term
        return total

    def cut(ref, at, size, along):
        return lambda: ref[at : at + size, :] if along == 0 else ref[:, at : at + size]

    wg_copy.wait()
    grads_t = product(
        g_copies, [(cut(g_ref, at, size, 1), cut(wg_ref, at, size, 1), 1) for at, size in g_cuts]
    ).T
    wx_copy.wait()
    wide_ref[...] = product(
        x_copies, [(cut(wx_ref, at, size, 1), cut(x_ref, at, size, 0), 0) for at, size in x_cuts]
    )
    rank = grads_t.shape[0]
    side = rank_ref[0] & 1
    for out, taken in ((keep_ref, side), (send_ref, side ^ 1)):
        out[:rank, :] = grads_t
        out[rank:, :] = wide_ref[pl.ds(pl.multiple_of(taken * own, own), own), :]


def project(inputs, out_grads, in_proj, out_proj, me, own):
    rank = in_proj.shape[1]
    tokens, hidden = inputs.shape
    width = out_grads.shape[1]
    copies = 2 + len(cuts_of(width, 512)) + len(cuts_of(hidden, 768))
    arrays = (inputs.T, out_grads, in_proj.T, out_proj.T)
    in_hbm = pl.BlockSpec(memory_space=pltpu.HBM)
    return pl.pallas_call(
        functools.partial(project_kernel, own),
        out_shape=[jax.ShapeDtypeStruct((rank + own, tokens), jnp.float32)] * 2,
        in_specs=[pl.BlockSpec(memory_space=pltpu.SMEM)] + [in_hbm] * len(arrays),
        out_specs=[pl.BlockSpec(memory_space=pltpu.VMEM)] * 2,
        scratch_shapes=[
            pltpu.VMEM((hidden, tokens), jnp.bfloat16),
            pltpu.VMEM((tokens, width), jnp.bfloat16),
            pltpu.VMEM((rank, hidden), jnp.bfloat16),
            pltpu.VMEM((rank, width), jnp.bfloat16),
            pltpu.VMEM((rank, tokens), jnp.float32),
            pltpu.SemaphoreType.DMA((copies,)),
        ],
        compiler_params=pltpu.CompilerParams(vmem_limit_bytes=VMEM_LIMIT),
        name="project",
    )(me, *(pltpu.with_memory_space_constraint(array, pltpu.HBM) for array in arrays))


def halve_kernel(own, rank_ref, kept_ref, came_ref, keep_ref, send_ref, sum_ref):
    sum_ref[...] = kept_ref[...] + came_ref[...]
    place = rank_ref[0] // 2
    for out, taken in ((keep_ref, place), (send_ref, place ^ 1)):
        out[:own, :] = sum_ref[pl.ds(pl.multiple_of(taken * own, own), own), :]
        out[own:, :] = sum_ref[-own:, :]


def halve(kept, came, me, own):
    rows, tokens = kept.shape
    whole = pl.BlockSpec(memory_space=pltpu.VMEM)
    return pl.pallas_call(
        functools.partial(halve_kernel, own),
        out_shape=[jax.ShapeDtypeStruct((2 * own, tokens), jnp.float32)] * 2,
        in_specs=[pl.BlockSpec(memory_space=pltpu.SMEM), whole, whole],
        out_specs=[whole] * 2,
        scratch_shapes=[pltpu.VMEM((rows, tokens), jnp.float32)],
        compiler_params=pltpu.CompilerParams(vmem_limit_bytes=VMEM_LIMIT),
        name="halve",
    )(me, kept, came)


def pick_kernel(rank, own, rank_ref, queries_ref, out_ref):
    lanes = out_ref.shape[1]
    wide = lanes * rank // own
    steps = own * own // lanes
    asked = queries_ref.shape[0]
    me = rank_ref[0]
    start = (me // 2) * (own * rank)
    rows = jnp.concatenate(
        [
            queries_ref[:, pl.ds(pl.multiple_of(start + i * wide, lanes), wide)]
            for i in range(steps)
        ],
        axis=0,
    )
    source = lax.broadcasted_iota(jnp.int32, (wide, lanes), 0)
    place = lax.broadcasted_iota(jnp.int32, (wide, lanes), 1)
    wanted = (place // own) * rank + place % own + (me & 1) * own
    chosen = jnp.where(source == wanted, 1.0, 0.0).astype(jnp.bfloat16)
    high = rows.astype(jnp.bfloat16)
    rest = rows - high.astype(jnp.float32)
    middle = rest.astype(jnp.bfloat16)
    low = (rest - middle.astype(jnp.float32)).astype(jnp.bfloat16)
    terms = [
        jnp.dot(term, chosen, preferred_element_type=jnp.float32) for term in (high, middle, low)
    ]
    out_ref[...] = terms[0] + (terms[1] + terms[2])


def pick(queries, me, rank, own):
    lanes = 128
    rows = queries.shape[0] * own * own // lanes
    whole = pl.BlockSpec(memory_space=pltpu.VMEM)
    return pl.pallas_call(
        functools.partial(pick_kernel, rank, own),
        out_shape=jax.ShapeDtypeStruct((rows, lanes), jnp.float32),
        in_specs=[pl.BlockSpec(memory_space=pltpu.SMEM), whole],
        out_specs=whole,
        compiler_params=pltpu.CompilerParams(vmem_limit_bytes=VMEM_LIMIT),
        name="pick",
    )(me, queries)


def grads_kernel(weights_ref, kept_ref, came_ref, asked_ref, out_ref):
    summed = kept_ref[...] + came_ref[...]
    weights = weights_ref[...]
    own = summed.shape[0] // 2
    group = out_ref.shape[1] // own
    inputs_t = summed[own:, :]
    zero = jnp.zeros_like(inputs_t)
    right = jnp.concatenate(
        [
            jnp.concatenate([inputs_t if j == k else zero for k in range(group)], axis=1)
            for j in range(group)
        ],
        axis=0,
    )
    rows = []
    for i in range(own // group):
        rows.append(
            jnp.concatenate(
                [weights * summed[group * i + j : group * i + j + 1, :] for j in range(group)],
                axis=1,
            )
        )
    left = jnp.concatenate(rows, axis=0)
    count = left.shape[0]
    out_ref[:count, :] = dot_nt(left, right)
    out_ref[count:, :] = asked_ref[...]


def gradients(weights, kept, came, asked):
    lanes = asked.shape[1]
    own = kept.shape[0] // 2
    rows = own * own // lanes * weights.shape[0] + asked.shape[0]
    return pl.pallas_call(
        grads_kernel,
        out_shape=jax.ShapeDtypeStruct((rows, lanes), jnp.float32),
        compiler_params=pltpu.CompilerParams(vmem_limit_bytes=VMEM_LIMIT),
        name="gradients",
    )(weights, kept, came, asked)


def grams_kernel(steps, seqs, me_ref, *refs):
    blocks, out_ref = refs[:-1], refs[-1]
    shifts = (*SHIFTS[len(blocks)], 0)
    blocks = [blocks[shifts.index(-m % len(blocks))] for m in range(len(blocks))]
    count = steps * seqs
    asked = (blocks[0].shape[0] - count) // steps
    given = [block[count:, :] for block in blocks]
    ordered = []
    for place in range(len(blocks)):
        chosen = given[0]
        for m in range(1, len(blocks)):
            ahead = lax.rem(place - me_ref[0] + len(blocks), len(blocks))
            chosen = jnp.where(ahead == m, given[m], chosen)
        ordered.append(chosen)
    lanes = []
    for i in range(steps):
        rows = [block[i * seqs : (i + 1) * seqs, :] for block in blocks]
        rows += [chosen[i * asked : (i + 1) * asked, :] for chosen in ordered]
        lanes.append(jnp.concatenate(rows, axis=0))
    both = jnp.concatenate(lanes, axis=1)
    result = dot_nt(both, both[: len(blocks) * seqs])
    half = result.shape[0] // 2
    out_ref[...] = jnp.concatenate([result[:half, :], result[half:, :]], axis=1)


def grams(me, blocks, steps, seqs):
    asked = blocks[0].shape[0] // steps - seqs
    total = len(blocks) * seqs
    whole = pl.BlockSpec(memory_space=pltpu.VMEM)
    return pl.pallas_call(
        functools.partial(grams_kernel, steps, seqs),
        out_shape=jax.ShapeDtypeStruct(((total + len(blocks) * asked) // 2, 2 * total), jnp.float32),
        in_specs=[pl.BlockSpec(memory_space=pltpu.SMEM)] + [whole] * len(blocks),
        out_specs=whole,
        compiler_params=pltpu.CompilerParams(vmem_limit_bytes=VMEM_LIMIT),
        name="grams",
    )(me, *blocks)


def scales(count):
    first = 2.0 / (1.0 + 1.0 / count)
    off = count / (count + 1.0)
    steps = []
    while off > 1e-7:
        steps.append(2.0 / (2.0 - off * off))
        off = off * off / (2.0 - off * off)
    return first, steps


def solve_kernel(seqs, *refs):
    parts, out_ref = refs[:-1], refs[-1]
    packed = (parts[0][...] + parts[1][...]) + (parts[2][...] + parts[3][...])
    lane = lax.broadcasted_iota(jnp.int32, packed.shape, 1)
    turned = pltpu.roll(packed, seqs, 1)
    both = jnp.concatenate(
        [jnp.where(lane < seqs, packed, turned), jnp.where(lane < seqs, turned, packed)], axis=0
    )
    lane = lax.broadcasted_iota(jnp.int32, both.shape, 1)
    row = lax.broadcasted_iota(jnp.int32, both.shape, 0)
    unit = jnp.where((lane & (seqs - 1)) == row, 1.0, 0.0)
    total = jnp.sum(jnp.where(lane == row, both, 0.0)[:seqs], axis=(0, 1), keepdims=True)
    first, steps = scales(seqs)
    state = first * (both / total + unit * (damping / seqs))
    left_lanes = lane < seqs
    for at, step in enumerate(steps):
        high = state.astype(jnp.bfloat16).astype(jnp.float32)
        low = state - high
        left = jnp.where(left_lanes, high, low).astype(jnp.bfloat16)
        high = high[:seqs].astype(jnp.bfloat16)
        low = low[:seqs].astype(jnp.bfloat16)
        right = jnp.concatenate([high, high, low, low], axis=0)
        if at + 1 == len(steps):
            left, state = left[seqs:], state[seqs:]
        product = jnp.dot(
            jnp.concatenate([left, left], axis=1), right, preferred_element_type=jnp.float32
        )
        state = step * (2.0 * state - product)
    out_ref[...] = state[:, : out_ref.shape[1]]


def solve(parts, seqs, asked, seq_dev):
    return pl.pallas_call(
        functools.partial(solve_kernel, seqs),
        out_shape=jax.ShapeDtypeStruct((asked, seq_dev), jnp.float32),
        compiler_params=pltpu.CompilerParams(vmem_limit_bytes=VMEM_LIMIT),
        name="solve",
    )(*parts)


def from_partner(value, axis, size, m):
    return lax.ppermute(value, axis, [(i, i ^ m) for i in range(size)])


def from_partners(value, axis, size):
    return [from_partner(value, axis, size, m) for m in reversed(range(1, size))] + [value]


def from_all(value, axis, size):
    shifts = [[(i, (i + s) % size) for i in range(size)] for s in SHIFTS[size]]
    return [lax.ppermute(value, axis, shift) for shift in shifts] + [value]


def finish_long(message, steps, first, seq_dev):
    every = lax.all_gather(message, "dp", axis=0)
    lanes = message.shape[1]

    def rows_of(block):
        block = block.reshape(block.shape[0], steps, -1, lanes).transpose(0, 2, 1, 3)
        return block.reshape(-1, steps * lanes)

    count = steps * seq_dev
    grads, asked = rows_of(every[:, :count]), rows_of(every[:, count:])
    both = jnp.einsum(
        "ik,jk->ij", jnp.concatenate([grads, asked], axis=0), grads,
        precision=lax.Precision.HIGHEST,
    )
    both = lax.psum(both, "tensor")
    count = grads.shape[0]
    kernel, products = both[:count], both[count:]
    damp = damping * jnp.trace(kernel) / count
    unit = jnp.eye(count, dtype=jnp.float32)
    factor = jnp.linalg.cholesky(kernel + damp * unit)
    picks = lax.dynamic_slice_in_dim(unit, first, seq_dev, 1)
    solved = jax.scipy.linalg.cho_solve((factor, True), picks)
    return jnp.dot(products, solved, precision=lax.Precision.HIGHEST)


def per_device(sizes, inputs, out_grads, in_proj, out_proj, seq_ids, counts, queries):
    parts, blocks = sizes
    rank = in_proj.shape[1]
    seq_dev = counts.shape[0]
    me = lax.axis_index("tensor")
    place = lax.axis_index("dp")
    first = place * seq_dev
    own = 2 * rank // parts
    rank_of = me.reshape(1)
    kept, sent = project(inputs, out_grads, in_proj, out_proj, rank_of, own)
    asked = pick(queries, rank_of, rank, own)
    weights = token_weights(seq_ids, counts, first)
    came = from_partner(sent, "tensor", parts, 1)
    kept, sent = halve(kept, came, rank_of, own)
    came = from_partner(sent, "tensor", parts, 2)
    message = gradients(weights, kept, came, asked)
    steps = own * own // message.shape[1]
    if blocks > SMALL:
        return finish_long(message, steps, first, seq_dev)
    partial = grams(place.reshape(1), from_all(message, "dp", blocks), steps, seq_dev)
    partial = from_partners(partial, "tensor", parts)
    return solve(partial, blocks * seq_dev, blocks * queries.shape[0], seq_dev)


def solution(mesh):
    in_specs = (
        P(("groups", "dp"), "tensor"),
        P(("groups", "dp"), "tensor"),
        P("tensor", None),
        P("tensor", None),
        P(("groups", "dp")),
        P(("groups", "dp")),
        P(("groups", "dp"), None),
    )
    sizes = (mesh.shape["tensor"], mesh.shape["dp"])
    return jax.shard_map(
        functools.partial(per_device, sizes),
        mesh=mesh,
        in_specs=in_specs,
        out_specs=P("groups", "dp"),
        check_vma=False,
    )
```

```python
import functools

import jax
import jax.numpy as jnp
from jax import lax
from jax.experimental import pallas as pl
from jax.experimental.pallas import tpu as pltpu
from jax.sharding import PartitionSpec as P

damping = 0.5
VMEM_LIMIT = 32 * 1024 * 1024
SMALL = 4


def token_weights(seq_ids, counts, first):
    local_ids = seq_ids - first
    slots = jnp.arange(counts.shape[0], dtype=jnp.int32)
    member = local_ids[None, :] == slots[:, None]
    starts = jnp.sum((local_ids[None, :] < slots[:, None]).astype(jnp.int32), axis=1)
    offset = jnp.arange(seq_ids.shape[0], dtype=jnp.int32)[None, :] - starts[:, None]
    scale = 1.0 / counts.astype(jnp.float32)
    return jnp.where(member & (offset < counts[:, None]), scale[:, None], 0.0)


def cuts_of(extent, step):
    return [(at, min(step, extent - at)) for at in range(0, extent, step)]


def two_terms(value):
    high = value.astype(jnp.bfloat16)
    low = (value - high.astype(jnp.float32)).astype(jnp.bfloat16)
    return high, low


def dot_nt(left, right):
    rows = left.shape[0]
    lh, ll = two_terms(left)
    rh, rl = two_terms(right)
    mul = functools.partial(
        lax.dot_general,
        dimension_numbers=(((1,), (1,)), ((), ())),
        preferred_element_type=jnp.float32,
    )
    both = mul(jnp.concatenate([lh, ll], axis=0), rh)
    return both[:rows] + (mul(lh, rl) + both[rows:])


def project_kernel(own, rank_ref, x_hbm, g_hbm, wx_hbm, wg_hbm, keep_ref, send_ref, *scratch):
    x_ref, g_ref, wx_ref, wg_ref, wide_ref, sems = scratch
    copies = []

    def fetch(src, dst, index):
        copy = pltpu.make_async_copy(src, dst, sems.at[index])
        copy.start()
        return copy

    g_cuts = cuts_of(g_ref.shape[1], 1024)
    x_cuts = cuts_of(x_ref.shape[0], 1024)
    wg_copy = fetch(wg_hbm, wg_ref, 0)
    index = 2
    g_copies = []
    for at, size in g_cuts:
        columns = pl.ds(at, size)
        g_copies.append(fetch(g_hbm.at[:, columns], g_ref.at[:, columns], index))
        index += 1
    wx_copy = fetch(wx_hbm, wx_ref, 1)
    x_copies = []
    for at, size in x_cuts:
        rows = pl.ds(at, size)
        x_copies.append(fetch(x_hbm.at[rows, :], x_ref.at[rows, :], index))
        index += 1

    def product(copies, terms):
        total = None
        for copy, (left, right, along) in zip(copies, terms):
            copy.wait()
            term = lax.dot_general(
                left(), right(), (((1,), (along,)), ((), ())), preferred_element_type=jnp.float32
            )
            total = term if total is None else total + term
        return total

    def cut(ref, at, size, along):
        return lambda: ref[at : at + size, :] if along == 0 else ref[:, at : at + size]

    wg_copy.wait()
    grads_t = product(
        g_copies, [(cut(g_ref, at, size, 1), cut(wg_ref, at, size, 1), 1) for at, size in g_cuts]
    ).T
    wx_copy.wait()
    wide_ref[...] = product(
        x_copies, [(cut(wx_ref, at, size, 1), cut(x_ref, at, size, 0), 0) for at, size in x_cuts]
    )
    rank = grads_t.shape[0]
    side = rank_ref[0] & 1
    for out, taken in ((keep_ref, side), (send_ref, side ^ 1)):
        out[:rank, :] = grads_t
        out[rank:, :] = wide_ref[pl.ds(pl.multiple_of(taken * own, own), own), :]


def project(inputs, out_grads, in_proj, out_proj, me, own):
    rank = in_proj.shape[1]
    tokens, hidden = inputs.shape
    width = out_grads.shape[1]
    copies = 2 + len(cuts_of(width, 1024)) + len(cuts_of(hidden, 1024))
    arrays = (inputs.T, out_grads, in_proj.T, out_proj.T)
    in_hbm = pl.BlockSpec(memory_space=pltpu.HBM)
    return pl.pallas_call(
        functools.partial(project_kernel, own),
        out_shape=[jax.ShapeDtypeStruct((rank + own, tokens), jnp.float32)] * 2,
        in_specs=[pl.BlockSpec(memory_space=pltpu.SMEM)] + [in_hbm] * len(arrays),
        out_specs=[pl.BlockSpec(memory_space=pltpu.VMEM)] * 2,
        scratch_shapes=[
            pltpu.VMEM((hidden, tokens), jnp.bfloat16),
            pltpu.VMEM((tokens, width), jnp.bfloat16),
            pltpu.VMEM((rank, hidden), jnp.bfloat16),
            pltpu.VMEM((rank, width), jnp.bfloat16),
            pltpu.VMEM((rank, tokens), jnp.float32),
            pltpu.SemaphoreType.DMA((copies,)),
        ],
        compiler_params=pltpu.CompilerParams(vmem_limit_bytes=VMEM_LIMIT),
        name="project",
    )(me, *(pltpu.with_memory_space_constraint(array, pltpu.HBM) for array in arrays))


def halve_kernel(own, rank_ref, kept_ref, came_ref, keep_ref, send_ref, sum_ref):
    sum_ref[...] = kept_ref[...] + came_ref[...]
    place = rank_ref[0] // 2
    for out, taken in ((keep_ref, place), (send_ref, place ^ 1)):
        out[:own, :] = sum_ref[pl.ds(pl.multiple_of(taken * own, own), own), :]
        out[own:, :] = sum_ref[-own:, :]


def halve(kept, came, me, own):
    rows, tokens = kept.shape
    whole = pl.BlockSpec(memory_space=pltpu.VMEM)
    return pl.pallas_call(
        functools.partial(halve_kernel, own),
        out_shape=[jax.ShapeDtypeStruct((2 * own, tokens), jnp.float32)] * 2,
        in_specs=[pl.BlockSpec(memory_space=pltpu.SMEM), whole, whole],
        out_specs=[whole] * 2,
        scratch_shapes=[pltpu.VMEM((rows, tokens), jnp.float32)],
        compiler_params=pltpu.CompilerParams(vmem_limit_bytes=VMEM_LIMIT),
        name="halve",
    )(me, kept, came)


def pick_kernel(rank, own, rank_ref, queries_ref, out_ref):
    lanes = out_ref.shape[1]
    wide = lanes * rank // own
    steps = own * own // lanes
    asked = queries_ref.shape[0]
    me = rank_ref[0]
    start = (me // 2) * (own * rank)
    rows = jnp.concatenate(
        [
            queries_ref[:, pl.ds(pl.multiple_of(start + i * wide, lanes), wide)]
            for i in range(steps)
        ],
        axis=0,
    )
    source = lax.broadcasted_iota(jnp.int32, (wide, lanes), 0)
    place = lax.broadcasted_iota(jnp.int32, (wide, lanes), 1)
    wanted = (place // own) * rank + place % own + (me & 1) * own
    chosen = jnp.where(source == wanted, 1.0, 0.0).astype(jnp.bfloat16)
    high = rows.astype(jnp.bfloat16)
    rest = rows - high.astype(jnp.float32)
    middle = rest.astype(jnp.bfloat16)
    low = (rest - middle.astype(jnp.float32)).astype(jnp.bfloat16)
    terms = [
        jnp.dot(term, chosen, preferred_element_type=jnp.float32) for term in (high, middle, low)
    ]
    out_ref[...] = terms[0] + (terms[1] + terms[2])


def pick(queries, me, rank, own):
    lanes = 128
    rows = queries.shape[0] * own * own // lanes
    whole = pl.BlockSpec(memory_space=pltpu.VMEM)
    return pl.pallas_call(
        functools.partial(pick_kernel, rank, own),
        out_shape=jax.ShapeDtypeStruct((rows, lanes), jnp.float32),
        in_specs=[pl.BlockSpec(memory_space=pltpu.SMEM), whole],
        out_specs=whole,
        compiler_params=pltpu.CompilerParams(vmem_limit_bytes=VMEM_LIMIT),
        name="pick",
    )(me, queries)


def grads_kernel(weights_ref, kept_ref, came_ref, asked_ref, out_ref):
    summed = kept_ref[...] + came_ref[...]
    weights = weights_ref[...]
    own = summed.shape[0] // 2
    group = out_ref.shape[1] // own
    inputs_t = summed[own:, :]
    zero = jnp.zeros_like(inputs_t)
    right = jnp.concatenate(
        [
            jnp.concatenate([inputs_t if j == k else zero for k in range(group)], axis=1)
            for j in range(group)
        ],
        axis=0,
    )
    rows = []
    for i in range(own // group):
        rows.append(
            jnp.concatenate(
                [weights * summed[group * i + j : group * i + j + 1, :] for j in range(group)],
                axis=1,
            )
        )
    left = jnp.concatenate(rows, axis=0)
    count = left.shape[0]
    out_ref[:count, :] = dot_nt(left, right)
    out_ref[count:, :] = asked_ref[...]


def gradients(weights, kept, came, asked):
    lanes = asked.shape[1]
    own = kept.shape[0] // 2
    rows = own * own // lanes * weights.shape[0] + asked.shape[0]
    return pl.pallas_call(
        grads_kernel,
        out_shape=jax.ShapeDtypeStruct((rows, lanes), jnp.float32),
        compiler_params=pltpu.CompilerParams(vmem_limit_bytes=VMEM_LIMIT),
        name="gradients",
    )(weights, kept, came, asked)


def grams_kernel(steps, seqs, me_ref, *refs):
    blocks, out_ref = refs[-2::-1], refs[-1]
    count = steps * seqs
    asked = (blocks[0].shape[0] - count) // steps
    given = [block[count:, :] for block in blocks]
    ordered = []
    for place in range(len(blocks)):
        chosen = given[0]
        for m in range(1, len(blocks)):
            ahead = lax.rem(place - me_ref[0] + len(blocks), len(blocks))
            chosen = jnp.where(ahead == m, given[m], chosen)
        ordered.append(chosen)
    lanes = []
    for i in range(steps):
        rows = [block[i * seqs : (i + 1) * seqs, :] for block in blocks]
        rows += [chosen[i * asked : (i + 1) * asked, :] for chosen in ordered]
        lanes.append(jnp.concatenate(rows, axis=0))
    both = jnp.concatenate(lanes, axis=1)
    result = dot_nt(both, both[: len(blocks) * seqs])
    half = result.shape[0] // 2
    out_ref[...] = jnp.concatenate([result[:half, :], result[half:, :]], axis=1)


def grams(me, blocks, steps, seqs):
    asked = blocks[0].shape[0] // steps - seqs
    total = len(blocks) * seqs
    whole = pl.BlockSpec(memory_space=pltpu.VMEM)
    return pl.pallas_call(
        functools.partial(grams_kernel, steps, seqs),
        out_shape=jax.ShapeDtypeStruct(((total + len(blocks) * asked) // 2, 2 * total), jnp.float32),
        in_specs=[pl.BlockSpec(memory_space=pltpu.SMEM)] + [whole] * len(blocks),
        out_specs=whole,
        compiler_params=pltpu.CompilerParams(vmem_limit_bytes=VMEM_LIMIT),
        name="grams",
    )(me, *blocks)


def scales(count):
    first = 2.0 / (1.0 + 1.0 / count)
    off = count / (count + 1.0)
    steps = []
    while off > 1e-7:
        steps.append(2.0 / (2.0 - off * off))
        off = off * off / (2.0 - off * off)
    return first, steps


def solve_kernel(seqs, *refs):
    parts, out_ref = refs[:-1], refs[-1]
    packed = (parts[1][...] + parts[3][...]) + (parts[0][...] + parts[2][...])
    lane = lax.broadcasted_iota(jnp.int32, packed.shape, 1)
    turned = pltpu.roll(packed, seqs, 1)
    both = jnp.concatenate(
        [jnp.where(lane < seqs, packed, turned), jnp.where(lane < seqs, turned, packed)], axis=0
    )
    lane = lax.broadcasted_iota(jnp.int32, both.shape, 1)
    row = lax.broadcasted_iota(jnp.int32, both.shape, 0)
    unit = jnp.where((lane & (seqs - 1)) == row, 1.0, 0.0)
    total = jnp.sum(jnp.where(lane == row, both, 0.0)[:seqs], axis=(0, 1), keepdims=True)
    first, steps = scales(seqs)
    state = first * (both / total + unit * (damping / seqs))
    left_lanes = lane < seqs
    for at, step in enumerate(steps):
        high = state.astype(jnp.bfloat16).astype(jnp.float32)
        low = state - high
        left = jnp.where(left_lanes, high, low).astype(jnp.bfloat16)
        high = high[:seqs].astype(jnp.bfloat16)
        low = low[:seqs].astype(jnp.bfloat16)
        right = jnp.concatenate([high, high, low, low], axis=0)
        if at + 1 == len(steps):
            left, state = left[seqs:], state[seqs:]
        product = jnp.dot(
            jnp.concatenate([left, left], axis=1), right, preferred_element_type=jnp.float32
        )
        state = step * (2.0 * state - product)
    out_ref[...] = state[:, : out_ref.shape[1]]


def solve(parts, seqs, asked, seq_dev):
    return pl.pallas_call(
        functools.partial(solve_kernel, seqs),
        out_shape=jax.ShapeDtypeStruct((asked, seq_dev), jnp.float32),
        compiler_params=pltpu.CompilerParams(vmem_limit_bytes=VMEM_LIMIT),
        name="solve",
    )(*parts)


def from_partner(value, axis, size, m):
    return lax.ppermute(value, axis, [(i, i ^ m) for i in range(size)])


def from_all(value, axis, size):
    shifts = [[(i, (i + s) % size) for i in range(size)] for s in range(1, size)]
    return [lax.ppermute(value, axis, shift) for shift in shifts] + [value]


def finish_long(message, steps, first, seq_dev):
    every = lax.all_gather(message, "dp", axis=0)
    lanes = message.shape[1]

    def rows_of(block):
        block = block.reshape(block.shape[0], steps, -1, lanes).transpose(0, 2, 1, 3)
        return block.reshape(-1, steps * lanes)

    count = steps * seq_dev
    grads, asked = rows_of(every[:, :count]), rows_of(every[:, count:])
    both = jnp.einsum(
        "ik,jk->ij", jnp.concatenate([grads, asked], axis=0), grads,
        precision=lax.Precision.HIGHEST,
    )
    both = lax.psum(both, "tensor")
    count = grads.shape[0]
    kernel, products = both[:count], both[count:]
    damp = damping * jnp.trace(kernel) / count
    unit = jnp.eye(count, dtype=jnp.float32)
    factor = jnp.linalg.cholesky(kernel + damp * unit)
    picks = lax.dynamic_slice_in_dim(unit, first, seq_dev, 1)
    solved = jax.scipy.linalg.cho_solve((factor, True), picks)
    return jnp.dot(products, solved, precision=lax.Precision.HIGHEST)


def per_device(sizes, inputs, out_grads, in_proj, out_proj, seq_ids, counts, queries):
    parts, blocks = sizes
    rank = in_proj.shape[1]
    seq_dev = counts.shape[0]
    me = lax.axis_index("tensor")
    place = lax.axis_index("dp")
    first = place * seq_dev
    own = 2 * rank // parts
    rank_of = me.reshape(1)
    kept, sent = project(inputs, out_grads, in_proj, out_proj, rank_of, own)
    asked = pick(queries, rank_of, rank, own)
    weights = token_weights(seq_ids, counts, first)
    came = from_partner(sent, "tensor", parts, 1)
    kept, sent = halve(kept, came, rank_of, own)
    came = from_partner(sent, "tensor", parts, 2)
    message = gradients(weights, kept, came, asked)
    steps = own * own // message.shape[1]
    if blocks > SMALL:
        return finish_long(message, steps, first, seq_dev)
    partial = grams(place.reshape(1), from_all(message, "dp", blocks), steps, seq_dev)
    partial = from_all(partial, "tensor", parts)
    return solve(partial, blocks * seq_dev, blocks * queries.shape[0], seq_dev)


def solution(mesh):
    in_specs = (
        P(("groups", "dp"), "tensor"),
        P(("groups", "dp"), "tensor"),
        P("tensor", None),
        P("tensor", None),
        P(("groups", "dp")),
        P(("groups", "dp")),
        P(("groups", "dp"), None),
    )
    sizes = (mesh.shape["tensor"], mesh.shape["dp"])
    return jax.shard_map(
        functools.partial(per_device, sizes),
        mesh=mesh,
        in_specs=in_specs,
        out_specs=P("groups", "dp"),
        check_vma=False,
    )
```

```python
import functools

import jax
import jax.numpy as jnp
from jax import lax
from jax.experimental import pallas as pl
from jax.experimental.pallas import tpu as pltpu
from jax.sharding import PartitionSpec as P

damping = 0.5
VMEM_LIMIT = 32 * 1024 * 1024
SMALL = 4


def token_weights(seq_ids, counts, first):
    local_ids = seq_ids - first
    slots = jnp.arange(counts.shape[0], dtype=jnp.int32)
    member = local_ids[None, :] == slots[:, None]
    starts = jnp.sum((local_ids[None, :] < slots[:, None]).astype(jnp.int32), axis=1)
    offset = jnp.arange(seq_ids.shape[0], dtype=jnp.int32)[None, :] - starts[:, None]
    scale = 1.0 / counts.astype(jnp.float32)
    scale = jnp.sum(jnp.where(member, scale[:, None], 0.0), axis=0, keepdims=True)
    return jnp.where(member & (offset < counts[:, None]), 1.0, 0.0).astype(jnp.bfloat16), scale


def cuts_of(extent, step):
    return [(at, min(step, extent - at)) for at in range(0, extent, step)]


def two_terms(value):
    high = value.astype(jnp.bfloat16)
    low = (value - high.astype(jnp.float32)).astype(jnp.bfloat16)
    return high, low


def dot_nt(left, right):
    return product_nt(*two_terms(left), *two_terms(right))


def product_nt(lh, ll, rh, rl):
    rows = lh.shape[0]
    mul = functools.partial(
        lax.dot_general,
        dimension_numbers=(((1,), (1,)), ((), ())),
        preferred_element_type=jnp.float32,
    )
    both = mul(jnp.concatenate([lh, ll], axis=0), rh)
    return both[:rows] + (mul(lh, rl) + both[rows:])


def project_kernel(own, rank_ref, x_hbm, g_hbm, wx_hbm, wg_hbm, keep_ref, send_ref, *scratch):
    x_ref, g_ref, wx_ref, wg_ref, wide_ref, sems = scratch
    copies = []

    def fetch(src, dst, index):
        copy = pltpu.make_async_copy(src, dst, sems.at[index])
        copy.start()
        return copy

    g_cuts = cuts_of(g_ref.shape[1], 1024)
    x_cuts = cuts_of(x_ref.shape[0], 1024)
    wg_copy = fetch(wg_hbm, wg_ref, 0)
    index = 2
    g_copies = []
    for at, size in g_cuts:
        columns = pl.ds(at, size)
        g_copies.append(fetch(g_hbm.at[:, columns], g_ref.at[:, columns], index))
        index += 1
    wx_copy = fetch(wx_hbm, wx_ref, 1)
    x_copies = []
    for at, size in x_cuts:
        rows = pl.ds(at, size)
        x_copies.append(fetch(x_hbm.at[rows, :], x_ref.at[rows, :], index))
        index += 1

    def product(copies, terms):
        total = None
        for copy, (left, right, along) in zip(copies, terms):
            copy.wait()
            term = lax.dot_general(
                left(), right(), (((1,), (along,)), ((), ())), preferred_element_type=jnp.float32
            )
            total = term if total is None else total + term
        return total

    def cut(ref, at, size, along):
        return lambda: ref[at : at + size, :] if along == 0 else ref[:, at : at + size]

    wg_copy.wait()
    grads_t = product(
        g_copies, [(cut(g_ref, at, size, 1), cut(wg_ref, at, size, 1), 1) for at, size in g_cuts]
    ).T
    wx_copy.wait()
    wide_ref[...] = product(
        x_copies, [(cut(wx_ref, at, size, 1), cut(x_ref, at, size, 0), 0) for at, size in x_cuts]
    )
    rank = grads_t.shape[0]
    side = rank_ref[0] & 1
    for out, taken in ((keep_ref, side), (send_ref, side ^ 1)):
        out[:rank, :] = grads_t
        out[rank:, :] = wide_ref[pl.ds(pl.multiple_of(taken * own, own), own), :]


def project(inputs, out_grads, in_proj, out_proj, me, own):
    rank = in_proj.shape[1]
    tokens, hidden = inputs.shape
    width = out_grads.shape[1]
    copies = 2 + len(cuts_of(width, 1024)) + len(cuts_of(hidden, 1024))
    arrays = (inputs.T, out_grads, in_proj.T, out_proj.T)
    in_hbm = pl.BlockSpec(memory_space=pltpu.HBM)
    return pl.pallas_call(
        functools.partial(project_kernel, own),
        out_shape=[jax.ShapeDtypeStruct((rank + own, tokens), jnp.float32)] * 2,
        in_specs=[pl.BlockSpec(memory_space=pltpu.SMEM)] + [in_hbm] * len(arrays),
        out_specs=[pl.BlockSpec(memory_space=pltpu.VMEM)] * 2,
        scratch_shapes=[
            pltpu.VMEM((hidden, tokens), jnp.bfloat16),
            pltpu.VMEM((tokens, width), jnp.bfloat16),
            pltpu.VMEM((rank, hidden), jnp.bfloat16),
            pltpu.VMEM((rank, width), jnp.bfloat16),
            pltpu.VMEM((rank, tokens), jnp.float32),
            pltpu.SemaphoreType.DMA((copies,)),
        ],
        compiler_params=pltpu.CompilerParams(vmem_limit_bytes=VMEM_LIMIT),
        name="project",
    )(me, *(pltpu.with_memory_space_constraint(array, pltpu.HBM) for array in arrays))


def halve_kernel(own, rank_ref, kept_ref, came_ref, keep_ref, send_ref, sum_ref):
    sum_ref[...] = kept_ref[...] + came_ref[...]
    place = rank_ref[0] // 2
    for out, taken in ((keep_ref, place), (send_ref, place ^ 1)):
        out[:own, :] = sum_ref[pl.ds(pl.multiple_of(taken * own, own), own), :]
        out[own:, :] = sum_ref[-own:, :]


def halve(kept, came, me, own):
    rows, tokens = kept.shape
    whole = pl.BlockSpec(memory_space=pltpu.VMEM)
    return pl.pallas_call(
        functools.partial(halve_kernel, own),
        out_shape=[jax.ShapeDtypeStruct((2 * own, tokens), jnp.float32)] * 2,
        in_specs=[pl.BlockSpec(memory_space=pltpu.SMEM), whole, whole],
        out_specs=[whole] * 2,
        scratch_shapes=[pltpu.VMEM((rows, tokens), jnp.float32)],
        compiler_params=pltpu.CompilerParams(vmem_limit_bytes=VMEM_LIMIT),
        name="halve",
    )(me, kept, came)


def pick_kernel(rank, own, rank_ref, queries_ref, out_ref):
    lanes = out_ref.shape[1]
    wide = lanes * rank // own
    steps = own * own // lanes
    asked = queries_ref.shape[0]
    me = rank_ref[0]
    start = (me // 2) * (own * rank)
    rows = jnp.concatenate(
        [
            queries_ref[:, pl.ds(pl.multiple_of(start + i * wide, lanes), wide)]
            for i in range(steps)
        ],
        axis=0,
    )
    source = lax.broadcasted_iota(jnp.int32, (wide, lanes), 0)
    place = lax.broadcasted_iota(jnp.int32, (wide, lanes), 1)
    wanted = (place // own) * rank + place % own + (me & 1) * own
    chosen = jnp.where(source == wanted, 1.0, 0.0).astype(jnp.bfloat16)
    high = rows.astype(jnp.bfloat16)
    rest = rows - high.astype(jnp.float32)
    middle = rest.astype(jnp.bfloat16)
    low = (rest - middle.astype(jnp.float32)).astype(jnp.bfloat16)
    terms = [
        jnp.dot(term, chosen, preferred_element_type=jnp.float32) for term in (high, middle, low)
    ]
    out_ref[...] = terms[0] + (terms[1] + terms[2])


def pick(queries, me, rank, own):
    lanes = 128
    rows = queries.shape[0] * own * own // lanes
    whole = pl.BlockSpec(memory_space=pltpu.VMEM)
    return pl.pallas_call(
        functools.partial(pick_kernel, rank, own),
        out_shape=jax.ShapeDtypeStruct((rows, lanes), jnp.float32),
        in_specs=[pl.BlockSpec(memory_space=pltpu.SMEM), whole],
        out_specs=whole,
        compiler_params=pltpu.CompilerParams(vmem_limit_bytes=VMEM_LIMIT),
        name="pick",
    )(me, queries)


def grads_kernel(member_ref, scale_ref, kept_ref, came_ref, asked_ref, out_ref):
    summed = kept_ref[...] + came_ref[...]
    member = member_ref[...]
    own = summed.shape[0] // 2
    group = out_ref.shape[1] // own
    inputs_t = summed[own:, :] * scale_ref[...]
    zero = jnp.zeros(inputs_t.shape, jnp.bfloat16)

    def diagonal(term):
        rows = [
            jnp.concatenate([term if j == k else zero for k in range(group)], axis=1)
            for j in range(group)
        ]
        return jnp.concatenate(rows, axis=0)

    def spread(term):
        rows = [
            jnp.concatenate([member * term[i + j : i + j + 1, :] for j in range(group)], axis=1)
            for i in range(0, own, group)
        ]
        return jnp.concatenate(rows, axis=0)

    lh, ll = (spread(term) for term in two_terms(summed[:own, :]))
    rh, rl = (diagonal(term) for term in two_terms(inputs_t))
    made = product_nt(lh, ll, rh, rl)
    count = made.shape[0]
    out_ref[:count, :] = made
    out_ref[count:, :] = asked_ref[...]


def gradients(weights, kept, came, asked):
    lanes = asked.shape[1]
    own = kept.shape[0] // 2
    rows = own * own // lanes * weights[0].shape[0] + asked.shape[0]
    return pl.pallas_call(
        grads_kernel,
        out_shape=jax.ShapeDtypeStruct((rows, lanes), jnp.float32),
        compiler_params=pltpu.CompilerParams(vmem_limit_bytes=VMEM_LIMIT),
        name="gradients",
    )(*weights, kept, came, asked)


def grams_kernel(steps, seqs, me_ref, *refs):
    blocks, out_ref = refs[-2::-1], refs[-1]
    count = steps * seqs
    asked = (blocks[0].shape[0] - count) // steps
    given = [block[count:, :] for block in blocks]
    ordered = []
    for place in range(len(blocks)):
        chosen = given[0]
        for m in range(1, len(blocks)):
            ahead = lax.rem(place - me_ref[0] + len(blocks), len(blocks))
            chosen = jnp.where(ahead == m, given[m], chosen)
        ordered.append(chosen)
    lanes = []
    for i in range(steps):
        rows = [block[i * seqs : (i + 1) * seqs, :] for block in blocks]
        rows += [chosen[i * asked : (i + 1) * asked, :] for chosen in ordered]
        lanes.append(jnp.concatenate(rows, axis=0))
    both = jnp.concatenate(lanes, axis=1)
    result = dot_nt(both, both[: len(blocks) * seqs])
    half = result.shape[0] // 2
    out_ref[...] = jnp.concatenate([result[:half, :], result[half:, :]], axis=1)


def grams(me, blocks, steps, seqs):
    asked = blocks[0].shape[0] // steps - seqs
    total = len(blocks) * seqs
    whole = pl.BlockSpec(memory_space=pltpu.VMEM)
    return pl.pallas_call(
        functools.partial(grams_kernel, steps, seqs),
        out_shape=jax.ShapeDtypeStruct(((total + len(blocks) * asked) // 2, 2 * total), jnp.float32),
        in_specs=[pl.BlockSpec(memory_space=pltpu.SMEM)] + [whole] * len(blocks),
        out_specs=whole,
        compiler_params=pltpu.CompilerParams(vmem_limit_bytes=VMEM_LIMIT),
        name="grams",
    )(me, *blocks)


def scales(count):
    first = 2.0 / (1.0 + 1.0 / count)
    off = count / (count + 1.0)
    steps = []
    while off > 1e-7:
        steps.append(2.0 / (2.0 - off * off))
        off = off * off / (2.0 - off * off)
    return first, steps


def solve_kernel(seqs, *refs):
    parts, out_ref = refs[:-1], refs[-1]
    packed = (parts[0][...] + parts[1][...]) + (parts[2][...] + parts[3][...])
    lane = lax.broadcasted_iota(jnp.int32, packed.shape, 1)
    turned = pltpu.roll(packed, seqs, 1)
    both = jnp.concatenate(
        [jnp.where(lane < seqs, packed, turned), jnp.where(lane < seqs, turned, packed)], axis=0
    )
    lane = lax.broadcasted_iota(jnp.int32, both.shape, 1)
    row = lax.broadcasted_iota(jnp.int32, both.shape, 0)
    unit = jnp.where((lane & (seqs - 1)) == row, 1.0, 0.0)
    total = jnp.sum(jnp.where(lane == row, both, 0.0)[:seqs], axis=(0, 1), keepdims=True)
    first, steps = scales(seqs)
    state = first * (both / total + unit * (damping / seqs))
    left_lanes = lane < seqs
    for at, step in enumerate(steps):
        high = state.astype(jnp.bfloat16).astype(jnp.float32)
        low = state - high
        left = jnp.where(left_lanes, high, low).astype(jnp.bfloat16)
        left = jnp.concatenate([left, high[:, :seqs].astype(jnp.bfloat16)], axis=1)
        high = high[:seqs].astype(jnp.bfloat16)
        low = low[:seqs].astype(jnp.bfloat16)
        right = jnp.concatenate([high, high, low], axis=0)
        if at + 1 == len(steps):
            left, state = left[seqs:], state[seqs:]
        product = jnp.dot(left, right, preferred_element_type=jnp.float32)
        state = step * (2.0 * state - product)
    out_ref[...] = state[:, : out_ref.shape[1]]


def solve(parts, seqs, asked, seq_dev):
    return pl.pallas_call(
        functools.partial(solve_kernel, seqs),
        out_shape=jax.ShapeDtypeStruct((asked, seq_dev), jnp.float32),
        compiler_params=pltpu.CompilerParams(vmem_limit_bytes=VMEM_LIMIT),
        name="solve",
    )(*parts)


def from_partner(value, axis, size, m):
    return lax.ppermute(value, axis, [(i, i ^ m) for i in range(size)])


def from_partners(value, axis, size):
    return [from_partner(value, axis, size, m) for m in reversed(range(1, size))] + [value]


def from_all(value, axis, size):
    shifts = [[(i, (i + s) % size) for i in range(size)] for s in range(1, size)]
    return [lax.ppermute(value, axis, shift) for shift in shifts] + [value]


def finish_long(message, steps, first, seq_dev):
    every = lax.all_gather(message, "dp", axis=0)
    lanes = message.shape[1]

    def rows_of(block):
        block = block.reshape(block.shape[0], steps, -1, lanes).transpose(0, 2, 1, 3)
        return block.reshape(-1, steps * lanes)

    count = steps * seq_dev
    grads, asked = rows_of(every[:, :count]), rows_of(every[:, count:])
    both = jnp.einsum(
        "ik,jk->ij", jnp.concatenate([grads, asked], axis=0), grads,
        precision=lax.Precision.HIGHEST,
    )
    both = lax.psum(both, "tensor")
    count = grads.shape[0]
    kernel, products = both[:count], both[count:]
    damp = damping * jnp.trace(kernel) / count
    unit = jnp.eye(count, dtype=jnp.float32)
    factor = jnp.linalg.cholesky(kernel + damp * unit)
    picks = lax.dynamic_slice_in_dim(unit, first, seq_dev, 1)
    solved = jax.scipy.linalg.cho_solve((factor, True), picks)
    return jnp.dot(products, solved, precision=lax.Precision.HIGHEST)


def per_device(sizes, inputs, out_grads, in_proj, out_proj, seq_ids, counts, queries):
    parts, blocks = sizes
    rank = in_proj.shape[1]
    seq_dev = counts.shape[0]
    me = lax.axis_index("tensor")
    place = lax.axis_index("dp")
    first = place * seq_dev
    own = 2 * rank // parts
    rank_of = me.reshape(1)
    kept, sent = project(inputs, out_grads, in_proj, out_proj, rank_of, own)
    asked = pick(queries, rank_of, rank, own)
    weights = token_weights(seq_ids, counts, first)
    came = from_partner(sent, "tensor", parts, 1)
    kept, sent = halve(kept, came, rank_of, own)
    came = from_partner(sent, "tensor", parts, 2)
    message = gradients(weights, kept, came, asked)
    steps = own * own // message.shape[1]
    if blocks > SMALL:
        return finish_long(message, steps, first, seq_dev)
    partial = grams(place.reshape(1), from_all(message, "dp", blocks), steps, seq_dev)
    partial = from_partners(partial, "tensor", parts)
    return solve(partial, blocks * seq_dev, blocks * queries.shape[0], seq_dev)


def solution(mesh):
    in_specs = (
        P(("groups", "dp"), "tensor"),
        P(("groups", "dp"), "tensor"),
        P("tensor", None),
        P("tensor", None),
        P(("groups", "dp")),
        P(("groups", "dp")),
        P(("groups", "dp"), None),
    )
    sizes = (mesh.shape["tensor"], mesh.shape["dp"])
    return jax.shard_map(
        functools.partial(per_device, sizes),
        mesh=mesh,
        in_specs=in_specs,
        out_specs=P("groups", "dp"),
        check_vma=False,
    )
```

```python
import functools

import jax
import jax.numpy as jnp
from jax import lax
from jax.experimental import pallas as pl
from jax.experimental.pallas import tpu as pltpu
from jax.sharding import PartitionSpec as P

damping = 0.5
VMEM_LIMIT = 32 * 1024 * 1024
SMALL = 4
SOURCES = {1: (), 2: ((1, 0),), 4: ((3, 2, 1, 0), (2, 0, 3, 1), (1, 3, 0, 2))}


def token_weights(seq_ids, counts, first):
    local_ids = seq_ids - first
    slots = jnp.arange(counts.shape[0], dtype=jnp.int32)
    member = local_ids[None, :] == slots[:, None]
    starts = jnp.sum((local_ids[None, :] < slots[:, None]).astype(jnp.int32), axis=1)
    offset = jnp.arange(seq_ids.shape[0], dtype=jnp.int32)[None, :] - starts[:, None]
    scale = 1.0 / counts.astype(jnp.float32)
    return jnp.where(member & (offset < counts[:, None]), scale[:, None], 0.0)


def cuts_of(extent, step):
    return [(at, min(step, extent - at)) for at in range(0, extent, step)]


def two_terms(value):
    high = value.astype(jnp.bfloat16)
    low = (value - high.astype(jnp.float32)).astype(jnp.bfloat16)
    return high, low


def dot_nt(left, right):
    rows = left.shape[0]
    lh, ll = two_terms(left)
    rh, rl = two_terms(right)
    mul = functools.partial(
        lax.dot_general,
        dimension_numbers=(((1,), (1,)), ((), ())),
        preferred_element_type=jnp.float32,
    )
    both = mul(jnp.concatenate([lh, ll], axis=0), rh)
    return both[:rows] + (mul(lh, rl) + both[rows:])


def project_kernel(own, rank_ref, x_hbm, g_hbm, wx_hbm, wg_hbm, keep_ref, send_ref, *scratch):
    x_ref, g_ref, wx_ref, wg_ref, wide_ref, sems = scratch
    copies = []

    def fetch(src, dst, index):
        copy = pltpu.make_async_copy(src, dst, sems.at[index])
        copy.start()
        return copy

    g_cuts = cuts_of(g_ref.shape[1], 1024)
    x_cuts = cuts_of(x_ref.shape[0], 1024)
    wg_copy = fetch(wg_hbm, wg_ref, 0)
    index = 2
    g_copies = []
    for at, size in g_cuts:
        columns = pl.ds(at, size)
        g_copies.append(fetch(g_hbm.at[:, columns], g_ref.at[:, columns], index))
        index += 1
    wx_copy = fetch(wx_hbm, wx_ref, 1)
    x_copies = []
    for at, size in x_cuts:
        rows = pl.ds(at, size)
        x_copies.append(fetch(x_hbm.at[rows, :], x_ref.at[rows, :], index))
        index += 1

    def product(copies, terms):
        total = None
        for copy, (left, right, along) in zip(copies, terms):
            copy.wait()
            term = lax.dot_general(
                left(), right(), (((1,), (along,)), ((), ())), preferred_element_type=jnp.float32
            )
            total = term if total is None else total + term
        return total

    def cut(ref, at, size, along):
        return lambda: ref[at : at + size, :] if along == 0 else ref[:, at : at + size]

    wg_copy.wait()
    grads_t = product(
        g_copies, [(cut(g_ref, at, size, 1), cut(wg_ref, at, size, 1), 1) for at, size in g_cuts]
    ).T
    wx_copy.wait()
    wide_ref[...] = product(
        x_copies, [(cut(wx_ref, at, size, 1), cut(x_ref, at, size, 0), 0) for at, size in x_cuts]
    )
    rank = grads_t.shape[0]
    side = rank_ref[0] & 1
    for out, taken in ((keep_ref, side), (send_ref, side ^ 1)):
        out[:rank, :] = grads_t
        out[rank:, :] = wide_ref[pl.ds(pl.multiple_of(taken * own, own), own), :]


def project(inputs, out_grads, in_proj, out_proj, me, own):
    rank = in_proj.shape[1]
    tokens, hidden = inputs.shape
    width = out_grads.shape[1]
    copies = 2 + len(cuts_of(width, 1024)) + len(cuts_of(hidden, 1024))
    arrays = (inputs.T, out_grads, in_proj.T, out_proj.T)
    in_hbm = pl.BlockSpec(memory_space=pltpu.HBM)
    return pl.pallas_call(
        functools.partial(project_kernel, own),
        out_shape=[jax.ShapeDtypeStruct((rank + own, tokens), jnp.float32)] * 2,
        in_specs=[pl.BlockSpec(memory_space=pltpu.SMEM)] + [in_hbm] * len(arrays),
        out_specs=[pl.BlockSpec(memory_space=pltpu.VMEM)] * 2,
        scratch_shapes=[
            pltpu.VMEM((hidden, tokens), jnp.bfloat16),
            pltpu.VMEM((tokens, width), jnp.bfloat16),
            pltpu.VMEM((rank, hidden), jnp.bfloat16),
            pltpu.VMEM((rank, width), jnp.bfloat16),
            pltpu.VMEM((rank, tokens), jnp.float32),
            pltpu.SemaphoreType.DMA((copies,)),
        ],
        compiler_params=pltpu.CompilerParams(vmem_limit_bytes=VMEM_LIMIT),
        name="project",
    )(me, *(pltpu.with_memory_space_constraint(array, pltpu.HBM) for array in arrays))


def halve_kernel(own, rank_ref, kept_ref, came_ref, keep_ref, send_ref, sum_ref):
    sum_ref[...] = kept_ref[...] + came_ref[...]
    place = rank_ref[0] // 2
    for out, taken in ((keep_ref, place), (send_ref, place ^ 1)):
        out[:own, :] = sum_ref[pl.ds(pl.multiple_of(taken * own, own), own), :]
        out[own:, :] = sum_ref[-own:, :]


def halve(kept, came, me, own):
    rows, tokens = kept.shape
    whole = pl.BlockSpec(memory_space=pltpu.VMEM)
    return pl.pallas_call(
        functools.partial(halve_kernel, own),
        out_shape=[jax.ShapeDtypeStruct((2 * own, tokens), jnp.float32)] * 2,
        in_specs=[pl.BlockSpec(memory_space=pltpu.SMEM), whole, whole],
        out_specs=[whole] * 2,
        scratch_shapes=[pltpu.VMEM((rows, tokens), jnp.float32)],
        compiler_params=pltpu.CompilerParams(vmem_limit_bytes=VMEM_LIMIT),
        name="halve",
    )(me, kept, came)


def pick_kernel(rank, own, rank_ref, queries_ref, out_ref):
    lanes = out_ref.shape[1]
    wide = lanes * rank // own
    steps = own * own // lanes
    asked = queries_ref.shape[0]
    me = rank_ref[0]
    start = (me // 2) * (own * rank)
    rows = jnp.concatenate(
        [
            queries_ref[:, pl.ds(pl.multiple_of(start + i * wide, lanes), wide)]
            for i in range(steps)
        ],
        axis=0,
    )
    source = lax.broadcasted_iota(jnp.int32, (wide, lanes), 0)
    place = lax.broadcasted_iota(jnp.int32, (wide, lanes), 1)
    wanted = (place // own) * rank + place % own + (me & 1) * own
    chosen = jnp.where(source == wanted, 1.0, 0.0).astype(jnp.bfloat16)
    high = rows.astype(jnp.bfloat16)
    rest = rows - high.astype(jnp.float32)
    middle = rest.astype(jnp.bfloat16)
    low = (rest - middle.astype(jnp.float32)).astype(jnp.bfloat16)
    terms = [
        jnp.dot(term, chosen, preferred_element_type=jnp.float32) for term in (high, middle, low)
    ]
    out_ref[...] = terms[0] + (terms[1] + terms[2])


def pick(queries, me, rank, own):
    lanes = 128
    rows = queries.shape[0] * own * own // lanes
    whole = pl.BlockSpec(memory_space=pltpu.VMEM)
    return pl.pallas_call(
        functools.partial(pick_kernel, rank, own),
        out_shape=jax.ShapeDtypeStruct((rows, lanes), jnp.float32),
        in_specs=[pl.BlockSpec(memory_space=pltpu.SMEM), whole],
        out_specs=whole,
        compiler_params=pltpu.CompilerParams(vmem_limit_bytes=VMEM_LIMIT),
        name="pick",
    )(me, queries)


def grads_kernel(weights_ref, kept_ref, came_ref, asked_ref, out_ref):
    summed = kept_ref[...] + came_ref[...]
    weights = weights_ref[...]
    own = summed.shape[0] // 2
    group = out_ref.shape[1] // own
    inputs_t = summed[own:, :]
    zero = jnp.zeros_like(inputs_t)
    right = jnp.concatenate(
        [
            jnp.concatenate([inputs_t if j == k else zero for k in range(group)], axis=1)
            for j in range(group)
        ],
        axis=0,
    )
    rows = []
    for i in range(own // group):
        rows.append(
            jnp.concatenate(
                [weights * summed[group * i + j : group * i + j + 1, :] for j in range(group)],
                axis=1,
            )
        )
    left = jnp.concatenate(rows, axis=0)
    count = left.shape[0]
    out_ref[:count, :] = dot_nt(left, right)
    out_ref[count:, :] = asked_ref[...]


def gradients(weights, kept, came, asked):
    lanes = asked.shape[1]
    own = kept.shape[0] // 2
    rows = own * own // lanes * weights.shape[0] + asked.shape[0]
    return pl.pallas_call(
        grads_kernel,
        out_shape=jax.ShapeDtypeStruct((rows, lanes), jnp.float32),
        compiler_params=pltpu.CompilerParams(vmem_limit_bytes=VMEM_LIMIT),
        name="gradients",
    )(weights, kept, came, asked)


def grams_kernel(steps, seqs, me_ref, *refs):
    blocks, out_ref = (refs[-2], *refs[:-2]), refs[-1]
    count = steps * seqs
    asked = (blocks[0].shape[0] - count) // steps
    given = [block[count:, :] for block in blocks]
    ordered = []
    for place in range(len(blocks)):
        chosen = given[0]
        for m, sources in enumerate(SOURCES[len(blocks)]):
            source = sum(jnp.where(me_ref[0] == i, j, 0) for i, j in enumerate(sources))
            chosen = jnp.where(source == place, given[m + 1], chosen)
        ordered.append(chosen)
    lanes = []
    for i in range(steps):
        rows = [block[i * seqs : (i + 1) * seqs, :] for block in blocks]
        rows += [chosen[i * asked : (i + 1) * asked, :] for chosen in ordered]
        lanes.append(jnp.concatenate(rows, axis=0))
    both = jnp.concatenate(lanes, axis=1)
    result = dot_nt(both, both[: len(blocks) * seqs])
    half = result.shape[0] // 2
    out_ref[...] = jnp.concatenate([result[:half, :], result[half:, :]], axis=1)


def grams(me, blocks, steps, seqs):
    asked = blocks[0].shape[0] // steps - seqs
    total = len(blocks) * seqs
    whole = pl.BlockSpec(memory_space=pltpu.VMEM)
    return pl.pallas_call(
        functools.partial(grams_kernel, steps, seqs),
        out_shape=jax.ShapeDtypeStruct(((total + len(blocks) * asked) // 2, 2 * total), jnp.float32),
        in_specs=[pl.BlockSpec(memory_space=pltpu.SMEM)] + [whole] * len(blocks),
        out_specs=whole,
        compiler_params=pltpu.CompilerParams(vmem_limit_bytes=VMEM_LIMIT),
        name="grams",
    )(me, *blocks)


def scales(count):
    first = 2.0 / (1.0 + 1.0 / count)
    off = count / (count + 1.0)
    steps = []
    while off > 1e-7:
        steps.append(2.0 / (2.0 - off * off))
        off = off * off / (2.0 - off * off)
    return first, steps


def solve_kernel(seqs, *refs):
    parts, out_ref = refs[:-1], refs[-1]
    packed = (parts[0][...] + parts[1][...]) + (parts[2][...] + parts[3][...])
    lane = lax.broadcasted_iota(jnp.int32, packed.shape, 1)
    turned = pltpu.roll(packed, seqs, 1)
    both = jnp.concatenate(
        [jnp.where(lane < seqs, packed, turned), jnp.where(lane < seqs, turned, packed)], axis=0
    )
    lane = lax.broadcasted_iota(jnp.int32, both.shape, 1)
    row = lax.broadcasted_iota(jnp.int32, both.shape, 0)
    unit = jnp.where((lane & (seqs - 1)) == row, 1.0, 0.0)
    total = jnp.sum(jnp.where(lane == row, both, 0.0)[:seqs], axis=(0, 1), keepdims=True)
    first, steps = scales(seqs)
    state = first * (both / total + unit * (damping / seqs))
    left_lanes = lane < seqs
    for at, step in enumerate(steps):
        high = state.astype(jnp.bfloat16).astype(jnp.float32)
        low = state - high
        left = jnp.where(left_lanes, high, low).astype(jnp.bfloat16)
        high = high[:seqs].astype(jnp.bfloat16)
        low = low[:seqs].astype(jnp.bfloat16)
        right = jnp.concatenate([high, high, low, low], axis=0)
        if at + 1 == len(steps):
            left, state = left[seqs:], state[seqs:]
        product = jnp.dot(
            jnp.concatenate([left, left], axis=1), right, preferred_element_type=jnp.float32
        )
        state = step * (2.0 * state - product)
    out_ref[...] = state[:, : out_ref.shape[1]]


def solve(parts, seqs, asked, seq_dev):
    return pl.pallas_call(
        functools.partial(solve_kernel, seqs),
        out_shape=jax.ShapeDtypeStruct((asked, seq_dev), jnp.float32),
        compiler_params=pltpu.CompilerParams(vmem_limit_bytes=VMEM_LIMIT),
        name="solve",
    )(*parts)


def from_partner(value, axis, size, m):
    return lax.ppermute(value, axis, [(i, i ^ m) for i in range(size)])


def from_partners(value, axis, size):
    return [from_partner(value, axis, size, m) for m in reversed(range(1, size))] + [value]


def from_all(value, axis, size):
    swaps = [[(source, i) for i, source in enumerate(sources)] for sources in SOURCES[size]]
    return [lax.ppermute(value, axis, swap) for swap in swaps] + [value]


def finish_long(message, steps, first, seq_dev):
    every = lax.all_gather(message, "dp", axis=0)
    lanes = message.shape[1]

    def rows_of(block):
        block = block.reshape(block.shape[0], steps, -1, lanes).transpose(0, 2, 1, 3)
        return block.reshape(-1, steps * lanes)

    count = steps * seq_dev
    grads, asked = rows_of(every[:, :count]), rows_of(every[:, count:])
    both = jnp.einsum(
        "ik,jk->ij", jnp.concatenate([grads, asked], axis=0), grads,
        precision=lax.Precision.HIGHEST,
    )
    both = lax.psum(both, "tensor")
    count = grads.shape[0]
    kernel, products = both[:count], both[count:]
    damp = damping * jnp.trace(kernel) / count
    unit = jnp.eye(count, dtype=jnp.float32)
    factor = jnp.linalg.cholesky(kernel + damp * unit)
    picks = lax.dynamic_slice_in_dim(unit, first, seq_dev, 1)
    solved = jax.scipy.linalg.cho_solve((factor, True), picks)
    return jnp.dot(products, solved, precision=lax.Precision.HIGHEST)


def per_device(sizes, inputs, out_grads, in_proj, out_proj, seq_ids, counts, queries):
    parts, blocks = sizes
    rank = in_proj.shape[1]
    seq_dev = counts.shape[0]
    me = lax.axis_index("tensor")
    place = lax.axis_index("dp")
    first = place * seq_dev
    own = 2 * rank // parts
    rank_of = me.reshape(1)
    kept, sent = project(inputs, out_grads, in_proj, out_proj, rank_of, own)
    asked = pick(queries, rank_of, rank, own)
    weights = token_weights(seq_ids, counts, first)
    came = from_partner(sent, "tensor", parts, 1)
    kept, sent = halve(kept, came, rank_of, own)
    came = from_partner(sent, "tensor", parts, 2)
    message = gradients(weights, kept, came, asked)
    steps = own * own // message.shape[1]
    if blocks > SMALL:
        return finish_long(message, steps, first, seq_dev)
    partial = grams(place.reshape(1), from_all(message, "dp", blocks), steps, seq_dev)
    partial = from_partners(partial, "tensor", parts)
    return solve(partial, blocks * seq_dev, blocks * queries.shape[0], seq_dev)


def solution(mesh):
    in_specs = (
        P(("groups", "dp"), "tensor"),
        P(("groups", "dp"), "tensor"),
        P("tensor", None),
        P("tensor", None),
        P(("groups", "dp")),
        P(("groups", "dp")),
        P(("groups", "dp"), None),
    )
    sizes = (mesh.shape["tensor"], mesh.shape["dp"])
    return jax.shard_map(
        functools.partial(per_device, sizes),
        mesh=mesh,
        in_specs=in_specs,
        out_specs=P("groups", "dp"),
        check_vma=False,
    )
```

```python
import functools

import jax
import jax.numpy as jnp
from jax import lax
from jax.experimental import pallas as pl
from jax.experimental.pallas import tpu as pltpu
from jax.sharding import PartitionSpec as P

damping = 0.5
VMEM_LIMIT = 32 * 1024 * 1024
SMALL = 4
SOURCES = {1: (), 2: ((1, 0),), 4: ((2, 0, 3, 1), (3, 2, 1, 0), (1, 3, 0, 2))}


def token_weights(seq_ids, counts, first):
    local_ids = seq_ids - first
    slots = jnp.arange(counts.shape[0], dtype=jnp.int32)
    member = local_ids[None, :] == slots[:, None]
    starts = jnp.sum((local_ids[None, :] < slots[:, None]).astype(jnp.int32), axis=1)
    offset = jnp.arange(seq_ids.shape[0], dtype=jnp.int32)[None, :] - starts[:, None]
    scale = 1.0 / counts.astype(jnp.float32)
    return jnp.where(member & (offset < counts[:, None]), scale[:, None], 0.0)


def cuts_of(extent, step):
    return [(at, min(step, extent - at)) for at in range(0, extent, step)]


def two_terms(value):
    high = value.astype(jnp.bfloat16)
    low = (value - high.astype(jnp.float32)).astype(jnp.bfloat16)
    return high, low


def dot_nt(left, right):
    rows = left.shape[0]
    lh, ll = two_terms(left)
    rh, rl = two_terms(right)
    mul = functools.partial(
        lax.dot_general,
        dimension_numbers=(((1,), (1,)), ((), ())),
        preferred_element_type=jnp.float32,
    )
    both = mul(jnp.concatenate([lh, ll], axis=0), rh)
    return both[:rows] + (mul(lh, rl) + both[rows:])


def project_kernel(own, rank_ref, x_hbm, g_hbm, wx_hbm, wg_hbm, keep_ref, send_ref, *scratch):
    x_ref, g_ref, wx_ref, wg_ref, wide_ref, sems = scratch
    copies = []

    def fetch(src, dst, index):
        copy = pltpu.make_async_copy(src, dst, sems.at[index])
        copy.start()
        return copy

    g_cuts = cuts_of(g_ref.shape[1], 1024)
    x_cuts = cuts_of(x_ref.shape[0], 1024)
    wg_copy = fetch(wg_hbm, wg_ref, 0)
    index = 2
    g_copies = []
    for at, size in g_cuts:
        columns = pl.ds(at, size)
        g_copies.append(fetch(g_hbm.at[:, columns], g_ref.at[:, columns], index))
        index += 1
    wx_copy = fetch(wx_hbm, wx_ref, 1)
    x_copies = []
    for at, size in x_cuts:
        rows = pl.ds(at, size)
        x_copies.append(fetch(x_hbm.at[rows, :], x_ref.at[rows, :], index))
        index += 1

    def product(copies, terms):
        total = None
        for copy, (left, right, along) in zip(copies, terms):
            copy.wait()
            term = lax.dot_general(
                left(), right(), (((1,), (along,)), ((), ())), preferred_element_type=jnp.float32
            )
            total = term if total is None else total + term
        return total

    def cut(ref, at, size, along):
        return lambda: ref[at : at + size, :] if along == 0 else ref[:, at : at + size]

    wg_copy.wait()
    grads_t = product(
        g_copies, [(cut(g_ref, at, size, 1), cut(wg_ref, at, size, 1), 1) for at, size in g_cuts]
    ).T
    wx_copy.wait()
    wide_ref[...] = product(
        x_copies, [(cut(wx_ref, at, size, 1), cut(x_ref, at, size, 0), 0) for at, size in x_cuts]
    )
    rank = grads_t.shape[0]
    side = rank_ref[0] & 1
    for out, taken in ((keep_ref, side), (send_ref, side ^ 1)):
        out[:rank, :] = grads_t
        out[rank:, :] = wide_ref[pl.ds(pl.multiple_of(taken * own, own), own), :]


def project(inputs, out_grads, in_proj, out_proj, me, own):
    rank = in_proj.shape[1]
    tokens, hidden = inputs.shape
    width = out_grads.shape[1]
    copies = 2 + len(cuts_of(width, 1024)) + len(cuts_of(hidden, 1024))
    arrays = (inputs.T, out_grads, in_proj.T, out_proj.T)
    in_hbm = pl.BlockSpec(memory_space=pltpu.HBM)
    return pl.pallas_call(
        functools.partial(project_kernel, own),
        out_shape=[jax.ShapeDtypeStruct((rank + own, tokens), jnp.float32)] * 2,
        in_specs=[pl.BlockSpec(memory_space=pltpu.SMEM)] + [in_hbm] * len(arrays),
        out_specs=[pl.BlockSpec(memory_space=pltpu.VMEM)] * 2,
        scratch_shapes=[
            pltpu.VMEM((hidden, tokens), jnp.bfloat16),
            pltpu.VMEM((tokens, width), jnp.bfloat16),
            pltpu.VMEM((rank, hidden), jnp.bfloat16),
            pltpu.VMEM((rank, width), jnp.bfloat16),
            pltpu.VMEM((rank, tokens), jnp.float32),
            pltpu.SemaphoreType.DMA((copies,)),
        ],
        compiler_params=pltpu.CompilerParams(vmem_limit_bytes=VMEM_LIMIT),
        name="project",
    )(me, *(pltpu.with_memory_space_constraint(array, pltpu.HBM) for array in arrays))


def halve_kernel(own, rank_ref, kept_ref, came_ref, keep_ref, send_ref, sum_ref):
    sum_ref[...] = kept_ref[...] + came_ref[...]
    place = rank_ref[0] // 2
    for out, taken in ((keep_ref, place), (send_ref, place ^ 1)):
        out[:own, :] = sum_ref[pl.ds(pl.multiple_of(taken * own, own), own), :]
        out[own:, :] = sum_ref[-own:, :]


def halve(kept, came, me, own):
    rows, tokens = kept.shape
    whole = pl.BlockSpec(memory_space=pltpu.VMEM)
    return pl.pallas_call(
        functools.partial(halve_kernel, own),
        out_shape=[jax.ShapeDtypeStruct((2 * own, tokens), jnp.float32)] * 2,
        in_specs=[pl.BlockSpec(memory_space=pltpu.SMEM), whole, whole],
        out_specs=[whole] * 2,
        scratch_shapes=[pltpu.VMEM((rows, tokens), jnp.float32)],
        compiler_params=pltpu.CompilerParams(vmem_limit_bytes=VMEM_LIMIT),
        name="halve",
    )(me, kept, came)


def pick_kernel(rank, own, rank_ref, queries_ref, out_ref):
    lanes = out_ref.shape[1]
    wide = lanes * rank // own
    steps = own * own // lanes
    asked = queries_ref.shape[0]
    me = rank_ref[0]
    start = (me // 2) * (own * rank)
    rows = jnp.concatenate(
        [
            queries_ref[:, pl.ds(pl.multiple_of(start + i * wide, lanes), wide)]
            for i in range(steps)
        ],
        axis=0,
    )
    source = lax.broadcasted_iota(jnp.int32, (wide, lanes), 0)
    place = lax.broadcasted_iota(jnp.int32, (wide, lanes), 1)
    wanted = (place // own) * rank + place % own + (me & 1) * own
    chosen = jnp.where(source == wanted, 1.0, 0.0).astype(jnp.bfloat16)
    high = rows.astype(jnp.bfloat16)
    rest = rows - high.astype(jnp.float32)
    middle = rest.astype(jnp.bfloat16)
    low = (rest - middle.astype(jnp.float32)).astype(jnp.bfloat16)
    terms = [
        jnp.dot(term, chosen, preferred_element_type=jnp.float32) for term in (high, middle, low)
    ]
    out_ref[...] = terms[0] + (terms[1] + terms[2])


def pick(queries, me, rank, own):
    lanes = 128
    rows = queries.shape[0] * own * own // lanes
    whole = pl.BlockSpec(memory_space=pltpu.VMEM)
    return pl.pallas_call(
        functools.partial(pick_kernel, rank, own),
        out_shape=jax.ShapeDtypeStruct((rows, lanes), jnp.float32),
        in_specs=[pl.BlockSpec(memory_space=pltpu.SMEM), whole],
        out_specs=whole,
        compiler_params=pltpu.CompilerParams(vmem_limit_bytes=VMEM_LIMIT),
        name="pick",
    )(me, queries)


def grads_kernel(weights_ref, kept_ref, came_ref, asked_ref, out_ref):
    summed = kept_ref[...] + came_ref[...]
    weights = weights_ref[...]
    own = summed.shape[0] // 2
    group = out_ref.shape[1] // own
    inputs_t = summed[own:, :]
    zero = jnp.zeros_like(inputs_t)
    right = jnp.concatenate(
        [
            jnp.concatenate([inputs_t if j == k else zero for k in range(group)], axis=1)
            for j in range(group)
        ],
        axis=0,
    )
    rows = []
    for i in range(own // group):
        rows.append(
            jnp.concatenate(
                [weights * summed[group * i + j : group * i + j + 1, :] for j in range(group)],
                axis=1,
            )
        )
    left = jnp.concatenate(rows, axis=0)
    count = left.shape[0]
    out_ref[:count, :] = dot_nt(left, right)
    out_ref[count:, :] = asked_ref[...]


def gradients(weights, kept, came, asked):
    lanes = asked.shape[1]
    own = kept.shape[0] // 2
    rows = own * own // lanes * weights.shape[0] + asked.shape[0]
    return pl.pallas_call(
        grads_kernel,
        out_shape=jax.ShapeDtypeStruct((rows, lanes), jnp.float32),
        compiler_params=pltpu.CompilerParams(vmem_limit_bytes=VMEM_LIMIT),
        name="gradients",
    )(weights, kept, came, asked)


def grams_kernel(steps, seqs, me_ref, *refs):
    blocks, out_ref = (refs[-2], *refs[:-2]), refs[-1]
    count = steps * seqs
    asked = (blocks[0].shape[0] - count) // steps
    given = [block[count:, :] for block in blocks]
    ordered = []
    for place in range(len(blocks)):
        chosen = given[0]
        for m, sources in enumerate(SOURCES[len(blocks)]):
            source = sum(jnp.where(me_ref[0] == i, j, 0) for i, j in enumerate(sources))
            chosen = jnp.where(source == place, given[m + 1], chosen)
        ordered.append(chosen)
    lanes = []
    for i in range(steps):
        rows = [block[i * seqs : (i + 1) * seqs, :] for block in blocks]
        rows += [chosen[i * asked : (i + 1) * asked, :] for chosen in ordered]
        lanes.append(jnp.concatenate(rows, axis=0))
    both = jnp.concatenate(lanes, axis=1)
    result = dot_nt(both, both[: len(blocks) * seqs])
    half = result.shape[0] // 2
    out_ref[...] = jnp.concatenate([result[:half, :], result[half:, :]], axis=1)


def grams(me, blocks, steps, seqs):
    asked = blocks[0].shape[0] // steps - seqs
    total = len(blocks) * seqs
    whole = pl.BlockSpec(memory_space=pltpu.VMEM)
    return pl.pallas_call(
        functools.partial(grams_kernel, steps, seqs),
        out_shape=jax.ShapeDtypeStruct(((total + len(blocks) * asked) // 2, 2 * total), jnp.float32),
        in_specs=[pl.BlockSpec(memory_space=pltpu.SMEM)] + [whole] * len(blocks),
        out_specs=whole,
        compiler_params=pltpu.CompilerParams(vmem_limit_bytes=VMEM_LIMIT),
        name="grams",
    )(me, *blocks)


def scales(count):
    first = 2.0 / (1.0 + 1.0 / count)
    off = count / (count + 1.0)
    steps = []
    while off > 1e-7:
        steps.append(2.0 / (2.0 - off * off))
        off = off * off / (2.0 - off * off)
    return first, steps


def solve_kernel(seqs, *refs):
    parts, out_ref = refs[:-1], refs[-1]
    packed = (parts[0][...] + parts[1][...]) + (parts[2][...] + parts[3][...])
    lane = lax.broadcasted_iota(jnp.int32, packed.shape, 1)
    turned = pltpu.roll(packed, seqs, 1)
    both = jnp.concatenate(
        [jnp.where(lane < seqs, packed, turned), jnp.where(lane < seqs, turned, packed)], axis=0
    )
    lane = lax.broadcasted_iota(jnp.int32, both.shape, 1)
    row = lax.broadcasted_iota(jnp.int32, both.shape, 0)
    unit = jnp.where((lane & (seqs - 1)) == row, 1.0, 0.0)
    total = jnp.sum(jnp.where(lane == row, both, 0.0)[:seqs], axis=(0, 1), keepdims=True)
    first, steps = scales(seqs)
    state = first * (both / total + unit * (damping / seqs))
    left_lanes = lane < seqs
    for at, step in enumerate(steps):
        high = state.astype(jnp.bfloat16).astype(jnp.float32)
        low = state - high
        left = jnp.where(left_lanes, high, low).astype(jnp.bfloat16)
        high = high[:seqs].astype(jnp.bfloat16)
        low = low[:seqs].astype(jnp.bfloat16)
        right = jnp.concatenate([high, high, low, low], axis=0)
        if at + 1 == len(steps):
            left, state = left[seqs:], state[seqs:]
        product = jnp.dot(
            jnp.concatenate([left, left], axis=1), right, preferred_element_type=jnp.float32
        )
        state = step * (2.0 * state - product)
    out_ref[...] = state[:, : out_ref.shape[1]]


def solve(parts, seqs, asked, seq_dev):
    return pl.pallas_call(
        functools.partial(solve_kernel, seqs),
        out_shape=jax.ShapeDtypeStruct((asked, seq_dev), jnp.float32),
        compiler_params=pltpu.CompilerParams(vmem_limit_bytes=VMEM_LIMIT),
        name="solve",
    )(*parts)


def from_partner(value, axis, size, m):
    return lax.ppermute(value, axis, [(i, i ^ m) for i in range(size)])


def from_partners(value, axis, size):
    return [from_partner(value, axis, size, m) for m in reversed(range(1, size))] + [value]


def from_all(value, axis, size):
    swaps = [[(source, i) for i, source in enumerate(sources)] for sources in SOURCES[size]]
    return [lax.ppermute(value, axis, swap) for swap in swaps] + [value]


def finish_long(message, steps, first, seq_dev):
    every = lax.all_gather(message, "dp", axis=0)
    lanes = message.shape[1]

    def rows_of(block):
        block = block.reshape(block.shape[0], steps, -1, lanes).transpose(0, 2, 1, 3)
        return block.reshape(-1, steps * lanes)

    count = steps * seq_dev
    grads, asked = rows_of(every[:, :count]), rows_of(every[:, count:])
    both = jnp.einsum(
        "ik,jk->ij", jnp.concatenate([grads, asked], axis=0), grads,
        precision=lax.Precision.HIGHEST,
    )
    both = lax.psum(both, "tensor")
    count = grads.shape[0]
    kernel, products = both[:count], both[count:]
    damp = damping * jnp.trace(kernel) / count
    unit = jnp.eye(count, dtype=jnp.float32)
    factor = jnp.linalg.cholesky(kernel + damp * unit)
    picks = lax.dynamic_slice_in_dim(unit, first, seq_dev, 1)
    solved = jax.scipy.linalg.cho_solve((factor, True), picks)
    return jnp.dot(products, solved, precision=lax.Precision.HIGHEST)


def per_device(sizes, inputs, out_grads, in_proj, out_proj, seq_ids, counts, queries):
    parts, blocks = sizes
    rank = in_proj.shape[1]
    seq_dev = counts.shape[0]
    me = lax.axis_index("tensor")
    place = lax.axis_index("dp")
    first = place * seq_dev
    own = 2 * rank // parts
    rank_of = me.reshape(1)
    kept, sent = project(inputs, out_grads, in_proj, out_proj, rank_of, own)
    asked = pick(queries, rank_of, rank, own)
    weights = token_weights(seq_ids, counts, first)
    came = from_partner(sent, "tensor", parts, 1)
    kept, sent = halve(kept, came, rank_of, own)
    came = from_partner(sent, "tensor", parts, 2)
    message = gradients(weights, kept, came, asked)
    steps = own * own // message.shape[1]
    if blocks > SMALL:
        return finish_long(message, steps, first, seq_dev)
    partial = grams(place.reshape(1), from_all(message, "dp", blocks), steps, seq_dev)
    partial = from_partners(partial, "tensor", parts)
    return solve(partial, blocks * seq_dev, blocks * queries.shape[0], seq_dev)


def solution(mesh):
    in_specs = (
        P(("groups", "dp"), "tensor"),
        P(("groups", "dp"), "tensor"),
        P("tensor", None),
        P("tensor", None),
        P(("groups", "dp")),
        P(("groups", "dp")),
        P(("groups", "dp"), None),
    )
    sizes = (mesh.shape["tensor"], mesh.shape["dp"])
    return jax.shard_map(
        functools.partial(per_device, sizes),
        mesh=mesh,
        in_specs=in_specs,
        out_specs=P("groups", "dp"),
        check_vma=False,
    )
```

```python
import functools

import jax
import jax.numpy as jnp
from jax import lax
from jax.experimental import pallas as pl
from jax.experimental.pallas import tpu as pltpu
from jax.sharding import PartitionSpec as P

damping = 0.5
VMEM_LIMIT = 32 * 1024 * 1024
SMALL = 4
SOURCES = {1: (), 2: ((1, 0),), 4: ((2, 0, 3, 1), (3, 2, 1, 0), (1, 3, 0, 2))}


def token_weights(seq_ids, counts, first):
    local_ids = seq_ids - first
    slots = jnp.arange(counts.shape[0], dtype=jnp.int32)
    member = local_ids[None, :] == slots[:, None]
    starts = jnp.sum((local_ids[None, :] < slots[:, None]).astype(jnp.int32), axis=1)
    offset = jnp.arange(seq_ids.shape[0], dtype=jnp.int32)[None, :] - starts[:, None]
    scale = 1.0 / counts.astype(jnp.float32)
    return jnp.where(member & (offset < counts[:, None]), scale[:, None], 0.0)


def cuts_of(extent, step):
    return [(at, min(step, extent - at)) for at in range(0, extent, step)]


def two_terms(value):
    high = value.astype(jnp.bfloat16)
    low = (value - high.astype(jnp.float32)).astype(jnp.bfloat16)
    return high, low


def dot_nt(left, right):
    rows = left.shape[0]
    lh, ll = two_terms(left)
    rh, rl = two_terms(right)
    mul = functools.partial(
        lax.dot_general,
        dimension_numbers=(((1,), (1,)), ((), ())),
        preferred_element_type=jnp.float32,
    )
    both = mul(jnp.concatenate([lh, ll], axis=0), rh)
    return both[:rows] + (mul(lh, rl) + both[rows:])


def project_kernel(own, rank_ref, x_hbm, g_hbm, wx_hbm, wg_hbm, keep_ref, send_ref, *scratch):
    x_ref, g_ref, wx_ref, wg_ref, wide_ref, sems = scratch
    copies = []

    def fetch(src, dst, index):
        copy = pltpu.make_async_copy(src, dst, sems.at[index])
        copy.start()
        return copy

    g_cuts = cuts_of(g_ref.shape[1], 1024)
    x_cuts = cuts_of(x_ref.shape[0], 1024)
    wg_copy = fetch(wg_hbm, wg_ref, 0)
    index = 2
    g_copies = []
    for at, size in g_cuts:
        columns = pl.ds(at, size)
        g_copies.append(fetch(g_hbm.at[:, columns], g_ref.at[:, columns], index))
        index += 1
    wx_copy = fetch(wx_hbm, wx_ref, 1)
    x_copies = []
    for at, size in x_cuts:
        rows = pl.ds(at, size)
        x_copies.append(fetch(x_hbm.at[rows, :], x_ref.at[rows, :], index))
        index += 1

    def product(copies, terms):
        total = None
        for copy, (left, right, along) in zip(copies, terms):
            copy.wait()
            term = lax.dot_general(
                left(), right(), (((1,), (along,)), ((), ())), preferred_element_type=jnp.float32
            )
            total = term if total is None else total + term
        return total

    def cut(ref, at, size, along):
        return lambda: ref[at : at + size, :] if along == 0 else ref[:, at : at + size]

    wg_copy.wait()
    grads_t = product(
        g_copies, [(cut(g_ref, at, size, 1), cut(wg_ref, at, size, 1), 1) for at, size in g_cuts]
    ).T
    wx_copy.wait()
    wide_ref[...] = product(
        x_copies, [(cut(wx_ref, at, size, 1), cut(x_ref, at, size, 0), 0) for at, size in x_cuts]
    )
    rank = grads_t.shape[0]
    side = rank_ref[0] & 1
    for out, taken in ((keep_ref, side), (send_ref, side ^ 1)):
        out[:rank, :] = grads_t
        out[rank:, :] = wide_ref[pl.ds(pl.multiple_of(taken * own, own), own), :]


def project(inputs, out_grads, in_proj, out_proj, me, own):
    rank = in_proj.shape[1]
    tokens, hidden = inputs.shape
    width = out_grads.shape[1]
    copies = 2 + len(cuts_of(width, 1024)) + len(cuts_of(hidden, 1024))
    arrays = (inputs.T, out_grads, in_proj.T, out_proj.T)
    in_hbm = pl.BlockSpec(memory_space=pltpu.HBM)
    return pl.pallas_call(
        functools.partial(project_kernel, own),
        out_shape=[jax.ShapeDtypeStruct((rank + own, tokens), jnp.float32)] * 2,
        in_specs=[pl.BlockSpec(memory_space=pltpu.SMEM)] + [in_hbm] * len(arrays),
        out_specs=[pl.BlockSpec(memory_space=pltpu.VMEM)] * 2,
        scratch_shapes=[
            pltpu.VMEM((hidden, tokens), jnp.bfloat16),
            pltpu.VMEM((tokens, width), jnp.bfloat16),
            pltpu.VMEM((rank, hidden), jnp.bfloat16),
            pltpu.VMEM((rank, width), jnp.bfloat16),
            pltpu.VMEM((rank, tokens), jnp.float32),
            pltpu.SemaphoreType.DMA((copies,)),
        ],
        compiler_params=pltpu.CompilerParams(vmem_limit_bytes=VMEM_LIMIT),
        name="project",
    )(me, *(pltpu.with_memory_space_constraint(array, pltpu.HBM) for array in arrays))


def halve_kernel(own, rank_ref, kept_ref, came_ref, keep_ref, send_ref, sum_ref):
    sum_ref[...] = kept_ref[...] + came_ref[...]
    place = rank_ref[0] // 2
    for out, taken in ((keep_ref, place), (send_ref, place ^ 1)):
        out[:own, :] = sum_ref[pl.ds(pl.multiple_of(taken * own, own), own), :]
        out[own:, :] = sum_ref[-own:, :]


def halve(kept, came, me, own):
    rows, tokens = kept.shape
    whole = pl.BlockSpec(memory_space=pltpu.VMEM)
    return pl.pallas_call(
        functools.partial(halve_kernel, own),
        out_shape=[jax.ShapeDtypeStruct((2 * own, tokens), jnp.float32)] * 2,
        in_specs=[pl.BlockSpec(memory_space=pltpu.SMEM), whole, whole],
        out_specs=[whole] * 2,
        scratch_shapes=[pltpu.VMEM((rows, tokens), jnp.float32)],
        compiler_params=pltpu.CompilerParams(vmem_limit_bytes=VMEM_LIMIT),
        name="halve",
    )(me, kept, came)


def pick_kernel(rank, own, rank_ref, queries_ref, out_ref):
    lanes = out_ref.shape[1]
    wide = lanes * rank // own
    steps = own * own // lanes
    asked = queries_ref.shape[0]
    me = rank_ref[0]
    start = (me // 2) * (own * rank)
    rows = jnp.concatenate(
        [
            queries_ref[:, pl.ds(pl.multiple_of(start + i * wide, lanes), wide)]
            for i in range(steps)
        ],
        axis=0,
    )
    source = lax.broadcasted_iota(jnp.int32, (wide, lanes), 0)
    place = lax.broadcasted_iota(jnp.int32, (wide, lanes), 1)
    wanted = (place // own) * rank + place % own + (me & 1) * own
    chosen = jnp.where(source == wanted, 1.0, 0.0).astype(jnp.bfloat16)
    high = rows.astype(jnp.bfloat16)
    rest = rows - high.astype(jnp.float32)
    middle = rest.astype(jnp.bfloat16)
    low = (rest - middle.astype(jnp.float32)).astype(jnp.bfloat16)
    terms = [
        jnp.dot(term, chosen, preferred_element_type=jnp.float32) for term in (high, middle, low)
    ]
    out_ref[...] = terms[0] + (terms[1] + terms[2])


def pick(queries, me, rank, own):
    lanes = 128
    rows = queries.shape[0] * own * own // lanes
    whole = pl.BlockSpec(memory_space=pltpu.VMEM)
    return pl.pallas_call(
        functools.partial(pick_kernel, rank, own),
        out_shape=jax.ShapeDtypeStruct((rows, lanes), jnp.float32),
        in_specs=[pl.BlockSpec(memory_space=pltpu.SMEM), whole],
        out_specs=whole,
        compiler_params=pltpu.CompilerParams(vmem_limit_bytes=VMEM_LIMIT),
        name="pick",
    )(me, queries)


def grads_kernel(weights_ref, kept_ref, came_ref, asked_ref, out_ref):
    summed = kept_ref[...] + came_ref[...]
    weights = weights_ref[...]
    own = summed.shape[0] // 2
    group = out_ref.shape[1] // own
    inputs_t = summed[own:, :]
    zero = jnp.zeros_like(inputs_t)
    right = jnp.concatenate(
        [
            jnp.concatenate([inputs_t if j == k else zero for k in range(group)], axis=1)
            for j in range(group)
        ],
        axis=0,
    )
    rows = []
    for i in range(own // group):
        rows.append(
            jnp.concatenate(
                [weights * summed[group * i + j : group * i + j + 1, :] for j in range(group)],
                axis=1,
            )
        )
    left = jnp.concatenate(rows, axis=0)
    count = left.shape[0]
    out_ref[:count, :] = dot_nt(left, right)
    out_ref[count:, :] = asked_ref[...]


def gradients(weights, kept, came, asked):
    lanes = asked.shape[1]
    own = kept.shape[0] // 2
    rows = own * own // lanes * weights.shape[0] + asked.shape[0]
    return pl.pallas_call(
        grads_kernel,
        out_shape=jax.ShapeDtypeStruct((rows, lanes), jnp.float32),
        compiler_params=pltpu.CompilerParams(vmem_limit_bytes=VMEM_LIMIT),
        name="gradients",
    )(weights, kept, came, asked)


def grams_kernel(steps, seqs, me_ref, *refs):
    blocks, out_ref = (refs[0], *refs[-3:0:-1]), refs[-1]
    count = steps * seqs
    asked = (blocks[0].shape[0] - count) // steps
    given = [block[count:, :] for block in blocks]
    ordered = []
    for place in range(len(blocks)):
        chosen = given[0]
        for m, sources in enumerate(SOURCES[len(blocks)]):
            source = sum(jnp.where(me_ref[0] == i, j, 0) for i, j in enumerate(sources))
            chosen = jnp.where(source == place, given[m + 1], chosen)
        ordered.append(chosen)
    lanes = []
    for i in range(steps):
        rows = [block[i * seqs : (i + 1) * seqs, :] for block in blocks]
        rows += [chosen[i * asked : (i + 1) * asked, :] for chosen in ordered]
        lanes.append(jnp.concatenate(rows, axis=0))
    both = jnp.concatenate(lanes, axis=1)
    result = dot_nt(both, both[: len(blocks) * seqs])
    half = result.shape[0] // 2
    out_ref[...] = jnp.concatenate([result[:half, :], result[half:, :]], axis=1)


def grams(me, level, blocks, steps, seqs):
    asked = blocks[0].shape[0] // steps - seqs
    total = len(blocks) * seqs
    whole = pl.BlockSpec(memory_space=pltpu.VMEM)
    return pl.pallas_call(
        functools.partial(grams_kernel, steps, seqs),
        out_shape=jax.ShapeDtypeStruct(((total + len(blocks) * asked) // 2, 2 * total), jnp.float32),
        in_specs=[pl.BlockSpec(memory_space=pltpu.SMEM)] + [whole] * (len(blocks) + 1),
        out_specs=whole,
        compiler_params=pltpu.CompilerParams(vmem_limit_bytes=VMEM_LIMIT),
        name="grams",
    )(me, *blocks[::-1], level)


def scales(count):
    first = 2.0 / (1.0 + 1.0 / count)
    off = count / (count + 1.0)
    steps = []
    while off > 1e-7:
        steps.append(2.0 / (2.0 - off * off))
        off = off * off / (2.0 - off * off)
    return first, steps


def solve_kernel(seqs, *refs):
    parts, out_ref = refs[:-1], refs[-1]
    packed = (parts[0][...] + parts[1][...]) + (parts[2][...] + parts[3][...])
    lane = lax.broadcasted_iota(jnp.int32, packed.shape, 1)
    turned = pltpu.roll(packed, seqs, 1)
    both = jnp.concatenate(
        [jnp.where(lane < seqs, packed, turned), jnp.where(lane < seqs, turned, packed)], axis=0
    )
    lane = lax.broadcasted_iota(jnp.int32, both.shape, 1)
    row = lax.broadcasted_iota(jnp.int32, both.shape, 0)
    unit = jnp.where((lane & (seqs - 1)) == row, 1.0, 0.0)
    total = jnp.sum(jnp.where(lane == row, both, 0.0)[:seqs], axis=(0, 1), keepdims=True)
    first, steps = scales(seqs)
    state = first * (both / total + unit * (damping / seqs))
    left_lanes = lane < seqs
    for at, step in enumerate(steps):
        high = state.astype(jnp.bfloat16).astype(jnp.float32)
        low = state - high
        left = jnp.where(left_lanes, high, low).astype(jnp.bfloat16)
        high = high[:seqs].astype(jnp.bfloat16)
        low = low[:seqs].astype(jnp.bfloat16)
        right = jnp.concatenate([high, high, low, low], axis=0)
        if at + 1 == len(steps):
            left, state = left[seqs:], state[seqs:]
        product = jnp.dot(
            jnp.concatenate([left, left], axis=1), right, preferred_element_type=jnp.float32
        )
        state = step * (2.0 * state - product)
    out_ref[...] = state[:, : out_ref.shape[1]]


def solve(parts, seqs, asked, seq_dev):
    return pl.pallas_call(
        functools.partial(solve_kernel, seqs),
        out_shape=jax.ShapeDtypeStruct((asked, seq_dev), jnp.float32),
        compiler_params=pltpu.CompilerParams(vmem_limit_bytes=VMEM_LIMIT),
        name="solve",
    )(*parts)


def from_partner(value, axis, size, m):
    return lax.ppermute(value, axis, [(i, i ^ m) for i in range(size)])


def from_partners(value, axis, size):
    return [from_partner(value, axis, size, m) for m in reversed(range(1, size))] + [value]


def from_all(value, axis, size):
    swaps = [[(source, i) for i, source in enumerate(sources)] for sources in SOURCES[size]]
    return [lax.ppermute(value, axis, swap) for swap in swaps] + [value]


def finish_long(message, steps, first, seq_dev):
    every = lax.all_gather(message, "dp", axis=0)
    lanes = message.shape[1]

    def rows_of(block):
        block = block.reshape(block.shape[0], steps, -1, lanes).transpose(0, 2, 1, 3)
        return block.reshape(-1, steps * lanes)

    count = steps * seq_dev
    grads, asked = rows_of(every[:, :count]), rows_of(every[:, count:])
    both = jnp.einsum(
        "ik,jk->ij", jnp.concatenate([grads, asked], axis=0), grads,
        precision=lax.Precision.HIGHEST,
    )
    both = lax.psum(both, "tensor")
    count = grads.shape[0]
    kernel, products = both[:count], both[count:]
    damp = damping * jnp.trace(kernel) / count
    unit = jnp.eye(count, dtype=jnp.float32)
    factor = jnp.linalg.cholesky(kernel + damp * unit)
    picks = lax.dynamic_slice_in_dim(unit, first, seq_dev, 1)
    solved = jax.scipy.linalg.cho_solve((factor, True), picks)
    return jnp.dot(products, solved, precision=lax.Precision.HIGHEST)


def per_device(sizes, inputs, out_grads, in_proj, out_proj, seq_ids, counts, queries):
    parts, blocks = sizes
    rank = in_proj.shape[1]
    seq_dev = counts.shape[0]
    me = lax.axis_index("tensor")
    place = lax.axis_index("dp")
    first = place * seq_dev
    own = 2 * rank // parts
    rank_of = me.reshape(1)
    kept, sent = project(inputs, out_grads, in_proj, out_proj, rank_of, own)
    asked = pick(queries, rank_of, rank, own)
    weights = token_weights(seq_ids, counts, first)
    came = from_partner(sent, "tensor", parts, 1)
    kept, sent = halve(kept, came, rank_of, own)
    came = from_partner(sent, "tensor", parts, 2)
    message = gradients(weights, kept, came, asked)
    steps = own * own // message.shape[1]
    if blocks > SMALL:
        return finish_long(message, steps, first, seq_dev)
    level = from_partner(message, "tensor", parts, 1)
    partial = grams(place.reshape(1), level, from_all(message, "dp", blocks), steps, seq_dev)
    partial = from_partners(partial, "tensor", parts)[::-1]
    return solve(partial, blocks * seq_dev, blocks * queries.shape[0], seq_dev)


def solution(mesh):
    in_specs = (
        P(("groups", "dp"), "tensor"),
        P(("groups", "dp"), "tensor"),
        P("tensor", None),
        P("tensor", None),
        P(("groups", "dp")),
        P(("groups", "dp")),
        P(("groups", "dp"), None),
    )
    sizes = (mesh.shape["tensor"], mesh.shape["dp"])
    return jax.shard_map(
        functools.partial(per_device, sizes),
        mesh=mesh,
        in_specs=in_specs,
        out_specs=P("groups", "dp"),
        check_vma=False,
    )
```

```python
import functools

import jax
import jax.numpy as jnp
from jax import lax
from jax.experimental import pallas as pl
from jax.experimental.pallas import tpu as pltpu
from jax.sharding import PartitionSpec as P

damping = 0.5
VMEM_LIMIT = 32 * 1024 * 1024
SMALL = 4
SOURCES = {1: (), 2: ((1, 0),), 4: ((2, 0, 3, 1), (1, 3, 0, 2), (3, 2, 1, 0))}


def token_weights(seq_ids, counts, first):
    local_ids = seq_ids - first
    slots = jnp.arange(counts.shape[0], dtype=jnp.int32)
    member = local_ids[None, :] == slots[:, None]
    starts = jnp.sum((local_ids[None, :] < slots[:, None]).astype(jnp.int32), axis=1)
    offset = jnp.arange(seq_ids.shape[0], dtype=jnp.int32)[None, :] - starts[:, None]
    scale = 1.0 / counts.astype(jnp.float32)
    return jnp.where(member & (offset < counts[:, None]), scale[:, None], 0.0)


def cuts_of(extent, step):
    return [(at, min(step, extent - at)) for at in range(0, extent, step)]


def two_terms(value):
    high = value.astype(jnp.bfloat16)
    low = (value - high.astype(jnp.float32)).astype(jnp.bfloat16)
    return high, low


def dot_nt(left, right):
    rows = left.shape[0]
    lh, ll = two_terms(left)
    rh, rl = two_terms(right)
    mul = functools.partial(
        lax.dot_general,
        dimension_numbers=(((1,), (1,)), ((), ())),
        preferred_element_type=jnp.float32,
    )
    both = mul(jnp.concatenate([lh, ll], axis=0), rh)
    return both[:rows] + (mul(lh, rl) + both[rows:])


def project_kernel(own, rank_ref, x_hbm, g_hbm, wx_hbm, wg_hbm, keep_ref, send_ref, *scratch):
    x_ref, g_ref, wx_ref, wg_ref, wide_ref, sems = scratch
    copies = []

    def fetch(src, dst, index):
        copy = pltpu.make_async_copy(src, dst, sems.at[index])
        copy.start()
        return copy

    g_cuts = cuts_of(g_ref.shape[1], 1024)
    x_cuts = cuts_of(x_ref.shape[0], 1024)
    wg_copy = fetch(wg_hbm, wg_ref, 0)
    index = 2
    g_copies = []
    for at, size in g_cuts:
        columns = pl.ds(at, size)
        g_copies.append(fetch(g_hbm.at[:, columns], g_ref.at[:, columns], index))
        index += 1
    wx_copy = fetch(wx_hbm, wx_ref, 1)
    x_copies = []
    for at, size in x_cuts:
        rows = pl.ds(at, size)
        x_copies.append(fetch(x_hbm.at[rows, :], x_ref.at[rows, :], index))
        index += 1

    def product(copies, terms):
        total = None
        for copy, (left, right, along) in zip(copies, terms):
            copy.wait()
            term = lax.dot_general(
                left(), right(), (((1,), (along,)), ((), ())), preferred_element_type=jnp.float32
            )
            total = term if total is None else total + term
        return total

    def cut(ref, at, size, along):
        return lambda: ref[at : at + size, :] if along == 0 else ref[:, at : at + size]

    wg_copy.wait()
    grads_t = product(
        g_copies, [(cut(g_ref, at, size, 1), cut(wg_ref, at, size, 1), 1) for at, size in g_cuts]
    ).T
    wx_copy.wait()
    wide_ref[...] = product(
        x_copies, [(cut(wx_ref, at, size, 1), cut(x_ref, at, size, 0), 0) for at, size in x_cuts]
    )
    rank = grads_t.shape[0]
    side = rank_ref[0] & 1
    for out, taken in ((keep_ref, side), (send_ref, side ^ 1)):
        out[:rank, :] = grads_t
        out[rank:, :] = wide_ref[pl.ds(pl.multiple_of(taken * own, own), own), :]


def project(inputs, out_grads, in_proj, out_proj, me, own):
    rank = in_proj.shape[1]
    tokens, hidden = inputs.shape
    width = out_grads.shape[1]
    copies = 2 + len(cuts_of(width, 1024)) + len(cuts_of(hidden, 1024))
    arrays = (inputs.T, out_grads, in_proj.T, out_proj.T)
    in_hbm = pl.BlockSpec(memory_space=pltpu.HBM)
    return pl.pallas_call(
        functools.partial(project_kernel, own),
        out_shape=[jax.ShapeDtypeStruct((rank + own, tokens), jnp.float32)] * 2,
        in_specs=[pl.BlockSpec(memory_space=pltpu.SMEM)] + [in_hbm] * len(arrays),
        out_specs=[pl.BlockSpec(memory_space=pltpu.VMEM)] * 2,
        scratch_shapes=[
            pltpu.VMEM((hidden, tokens), jnp.bfloat16),
            pltpu.VMEM((tokens, width), jnp.bfloat16),
            pltpu.VMEM((rank, hidden), jnp.bfloat16),
            pltpu.VMEM((rank, width), jnp.bfloat16),
            pltpu.VMEM((rank, tokens), jnp.float32),
            pltpu.SemaphoreType.DMA((copies,)),
        ],
        compiler_params=pltpu.CompilerParams(vmem_limit_bytes=VMEM_LIMIT),
        name="project",
    )(me, *(pltpu.with_memory_space_constraint(array, pltpu.HBM) for array in arrays))


def halve_kernel(own, rank_ref, kept_ref, came_ref, keep_ref, send_ref, sum_ref):
    sum_ref[...] = kept_ref[...] + came_ref[...]
    place = rank_ref[0] // 2
    for out, taken in ((keep_ref, place), (send_ref, place ^ 1)):
        out[:own, :] = sum_ref[pl.ds(pl.multiple_of(taken * own, own), own), :]
        out[own:, :] = sum_ref[-own:, :]


def halve(kept, came, me, own):
    rows, tokens = kept.shape
    whole = pl.BlockSpec(memory_space=pltpu.VMEM)
    return pl.pallas_call(
        functools.partial(halve_kernel, own),
        out_shape=[jax.ShapeDtypeStruct((2 * own, tokens), jnp.float32)] * 2,
        in_specs=[pl.BlockSpec(memory_space=pltpu.SMEM), whole, whole],
        out_specs=[whole] * 2,
        scratch_shapes=[pltpu.VMEM((rows, tokens), jnp.float32)],
        compiler_params=pltpu.CompilerParams(vmem_limit_bytes=VMEM_LIMIT),
        name="halve",
    )(me, kept, came)


def pick_kernel(rank, own, rank_ref, queries_ref, out_ref):
    lanes = out_ref.shape[1]
    wide = lanes * rank // own
    steps = own * own // lanes
    asked = queries_ref.shape[0]
    me = rank_ref[0]
    start = (me // 2) * (own * rank)
    rows = jnp.concatenate(
        [
            queries_ref[:, pl.ds(pl.multiple_of(start + i * wide, lanes), wide)]
            for i in range(steps)
        ],
        axis=0,
    )
    source = lax.broadcasted_iota(jnp.int32, (wide, lanes), 0)
    place = lax.broadcasted_iota(jnp.int32, (wide, lanes), 1)
    wanted = (place // own) * rank + place % own + (me & 1) * own
    chosen = jnp.where(source == wanted, 1.0, 0.0).astype(jnp.bfloat16)
    high = rows.astype(jnp.bfloat16)
    rest = rows - high.astype(jnp.float32)
    middle = rest.astype(jnp.bfloat16)
    low = (rest - middle.astype(jnp.float32)).astype(jnp.bfloat16)
    terms = [
        jnp.dot(term, chosen, preferred_element_type=jnp.float32) for term in (high, middle, low)
    ]
    out_ref[...] = terms[0] + (terms[1] + terms[2])


def pick(queries, me, rank, own):
    lanes = 128
    rows = queries.shape[0] * own * own // lanes
    whole = pl.BlockSpec(memory_space=pltpu.VMEM)
    return pl.pallas_call(
        functools.partial(pick_kernel, rank, own),
        out_shape=jax.ShapeDtypeStruct((rows, lanes), jnp.float32),
        in_specs=[pl.BlockSpec(memory_space=pltpu.SMEM), whole],
        out_specs=whole,
        compiler_params=pltpu.CompilerParams(vmem_limit_bytes=VMEM_LIMIT),
        name="pick",
    )(me, queries)


def grads_kernel(weights_ref, kept_ref, came_ref, asked_ref, out_ref):
    summed = kept_ref[...] + came_ref[...]
    weights = weights_ref[...]
    own = summed.shape[0] // 2
    group = out_ref.shape[1] // own
    inputs_t = summed[own:, :]
    zero = jnp.zeros_like(inputs_t)
    right = jnp.concatenate(
        [
            jnp.concatenate([inputs_t if j == k else zero for k in range(group)], axis=1)
            for j in range(group)
        ],
        axis=0,
    )
    rows = []
    for i in range(own // group):
        rows.append(
            jnp.concatenate(
                [weights * summed[group * i + j : group * i + j + 1, :] for j in range(group)],
                axis=1,
            )
        )
    left = jnp.concatenate(rows, axis=0)
    count = left.shape[0]
    out_ref[:count, :] = dot_nt(left, right)
    out_ref[count:, :] = asked_ref[...]


def gradients(weights, kept, came, asked):
    lanes = asked.shape[1]
    own = kept.shape[0] // 2
    rows = own * own // lanes * weights.shape[0] + asked.shape[0]
    return pl.pallas_call(
        grads_kernel,
        out_shape=jax.ShapeDtypeStruct((rows, lanes), jnp.float32),
        compiler_params=pltpu.CompilerParams(vmem_limit_bytes=VMEM_LIMIT),
        name="gradients",
    )(weights, kept, came, asked)


def grams_kernel(steps, seqs, me_ref, *refs):
    blocks, out_ref = (refs[-2], *refs[:-2]), refs[-1]
    count = steps * seqs
    asked = (blocks[0].shape[0] - count) // steps
    given = [block[count:, :] for block in blocks]
    ordered = []
    for place in range(len(blocks)):
        chosen = given[0]
        for m, sources in enumerate(SOURCES[len(blocks)]):
            source = sum(jnp.where(me_ref[0] == i, j, 0) for i, j in enumerate(sources))
            chosen = jnp.where(source == place, given[m + 1], chosen)
        ordered.append(chosen)
    lanes = []
    for i in range(steps):
        rows = [block[i * seqs : (i + 1) * seqs, :] for block in blocks]
        rows += [chosen[i * asked : (i + 1) * asked, :] for chosen in ordered]
        lanes.append(jnp.concatenate(rows, axis=0))
    both = jnp.concatenate(lanes, axis=1)
    result = dot_nt(both, both[: len(blocks) * seqs])
    half = result.shape[0] // 2
    out_ref[...] = jnp.concatenate([result[:half, :], result[half:, :]], axis=1)


def grams(me, blocks, steps, seqs):
    asked = blocks[0].shape[0] // steps - seqs
    total = len(blocks) * seqs
    whole = pl.BlockSpec(memory_space=pltpu.VMEM)
    return pl.pallas_call(
        functools.partial(grams_kernel, steps, seqs),
        out_shape=jax.ShapeDtypeStruct(((total + len(blocks) * asked) // 2, 2 * total), jnp.float32),
        in_specs=[pl.BlockSpec(memory_space=pltpu.SMEM)] + [whole] * len(blocks),
        out_specs=whole,
        compiler_params=pltpu.CompilerParams(vmem_limit_bytes=VMEM_LIMIT),
        name="grams",
    )(me, *blocks)


def scales(count):
    first = 2.0 / (1.0 + 1.0 / count)
    off = count / (count + 1.0)
    steps = []
    while off > 1e-7:
        steps.append(2.0 / (2.0 - off * off))
        off = off * off / (2.0 - off * off)
    return first, steps


def solve_kernel(seqs, *refs):
    parts, out_ref = refs[:-1], refs[-1]
    packed = (parts[0][...] + parts[1][...]) + (parts[2][...] + parts[3][...])
    lane = lax.broadcasted_iota(jnp.int32, packed.shape, 1)
    turned = pltpu.roll(packed, seqs, 1)
    both = jnp.concatenate(
        [jnp.where(lane < seqs, packed, turned), jnp.where(lane < seqs, turned, packed)], axis=0
    )
    lane = lax.broadcasted_iota(jnp.int32, both.shape, 1)
    row = lax.broadcasted_iota(jnp.int32, both.shape, 0)
    unit = jnp.where((lane & (seqs - 1)) == row, 1.0, 0.0)
    total = jnp.sum(jnp.where(lane == row, both, 0.0)[:seqs], axis=(0, 1), keepdims=True)
    first, steps = scales(seqs)
    state = first * (both / total + unit * (damping / seqs))
    left_lanes = lane < seqs
    for at, step in enumerate(steps):
        high = state.astype(jnp.bfloat16).astype(jnp.float32)
        low = state - high
        left = jnp.where(left_lanes, high, low).astype(jnp.bfloat16)
        high = high[:seqs].astype(jnp.bfloat16)
        low = low[:seqs].astype(jnp.bfloat16)
        right = jnp.concatenate([high, high, low, low], axis=0)
        if at + 1 == len(steps):
            left, state = left[seqs:], state[seqs:]
        product = jnp.dot(
            jnp.concatenate([left, left], axis=1), right, preferred_element_type=jnp.float32
        )
        state = step * (2.0 * state - product)
    out_ref[...] = state[:, : out_ref.shape[1]]


def solve(parts, seqs, asked, seq_dev):
    return pl.pallas_call(
        functools.partial(solve_kernel, seqs),
        out_shape=jax.ShapeDtypeStruct((asked, seq_dev), jnp.float32),
        compiler_params=pltpu.CompilerParams(vmem_limit_bytes=VMEM_LIMIT),
        name="solve",
    )(*parts)


def from_partner(value, axis, size, m):
    return lax.ppermute(value, axis, [(i, i ^ m) for i in range(size)])


def from_partners(value, axis, size):
    return [from_partner(value, axis, size, m) for m in reversed(range(1, size))] + [value]


def from_all(value, axis, size):
    swaps = [[(source, i) for i, source in enumerate(sources)] for sources in SOURCES[size]]
    return [lax.ppermute(value, axis, swap) for swap in swaps] + [value]


def finish_long(message, steps, first, seq_dev):
    every = lax.all_gather(message, "dp", axis=0)
    lanes = message.shape[1]

    def rows_of(block):
        block = block.reshape(block.shape[0], steps, -1, lanes).transpose(0, 2, 1, 3)
        return block.reshape(-1, steps * lanes)

    count = steps * seq_dev
    grads, asked = rows_of(every[:, :count]), rows_of(every[:, count:])
    both = jnp.einsum(
        "ik,jk->ij", jnp.concatenate([grads, asked], axis=0), grads,
        precision=lax.Precision.HIGHEST,
    )
    both = lax.psum(both, "tensor")
    count = grads.shape[0]
    kernel, products = both[:count], both[count:]
    damp = damping * jnp.trace(kernel) / count
    unit = jnp.eye(count, dtype=jnp.float32)
    factor = jnp.linalg.cholesky(kernel + damp * unit)
    picks = lax.dynamic_slice_in_dim(unit, first, seq_dev, 1)
    solved = jax.scipy.linalg.cho_solve((factor, True), picks)
    return jnp.dot(products, solved, precision=lax.Precision.HIGHEST)


def per_device(sizes, inputs, out_grads, in_proj, out_proj, seq_ids, counts, queries):
    parts, blocks = sizes
    rank = in_proj.shape[1]
    seq_dev = counts.shape[0]
    me = lax.axis_index("tensor")
    place = lax.axis_index("dp")
    first = place * seq_dev
    own = 2 * rank // parts
    rank_of = me.reshape(1)
    kept, sent = project(inputs, out_grads, in_proj, out_proj, rank_of, own)
    asked = pick(queries, rank_of, rank, own)
    weights = token_weights(seq_ids, counts, first)
    came = from_partner(sent, "tensor", parts, 1)
    kept, sent = halve(kept, came, rank_of, own)
    came = from_partner(sent, "tensor", parts, 2)
    message = gradients(weights, kept, came, asked)
    steps = own * own // message.shape[1]
    if blocks > SMALL:
        return finish_long(message, steps, first, seq_dev)
    partial = grams(place.reshape(1), from_all(message, "dp", blocks), steps, seq_dev)
    partial = from_partners(partial, "tensor", parts)
    return solve(partial, blocks * seq_dev, blocks * queries.shape[0], seq_dev)


def solution(mesh):
    in_specs = (
        P(("groups", "dp"), "tensor"),
        P(("groups", "dp"), "tensor"),
        P("tensor", None),
        P("tensor", None),
        P(("groups", "dp")),
        P(("groups", "dp")),
        P(("groups", "dp"), None),
    )
    sizes = (mesh.shape["tensor"], mesh.shape["dp"])
    return jax.shard_map(
        functools.partial(per_device, sizes),
        mesh=mesh,
        in_specs=in_specs,
        out_specs=P("groups", "dp"),
        check_vma=False,
    )
```

```python
import functools

import jax
import jax.numpy as jnp
from jax import lax
from jax.experimental import pallas as pl
from jax.experimental.pallas import tpu as pltpu
from jax.sharding import PartitionSpec as P

damping = 0.5
VMEM_LIMIT = 32 * 1024 * 1024
SMALL = 4
SHIFTS = {1: (), 2: (1,), 4: (1, 3, 2)}


def token_weights(seq_ids, counts, first):
    local_ids = seq_ids - first
    slots = jnp.arange(counts.shape[0], dtype=jnp.int32)
    member = local_ids[None, :] == slots[:, None]
    starts = jnp.sum((local_ids[None, :] < slots[:, None]).astype(jnp.int32), axis=1)
    offset = jnp.arange(seq_ids.shape[0], dtype=jnp.int32)[None, :] - starts[:, None]
    scale = 1.0 / counts.astype(jnp.float32)
    return jnp.where(member & (offset < counts[:, None]), scale[:, None], 0.0)


def cuts_of(extent, step):
    return [(at, min(step, extent - at)) for at in range(0, extent, step)]


def two_terms(value):
    high = value.astype(jnp.bfloat16)
    low = (value - high.astype(jnp.float32)).astype(jnp.bfloat16)
    return high, low


def dot_nt(left, right):
    rows = left.shape[0]
    lh, ll = two_terms(left)
    rh, rl = two_terms(right)
    mul = functools.partial(
        lax.dot_general,
        dimension_numbers=(((1,), (1,)), ((), ())),
        preferred_element_type=jnp.float32,
    )
    both = mul(jnp.concatenate([lh, ll], axis=0), rh)
    return both[:rows] + (mul(lh, rl) + both[rows:])


def project_kernel(own, rank_ref, x_hbm, g_hbm, wx_hbm, wg_hbm, keep_ref, send_ref, *scratch):
    x_ref, g_ref, wx_ref, wg_ref, wide_ref, sems = scratch
    copies = []

    def fetch(src, dst, index):
        copy = pltpu.make_async_copy(src, dst, sems.at[index])
        copy.start()
        return copy

    g_cuts = cuts_of(g_ref.shape[1], 1024)
    x_cuts = cuts_of(x_ref.shape[0], 1024)
    wg_copy = fetch(wg_hbm, wg_ref, 0)
    index = 2
    g_copies = []
    for at, size in g_cuts:
        columns = pl.ds(at, size)
        g_copies.append(fetch(g_hbm.at[:, columns], g_ref.at[:, columns], index))
        index += 1
    wx_copy = fetch(wx_hbm, wx_ref, 1)
    x_copies = []
    for at, size in x_cuts:
        rows = pl.ds(at, size)
        x_copies.append(fetch(x_hbm.at[rows, :], x_ref.at[rows, :], index))
        index += 1

    def product(copies, terms):
        total = None
        for copy, (left, right, along) in zip(copies, terms):
            copy.wait()
            term = lax.dot_general(
                left(), right(), (((1,), (along,)), ((), ())), preferred_element_type=jnp.float32
            )
            total = term if total is None else total + term
        return total

    def cut(ref, at, size, along):
        return lambda: ref[at : at + size, :] if along == 0 else ref[:, at : at + size]

    wg_copy.wait()
    grads_t = product(
        g_copies, [(cut(g_ref, at, size, 1), cut(wg_ref, at, size, 1), 1) for at, size in g_cuts]
    ).T
    wx_copy.wait()
    wide_ref[...] = product(
        x_copies, [(cut(wx_ref, at, size, 1), cut(x_ref, at, size, 0), 0) for at, size in x_cuts]
    )
    rank = grads_t.shape[0]
    side = rank_ref[0] & 1
    for out, taken in ((keep_ref, side), (send_ref, side ^ 1)):
        out[:rank, :] = grads_t
        out[rank:, :] = wide_ref[pl.ds(pl.multiple_of(taken * own, own), own), :]


def project(inputs, out_grads, in_proj, out_proj, me, own):
    rank = in_proj.shape[1]
    tokens, hidden = inputs.shape
    width = out_grads.shape[1]
    copies = 2 + len(cuts_of(width, 1024)) + len(cuts_of(hidden, 1024))
    arrays = (inputs.T, out_grads, in_proj.T, out_proj.T)
    in_hbm = pl.BlockSpec(memory_space=pltpu.HBM)
    return pl.pallas_call(
        functools.partial(project_kernel, own),
        out_shape=[jax.ShapeDtypeStruct((rank + own, tokens), jnp.float32)] * 2,
        in_specs=[pl.BlockSpec(memory_space=pltpu.SMEM)] + [in_hbm] * len(arrays),
        out_specs=[pl.BlockSpec(memory_space=pltpu.VMEM)] * 2,
        scratch_shapes=[
            pltpu.VMEM((hidden, tokens), jnp.bfloat16),
            pltpu.VMEM((tokens, width), jnp.bfloat16),
            pltpu.VMEM((rank, hidden), jnp.bfloat16),
            pltpu.VMEM((rank, width), jnp.bfloat16),
            pltpu.VMEM((rank, tokens), jnp.float32),
            pltpu.SemaphoreType.DMA((copies,)),
        ],
        compiler_params=pltpu.CompilerParams(vmem_limit_bytes=VMEM_LIMIT),
        name="project",
    )(me, *(pltpu.with_memory_space_constraint(array, pltpu.HBM) for array in arrays))


def halve_kernel(own, rank_ref, kept_ref, came_ref, keep_ref, send_ref, sum_ref):
    sum_ref[...] = kept_ref[...] + came_ref[...]
    place = rank_ref[0] // 2
    for out, taken in ((keep_ref, place), (send_ref, place ^ 1)):
        out[:own, :] = sum_ref[pl.ds(pl.multiple_of(taken * own, own), own), :]
        out[own:, :] = sum_ref[-own:, :]


def halve(kept, came, me, own):
    rows, tokens = kept.shape
    whole = pl.BlockSpec(memory_space=pltpu.VMEM)
    return pl.pallas_call(
        functools.partial(halve_kernel, own),
        out_shape=[jax.ShapeDtypeStruct((2 * own, tokens), jnp.float32)] * 2,
        in_specs=[pl.BlockSpec(memory_space=pltpu.SMEM), whole, whole],
        out_specs=[whole] * 2,
        scratch_shapes=[pltpu.VMEM((rows, tokens), jnp.float32)],
        compiler_params=pltpu.CompilerParams(vmem_limit_bytes=VMEM_LIMIT),
        name="halve",
    )(me, kept, came)


def pick_kernel(rank, own, rank_ref, queries_ref, out_ref):
    lanes = out_ref.shape[1]
    wide = lanes * rank // own
    steps = own * own // lanes
    asked = queries_ref.shape[0]
    me = rank_ref[0]
    start = (me // 2) * (own * rank)
    rows = jnp.concatenate(
        [
            queries_ref[:, pl.ds(pl.multiple_of(start + i * wide, lanes), wide)]
            for i in range(steps)
        ],
        axis=0,
    )
    source = lax.broadcasted_iota(jnp.int32, (wide, lanes), 0)
    place = lax.broadcasted_iota(jnp.int32, (wide, lanes), 1)
    wanted = (place // own) * rank + place % own + (me & 1) * own
    chosen = jnp.where(source == wanted, 1.0, 0.0).astype(jnp.bfloat16)
    high = rows.astype(jnp.bfloat16)
    rest = rows - high.astype(jnp.float32)
    middle = rest.astype(jnp.bfloat16)
    low = (rest - middle.astype(jnp.float32)).astype(jnp.bfloat16)
    terms = [
        jnp.dot(term, chosen, preferred_element_type=jnp.float32) for term in (high, middle, low)
    ]
    out_ref[...] = terms[0] + (terms[1] + terms[2])


def pick(queries, me, rank, own):
    lanes = 128
    rows = queries.shape[0] * own * own // lanes
    whole = pl.BlockSpec(memory_space=pltpu.VMEM)
    return pl.pallas_call(
        functools.partial(pick_kernel, rank, own),
        out_shape=jax.ShapeDtypeStruct((rows, lanes), jnp.float32),
        in_specs=[pl.BlockSpec(memory_space=pltpu.SMEM), whole],
        out_specs=whole,
        compiler_params=pltpu.CompilerParams(vmem_limit_bytes=VMEM_LIMIT),
        name="pick",
    )(me, queries)


def grads_kernel(weights_ref, kept_ref, came_ref, asked_ref, out_ref):
    summed = kept_ref[...] + came_ref[...]
    weights = weights_ref[...]
    own = summed.shape[0] // 2
    group = out_ref.shape[1] // own
    inputs_t = summed[own:, :]
    zero = jnp.zeros_like(inputs_t)
    right = jnp.concatenate(
        [
            jnp.concatenate([inputs_t if j == k else zero for k in range(group)], axis=1)
            for j in range(group)
        ],
        axis=0,
    )
    rows = []
    for i in range(own // group):
        rows.append(
            jnp.concatenate(
                [weights * summed[group * i + j : group * i + j + 1, :] for j in range(group)],
                axis=1,
            )
        )
    left = jnp.concatenate(rows, axis=0)
    count = left.shape[0]
    out_ref[:count, :] = dot_nt(left, right)
    out_ref[count:, :] = asked_ref[...]


def gradients(weights, kept, came, asked):
    lanes = asked.shape[1]
    own = kept.shape[0] // 2
    rows = own * own // lanes * weights.shape[0] + asked.shape[0]
    return pl.pallas_call(
        grads_kernel,
        out_shape=jax.ShapeDtypeStruct((rows, lanes), jnp.float32),
        compiler_params=pltpu.CompilerParams(vmem_limit_bytes=VMEM_LIMIT),
        name="gradients",
    )(weights, kept, came, asked)


def grams_kernel(steps, seqs, me_ref, *refs):
    blocks, out_ref = refs[:-1], refs[-1]
    shifts = (*SHIFTS[len(blocks)], 0)
    blocks = [blocks[shifts.index(-m % len(blocks))] for m in range(len(blocks))]
    count = steps * seqs
    asked = (blocks[0].shape[0] - count) // steps
    given = [block[count:, :] for block in blocks]
    ordered = []
    for place in range(len(blocks)):
        chosen = given[0]
        for m in range(1, len(blocks)):
            ahead = lax.rem(place - me_ref[0] + len(blocks), len(blocks))
            chosen = jnp.where(ahead == m, given[m], chosen)
        ordered.append(chosen)
    lanes = []
    for i in range(steps):
        rows = [block[i * seqs : (i + 1) * seqs, :] for block in blocks]
        rows += [chosen[i * asked : (i + 1) * asked, :] for chosen in ordered]
        lanes.append(jnp.concatenate(rows, axis=0))
    both = jnp.concatenate(lanes, axis=1)
    result = dot_nt(both, both[: len(blocks) * seqs])
    half = result.shape[0] // 2
    out_ref[...] = jnp.concatenate([result[:half, :], result[half:, :]], axis=1)


def grams(me, blocks, steps, seqs):
    asked = blocks[0].shape[0] // steps - seqs
    total = len(blocks) * seqs
    whole = pl.BlockSpec(memory_space=pltpu.VMEM)
    return pl.pallas_call(
        functools.partial(grams_kernel, steps, seqs),
        out_shape=jax.ShapeDtypeStruct(((total + len(blocks) * asked) // 2, 2 * total), jnp.float32),
        in_specs=[pl.BlockSpec(memory_space=pltpu.SMEM)] + [whole] * len(blocks),
        out_specs=whole,
        compiler_params=pltpu.CompilerParams(vmem_limit_bytes=VMEM_LIMIT),
        name="grams",
    )(me, *blocks)


def scales(count):
    first = 2.0 / (1.0 + 1.0 / count)
    off = count / (count + 1.0)
    steps = []
    while off > 1e-7:
        steps.append(2.0 / (2.0 - off * off))
        off = off * off / (2.0 - off * off)
    return first, steps


def solve_kernel(seqs, *refs):
    parts, out_ref = refs[:-1], refs[-1]
    packed = (parts[0][...] + parts[1][...]) + (parts[2][...] + parts[3][...])
    lane = lax.broadcasted_iota(jnp.int32, packed.shape, 1)
    turned = pltpu.roll(packed, seqs, 1)
    both = jnp.concatenate(
        [jnp.where(lane < seqs, packed, turned), jnp.where(lane < seqs, turned, packed)], axis=0
    )
    lane = lax.broadcasted_iota(jnp.int32, both.shape, 1)
    row = lax.broadcasted_iota(jnp.int32, both.shape, 0)
    unit = jnp.where((lane & (seqs - 1)) == row, 1.0, 0.0)
    total = jnp.sum(jnp.where(lane == row, both, 0.0)[:seqs], axis=(0, 1), keepdims=True)
    first, steps = scales(seqs)
    state = first * (both / total + unit * (damping / seqs))
    left_lanes = lane < seqs
    for at, step in enumerate(steps):
        high = state.astype(jnp.bfloat16).astype(jnp.float32)
        low = state - high
        left = jnp.where(left_lanes, high, low).astype(jnp.bfloat16)
        high = high[:seqs].astype(jnp.bfloat16)
        low = low[:seqs].astype(jnp.bfloat16)
        right = jnp.concatenate([high, high, low, low], axis=0)
        if at + 1 == len(steps):
            left, state = left[seqs:], state[seqs:]
        product = jnp.dot(
            jnp.concatenate([left, left], axis=1), right, preferred_element_type=jnp.float32
        )
        state = step * (2.0 * state - product)
    out_ref[...] = state[:, : out_ref.shape[1]]


def solve(parts, seqs, asked, seq_dev):
    return pl.pallas_call(
        functools.partial(solve_kernel, seqs),
        out_shape=jax.ShapeDtypeStruct((asked, seq_dev), jnp.float32),
        compiler_params=pltpu.CompilerParams(vmem_limit_bytes=VMEM_LIMIT),
        name="solve",
    )(*parts)


def from_partner(value, axis, size, m):
    return lax.ppermute(value, axis, [(i, i ^ m) for i in range(size)])


def from_partners(value, axis, size):
    return [from_partner(value, axis, size, m) for m in reversed(range(1, size))] + [value]


def from_all(value, axis, size):
    shifts = [[(i, (i + s) % size) for i in range(size)] for s in SHIFTS[size]]
    return [lax.ppermute(value, axis, shift) for shift in shifts] + [value]


def finish_long(message, steps, first, seq_dev):
    every = lax.all_gather(message, "dp", axis=0)
    lanes = message.shape[1]

    def rows_of(block):
        block = block.reshape(block.shape[0], steps, -1, lanes).transpose(0, 2, 1, 3)
        return block.reshape(-1, steps * lanes)

    count = steps * seq_dev
    grads, asked = rows_of(every[:, :count]), rows_of(every[:, count:])
    both = jnp.einsum(
        "ik,jk->ij", jnp.concatenate([grads, asked], axis=0), grads,
        precision=lax.Precision.HIGHEST,
    )
    both = lax.psum(both, "tensor")
    count = grads.shape[0]
    kernel, products = both[:count], both[count:]
    damp = damping * jnp.trace(kernel) / count
    unit = jnp.eye(count, dtype=jnp.float32)
    factor = jnp.linalg.cholesky(kernel + damp * unit)
    picks = lax.dynamic_slice_in_dim(unit, first, seq_dev, 1)
    solved = jax.scipy.linalg.cho_solve((factor, True), picks)
    return jnp.dot(products, solved, precision=lax.Precision.HIGHEST)


def per_device(sizes, inputs, out_grads, in_proj, out_proj, seq_ids, counts, queries):
    parts, blocks = sizes
    rank = in_proj.shape[1]
    seq_dev = counts.shape[0]
    me = lax.axis_index("tensor")
    place = lax.axis_index("dp")
    first = place * seq_dev
    own = 2 * rank // parts
    rank_of = me.reshape(1)
    kept, sent = project(inputs, out_grads, in_proj, out_proj, rank_of, own)
    asked = pick(queries, rank_of, rank, own)
    weights = token_weights(seq_ids, counts, first)
    came = from_partner(sent, "tensor", parts, 1)
    kept, sent = halve(kept, came, rank_of, own)
    came = from_partner(sent, "tensor", parts, 2)
    message = gradients(weights, kept, came, asked)
    steps = own * own // message.shape[1]
    if blocks > SMALL:
        return finish_long(message, steps, first, seq_dev)
    partial = grams(place.reshape(1), from_all(message, "dp", blocks), steps, seq_dev)
    partial = from_partners(partial, "tensor", parts)
    return solve(partial, blocks * seq_dev, blocks * queries.shape[0], seq_dev)


def solution(mesh):
    in_specs = (
        P(("groups", "dp"), "tensor"),
        P(("groups", "dp"), "tensor"),
        P("tensor", None),
        P("tensor", None),
        P(("groups", "dp")),
        P(("groups", "dp")),
        P(("groups", "dp"), None),
    )
    sizes = (mesh.shape["tensor"], mesh.shape["dp"])
    return jax.shard_map(
        functools.partial(per_device, sizes),
        mesh=mesh,
        in_specs=in_specs,
        out_specs=P("groups", "dp"),
        check_vma=False,
    )
```

```python
import functools

import jax
import jax.numpy as jnp
from jax import lax
from jax.experimental import pallas as pl
from jax.experimental.pallas import tpu as pltpu
from jax.sharding import PartitionSpec as P

damping = 0.5
VMEM_LIMIT = 32 * 1024 * 1024
SMALL = 4
SOURCES = {1: (), 2: ((1, 0),), 4: ((1, 0, 3, 2), (3, 2, 0, 1), (2, 3, 1, 0))}


def token_weights(seq_ids, counts, first):
    local_ids = seq_ids - first
    slots = jnp.arange(counts.shape[0], dtype=jnp.int32)
    member = local_ids[None, :] == slots[:, None]
    starts = jnp.sum((local_ids[None, :] < slots[:, None]).astype(jnp.int32), axis=1)
    offset = jnp.arange(seq_ids.shape[0], dtype=jnp.int32)[None, :] - starts[:, None]
    scale = 1.0 / counts.astype(jnp.float32)
    return jnp.where(member & (offset < counts[:, None]), scale[:, None], 0.0)


def cuts_of(extent, step):
    return [(at, min(step, extent - at)) for at in range(0, extent, step)]


def two_terms(value):
    high = value.astype(jnp.bfloat16)
    low = (value - high.astype(jnp.float32)).astype(jnp.bfloat16)
    return high, low


def dot_nt(left, right):
    rows = left.shape[0]
    lh, ll = two_terms(left)
    rh, rl = two_terms(right)
    mul = functools.partial(
        lax.dot_general,
        dimension_numbers=(((1,), (1,)), ((), ())),
        preferred_element_type=jnp.float32,
    )
    both = mul(jnp.concatenate([lh, ll], axis=0), rh)
    return both[:rows] + (mul(lh, rl) + both[rows:])


def project_kernel(own, rank_ref, x_hbm, g_hbm, wx_hbm, wg_hbm, keep_ref, send_ref, *scratch):
    x_ref, g_ref, wx_ref, wg_ref, wide_ref, sems = scratch
    copies = []

    def fetch(src, dst, index):
        copy = pltpu.make_async_copy(src, dst, sems.at[index])
        copy.start()
        return copy

    g_cuts = cuts_of(g_ref.shape[1], 1024)
    x_cuts = cuts_of(x_ref.shape[0], 1024)
    wg_copy = fetch(wg_hbm, wg_ref, 0)
    index = 2
    g_copies = []
    for at, size in g_cuts:
        columns = pl.ds(at, size)
        g_copies.append(fetch(g_hbm.at[:, columns], g_ref.at[:, columns], index))
        index += 1
    wx_copy = fetch(wx_hbm, wx_ref, 1)
    x_copies = []
    for at, size in x_cuts:
        rows = pl.ds(at, size)
        x_copies.append(fetch(x_hbm.at[rows, :], x_ref.at[rows, :], index))
        index += 1

    def product(copies, terms):
        total = None
        for copy, (left, right, along) in zip(copies, terms):
            copy.wait()
            term = lax.dot_general(
                left(), right(), (((1,), (along,)), ((), ())), preferred_element_type=jnp.float32
            )
            total = term if total is None else total + term
        return total

    def cut(ref, at, size, along):
        return lambda: ref[at : at + size, :] if along == 0 else ref[:, at : at + size]

    wg_copy.wait()
    grads_t = product(
        g_copies, [(cut(g_ref, at, size, 1), cut(wg_ref, at, size, 1), 1) for at, size in g_cuts]
    ).T
    wx_copy.wait()
    wide_ref[...] = product(
        x_copies, [(cut(wx_ref, at, size, 1), cut(x_ref, at, size, 0), 0) for at, size in x_cuts]
    )
    rank = grads_t.shape[0]
    side = rank_ref[0] & 1
    for out, taken in ((keep_ref, side), (send_ref, side ^ 1)):
        out[:rank, :] = grads_t
        out[rank:, :] = wide_ref[pl.ds(pl.multiple_of(taken * own, own), own), :]


def project(inputs, out_grads, in_proj, out_proj, me, own):
    rank = in_proj.shape[1]
    tokens, hidden = inputs.shape
    width = out_grads.shape[1]
    copies = 2 + len(cuts_of(width, 1024)) + len(cuts_of(hidden, 1024))
    arrays = (inputs.T, out_grads, in_proj.T, out_proj.T)
    in_hbm = pl.BlockSpec(memory_space=pltpu.HBM)
    return pl.pallas_call(
        functools.partial(project_kernel, own),
        out_shape=[jax.ShapeDtypeStruct((rank + own, tokens), jnp.float32)] * 2,
        in_specs=[pl.BlockSpec(memory_space=pltpu.SMEM)] + [in_hbm] * len(arrays),
        out_specs=[pl.BlockSpec(memory_space=pltpu.VMEM)] * 2,
        scratch_shapes=[
            pltpu.VMEM((hidden, tokens), jnp.bfloat16),
            pltpu.VMEM((tokens, width), jnp.bfloat16),
            pltpu.VMEM((rank, hidden), jnp.bfloat16),
            pltpu.VMEM((rank, width), jnp.bfloat16),
            pltpu.VMEM((rank, tokens), jnp.float32),
            pltpu.SemaphoreType.DMA((copies,)),
        ],
        compiler_params=pltpu.CompilerParams(vmem_limit_bytes=VMEM_LIMIT),
        name="project",
    )(me, *(pltpu.with_memory_space_constraint(array, pltpu.HBM) for array in arrays))


def halve_kernel(own, rank_ref, kept_ref, came_ref, keep_ref, send_ref, sum_ref):
    sum_ref[...] = kept_ref[...] + came_ref[...]
    place = rank_ref[0] // 2
    for out, taken in ((keep_ref, place), (send_ref, place ^ 1)):
        out[:own, :] = sum_ref[pl.ds(pl.multiple_of(taken * own, own), own), :]
        out[own:, :] = sum_ref[-own:, :]


def halve(kept, came, me, own):
    rows, tokens = kept.shape
    whole = pl.BlockSpec(memory_space=pltpu.VMEM)
    return pl.pallas_call(
        functools.partial(halve_kernel, own),
        out_shape=[jax.ShapeDtypeStruct((2 * own, tokens), jnp.float32)] * 2,
        in_specs=[pl.BlockSpec(memory_space=pltpu.SMEM), whole, whole],
        out_specs=[whole] * 2,
        scratch_shapes=[pltpu.VMEM((rows, tokens), jnp.float32)],
        compiler_params=pltpu.CompilerParams(vmem_limit_bytes=VMEM_LIMIT),
        name="halve",
    )(me, kept, came)


def pick_kernel(rank, own, rank_ref, queries_ref, out_ref):
    lanes = out_ref.shape[1]
    wide = lanes * rank // own
    steps = own * own // lanes
    asked = queries_ref.shape[0]
    me = rank_ref[0]
    start = (me // 2) * (own * rank)
    rows = jnp.concatenate(
        [
            queries_ref[:, pl.ds(pl.multiple_of(start + i * wide, lanes), wide)]
            for i in range(steps)
        ],
        axis=0,
    )
    source = lax.broadcasted_iota(jnp.int32, (wide, lanes), 0)
    place = lax.broadcasted_iota(jnp.int32, (wide, lanes), 1)
    wanted = (place // own) * rank + place % own + (me & 1) * own
    chosen = jnp.where(source == wanted, 1.0, 0.0).astype(jnp.bfloat16)
    high = rows.astype(jnp.bfloat16)
    rest = rows - high.astype(jnp.float32)
    middle = rest.astype(jnp.bfloat16)
    low = (rest - middle.astype(jnp.float32)).astype(jnp.bfloat16)
    terms = [
        jnp.dot(term, chosen, preferred_element_type=jnp.float32) for term in (high, middle, low)
    ]
    out_ref[...] = terms[0] + (terms[1] + terms[2])


def pick(queries, me, rank, own):
    lanes = 128
    rows = queries.shape[0] * own * own // lanes
    whole = pl.BlockSpec(memory_space=pltpu.VMEM)
    return pl.pallas_call(
        functools.partial(pick_kernel, rank, own),
        out_shape=jax.ShapeDtypeStruct((rows, lanes), jnp.float32),
        in_specs=[pl.BlockSpec(memory_space=pltpu.SMEM), whole],
        out_specs=whole,
        compiler_params=pltpu.CompilerParams(vmem_limit_bytes=VMEM_LIMIT),
        name="pick",
    )(me, queries)


def grads_kernel(weights_ref, kept_ref, came_ref, asked_ref, out_ref):
    summed = kept_ref[...] + came_ref[...]
    weights = weights_ref[...]
    own = summed.shape[0] // 2
    group = out_ref.shape[1] // own
    inputs_t = summed[own:, :]
    zero = jnp.zeros_like(inputs_t)
    right = jnp.concatenate(
        [
            jnp.concatenate([inputs_t if j == k else zero for k in range(group)], axis=1)
            for j in range(group)
        ],
        axis=0,
    )
    rows = []
    for i in range(own // group):
        rows.append(
            jnp.concatenate(
                [weights * summed[group * i + j : group * i + j + 1, :] for j in range(group)],
                axis=1,
            )
        )
    left = jnp.concatenate(rows, axis=0)
    count = left.shape[0]
    out_ref[:count, :] = dot_nt(left, right)
    out_ref[count:, :] = asked_ref[...]


def gradients(weights, kept, came, asked):
    lanes = asked.shape[1]
    own = kept.shape[0] // 2
    rows = own * own // lanes * weights.shape[0] + asked.shape[0]
    return pl.pallas_call(
        grads_kernel,
        out_shape=jax.ShapeDtypeStruct((rows, lanes), jnp.float32),
        compiler_params=pltpu.CompilerParams(vmem_limit_bytes=VMEM_LIMIT),
        name="gradients",
    )(weights, kept, came, asked)


def grams_kernel(steps, seqs, me_ref, *refs):
    blocks, out_ref = (refs[-2], *refs[:-2]), refs[-1]
    count = steps * seqs
    asked = (blocks[0].shape[0] - count) // steps
    given = [block[count:, :] for block in blocks]
    ordered = []
    for place in range(len(blocks)):
        chosen = given[0]
        for m, sources in enumerate(SOURCES[len(blocks)]):
            source = sum(jnp.where(me_ref[0] == i, j, 0) for i, j in enumerate(sources))
            chosen = jnp.where(source == place, given[m + 1], chosen)
        ordered.append(chosen)
    lanes = []
    for i in range(steps):
        rows = [block[i * seqs : (i + 1) * seqs, :] for block in blocks]
        rows += [chosen[i * asked : (i + 1) * asked, :] for chosen in ordered]
        lanes.append(jnp.concatenate(rows, axis=0))
    both = jnp.concatenate(lanes, axis=1)
    result = dot_nt(both, both[: len(blocks) * seqs])
    half = result.shape[0] // 2
    out_ref[...] = jnp.concatenate([result[:half, :], result[half:, :]], axis=1)


def grams(me, blocks, steps, seqs):
    asked = blocks[0].shape[0] // steps - seqs
    total = len(blocks) * seqs
    whole = pl.BlockSpec(memory_space=pltpu.VMEM)
    return pl.pallas_call(
        functools.partial(grams_kernel, steps, seqs),
        out_shape=jax.ShapeDtypeStruct(((total + len(blocks) * asked) // 2, 2 * total), jnp.float32),
        in_specs=[pl.BlockSpec(memory_space=pltpu.SMEM)] + [whole] * len(blocks),
        out_specs=whole,
        compiler_params=pltpu.CompilerParams(vmem_limit_bytes=VMEM_LIMIT),
        name="grams",
    )(me, *blocks)


def scales(count):
    first = 2.0 / (1.0 + 1.0 / count)
    off = count / (count + 1.0)
    steps = []
    while off > 1e-7:
        steps.append(2.0 / (2.0 - off * off))
        off = off * off / (2.0 - off * off)
    return first, steps


def solve_kernel(seqs, *refs):
    parts, out_ref = refs[:-1], refs[-1]
    packed = (parts[0][...] + parts[1][...]) + (parts[2][...] + parts[3][...])
    lane = lax.broadcasted_iota(jnp.int32, packed.shape, 1)
    turned = pltpu.roll(packed, seqs, 1)
    both = jnp.concatenate(
        [jnp.where(lane < seqs, packed, turned), jnp.where(lane < seqs, turned, packed)], axis=0
    )
    lane = lax.broadcasted_iota(jnp.int32, both.shape, 1)
    row = lax.broadcasted_iota(jnp.int32, both.shape, 0)
    unit = jnp.where((lane & (seqs - 1)) == row, 1.0, 0.0)
    total = jnp.sum(jnp.where(lane == row, both, 0.0)[:seqs], axis=(0, 1), keepdims=True)
    first, steps = scales(seqs)
    state = first * (both / total + unit * (damping / seqs))
    left_lanes = lane < seqs
    for at, step in enumerate(steps):
        high = state.astype(jnp.bfloat16).astype(jnp.float32)
        low = state - high
        left = jnp.where(left_lanes, high, low).astype(jnp.bfloat16)
        high = high[:seqs].astype(jnp.bfloat16)
        low = low[:seqs].astype(jnp.bfloat16)
        right = jnp.concatenate([high, high, low, low], axis=0)
        if at + 1 == len(steps):
            left, state = left[seqs:], state[seqs:]
        product = jnp.dot(
            jnp.concatenate([left, left], axis=1), right, preferred_element_type=jnp.float32
        )
        state = step * (2.0 * state - product)
    out_ref[...] = state[:, : out_ref.shape[1]]


def solve(parts, seqs, asked, seq_dev):
    return pl.pallas_call(
        functools.partial(solve_kernel, seqs),
        out_shape=jax.ShapeDtypeStruct((asked, seq_dev), jnp.float32),
        compiler_params=pltpu.CompilerParams(vmem_limit_bytes=VMEM_LIMIT),
        name="solve",
    )(*parts)


def from_partner(value, axis, size, m):
    return lax.ppermute(value, axis, [(i, i ^ m) for i in range(size)])


def from_partners(value, axis, size):
    return [from_partner(value, axis, size, m) for m in reversed(range(1, size))] + [value]


def from_all(value, axis, size):
    swaps = [[(source, i) for i, source in enumerate(sources)] for sources in SOURCES[size]]
    return [lax.ppermute(value, axis, swap) for swap in swaps] + [value]


def finish_long(message, steps, first, seq_dev):
    every = lax.all_gather(message, "dp", axis=0)
    lanes = message.shape[1]

    def rows_of(block):
        block = block.reshape(block.shape[0], steps, -1, lanes).transpose(0, 2, 1, 3)
        return block.reshape(-1, steps * lanes)

    count = steps * seq_dev
    grads, asked = rows_of(every[:, :count]), rows_of(every[:, count:])
    both = jnp.einsum(
        "ik,jk->ij", jnp.concatenate([grads, asked], axis=0), grads,
        precision=lax.Precision.HIGHEST,
    )
    both = lax.psum(both, "tensor")
    count = grads.shape[0]
    kernel, products = both[:count], both[count:]
    damp = damping * jnp.trace(kernel) / count
    unit = jnp.eye(count, dtype=jnp.float32)
    factor = jnp.linalg.cholesky(kernel + damp * unit)
    picks = lax.dynamic_slice_in_dim(unit, first, seq_dev, 1)
    solved = jax.scipy.linalg.cho_solve((factor, True), picks)
    return jnp.dot(products, solved, precision=lax.Precision.HIGHEST)


def per_device(sizes, inputs, out_grads, in_proj, out_proj, seq_ids, counts, queries):
    parts, blocks = sizes
    rank = in_proj.shape[1]
    seq_dev = counts.shape[0]
    me = lax.axis_index("tensor")
    place = lax.axis_index("dp")
    first = place * seq_dev
    own = 2 * rank // parts
    rank_of = me.reshape(1)
    kept, sent = project(inputs, out_grads, in_proj, out_proj, rank_of, own)
    asked = pick(queries, rank_of, rank, own)
    weights = token_weights(seq_ids, counts, first)
    came = from_partner(sent, "tensor", parts, 1)
    kept, sent = halve(kept, came, rank_of, own)
    came = from_partner(sent, "tensor", parts, 2)
    message = gradients(weights, kept, came, asked)
    steps = own * own // message.shape[1]
    if blocks > SMALL:
        return finish_long(message, steps, first, seq_dev)
    partial = grams(place.reshape(1), from_all(message, "dp", blocks), steps, seq_dev)
    partial = from_partners(partial, "tensor", parts)
    return solve(partial, blocks * seq_dev, blocks * queries.shape[0], seq_dev)


def solution(mesh):
    in_specs = (
        P(("groups", "dp"), "tensor"),
        P(("groups", "dp"), "tensor"),
        P("tensor", None),
        P("tensor", None),
        P(("groups", "dp")),
        P(("groups", "dp")),
        P(("groups", "dp"), None),
    )
    sizes = (mesh.shape["tensor"], mesh.shape["dp"])
    return jax.shard_map(
        functools.partial(per_device, sizes),
        mesh=mesh,
        in_specs=in_specs,
        out_specs=P("groups", "dp"),
        check_vma=False,
    )
```

```python
import functools

import jax
import jax.numpy as jnp
from jax import lax
from jax.experimental import pallas as pl
from jax.experimental.pallas import tpu as pltpu
from jax.sharding import PartitionSpec as P

damping = 0.5
VMEM_LIMIT = 32 * 1024 * 1024
SMALL = 4


def token_weights(seq_ids, counts, first):
    local_ids = seq_ids - first
    slots = jnp.arange(counts.shape[0], dtype=jnp.int32)
    member = local_ids[None, :] == slots[:, None]
    starts = jnp.sum((local_ids[None, :] < slots[:, None]).astype(jnp.int32), axis=1)
    offset = jnp.arange(seq_ids.shape[0], dtype=jnp.int32)[None, :] - starts[:, None]
    scale = 1.0 / counts.astype(jnp.float32)
    return jnp.where(member & (offset < counts[:, None]), scale[:, None], 0.0)


def cuts_of(extent, step):
    return [(at, min(step, extent - at)) for at in range(0, extent, step)]


def two_terms(value):
    high = value.astype(jnp.bfloat16)
    low = (value - high.astype(jnp.float32)).astype(jnp.bfloat16)
    return high, low


def dot_nt(left, right):
    rows = left.shape[0]
    lh, ll = two_terms(left)
    rh, rl = two_terms(right)
    mul = functools.partial(
        lax.dot_general,
        dimension_numbers=(((1,), (1,)), ((), ())),
        preferred_element_type=jnp.float32,
    )
    both = mul(jnp.concatenate([lh, ll], axis=0), rh)
    return both[:rows] + (mul(lh, rl) + both[rows:])


def project_kernel(own, rank_ref, x_hbm, g_hbm, wx_hbm, wg_hbm, keep_ref, send_ref, *scratch):
    x_ref, g_ref, wx_ref, wg_ref, wide_ref, sems = scratch
    copies = []

    def fetch(src, dst, index):
        copy = pltpu.make_async_copy(src, dst, sems.at[index])
        copy.start()
        return copy

    g_cuts = cuts_of(g_ref.shape[1], 1024)
    x_cuts = cuts_of(x_ref.shape[0], 1024)
    wg_copy = fetch(wg_hbm, wg_ref, 0)
    index = 2
    g_copies = []
    for at, size in g_cuts:
        columns = pl.ds(at, size)
        g_copies.append(fetch(g_hbm.at[:, columns], g_ref.at[:, columns], index))
        index += 1
    wx_copy = fetch(wx_hbm, wx_ref, 1)
    x_copies = []
    for at, size in x_cuts:
        rows = pl.ds(at, size)
        x_copies.append(fetch(x_hbm.at[rows, :], x_ref.at[rows, :], index))
        index += 1

    def product(copies, terms):
        total = None
        for copy, (left, right, along) in zip(copies, terms):
            copy.wait()
            term = lax.dot_general(
                left(), right(), (((1,), (along,)), ((), ())), preferred_element_type=jnp.float32
            )
            total = term if total is None else total + term
        return total

    def cut(ref, at, size, along):
        return lambda: ref[at : at + size, :] if along == 0 else ref[:, at : at + size]

    wg_copy.wait()
    grads_t = product(
        g_copies, [(cut(g_ref, at, size, 1), cut(wg_ref, at, size, 1), 1) for at, size in g_cuts]
    ).T
    wx_copy.wait()
    wide_ref[...] = product(
        x_copies, [(cut(wx_ref, at, size, 1), cut(x_ref, at, size, 0), 0) for at, size in x_cuts]
    )
    rank = grads_t.shape[0]
    side = rank_ref[0] & 1
    for out, taken in ((keep_ref, side), (send_ref, side ^ 1)):
        out[:rank, :] = grads_t
        out[rank:, :] = wide_ref[pl.ds(pl.multiple_of(taken * own, own), own), :]


def project(inputs, out_grads, in_proj, out_proj, me, own):
    rank = in_proj.shape[1]
    tokens, hidden = inputs.shape
    width = out_grads.shape[1]
    copies = 2 + len(cuts_of(width, 1024)) + len(cuts_of(hidden, 1024))
    arrays = (inputs.T, out_grads, in_proj.T, out_proj.T)
    in_hbm = pl.BlockSpec(memory_space=pltpu.HBM)
    return pl.pallas_call(
        functools.partial(project_kernel, own),
        out_shape=[jax.ShapeDtypeStruct((rank + own, tokens), jnp.float32)] * 2,
        in_specs=[pl.BlockSpec(memory_space=pltpu.SMEM)] + [in_hbm] * len(arrays),
        out_specs=[pl.BlockSpec(memory_space=pltpu.VMEM)] * 2,
        scratch_shapes=[
            pltpu.VMEM((hidden, tokens), jnp.bfloat16),
            pltpu.VMEM((tokens, width), jnp.bfloat16),
            pltpu.VMEM((rank, hidden), jnp.bfloat16),
            pltpu.VMEM((rank, width), jnp.bfloat16),
            pltpu.VMEM((rank, tokens), jnp.float32),
            pltpu.SemaphoreType.DMA((copies,)),
        ],
        compiler_params=pltpu.CompilerParams(vmem_limit_bytes=VMEM_LIMIT),
        name="project",
    )(me, *(pltpu.with_memory_space_constraint(array, pltpu.HBM) for array in arrays))


def halve_kernel(own, rank_ref, kept_ref, came_ref, keep_ref, send_ref, sum_ref):
    sum_ref[...] = kept_ref[...] + came_ref[...]
    place = rank_ref[0] // 2
    for out, taken in ((keep_ref, place), (send_ref, place ^ 1)):
        out[:own, :] = sum_ref[pl.ds(pl.multiple_of(taken * own, own), own), :]
        out[own:, :] = sum_ref[-own:, :]


def halve(kept, came, me, own):
    rows, tokens = kept.shape
    whole = pl.BlockSpec(memory_space=pltpu.VMEM)
    return pl.pallas_call(
        functools.partial(halve_kernel, own),
        out_shape=[jax.ShapeDtypeStruct((2 * own, tokens), jnp.float32)] * 2,
        in_specs=[pl.BlockSpec(memory_space=pltpu.SMEM), whole, whole],
        out_specs=[whole] * 2,
        scratch_shapes=[pltpu.VMEM((rows, tokens), jnp.float32)],
        compiler_params=pltpu.CompilerParams(vmem_limit_bytes=VMEM_LIMIT),
        name="halve",
    )(me, kept, came)


def pick_kernel(rank, own, rank_ref, queries_ref, out_ref):
    lanes = out_ref.shape[1]
    wide = lanes * rank // own
    steps = own * own // lanes
    asked = queries_ref.shape[0]
    me = rank_ref[0]
    start = (me // 2) * (own * rank)
    rows = jnp.concatenate(
        [
            queries_ref[:, pl.ds(pl.multiple_of(start + i * wide, lanes), wide)]
            for i in range(steps)
        ],
        axis=0,
    )
    source = lax.broadcasted_iota(jnp.int32, (wide, lanes), 0)
    place = lax.broadcasted_iota(jnp.int32, (wide, lanes), 1)
    wanted = (place // own) * rank + place % own + (me & 1) * own
    chosen = jnp.where(source == wanted, 1.0, 0.0).astype(jnp.bfloat16)
    high = rows.astype(jnp.bfloat16)
    rest = rows - high.astype(jnp.float32)
    middle = rest.astype(jnp.bfloat16)
    low = (rest - middle.astype(jnp.float32)).astype(jnp.bfloat16)
    terms = [
        jnp.dot(term, chosen, preferred_element_type=jnp.float32) for term in (high, middle, low)
    ]
    out_ref[...] = terms[0] + (terms[1] + terms[2])


def pick(queries, me, rank, own):
    lanes = 128
    rows = queries.shape[0] * own * own // lanes
    whole = pl.BlockSpec(memory_space=pltpu.VMEM)
    return pl.pallas_call(
        functools.partial(pick_kernel, rank, own),
        out_shape=jax.ShapeDtypeStruct((rows, lanes), jnp.float32),
        in_specs=[pl.BlockSpec(memory_space=pltpu.SMEM), whole],
        out_specs=whole,
        compiler_params=pltpu.CompilerParams(vmem_limit_bytes=VMEM_LIMIT),
        name="pick",
    )(me, queries)


def grads_kernel(weights_ref, kept_ref, came_ref, asked_ref, out_ref):
    summed = kept_ref[...] + came_ref[...]
    weights = weights_ref[...]
    own = summed.shape[0] // 2
    group = out_ref.shape[1] // own
    inputs_t = summed[own:, :]
    zero = jnp.zeros_like(inputs_t)
    right = jnp.concatenate(
        [
            jnp.concatenate([inputs_t if j == k else zero for k in range(group)], axis=1)
            for j in range(group)
        ],
        axis=0,
    )
    rows = []
    for i in range(own // group):
        rows.append(
            jnp.concatenate(
                [weights * summed[group * i + j : group * i + j + 1, :] for j in range(group)],
                axis=1,
            )
        )
    left = jnp.concatenate(rows, axis=0)
    count = left.shape[0]
    out_ref[:count, :] = dot_nt(left, right)
    out_ref[count:, :] = asked_ref[...]


def gradients(weights, kept, came, asked):
    lanes = asked.shape[1]
    own = kept.shape[0] // 2
    rows = own * own // lanes * weights.shape[0] + asked.shape[0]
    return pl.pallas_call(
        grads_kernel,
        out_shape=jax.ShapeDtypeStruct((rows, lanes), jnp.float32),
        compiler_params=pltpu.CompilerParams(vmem_limit_bytes=VMEM_LIMIT),
        name="gradients",
    )(weights, kept, came, asked)


def grams_kernel(steps, seqs, me_ref, *refs):
    own_ref, others, out_ref = refs[-2], refs[:-2], refs[-1]
    odd = me_ref[1] == 1
    blocks = [own_ref[...]] + [
        jnp.where(odd, lower[...], upper[...]) for lower, upper in zip(others, others[::-1])
    ]
    count = steps * seqs
    asked = (blocks[0].shape[0] - count) // steps
    given = [block[count:, :] for block in blocks]
    ordered = []
    for place in range(len(blocks)):
        chosen = given[0]
        for m in range(1, len(blocks)):
            ahead = lax.rem(place - me_ref[0] + len(blocks), len(blocks))
            chosen = jnp.where(ahead == m, given[m], chosen)
        ordered.append(chosen)
    lanes = []
    for i in range(steps):
        rows = [block[i * seqs : (i + 1) * seqs, :] for block in blocks]
        rows += [chosen[i * asked : (i + 1) * asked, :] for chosen in ordered]
        lanes.append(jnp.concatenate(rows, axis=0))
    both = jnp.concatenate(lanes, axis=1)
    result = dot_nt(both, both[: len(blocks) * seqs])
    half = result.shape[0] // 2
    out_ref[...] = jnp.concatenate([result[:half, :], result[half:, :]], axis=1)


def grams(me, blocks, steps, seqs):
    asked = blocks[0].shape[0] // steps - seqs
    total = len(blocks) * seqs
    whole = pl.BlockSpec(memory_space=pltpu.VMEM)
    return pl.pallas_call(
        functools.partial(grams_kernel, steps, seqs),
        out_shape=jax.ShapeDtypeStruct(((total + len(blocks) * asked) // 2, 2 * total), jnp.float32),
        in_specs=[pl.BlockSpec(memory_space=pltpu.SMEM)] + [whole] * len(blocks),
        out_specs=whole,
        compiler_params=pltpu.CompilerParams(vmem_limit_bytes=VMEM_LIMIT),
        name="grams",
    )(me, *blocks)


def scales(count):
    first = 2.0 / (1.0 + 1.0 / count)
    off = count / (count + 1.0)
    steps = []
    while off > 1e-7:
        steps.append(2.0 / (2.0 - off * off))
        off = off * off / (2.0 - off * off)
    return first, steps


def solve_kernel(seqs, *refs):
    parts, out_ref = refs[:-1], refs[-1]
    packed = (parts[0][...] + parts[1][...]) + (parts[2][...] + parts[3][...])
    lane = lax.broadcasted_iota(jnp.int32, packed.shape, 1)
    turned = pltpu.roll(packed, seqs, 1)
    both = jnp.concatenate(
        [jnp.where(lane < seqs, packed, turned), jnp.where(lane < seqs, turned, packed)], axis=0
    )
    lane = lax.broadcasted_iota(jnp.int32, both.shape, 1)
    row = lax.broadcasted_iota(jnp.int32, both.shape, 0)
    unit = jnp.where((lane & (seqs - 1)) == row, 1.0, 0.0)
    total = jnp.sum(jnp.where(lane == row, both, 0.0)[:seqs], axis=(0, 1), keepdims=True)
    first, steps = scales(seqs)
    state = first * (both / total + unit * (damping / seqs))
    left_lanes = lane < seqs
    for at, step in enumerate(steps):
        high = state.astype(jnp.bfloat16).astype(jnp.float32)
        low = state - high
        left = jnp.where(left_lanes, high, low).astype(jnp.bfloat16)
        high = high[:seqs].astype(jnp.bfloat16)
        low = low[:seqs].astype(jnp.bfloat16)
        right = jnp.concatenate([high, high, low, low], axis=0)
        if at + 1 == len(steps):
            left, state = left[seqs:], state[seqs:]
        product = jnp.dot(
            jnp.concatenate([left, left], axis=1), right, preferred_element_type=jnp.float32
        )
        state = step * (2.0 * state - product)
    out_ref[...] = state[:, : out_ref.shape[1]]


def solve(parts, seqs, asked, seq_dev):
    return pl.pallas_call(
        functools.partial(solve_kernel, seqs),
        out_shape=jax.ShapeDtypeStruct((asked, seq_dev), jnp.float32),
        compiler_params=pltpu.CompilerParams(vmem_limit_bytes=VMEM_LIMIT),
        name="solve",
    )(*parts)


def from_partner(value, axis, size, m):
    return lax.ppermute(value, axis, [(i, i ^ m) for i in range(size)])


def from_partners(value, axis, size):
    return [from_partner(value, axis, size, m) for m in reversed(range(1, size))] + [value]


def from_all(value, sizes):
    parts, blocks = sizes
    came = []
    for s in range(1, blocks):
        pairs = []
        for i in range(blocks):
            for r in range(parts):
                to = (i + (s if r % 2 == 0 else blocks - s)) % blocks
                pairs.append((i * parts + r, to * parts + r))
        came.append(lax.ppermute(value, ("dp", "tensor"), pairs))
    return came + [value]


def finish_long(message, steps, first, seq_dev):
    every = lax.all_gather(message, "dp", axis=0)
    lanes = message.shape[1]

    def rows_of(block):
        block = block.reshape(block.shape[0], steps, -1, lanes).transpose(0, 2, 1, 3)
        return block.reshape(-1, steps * lanes)

    count = steps * seq_dev
    grads, asked = rows_of(every[:, :count]), rows_of(every[:, count:])
    both = jnp.einsum(
        "ik,jk->ij", jnp.concatenate([grads, asked], axis=0), grads,
        precision=lax.Precision.HIGHEST,
    )
    both = lax.psum(both, "tensor")
    count = grads.shape[0]
    kernel, products = both[:count], both[count:]
    damp = damping * jnp.trace(kernel) / count
    unit = jnp.eye(count, dtype=jnp.float32)
    factor = jnp.linalg.cholesky(kernel + damp * unit)
    picks = lax.dynamic_slice_in_dim(unit, first, seq_dev, 1)
    solved = jax.scipy.linalg.cho_solve((factor, True), picks)
    return jnp.dot(products, solved, precision=lax.Precision.HIGHEST)


def per_device(sizes, inputs, out_grads, in_proj, out_proj, seq_ids, counts, queries):
    parts, blocks = sizes
    rank = in_proj.shape[1]
    seq_dev = counts.shape[0]
    me = lax.axis_index("tensor")
    place = lax.axis_index("dp")
    first = place * seq_dev
    own = 2 * rank // parts
    rank_of = me.reshape(1)
    kept, sent = project(inputs, out_grads, in_proj, out_proj, rank_of, own)
    asked = pick(queries, rank_of, rank, own)
    weights = token_weights(seq_ids, counts, first)
    came = from_partner(sent, "tensor", parts, 1)
    kept, sent = halve(kept, came, rank_of, own)
    came = from_partner(sent, "tensor", parts, 2)
    message = gradients(weights, kept, came, asked)
    steps = own * own // message.shape[1]
    if blocks > SMALL:
        return finish_long(message, steps, first, seq_dev)
    partial = grams(jnp.stack([place, me % 2]), from_all(message, sizes), steps, seq_dev)
    partial = from_partners(partial, "tensor", parts)
    return solve(partial, blocks * seq_dev, blocks * queries.shape[0], seq_dev)


def solution(mesh):
    in_specs = (
        P(("groups", "dp"), "tensor"),
        P(("groups", "dp"), "tensor"),
        P("tensor", None),
        P("tensor", None),
        P(("groups", "dp")),
        P(("groups", "dp")),
        P(("groups", "dp"), None),
    )
    sizes = (mesh.shape["tensor"], mesh.shape["dp"])
    return jax.shard_map(
        functools.partial(per_device, sizes),
        mesh=mesh,
        in_specs=in_specs,
        out_specs=P("groups", "dp"),
        check_vma=False,
    )
```

```python
import functools

import jax
import jax.numpy as jnp
from jax import lax
from jax.experimental import pallas as pl
from jax.experimental.pallas import tpu as pltpu
from jax.sharding import PartitionSpec as P

damping = 0.5
VMEM_LIMIT = 32 * 1024 * 1024
SMALL = 4
SHIFTS = {1: ((), ()), 2: ((1,), (1,)), 4: ((1, 2, 3), (2, 1, 3))}


def token_weights(seq_ids, counts, first):
    local_ids = seq_ids - first
    slots = jnp.arange(counts.shape[0], dtype=jnp.int32)
    member = local_ids[None, :] == slots[:, None]
    starts = jnp.sum((local_ids[None, :] < slots[:, None]).astype(jnp.int32), axis=1)
    offset = jnp.arange(seq_ids.shape[0], dtype=jnp.int32)[None, :] - starts[:, None]
    scale = 1.0 / counts.astype(jnp.float32)
    return jnp.where(member & (offset < counts[:, None]), scale[:, None], 0.0)


def cuts_of(extent, step):
    return [(at, min(step, extent - at)) for at in range(0, extent, step)]


def two_terms(value):
    high = value.astype(jnp.bfloat16)
    low = (value - high.astype(jnp.float32)).astype(jnp.bfloat16)
    return high, low


def dot_nt(left, right):
    rows = left.shape[0]
    lh, ll = two_terms(left)
    rh, rl = two_terms(right)
    mul = functools.partial(
        lax.dot_general,
        dimension_numbers=(((1,), (1,)), ((), ())),
        preferred_element_type=jnp.float32,
    )
    both = mul(jnp.concatenate([lh, ll], axis=0), rh)
    return both[:rows] + (mul(lh, rl) + both[rows:])


def project_kernel(own, rank_ref, x_hbm, g_hbm, wx_hbm, wg_hbm, keep_ref, send_ref, *scratch):
    x_ref, g_ref, wx_ref, wg_ref, wide_ref, sems = scratch
    copies = []

    def fetch(src, dst, index):
        copy = pltpu.make_async_copy(src, dst, sems.at[index])
        copy.start()
        return copy

    g_cuts = cuts_of(g_ref.shape[1], 1024)
    x_cuts = cuts_of(x_ref.shape[0], 1024)
    wg_copy = fetch(wg_hbm, wg_ref, 0)
    index = 2
    g_copies = []
    for at, size in g_cuts:
        columns = pl.ds(at, size)
        g_copies.append(fetch(g_hbm.at[:, columns], g_ref.at[:, columns], index))
        index += 1
    wx_copy = fetch(wx_hbm, wx_ref, 1)
    x_copies = []
    for at, size in x_cuts:
        rows = pl.ds(at, size)
        x_copies.append(fetch(x_hbm.at[rows, :], x_ref.at[rows, :], index))
        index += 1

    def product(copies, terms):
        total = None
        for copy, (left, right, along) in zip(copies, terms):
            copy.wait()
            term = lax.dot_general(
                left(), right(), (((1,), (along,)), ((), ())), preferred_element_type=jnp.float32
            )
            total = term if total is None else total + term
        return total

    def cut(ref, at, size, along):
        return lambda: ref[at : at + size, :] if along == 0 else ref[:, at : at + size]

    wg_copy.wait()
    grads_t = product(
        g_copies, [(cut(g_ref, at, size, 1), cut(wg_ref, at, size, 1), 1) for at, size in g_cuts]
    ).T
    wx_copy.wait()
    wide_ref[...] = product(
        x_copies, [(cut(wx_ref, at, size, 1), cut(x_ref, at, size, 0), 0) for at, size in x_cuts]
    )
    rank = grads_t.shape[0]
    side = rank_ref[0] & 1
    for out, taken in ((keep_ref, side), (send_ref, side ^ 1)):
        out[:rank, :] = grads_t
        out[rank:, :] = wide_ref[pl.ds(pl.multiple_of(taken * own, own), own), :]


def project(inputs, out_grads, in_proj, out_proj, me, own):
    rank = in_proj.shape[1]
    tokens, hidden = inputs.shape
    width = out_grads.shape[1]
    copies = 2 + len(cuts_of(width, 1024)) + len(cuts_of(hidden, 1024))
    arrays = (inputs.T, out_grads, in_proj.T, out_proj.T)
    in_hbm = pl.BlockSpec(memory_space=pltpu.HBM)
    return pl.pallas_call(
        functools.partial(project_kernel, own),
        out_shape=[jax.ShapeDtypeStruct((rank + own, tokens), jnp.float32)] * 2,
        in_specs=[pl.BlockSpec(memory_space=pltpu.SMEM)] + [in_hbm] * len(arrays),
        out_specs=[pl.BlockSpec(memory_space=pltpu.VMEM)] * 2,
        scratch_shapes=[
            pltpu.VMEM((hidden, tokens), jnp.bfloat16),
            pltpu.VMEM((tokens, width), jnp.bfloat16),
            pltpu.VMEM((rank, hidden), jnp.bfloat16),
            pltpu.VMEM((rank, width), jnp.bfloat16),
            pltpu.VMEM((rank, tokens), jnp.float32),
            pltpu.SemaphoreType.DMA((copies,)),
        ],
        compiler_params=pltpu.CompilerParams(vmem_limit_bytes=VMEM_LIMIT),
        name="project",
    )(me, *(pltpu.with_memory_space_constraint(array, pltpu.HBM) for array in arrays))


def halve_kernel(own, rank_ref, kept_ref, came_ref, keep_ref, send_ref, sum_ref):
    sum_ref[...] = kept_ref[...] + came_ref[...]
    place = rank_ref[0] // 2
    for out, taken in ((keep_ref, place), (send_ref, place ^ 1)):
        out[:own, :] = sum_ref[pl.ds(pl.multiple_of(taken * own, own), own), :]
        out[own:, :] = sum_ref[-own:, :]


def halve(kept, came, me, own):
    rows, tokens = kept.shape
    whole = pl.BlockSpec(memory_space=pltpu.VMEM)
    return pl.pallas_call(
        functools.partial(halve_kernel, own),
        out_shape=[jax.ShapeDtypeStruct((2 * own, tokens), jnp.float32)] * 2,
        in_specs=[pl.BlockSpec(memory_space=pltpu.SMEM), whole, whole],
        out_specs=[whole] * 2,
        scratch_shapes=[pltpu.VMEM((rows, tokens), jnp.float32)],
        compiler_params=pltpu.CompilerParams(vmem_limit_bytes=VMEM_LIMIT),
        name="halve",
    )(me, kept, came)


def pick_kernel(rank, own, rank_ref, queries_ref, out_ref):
    lanes = out_ref.shape[1]
    wide = lanes * rank // own
    steps = own * own // lanes
    asked = queries_ref.shape[0]
    me = rank_ref[0]
    start = (me // 2) * (own * rank)
    rows = jnp.concatenate(
        [
            queries_ref[:, pl.ds(pl.multiple_of(start + i * wide, lanes), wide)]
            for i in range(steps)
        ],
        axis=0,
    )
    source = lax.broadcasted_iota(jnp.int32, (wide, lanes), 0)
    place = lax.broadcasted_iota(jnp.int32, (wide, lanes), 1)
    wanted = (place // own) * rank + place % own + (me & 1) * own
    chosen = jnp.where(source == wanted, 1.0, 0.0).astype(jnp.bfloat16)
    high = rows.astype(jnp.bfloat16)
    rest = rows - high.astype(jnp.float32)
    middle = rest.astype(jnp.bfloat16)
    low = (rest - middle.astype(jnp.float32)).astype(jnp.bfloat16)
    terms = [
        jnp.dot(term, chosen, preferred_element_type=jnp.float32) for term in (high, middle, low)
    ]
    out_ref[...] = terms[0] + (terms[1] + terms[2])


def pick(queries, me, rank, own):
    lanes = 128
    rows = queries.shape[0] * own * own // lanes
    whole = pl.BlockSpec(memory_space=pltpu.VMEM)
    return pl.pallas_call(
        functools.partial(pick_kernel, rank, own),
        out_shape=jax.ShapeDtypeStruct((rows, lanes), jnp.float32),
        in_specs=[pl.BlockSpec(memory_space=pltpu.SMEM), whole],
        out_specs=whole,
        compiler_params=pltpu.CompilerParams(vmem_limit_bytes=VMEM_LIMIT),
        name="pick",
    )(me, queries)


def grads_kernel(weights_ref, kept_ref, came_ref, asked_ref, out_ref):
    summed = kept_ref[...] + came_ref[...]
    weights = weights_ref[...]
    own = summed.shape[0] // 2
    group = out_ref.shape[1] // own
    inputs_t = summed[own:, :]
    zero = jnp.zeros_like(inputs_t)
    right = jnp.concatenate(
        [
            jnp.concatenate([inputs_t if j == k else zero for k in range(group)], axis=1)
            for j in range(group)
        ],
        axis=0,
    )
    rows = []
    for i in range(own // group):
        rows.append(
            jnp.concatenate(
                [weights * summed[group * i + j : group * i + j + 1, :] for j in range(group)],
                axis=1,
            )
        )
    left = jnp.concatenate(rows, axis=0)
    count = left.shape[0]
    out_ref[:count, :] = dot_nt(left, right)
    out_ref[count:, :] = asked_ref[...]


def gradients(weights, kept, came, asked):
    lanes = asked.shape[1]
    own = kept.shape[0] // 2
    rows = own * own // lanes * weights.shape[0] + asked.shape[0]
    return pl.pallas_call(
        grads_kernel,
        out_shape=jax.ShapeDtypeStruct((rows, lanes), jnp.float32),
        compiler_params=pltpu.CompilerParams(vmem_limit_bytes=VMEM_LIMIT),
        name="gradients",
    )(weights, kept, came, asked)


def grams_kernel(steps, seqs, me_ref, *refs):
    own_ref, others, out_ref = refs[-2], refs[:-2], refs[-1]
    odd = me_ref[1] == 1
    even, uneven = SHIFTS[len(others) + 1]
    blocks = [own_ref[...]] + [
        jnp.where(odd, others[uneven.index(s)][...], others[even.index(s)][...])
        for s in range(len(others), 0, -1)
    ]
    count = steps * seqs
    asked = (blocks[0].shape[0] - count) // steps
    given = [block[count:, :] for block in blocks]
    ordered = []
    for place in range(len(blocks)):
        chosen = given[0]
        for m in range(1, len(blocks)):
            ahead = lax.rem(place - me_ref[0] + len(blocks), len(blocks))
            chosen = jnp.where(ahead == m, given[m], chosen)
        ordered.append(chosen)
    lanes = []
    for i in range(steps):
        rows = [block[i * seqs : (i + 1) * seqs, :] for block in blocks]
        rows += [chosen[i * asked : (i + 1) * asked, :] for chosen in ordered]
        lanes.append(jnp.concatenate(rows, axis=0))
    both = jnp.concatenate(lanes, axis=1)
    result = dot_nt(both, both[: len(blocks) * seqs])
    half = result.shape[0] // 2
    out_ref[...] = jnp.concatenate([result[:half, :], result[half:, :]], axis=1)


def grams(me, blocks, steps, seqs):
    asked = blocks[0].shape[0] // steps - seqs
    total = len(blocks) * seqs
    whole = pl.BlockSpec(memory_space=pltpu.VMEM)
    return pl.pallas_call(
        functools.partial(grams_kernel, steps, seqs),
        out_shape=jax.ShapeDtypeStruct(((total + len(blocks) * asked) // 2, 2 * total), jnp.float32),
        in_specs=[pl.BlockSpec(memory_space=pltpu.SMEM)] + [whole] * len(blocks),
        out_specs=whole,
        compiler_params=pltpu.CompilerParams(vmem_limit_bytes=VMEM_LIMIT),
        name="grams",
    )(me, *blocks)


def scales(count):
    first = 2.0 / (1.0 + 1.0 / count)
    off = count / (count + 1.0)
    steps = []
    while off > 1e-7:
        steps.append(2.0 / (2.0 - off * off))
        off = off * off / (2.0 - off * off)
    return first, steps


def solve_kernel(seqs, *refs):
    parts, out_ref = refs[:-1], refs[-1]
    packed = (parts[0][...] + parts[1][...]) + (parts[2][...] + parts[3][...])
    lane = lax.broadcasted_iota(jnp.int32, packed.shape, 1)
    turned = pltpu.roll(packed, seqs, 1)
    both = jnp.concatenate(
        [jnp.where(lane < seqs, packed, turned), jnp.where(lane < seqs, turned, packed)], axis=0
    )
    lane = lax.broadcasted_iota(jnp.int32, both.shape, 1)
    row = lax.broadcasted_iota(jnp.int32, both.shape, 0)
    unit = jnp.where((lane & (seqs - 1)) == row, 1.0, 0.0)
    total = jnp.sum(jnp.where(lane == row, both, 0.0)[:seqs], axis=(0, 1), keepdims=True)
    first, steps = scales(seqs)
    state = first * (both / total + unit * (damping / seqs))
    left_lanes = lane < seqs
    for at, step in enumerate(steps):
        high = state.astype(jnp.bfloat16).astype(jnp.float32)
        low = state - high
        left = jnp.where(left_lanes, high, low).astype(jnp.bfloat16)
        high = high[:seqs].astype(jnp.bfloat16)
        low = low[:seqs].astype(jnp.bfloat16)
        right = jnp.concatenate([high, high, low, low], axis=0)
        if at + 1 == len(steps):
            left, state = left[seqs:], state[seqs:]
        product = jnp.dot(
            jnp.concatenate([left, left], axis=1), right, preferred_element_type=jnp.float32
        )
        state = step * (2.0 * state - product)
    out_ref[...] = state[:, : out_ref.shape[1]]


def solve(parts, seqs, asked, seq_dev):
    return pl.pallas_call(
        functools.partial(solve_kernel, seqs),
        out_shape=jax.ShapeDtypeStruct((asked, seq_dev), jnp.float32),
        compiler_params=pltpu.CompilerParams(vmem_limit_bytes=VMEM_LIMIT),
        name="solve",
    )(*parts)


def from_partner(value, axis, size, m):
    return lax.ppermute(value, axis, [(i, i ^ m) for i in range(size)])


def from_partners(value, axis, size):
    return [from_partner(value, axis, size, m) for m in reversed(range(1, size))] + [value]


def from_all(value, sizes):
    parts, blocks = sizes
    came = []
    for shifts in zip(*SHIFTS[blocks]):
        pairs = []
        for i in range(blocks):
            for r in range(parts):
                pairs.append((i * parts + r, (i + shifts[r % 2]) % blocks * parts + r))
        came.append(lax.ppermute(value, ("dp", "tensor"), pairs))
    return came + [value]


def finish_long(message, steps, first, seq_dev):
    every = lax.all_gather(message, "dp", axis=0)
    lanes = message.shape[1]

    def rows_of(block):
        block = block.reshape(block.shape[0], steps, -1, lanes).transpose(0, 2, 1, 3)
        return block.reshape(-1, steps * lanes)

    count = steps * seq_dev
    grads, asked = rows_of(every[:, :count]), rows_of(every[:, count:])
    both = jnp.einsum(
        "ik,jk->ij", jnp.concatenate([grads, asked], axis=0), grads,
        precision=lax.Precision.HIGHEST,
    )
    both = lax.psum(both, "tensor")
    count = grads.shape[0]
    kernel, products = both[:count], both[count:]
    damp = damping * jnp.trace(kernel) / count
    unit = jnp.eye(count, dtype=jnp.float32)
    factor = jnp.linalg.cholesky(kernel + damp * unit)
    picks = lax.dynamic_slice_in_dim(unit, first, seq_dev, 1)
    solved = jax.scipy.linalg.cho_solve((factor, True), picks)
    return jnp.dot(products, solved, precision=lax.Precision.HIGHEST)


def per_device(sizes, inputs, out_grads, in_proj, out_proj, seq_ids, counts, queries):
    parts, blocks = sizes
    rank = in_proj.shape[1]
    seq_dev = counts.shape[0]
    me = lax.axis_index("tensor")
    place = lax.axis_index("dp")
    first = place * seq_dev
    own = 2 * rank // parts
    rank_of = me.reshape(1)
    kept, sent = project(inputs, out_grads, in_proj, out_proj, rank_of, own)
    asked = pick(queries, rank_of, rank, own)
    weights = token_weights(seq_ids, counts, first)
    came = from_partner(sent, "tensor", parts, 1)
    kept, sent = halve(kept, came, rank_of, own)
    came = from_partner(sent, "tensor", parts, 2)
    message = gradients(weights, kept, came, asked)
    steps = own * own // message.shape[1]
    if blocks > SMALL:
        return finish_long(message, steps, first, seq_dev)
    partial = grams(jnp.stack([place, me % 2]), from_all(message, sizes), steps, seq_dev)
    partial = from_partners(partial, "tensor", parts)
    return solve(partial, blocks * seq_dev, blocks * queries.shape[0], seq_dev)


def solution(mesh):
    in_specs = (
        P(("groups", "dp"), "tensor"),
        P(("groups", "dp"), "tensor"),
        P("tensor", None),
        P("tensor", None),
        P(("groups", "dp")),
        P(("groups", "dp")),
        P(("groups", "dp"), None),
    )
    sizes = (mesh.shape["tensor"], mesh.shape["dp"])
    return jax.shard_map(
        functools.partial(per_device, sizes),
        mesh=mesh,
        in_specs=in_specs,
        out_specs=P("groups", "dp"),
        check_vma=False,
    )
```

```python
import functools

import jax
import jax.numpy as jnp
from jax import lax
from jax.experimental import pallas as pl
from jax.experimental.pallas import tpu as pltpu
from jax.sharding import PartitionSpec as P

damping = 0.5
VMEM_LIMIT = 32 * 1024 * 1024
SMALL = 4


def token_weights(seq_ids, counts, first):
    local_ids = seq_ids - first
    slots = jnp.arange(counts.shape[0], dtype=jnp.int32)
    member = local_ids[None, :] == slots[:, None]
    starts = jnp.sum((local_ids[None, :] < slots[:, None]).astype(jnp.int32), axis=1)
    offset = jnp.arange(seq_ids.shape[0], dtype=jnp.int32)[None, :] - starts[:, None]
    scale = 1.0 / counts.astype(jnp.float32)
    return jnp.where(member & (offset < counts[:, None]), scale[:, None], 0.0)


def cuts_of(extent, step):
    return [(at, min(step, extent - at)) for at in range(0, extent, step)]


def two_terms(value):
    high = value.astype(jnp.bfloat16)
    low = (value - high.astype(jnp.float32)).astype(jnp.bfloat16)
    return high, low


def dot_nt(left, right):
    rows = left.shape[0]
    lh, ll = two_terms(left)
    rh, rl = two_terms(right)
    mul = functools.partial(
        lax.dot_general,
        dimension_numbers=(((1,), (1,)), ((), ())),
        preferred_element_type=jnp.float32,
    )
    both = mul(jnp.concatenate([lh, ll], axis=0), rh)
    return both[:rows] + (mul(lh, rl) + both[rows:])


def project_kernel(own, rank_ref, x_hbm, g_hbm, wx_hbm, wg_hbm, keep_ref, send_ref, *scratch):
    x_ref, g_ref, wx_ref, wg_ref, wide_ref, sems = scratch
    copies = []

    def fetch(src, dst, index):
        copy = pltpu.make_async_copy(src, dst, sems.at[index])
        copy.start()
        return copy

    g_cuts = cuts_of(g_ref.shape[1], 1024)
    x_cuts = cuts_of(x_ref.shape[0], 1024)
    wg_copy = fetch(wg_hbm, wg_ref, 0)
    index = 2
    g_copies = []
    for at, size in g_cuts:
        columns = pl.ds(at, size)
        g_copies.append(fetch(g_hbm.at[:, columns], g_ref.at[:, columns], index))
        index += 1
    wx_copy = fetch(wx_hbm, wx_ref, 1)
    x_copies = []
    for at, size in x_cuts:
        rows = pl.ds(at, size)
        x_copies.append(fetch(x_hbm.at[rows, :], x_ref.at[rows, :], index))
        index += 1

    def product(copies, terms):
        total = None
        for copy, (left, right, along) in zip(copies, terms):
            copy.wait()
            term = lax.dot_general(
                left(), right(), (((1,), (along,)), ((), ())), preferred_element_type=jnp.float32
            )
            total = term if total is None else total + term
        return total

    def cut(ref, at, size, along):
        return lambda: ref[at : at + size, :] if along == 0 else ref[:, at : at + size]

    wg_copy.wait()
    grads_t = product(
        g_copies, [(cut(g_ref, at, size, 1), cut(wg_ref, at, size, 1), 1) for at, size in g_cuts]
    ).T
    wx_copy.wait()
    wide_ref[...] = product(
        x_copies, [(cut(wx_ref, at, size, 1), cut(x_ref, at, size, 0), 0) for at, size in x_cuts]
    )
    rank = grads_t.shape[0]
    side = rank_ref[0] & 1
    for out, taken in ((keep_ref, side), (send_ref, side ^ 1)):
        out[:rank, :] = grads_t
        out[rank:, :] = wide_ref[pl.ds(pl.multiple_of(taken * own, own), own), :]


def project(inputs, out_grads, in_proj, out_proj, me, own):
    rank = in_proj.shape[1]
    tokens, hidden = inputs.shape
    width = out_grads.shape[1]
    copies = 2 + len(cuts_of(width, 1024)) + len(cuts_of(hidden, 1024))
    arrays = (inputs.T, out_grads, in_proj.T, out_proj.T)
    in_hbm = pl.BlockSpec(memory_space=pltpu.HBM)
    return pl.pallas_call(
        functools.partial(project_kernel, own),
        out_shape=[jax.ShapeDtypeStruct((rank + own, tokens), jnp.float32)] * 2,
        in_specs=[pl.BlockSpec(memory_space=pltpu.SMEM)] + [in_hbm] * len(arrays),
        out_specs=[pl.BlockSpec(memory_space=pltpu.VMEM)] * 2,
        scratch_shapes=[
            pltpu.VMEM((hidden, tokens), jnp.bfloat16),
            pltpu.VMEM((tokens, width), jnp.bfloat16),
            pltpu.VMEM((rank, hidden), jnp.bfloat16),
            pltpu.VMEM((rank, width), jnp.bfloat16),
            pltpu.VMEM((rank, tokens), jnp.float32),
            pltpu.SemaphoreType.DMA((copies,)),
        ],
        compiler_params=pltpu.CompilerParams(vmem_limit_bytes=VMEM_LIMIT),
        name="project",
    )(me, *(pltpu.with_memory_space_constraint(array, pltpu.HBM) for array in arrays))


def halve_kernel(own, rank_ref, kept_ref, came_ref, keep_ref, send_ref, sum_ref):
    sum_ref[...] = kept_ref[...] + came_ref[...]
    place = rank_ref[0] // 2
    for out, taken in ((keep_ref, place), (send_ref, place ^ 1)):
        out[:own, :] = sum_ref[pl.ds(pl.multiple_of(taken * own, own), own), :]
        out[own:, :] = sum_ref[-own:, :]


def halve(kept, came, me, own):
    rows, tokens = kept.shape
    whole = pl.BlockSpec(memory_space=pltpu.VMEM)
    return pl.pallas_call(
        functools.partial(halve_kernel, own),
        out_shape=[jax.ShapeDtypeStruct((2 * own, tokens), jnp.float32)] * 2,
        in_specs=[pl.BlockSpec(memory_space=pltpu.SMEM), whole, whole],
        out_specs=[whole] * 2,
        scratch_shapes=[pltpu.VMEM((rows, tokens), jnp.float32)],
        compiler_params=pltpu.CompilerParams(vmem_limit_bytes=VMEM_LIMIT),
        name="halve",
    )(me, kept, came)


def pick_kernel(rank, own, rank_ref, queries_ref, out_ref):
    lanes = out_ref.shape[1]
    wide = lanes * rank // own
    steps = own * own // lanes
    asked = queries_ref.shape[0]
    me = rank_ref[0]
    start = (me // 2) * (own * rank)
    rows = jnp.concatenate(
        [
            queries_ref[:, pl.ds(pl.multiple_of(start + i * wide, lanes), wide)]
            for i in range(steps)
        ],
        axis=0,
    )
    source = lax.broadcasted_iota(jnp.int32, (wide, lanes), 0)
    place = lax.broadcasted_iota(jnp.int32, (wide, lanes), 1)
    wanted = (place // own) * rank + place % own + (me & 1) * own
    chosen = jnp.where(source == wanted, 1.0, 0.0).astype(jnp.bfloat16)
    high = rows.astype(jnp.bfloat16)
    rest = rows - high.astype(jnp.float32)
    middle = rest.astype(jnp.bfloat16)
    low = (rest - middle.astype(jnp.float32)).astype(jnp.bfloat16)
    terms = [
        jnp.dot(term, chosen, preferred_element_type=jnp.float32) for term in (high, middle, low)
    ]
    out_ref[...] = terms[0] + (terms[1] + terms[2])


def pick(queries, me, rank, own):
    lanes = 128
    rows = queries.shape[0] * own * own // lanes
    whole = pl.BlockSpec(memory_space=pltpu.VMEM)
    return pl.pallas_call(
        functools.partial(pick_kernel, rank, own),
        out_shape=jax.ShapeDtypeStruct((rows, lanes), jnp.float32),
        in_specs=[pl.BlockSpec(memory_space=pltpu.SMEM), whole],
        out_specs=whole,
        compiler_params=pltpu.CompilerParams(vmem_limit_bytes=VMEM_LIMIT),
        name="pick",
    )(me, queries)


def grads_kernel(weights_ref, kept_ref, came_ref, asked_ref, out_ref):
    summed = kept_ref[...] + came_ref[...]
    weights = weights_ref[...]
    own = summed.shape[0] // 2
    group = out_ref.shape[1] // own
    inputs_t = summed[own:, :]
    zero = jnp.zeros_like(inputs_t)
    half = group // 2
    right = jnp.concatenate(
        [
            jnp.concatenate([inputs_t if j == k else zero for k in range(half)], axis=1)
            for j in range(half)
        ],
        axis=0,
    )
    made = []
    for first in (0, half):
        rows = []
        for i in range(first, own, group):
            rows.append(
                jnp.concatenate(
                    [weights * summed[i + j : i + j + 1, :] for j in range(half)], axis=1
                )
            )
        made.append(dot_nt(jnp.concatenate(rows, axis=0), right))
    count = made[0].shape[0]
    out_ref[:count, :] = jnp.concatenate(made, axis=1)
    out_ref[count:, :] = asked_ref[...]


def gradients(weights, kept, came, asked):
    lanes = asked.shape[1]
    own = kept.shape[0] // 2
    rows = own * own // lanes * weights.shape[0] + asked.shape[0]
    return pl.pallas_call(
        grads_kernel,
        out_shape=jax.ShapeDtypeStruct((rows, lanes), jnp.float32),
        compiler_params=pltpu.CompilerParams(vmem_limit_bytes=VMEM_LIMIT),
        name="gradients",
    )(weights, kept, came, asked)


def grams_kernel(steps, seqs, me_ref, *refs):
    blocks, out_ref = refs[-2::-1], refs[-1]
    count = steps * seqs
    asked = (blocks[0].shape[0] - count) // steps
    given = [block[count:, :] for block in blocks]
    ordered = []
    for place in range(len(blocks)):
        chosen = given[0]
        for m in range(1, len(blocks)):
            ahead = lax.rem(place - me_ref[0] + len(blocks), len(blocks))
            chosen = jnp.where(ahead == m, given[m], chosen)
        ordered.append(chosen)
    lanes = []
    for i in range(steps):
        rows = [block[i * seqs : (i + 1) * seqs, :] for block in blocks]
        rows += [chosen[i * asked : (i + 1) * asked, :] for chosen in ordered]
        lanes.append(jnp.concatenate(rows, axis=0))
    both = jnp.concatenate(lanes, axis=1)
    result = dot_nt(both, both[: len(blocks) * seqs])
    half = result.shape[0] // 2
    out_ref[...] = jnp.concatenate([result[:half, :], result[half:, :]], axis=1)


def grams(me, blocks, steps, seqs):
    asked = blocks[0].shape[0] // steps - seqs
    total = len(blocks) * seqs
    whole = pl.BlockSpec(memory_space=pltpu.VMEM)
    return pl.pallas_call(
        functools.partial(grams_kernel, steps, seqs),
        out_shape=jax.ShapeDtypeStruct(((total + len(blocks) * asked) // 2, 2 * total), jnp.float32),
        in_specs=[pl.BlockSpec(memory_space=pltpu.SMEM)] + [whole] * len(blocks),
        out_specs=whole,
        compiler_params=pltpu.CompilerParams(vmem_limit_bytes=VMEM_LIMIT),
        name="grams",
    )(me, *blocks)


def scales(count):
    first = 2.0 / (1.0 + 1.0 / count)
    off = count / (count + 1.0)
    steps = []
    while off > 1e-7:
        steps.append(2.0 / (2.0 - off * off))
        off = off * off / (2.0 - off * off)
    return first, steps


def solve_kernel(seqs, *refs):
    parts, out_ref = refs[:-1], refs[-1]
    packed = (parts[0][...] + parts[1][...]) + (parts[2][...] + parts[3][...])
    lane = lax.broadcasted_iota(jnp.int32, packed.shape, 1)
    turned = pltpu.roll(packed, seqs, 1)
    both = jnp.concatenate(
        [jnp.where(lane < seqs, packed, turned), jnp.where(lane < seqs, turned, packed)], axis=0
    )
    lane = lax.broadcasted_iota(jnp.int32, both.shape, 1)
    row = lax.broadcasted_iota(jnp.int32, both.shape, 0)
    unit = jnp.where((lane & (seqs - 1)) == row, 1.0, 0.0)
    total = jnp.sum(jnp.where(lane == row, both, 0.0)[:seqs], axis=(0, 1), keepdims=True)
    first, steps = scales(seqs)
    state = first * (both / total + unit * (damping / seqs))
    left_lanes = lane < seqs
    for at, step in enumerate(steps):
        high = state.astype(jnp.bfloat16).astype(jnp.float32)
        low = state - high
        left = jnp.where(left_lanes, high, low).astype(jnp.bfloat16)
        high = high[:seqs].astype(jnp.bfloat16)
        low = low[:seqs].astype(jnp.bfloat16)
        right = jnp.concatenate([high, high, low, low], axis=0)
        if at + 1 == len(steps):
            left, state = left[seqs:], state[seqs:]
        product = jnp.dot(
            jnp.concatenate([left, left], axis=1), right, preferred_element_type=jnp.float32
        )
        state = step * (2.0 * state - product)
    out_ref[...] = state[:, : out_ref.shape[1]]


def solve(parts, seqs, asked, seq_dev):
    return pl.pallas_call(
        functools.partial(solve_kernel, seqs),
        out_shape=jax.ShapeDtypeStruct((asked, seq_dev), jnp.float32),
        compiler_params=pltpu.CompilerParams(vmem_limit_bytes=VMEM_LIMIT),
        name="solve",
    )(*parts)


def from_partner(value, axis, size, m):
    return lax.ppermute(value, axis, [(i, i ^ m) for i in range(size)])


def from_partners(value, axis, size):
    return [from_partner(value, axis, size, m) for m in reversed(range(1, size))] + [value]


def from_all(value, axis, size):
    shifts = [[(i, (i + s) % size) for i in range(size)] for s in range(1, size)]
    return [lax.ppermute(value, axis, shift) for shift in shifts] + [value]


def finish_long(message, steps, first, seq_dev):
    every = lax.all_gather(message, "dp", axis=0)
    lanes = message.shape[1]

    def rows_of(block):
        block = block.reshape(block.shape[0], steps, -1, lanes).transpose(0, 2, 1, 3)
        return block.reshape(-1, steps * lanes)

    count = steps * seq_dev
    grads, asked = rows_of(every[:, :count]), rows_of(every[:, count:])
    both = jnp.einsum(
        "ik,jk->ij", jnp.concatenate([grads, asked], axis=0), grads,
        precision=lax.Precision.HIGHEST,
    )
    both = lax.psum(both, "tensor")
    count = grads.shape[0]
    kernel, products = both[:count], both[count:]
    damp = damping * jnp.trace(kernel) / count
    unit = jnp.eye(count, dtype=jnp.float32)
    factor = jnp.linalg.cholesky(kernel + damp * unit)
    picks = lax.dynamic_slice_in_dim(unit, first, seq_dev, 1)
    solved = jax.scipy.linalg.cho_solve((factor, True), picks)
    return jnp.dot(products, solved, precision=lax.Precision.HIGHEST)


def per_device(sizes, inputs, out_grads, in_proj, out_proj, seq_ids, counts, queries):
    parts, blocks = sizes
    rank = in_proj.shape[1]
    seq_dev = counts.shape[0]
    me = lax.axis_index("tensor")
    place = lax.axis_index("dp")
    first = place * seq_dev
    own = 2 * rank // parts
    rank_of = me.reshape(1)
    kept, sent = project(inputs, out_grads, in_proj, out_proj, rank_of, own)
    asked = pick(queries, rank_of, rank, own)
    weights = token_weights(seq_ids, counts, first)
    came = from_partner(sent, "tensor", parts, 1)
    kept, sent = halve(kept, came, rank_of, own)
    came = from_partner(sent, "tensor", parts, 2)
    message = gradients(weights, kept, came, asked)
    steps = own * own // message.shape[1]
    if blocks > SMALL:
        return finish_long(message, steps, first, seq_dev)
    partial = grams(place.reshape(1), from_all(message, "dp", blocks), steps, seq_dev)
    partial = from_partners(partial, "tensor", parts)
    return solve(partial, blocks * seq_dev, blocks * queries.shape[0], seq_dev)


def solution(mesh):
    in_specs = (
        P(("groups", "dp"), "tensor"),
        P(("groups", "dp"), "tensor"),
        P("tensor", None),
        P("tensor", None),
        P(("groups", "dp")),
        P(("groups", "dp")),
        P(("groups", "dp"), None),
    )
    sizes = (mesh.shape["tensor"], mesh.shape["dp"])
    return jax.shard_map(
        functools.partial(per_device, sizes),
        mesh=mesh,
        in_specs=in_specs,
        out_specs=P("groups", "dp"),
        check_vma=False,
    )
```
